32 devices in a mesh: seq: 8 (over y, x, core), head: 4 (over z).
Axes of the slice: x: 2, y: 2, z: 4, core: 2. Of those that a mesh axis runs over, the one named last changes fastest.
Arguments:
- query: bfloat16 [6144, 4096], P('seq', 'head'), may hold values from -6 to 6
- key_in: bfloat16 [6144, 4096], P('seq', 'head'), may hold values from -6 to 6
- value: bfloat16 [6144, 4096], P('seq', 'head'), may hold values from -60 to 60
- out_grad: bfloat16 [6144, 4096], P('seq', 'head'), may hold values from -6 to 6
- gain: float32 [4096], P('head'), may hold values from 0.1 to 1.9
Outputs:
- query_grad: bfloat16 [6144, 4096], P('seq', 'head')
- key_grad: bfloat16 [6144, 4096], P('seq', 'head')
- value_grad: bfloat16 [6144, 4096], P('seq', 'head')
The draws below stay inside these ranges and needn't reach their ends.
All inputs are finite; a program needn't handle non-finite values.
Results may differ from the reference program's by a relative error of at most 0.0058.
Values sent between devices are 32-bit elements; how exact they have to be, the bound alone decides.
No kernel may reach another device: no remote copies, remote signals or barrier semaphores. Data moves between devices by JAX's collectives and lax.ppermute only.
A program may use at most 128 MiB of HBM per device.

```python
import jax
import jax.numpy as jnp
from jax import lax

HEAD_DIM = 128
HEADS = 32
TOK_DEV = 768
TOKENS = 6144


def draw_value(key, part):
    width = HEADS * HEAD_DIM
    first, second = jax.random.split(key, 2)
    head_of = (jnp.arange(width) // HEAD_DIM).astype(jnp.float32)
    rising = 3.0 ** (head_of / max(HEADS - 1, 1))
    spread = 10.0 ** jax.random.uniform(second, (width,), jnp.float32, -0.5, 0.5)
    base = jnp.clip(jax.random.normal(first, (TOKENS, width), jnp.float32), -6.0, 6.0)
    return (base * rising * spread).astype(jnp.bfloat16)


def block_scale(stream_key, shape, shards, least, high):
    level, own = 1.0, jax.random.fold_in(stream_key, 6)
    for position, shards_of in shards:
        steps = jnp.exp(jax.random.uniform(jax.random.fold_in(own, position), (shards_of,), jnp.float32, least / len(shards), high / len(shards)))
        level = level * jnp.repeat(steps, shape[position] // shards_of).reshape([-1 if axis == position else 1 for axis in range(len(shape))])
    return level


def bell_draw(own_key, extent, scale, limit, shards=(), kind=jnp.bfloat16):
    entries = scale * jax.random.normal(own_key, extent, jnp.float32)
    if shards:
        entries = entries * block_scale(own_key, extent, shards, -0.22, 0.18)
    return jnp.clip(entries, -limit, limit).astype(kind)


def setup_inputs(seed: int = 0) -> dict:
    keys = jax.random.split(jax.random.key(seed), 6)
    query = bell_draw(keys[0], (TOKENS, HEADS * HEAD_DIM), 1.0, 6.0, ((0, 8), (1, 4)))
    key_in = bell_draw(keys[1], (TOKENS, HEADS * HEAD_DIM), 1.0, 6.0, ((0, 8), (1, 4)))
    value = draw_value(jax.random.fold_in(keys[5], 71), 0)
    out_grad = bell_draw(keys[3], (TOKENS, HEADS * HEAD_DIM), 1.0, 6.0, ((0, 8), (1, 4)))
    gain = jnp.clip(1.0 + 0.18 * jax.random.normal(keys[4], (HEADS * HEAD_DIM,), jnp.float32), 0.1, 1.9)
    return dict(query=query, key_in=key_in, value=value, out_grad=out_grad, gain=gain)


def heads_first(x):
    blocks = TOKENS // TOK_DEV
    return x.reshape(blocks, TOK_DEV, HEADS, HEAD_DIM).transpose(2, 0, 1, 3)

def tokens_first(x):
    return x.transpose(1, 2, 0, 3).reshape(TOKENS, HEADS * HEAD_DIM)

def causal_mask():
    rows = jnp.arange(TOK_DEV)[:, None]
    cols = jnp.arange(TOK_DEV)[None, :]
    return rows >= cols

def forward_head(args):
    qpart, kpart, vpart, state = args
    qf = qpart.astype(jnp.float32)
    scores = jnp.einsum('ctd,csd->cts', qf, kpart.astype(jnp.float32))
    scores = jnp.where(causal_mask()[None], scores, 0.0).astype(jnp.bfloat16)
    inner = jnp.einsum('cts,cse->cte', scores.astype(jnp.float32), vpart.astype(jnp.float32))
    outer = jnp.einsum('ctd,cde->cte', qf, state.astype(jnp.float32))
    return inner + outer

def backward_head(args):
    qpart, kpart, vpart, gpart, state, gstate = args
    qf = qpart.astype(jnp.float32)
    kf = kpart.astype(jnp.float32)
    vf = vpart.astype(jnp.float32)
    gf = gpart.astype(jnp.float32)
    mask = causal_mask()[None]
    scores = jnp.where(mask, jnp.einsum('ctd,csd->cts', qf, kf), 0.0).astype(jnp.bfloat16).astype(jnp.float32)
    gscores = jnp.where(mask, jnp.einsum('cte,cse->cts', gf, vf), 0.0).astype(jnp.bfloat16).astype(jnp.float32)
    sf = state.astype(jnp.float32)
    gsf = gstate.astype(jnp.float32)
    qgrad = jnp.einsum('cts,csd->ctd', gscores, kf) + jnp.einsum('cte,cde->ctd', gf, sf)
    kgrad = jnp.einsum('cts,ctd->csd', gscores, qf) + jnp.einsum('cse,cde->csd', vf, gsf)
    vgrad = jnp.einsum('cts,cte->cse', scores, gf) + jnp.einsum('csd,cde->cse', kf, gsf)
    return (qgrad.astype(jnp.bfloat16), kgrad.astype(jnp.bfloat16), vgrad.astype(jnp.bfloat16))

def reference(query, key_in, value, out_grad, gain):
    qh = heads_first(query)
    kh = heads_first(key_in)
    vh = heads_first(value)
    kv_local = jnp.einsum('hctd,hcte->hcde', kh.astype(jnp.float32), vh.astype(jnp.float32))
    zero_state = jnp.zeros((HEADS, 1, HEAD_DIM, HEAD_DIM), jnp.float32)
    kv_before = jnp.concatenate([zero_state, jnp.cumsum(kv_local, axis=1)[:, :-1]], axis=1).astype(jnp.bfloat16)
    attn = tokens_first(lax.map(forward_head, (qh, kh, vh, kv_before)))
    full = HEADS * HEAD_DIM
    scaled = gain[None, :] * out_grad.astype(jnp.float32)
    square_mean = lax.optimization_barrier(jnp.sum(attn * attn, axis=1)) / full
    cross_mean = lax.optimization_barrier(jnp.sum(scaled * attn, axis=1)) / full
    inv = lax.rsqrt(square_mean + 1e-06)
    attn_grad = (inv[:, None] * scaled - attn * (inv * inv * inv * cross_mean)[:, None]).astype(jnp.bfloat16)
    gh = heads_first(attn_grad)
    dkv_local = jnp.einsum('hctd,hcte->hcde', qh.astype(jnp.float32), gh.astype(jnp.float32))
    reversed_sum = jnp.cumsum(jnp.flip(dkv_local, 1), axis=1)
    dkv_after = jnp.flip(jnp.concatenate([zero_state, reversed_sum[:, :-1]], axis=1), 1).astype(jnp.bfloat16)
    qgrad, kgrad, vgrad = lax.map(backward_head, (qh, kh, vh, gh, kv_before, dkv_after))
    return (tokens_first(qgrad), tokens_first(kgrad), tokens_first(vgrad))
```

```python
import functools

import jax
import jax.numpy as jnp
from jax import lax
from jax.experimental import pallas as pl
from jax.experimental.pallas import tpu as pltpu
from jax.sharding import PartitionSpec as P

HEAD_DIM = 128
CHUNK = 256
GROUP = 2
VMEM_BYTES = 24 * 2**20
F32 = jnp.float32
BF16 = jnp.bfloat16


def dot(a, b, contract_a=1, contract_b=0):
    dims = (((contract_a,), (contract_b,)), ((), ()))
    return lax.dot_general(a, b, dims, preferred_element_type=F32)


def chunk_of(rows):
    return CHUNK if rows % CHUNK == 0 else rows


def call(kernel, flops, nbytes, **kwargs):
    return pl.pallas_call(
        kernel,
        cost_estimate=pl.CostEstimate(flops=flops, bytes_accessed=nbytes, transcendentals=0),
        compiler_params=pltpu.CompilerParams(vmem_limit_bytes=VMEM_BYTES),
        **kwargs,
    )


def column(rows, width):
    return pl.BlockSpec((rows, width), lambda g: (0, g))


def whole(*shape):
    return pl.BlockSpec(shape, lambda g: (0,) * len(shape))


def parity(backward):
    rank = lax.axis_index("seq")
    if backward:
        rank = lax.axis_size("seq") - 1 - rank
    return lax.rem(rank, 2)


def store_half(keep_ref, send_ref, head, value, backward):
    half = keep_ref.shape[0]
    mine = (head // half) == parity(backward)
    slot = head % half

    @pl.when(mine)
    def _():
        keep_ref[slot] = value

    @pl.when(jnp.logical_not(mine))
    def _():
        send_ref[slot] = value


def load_half(mine_ref, extra_ref, other_ref, head, backward):
    half = mine_ref.shape[0]
    odd = parity(backward)
    slot = head % half
    own = mine_ref[slot] + jnp.where(odd == 1, extra_ref[slot], 0.0)
    return jnp.where((head // half) == odd, own, other_ref[slot])


def heads_of(width):
    return width // HEAD_DIM


def state_kernel(k_ref, v_ref, keep_ref, send_ref, pre_ref):
    rows = k_ref.shape[0]
    chunk = chunk_of(rows)
    for j in range(GROUP):
        lanes = slice(j * HEAD_DIM, (j + 1) * HEAD_DIM)
        total = None
        for i in range(rows // chunk):
            part = slice(i * chunk, (i + 1) * chunk)
            term = dot(k_ref[part, lanes], v_ref[part, lanes], 0, 0)
            pre_ref[j, i] = (jnp.zeros_like(term) if total is None else total).astype(BF16)
            total = term if total is None else total + term
        store_half(keep_ref, send_ref, pl.program_id(0) * GROUP + j, total, False)


def lower(chunk):
    row = lax.broadcasted_iota(jnp.int32, (chunk, chunk), 0)
    col = lax.broadcasted_iota(jnp.int32, (chunk, chunk), 1)
    return row >= col


def upper(chunk):
    row = lax.broadcasted_iota(jnp.int32, (chunk, chunk), 0)
    col = lax.broadcasted_iota(jnp.int32, (chunk, chunk), 1)
    return row <= col


def inner_kernel(q_ref, k_ref, v_ref, pre_ref, inner_ref):
    rows = q_ref.shape[0]
    chunk = chunk_of(rows)
    keep = lower(chunk)
    for j in range(GROUP):
        lanes = slice(j * HEAD_DIM, (j + 1) * HEAD_DIM)
        for i in range(rows // chunk):
            part = slice(i * chunk, (i + 1) * chunk)
            q = q_ref[part, lanes]
            scores = jnp.where(keep, dot(q, k_ref[part, lanes], 1, 1), 0.0).astype(BF16)
            total = dot(scores, v_ref[part, lanes])
            if i:
                total = total + dot(q, pre_ref[j, i])
            inner_ref[part, lanes] = total


def attn_kernel(
    q_ref, inner_ref, og_ref, gain_ref, mine_ref, extra_ref, other_ref,
    attn_ref, state_ref, sums_ref, square_ref, cross_ref,
):
    g = pl.program_id(0)

    @pl.when(g == 0)
    def _():
        square_ref[...] = jnp.zeros_like(square_ref)
        cross_ref[...] = jnp.zeros_like(cross_ref)

    for j in range(GROUP):
        lanes = slice(j * HEAD_DIM, (j + 1) * HEAD_DIM)
        state = load_half(mine_ref, extra_ref, other_ref, g * GROUP + j, False).astype(BF16)
        state_ref[j] = state
        attn = inner_ref[:, lanes] + dot(q_ref[:, lanes], state)
        attn_ref[:, lanes] = attn
        scaled = gain_ref[:, lanes] * og_ref[:, lanes].astype(F32)
        square_ref[...] += attn * attn
        cross_ref[...] += scaled * attn

    @pl.when(g == pl.num_programs(0) - 1)
    def _():
        square = jnp.sum(square_ref[...].T, axis=0, keepdims=True)
        cross = jnp.sum(cross_ref[...].T, axis=0, keepdims=True)
        row = lax.broadcasted_iota(jnp.int32, sums_ref.shape, 0)
        sums_ref[...] = jnp.where(row == 0, square, jnp.where(row == 1, cross, 0.0))


def grad_kernel(full, parts, *refs):
    sums = refs[:parts]
    attn_ref, og_ref, q_ref, gain_ref, g_ref, keep_ref, send_ref, post_ref, inv_ref, mean_ref = refs[parts:]
    g = pl.program_id(0)
    rows = q_ref.shape[0]
    chunk = chunk_of(rows)

    @pl.when(g == 0)
    def _():
        total = sums[0][...]
        for ref in sums[1:]:
            total = total + ref[...]
        inv = lax.rsqrt(total[0:1] / full + 1e-6)
        slope = inv * inv * inv * (total[1:2] / full)
        row = lax.broadcasted_iota(jnp.int32, total.shape, 0)
        both = jnp.where(row == 0, inv, slope).T
        inv_ref[...] = jnp.broadcast_to(both[:, 0:1], inv_ref.shape)
        mean_ref[...] = jnp.broadcast_to(both[:, 1:2], mean_ref.shape)

    for j in range(GROUP):
        lanes = slice(j * HEAD_DIM, (j + 1) * HEAD_DIM)
        total = None
        for i in reversed(range(rows // chunk)):
            part = slice(i * chunk, (i + 1) * chunk)
            scaled = gain_ref[:, lanes] * og_ref[part, lanes].astype(F32)
            grad = (inv_ref[part] * scaled - attn_ref[part, lanes] * mean_ref[part]).astype(BF16)
            g_ref[part, lanes] = grad
            term = dot(q_ref[part, lanes], grad, 0, 0)
            post_ref[j, i] = (jnp.zeros_like(term) if total is None else total).astype(BF16)
            total = term if total is None else total + term
        store_half(keep_ref, send_ref, g * GROUP + j, total, True)


def local_kernel(q_ref, k_ref, v_ref, g_ref, state_ref, pre_ref, post_ref, qgrad_ref, kpart_ref, vpart_ref):
    rows = q_ref.shape[0]
    chunk = chunk_of(rows)
    low, up = lower(chunk), upper(chunk)
    count = rows // chunk
    for j in range(GROUP):
        lanes = slice(j * HEAD_DIM, (j + 1) * HEAD_DIM)
        for i in range(count):
            part = slice(i * chunk, (i + 1) * chunk)
            q, k, v, g = (ref[part, lanes] for ref in (q_ref, k_ref, v_ref, g_ref))
            gscores = jnp.where(low, dot(g, v, 1, 1), 0.0).astype(BF16)
            gturned = jnp.where(up, dot(v, g, 1, 1), 0.0).astype(BF16)
            turned = jnp.where(up, dot(k, q, 1, 1), 0.0).astype(BF16)
            qgrad = dot(gscores, k) + dot(g, state_ref[j], 1, 1)
            if i:
                qgrad = qgrad + dot(g, pre_ref[j, i], 1, 1)
            kgrad = dot(gturned, q)
            vgrad = dot(turned, g)
            if i < count - 1:
                kgrad = kgrad + dot(v, post_ref[j, i], 1, 1)
                vgrad = vgrad + dot(k, post_ref[j, i])
            qgrad_ref[part, lanes] = qgrad.astype(BF16)
            kpart_ref[part, lanes] = kgrad
            vpart_ref[part, lanes] = vgrad


def final_kernel(k_ref, v_ref, kpart_ref, vpart_ref, mine_ref, extra_ref, other_ref, kgrad_ref, vgrad_ref):
    for j in range(GROUP):
        lanes = slice(j * HEAD_DIM, (j + 1) * HEAD_DIM)
        head = pl.program_id(0) * GROUP + j
        state = load_half(mine_ref, extra_ref, other_ref, head, True).astype(BF16)
        kgrad_ref[:, lanes] = (kpart_ref[:, lanes] + dot(v_ref[:, lanes], state, 1, 1)).astype(BF16)
        vgrad_ref[:, lanes] = (vpart_ref[:, lanes] + dot(k_ref[:, lanes], state)).astype(BF16)


def scan_states(keep, send, backward):
    count = lax.axis_size("seq")
    bits = count.bit_length() - 1
    rank = lax.axis_index("seq")
    if backward:
        rank = count - 1 - rank
    odd = lax.rem(rank, 2) == 1

    def move(value, pairs):
        if backward:
            pairs = [(count - 1 - a, count - 1 - b) for a, b in pairs]
        return lax.ppermute(value, "seq", pairs)

    nearby = [(r, r ^ 1) for r in range(count)]
    extra = move(send, nearby)
    total, before = keep + extra, jnp.zeros_like(keep)
    for stage in range(bits - 1):
        rising, falling = 1 + stage, bits - 1 - stage
        pairs = []
        for r in range(count):
            bit = falling if r & 1 else rising
            high = (r >> bit) & 1
            useless = stage == 0 if r & 1 else stage == bits - 2
            if not (high and useless):
                pairs.append((r, r ^ (1 << bit)))
        high = (jnp.where(odd, rank >> falling, rank >> rising) & 1) == 1
        message = jnp.where(odd, before + jnp.where(high, 0.0, total), total)
        came = move(message, pairs)
        total = jnp.where(odd, total, total + came)
        before = before + jnp.where(odd | high, came, 0.0)
    other = move(jnp.where(odd, before, before + keep), nearby)
    return before, extra, other


def shards(query, key_in, value, out_grad, gain):
    rows, width = query.shape
    heads = heads_of(width)
    half = heads // 2
    chunks = rows // chunk_of(rows)
    steps = heads // GROUP
    full = width * lax.axis_size("head")
    gain = gain.reshape(1, width)
    square = rows * HEAD_DIM * HEAD_DIM * 2 * heads
    size = rows * width

    cols = column(rows, GROUP * HEAD_DIM)
    gain_cols = column(1, GROUP * HEAD_DIM)
    halves = whole(half, HEAD_DIM, HEAD_DIM)
    inside = pl.BlockSpec((GROUP, chunks, HEAD_DIM, HEAD_DIM), lambda g: (g, 0, 0, 0))
    one = pl.BlockSpec((GROUP, HEAD_DIM, HEAD_DIM), lambda g: (g, 0, 0))
    sums_spec = whole(8, rows)

    half_shape = jax.ShapeDtypeStruct((half, HEAD_DIM, HEAD_DIM), F32)
    inside_shape = jax.ShapeDtypeStruct((heads, chunks, HEAD_DIM, HEAD_DIM), BF16)
    wide = jax.ShapeDtypeStruct((rows, width), F32)
    thin = jax.ShapeDtypeStruct((rows, width), BF16)

    keep, send, pre = call(
        state_kernel, square, 4 * size,
        grid=(steps,),
        in_specs=[cols, cols],
        out_specs=[halves, halves, inside],
        out_shape=[half_shape, half_shape, inside_shape],
    )(key_in, value)
    before = scan_states(keep, send, False)

    inner = call(
        inner_kernel, 5 * square, 10 * size,
        grid=(steps,),
        in_specs=[cols, cols, cols, inside],
        out_specs=cols,
        out_shape=wide,
    )(query, key_in, value, pre)

    attn, state, sums = call(
        attn_kernel, square, 12 * size,
        grid=(steps,),
        in_specs=[cols, cols, cols, gain_cols, halves, halves, halves],
        out_specs=[cols, one, sums_spec],
        out_shape=[
            wide,
            jax.ShapeDtypeStruct((heads, HEAD_DIM, HEAD_DIM), BF16),
            jax.ShapeDtypeStruct((8, rows), F32),
        ],
        scratch_shapes=[pltpu.VMEM((rows, HEAD_DIM), F32), pltpu.VMEM((rows, HEAD_DIM), F32)],
    )(query, inner, out_grad, gain, *before)

    peers = lax.axis_size("head")
    parts = [sums] + [
        lax.ppermute(sums, "head", [(r, (r + shift) % peers) for r in range(peers)])
        for shift in range(1, peers)
    ]

    grad, gkeep, gsend, post = call(
        functools.partial(grad_kernel, full, peers), square, 10 * size,
        grid=(steps,),
        in_specs=[sums_spec] * peers + [cols, cols, cols, gain_cols],
        out_specs=[cols, halves, halves, inside],
        out_shape=[thin, half_shape, half_shape, inside_shape],
        scratch_shapes=[pltpu.VMEM((rows, HEAD_DIM), F32), pltpu.VMEM((rows, HEAD_DIM), F32)],
    )(*parts, attn, out_grad, query, gain)
    after = scan_states(gkeep, gsend, True)

    qgrad, kpart, vpart = call(
        local_kernel, 15 * square, 18 * size,
        grid=(steps,),
        in_specs=[cols, cols, cols, cols, one, inside, inside],
        out_specs=[cols, cols, cols],
        out_shape=[thin, wide, wide],
    )(query, key_in, value, grad, state, pre, post)

    kgrad, vgrad = call(
        final_kernel, 2 * square, 16 * size,
        grid=(steps,),
        in_specs=[cols, cols, cols, cols, halves, halves, halves],
        out_specs=[cols, cols],
        out_shape=[thin, thin],
    )(key_in, value, kpart, vpart, *after)
    return qgrad, kgrad, vgrad


def solution(mesh):
    spec = P("seq", "head")
    return jax.shard_map(
        shards,
        mesh=mesh,
        in_specs=(spec, spec, spec, spec, P("head")),
        out_specs=(spec, spec, spec),
        check_vma=False,
    )
```

```python
import functools

import jax
import jax.numpy as jnp
from jax import lax
from jax.experimental import pallas as pl
from jax.experimental.pallas import tpu as pltpu
from jax.sharding import PartitionSpec as P

HEAD_DIM = 128
CHUNK = 256
VMEM_BYTES = 16 * 2**20
F32 = jnp.float32
BF16 = jnp.bfloat16


def dot(a, b, contract_a=1, contract_b=0):
    dims = (((contract_a,), (contract_b,)), ((), ()))
    return lax.dot_general(a, b, dims, preferred_element_type=F32)


def chunk_of(rows):
    return CHUNK if rows % CHUNK == 0 else rows


def shape(dims, dtype):
    return jax.ShapeDtypeStruct(dims, dtype)


def lanes_of(j):
    return slice(j * HEAD_DIM, (j + 1) * HEAD_DIM)


def lower(chunk):
    row = lax.broadcasted_iota(jnp.int32, (chunk, chunk), 0)
    return row >= lax.broadcasted_iota(jnp.int32, (chunk, chunk), 1)


def upper(chunk):
    row = lax.broadcasted_iota(jnp.int32, (chunk, chunk), 0)
    return row <= lax.broadcasted_iota(jnp.int32, (chunk, chunk), 1)


def state_kernel(odd_ref, k_ref, v_ref, sum_ref, pre_ref):
    @pl.when(pl.program_id(0) == 0)
    def _():
        sum_ref[...] = jnp.zeros_like(sum_ref)

    for j in range(sum_ref.shape[0]):
        total = sum_ref[j]
        pre_ref[0, j] = total.astype(BF16)
        sum_ref[j] = total + dot(k_ref[:, lanes_of(j)], v_ref[:, lanes_of(j)], 0, 0)


def inner_kernel(odd_ref, q_ref, k_ref, v_ref, pre_ref, after_ref, inner_ref, turned_ref):
    keep = lower(q_ref.shape[0])
    for j in range(pre_ref.shape[1]):
        lanes = lanes_of(j)
        q = q_ref[:, lanes]
        scores = jnp.where(keep, dot(q, k_ref[:, lanes], 1, 1), 0.0).astype(BF16)
        inner_ref[:, lanes] = dot(scores, v_ref[:, lanes]) + dot(q, pre_ref[0, j])
        turned_ref[lanes, :] = q.T


def attn_kernel(last, odd_ref, q_ref, og_ref, gain_ref, inner_ref, state_ref, *refs):
    if last:
        square_in, cross_in, attn_ref, sums_ref = refs
        square, cross = square_in[...], cross_in[...]
    else:
        attn_ref, square_ref, cross_ref = refs
        square = cross = None
    for j in range(state_ref.shape[0]):
        lanes = lanes_of(j)
        attn = inner_ref[:, lanes] + dot(q_ref[:, lanes], state_ref[j].astype(BF16))
        attn_ref[:, lanes] = attn
        more = attn * attn
        crossed = gain_ref[:, lanes] * og_ref[:, lanes].astype(F32) * attn
        square = more if square is None else square + more
        cross = crossed if cross is None else cross + crossed
    if last:
        square = jnp.sum(square.T, axis=0, keepdims=True)
        cross = jnp.sum(cross.T, axis=0, keepdims=True)
        row = lax.broadcasted_iota(jnp.int32, sums_ref.shape, 0)
        sums_ref[...] = jnp.where(row == 0, square, jnp.where(row == 1, cross, 0.0))
    else:
        square_ref[...] = square
        cross_ref[...] = cross


def grad_kernel(full, parts, odd_ref, *refs):
    sums = refs[:parts]
    attn_ref, og_ref, gain_ref, turned_ref, g_ref, sum_ref, post_ref = refs[parts:]

    @pl.when(pl.program_id(0) == 0)
    def _():
        sum_ref[...] = jnp.zeros_like(sum_ref)

    total = sums[0][...]
    for ref in sums[1:]:
        total = total + ref[...]
    inv = lax.rsqrt(total[0:1] / full + 1e-6)
    slope = inv * inv * inv * (total[1:2] / full)
    row = lax.broadcasted_iota(jnp.int32, total.shape, 0)
    both = jnp.where(row == 0, inv, slope).T
    inv = jnp.broadcast_to(both[:, 0:1], (both.shape[0], HEAD_DIM))
    slope = jnp.broadcast_to(both[:, 1:2], (both.shape[0], HEAD_DIM))
    for j in range(sum_ref.shape[0]):
        lanes = lanes_of(j)
        scaled = gain_ref[:, lanes] * og_ref[:, lanes].astype(F32)
        grad = (inv * scaled - attn_ref[:, lanes] * slope).astype(BF16)
        g_ref[:, lanes] = grad
        total = sum_ref[j]
        post_ref[0, j] = total.astype(BF16)
        sum_ref[j] = total + dot(turned_ref[lanes, :], grad)


def local_kernel(odd_ref, q_ref, k_ref, v_ref, g_ref, state_ref, pre_ref, post_ref, after_ref, *refs):
    qgrad_ref, kpart_ref, vpart_ref = refs[-3:]
    low, up = lower(q_ref.shape[0]), upper(q_ref.shape[0])
    for j in range(state_ref.shape[0]):
        lanes = lanes_of(j)
        q, k, v, g = (ref[:, lanes] for ref in (q_ref, k_ref, v_ref, g_ref))
        gscores = jnp.where(low, dot(g, v, 1, 1), 0.0).astype(BF16)
        gturned = jnp.where(up, dot(v, g, 1, 1), 0.0).astype(BF16)
        turned = jnp.where(up, dot(k, q, 1, 1), 0.0).astype(BF16)
        qgrad = dot(gscores, k) + dot(g, state_ref[j].astype(BF16), 1, 1) + dot(g, pre_ref[0, j], 1, 1)
        qgrad_ref[:, lanes] = qgrad.astype(BF16)
        kpart_ref[:, lanes] = dot(gturned, q) + dot(v, post_ref[0, j], 1, 1)
        vpart_ref[:, lanes] = dot(turned, g) + dot(k, post_ref[0, j])


def final_kernel(odd_ref, k_ref, v_ref, kpart_ref, vpart_ref, state_ref, *refs):
    kgrad_ref, vgrad_ref = refs[-2:]
    for j in range(state_ref.shape[0]):
        lanes = lanes_of(j)
        state = state_ref[j].astype(BF16)
        kgrad_ref[:, lanes] = (kpart_ref[:, lanes] + dot(v_ref[:, lanes], state, 1, 1)).astype(BF16)
        vgrad_ref[:, lanes] = (vpart_ref[:, lanes] + dot(k_ref[:, lanes], state)).astype(BF16)


class Half:
    def __init__(self, odd, same, rows, width, reverse=False):
        self.odd, self.same, self.reverse = odd, same, reverse
        self.rows, self.width = rows, width // 2
        self.chunk = chunk_of(rows)
        self.steps = rows // self.chunk
        self.heads = self.width // HEAD_DIM

    def at(self, i):
        return self.steps - 1 - i if self.reverse else i

    def pick(self, odd_ref):
        return odd_ref[0] if self.same else 1 - odd_ref[0]

    def arg(self):
        return pl.BlockSpec((self.chunk, self.width), lambda i, odd: (self.at(i), self.pick(odd)))

    def gain(self):
        return pl.BlockSpec((1, self.width), lambda i, odd: (0, self.pick(odd)))

    def own(self, width=None):
        return pl.BlockSpec((self.chunk, width or self.width), lambda i, odd: (self.at(i), 0))

    def turned(self, height=None):
        return pl.BlockSpec((height or self.width, self.chunk), lambda i, odd: (0, self.at(i)))

    def states(self):
        return pl.BlockSpec((self.heads, HEAD_DIM, HEAD_DIM), lambda i, odd: (0, 0, 0))

    def inside(self):
        return pl.BlockSpec(
            (1, self.heads, HEAD_DIM, HEAD_DIM), lambda i, odd: (self.at(i), 0, 0, 0)
        )

    def anywhere(self):
        return pl.BlockSpec(memory_space=pl.ANY)

    def run(self, kernel, units, in_specs, out_specs, out_shape, args, aliases=None):
        flops = units * 2 * self.rows * self.width * HEAD_DIM
        nbytes = sum(a.size * a.dtype.itemsize for a in args) // 2
        return pl.pallas_call(
            kernel,
            grid_spec=pltpu.PrefetchScalarGridSpec(
                num_scalar_prefetch=1,
                grid=(self.steps,),
                in_specs=in_specs,
                out_specs=out_specs,
            ),
            out_shape=out_shape,
            input_output_aliases=aliases or {},
            cost_estimate=pl.CostEstimate(flops=flops, bytes_accessed=nbytes, transcendentals=0),
            compiler_params=pltpu.CompilerParams(vmem_limit_bytes=VMEM_BYTES),
        )(self.odd, *args)


def scan_plan(count):
    bits = count.bit_length() - 1
    stages = []
    for stage in range(bits - 1):
        rising, falling = 1 + stage, bits - 1 - stage
        pairs = []
        for r in range(count):
            bit = falling if r & 1 else rising
            useless = stage == 0 if r & 1 else stage == bits - 2
            if not ((r >> bit) & 1 and useless):
                pairs.append((r, r ^ (1 << bit)))
        stages.append((rising, falling, pairs))
    return stages


def join_kernel(backward, done, final, *refs):
    count = lax.axis_size("seq")
    rank = lax.axis_index("seq")
    if backward:
        rank = count - 1 - rank
    odd = (rank & 1) == 1
    plan = scan_plan(count)
    keep_ref, extra_ref = refs[:2]
    came = refs[2:2 + done]
    total = keep_ref[...] + extra_ref[...]
    before = jnp.zeros_like(total)
    for (rising, falling, _), ref in zip(plan, came):
        high = (jnp.where(odd, rank >> falling, rank >> rising) & 1) == 1
        value = ref[...]
        before = before + jnp.where(odd | high, value, 0.0)
        total = total + jnp.where(odd, 0.0, value)
    if final:
        message_ref, state_ref = refs[-2:]
        message_ref[...] = before + jnp.where(odd, 0.0, keep_ref[...])
        state_ref[...] = before + jnp.where(odd, extra_ref[...], 0.0)
    else:
        rising, falling, _ = plan[done]
        high = (jnp.where(odd, rank >> falling, rank >> rising) & 1) == 1
        refs[-1][...] = jnp.where(odd, before + jnp.where(high, 0.0, total), total)


def join(backward, keep, extra, came, final, after=()):
    vmem = pl.BlockSpec(memory_space=pltpu.VMEM)
    anywhere = pl.BlockSpec(memory_space=pl.ANY)
    like = shape(keep.shape, F32)
    return pl.pallas_call(
        functools.partial(join_kernel, backward, len(came), final),
        in_specs=[vmem] * (2 + len(came)) + [anywhere] * len(after),
        out_specs=[vmem, vmem] if final else vmem,
        out_shape=[like, like] if final else like,
        cost_estimate=pl.CostEstimate(
            flops=4 * keep.size, bytes_accessed=16 * keep.size, transcendentals=0
        ),
        compiler_params=pltpu.CompilerParams(vmem_limit_bytes=VMEM_BYTES),
    )(keep, extra, *came, *after)


def scan_states(keep, extra, backward, beside):
    count = lax.axis_size("seq")
    plan = scan_plan(count)
    came, results = [], []
    message = join(backward, keep, extra, came, not plan)
    for stage, (_, _, pairs) in enumerate(plan):
        arrived = move(message, pairs, backward)
        mine = beside[stage::len(plan)] if stage < len(beside) else []
        made = [work(message) for work in mine]
        results += made
        came = came + [arrived]
        after = [leaf for item in made for leaf in item[-1:]]
        message = join(backward, keep, extra, came, stage == len(plan) - 1, after)
    message, state = message
    return state, nearby(message, backward), results


def move(value, pairs, backward):
    count = lax.axis_size("seq")
    if backward:
        pairs = [(count - 1 - a, count - 1 - b) for a, b in pairs]
    return lax.ppermute(value, "seq", pairs)


def nearby(value, backward):
    return move(value, [(r, r ^ 1) for r in range(lax.axis_size("seq"))], backward)


def shards(query, key_in, value, out_grad, gain):
    rows, width = query.shape
    full = width * lax.axis_size("head")
    gain = gain.reshape(1, width)
    pin = lambda x: pltpu.with_memory_space_constraint(x, pltpu.HBM)
    query, key_in, value, out_grad = (pin(x) for x in (query, key_in, value, out_grad))
    odd = lax.rem(lax.axis_index("seq"), 2).astype(jnp.int32).reshape(1)

    mine = Half(odd, True, rows, width)
    theirs = Half(odd, False, rows, width)
    heads = mine.heads
    states = shape((heads, HEAD_DIM, HEAD_DIM), F32)
    inside = shape((mine.steps, heads, HEAD_DIM, HEAD_DIM), BF16)
    part_wide = shape((rows, mine.width), F32)
    part_thin = shape((rows, mine.width), BF16)
    part_turned = shape((mine.width, rows), BF16)
    lane_sums = shape((rows, HEAD_DIM), F32)
    thin = shape((rows, width), BF16)

    def local_states(h):
        return h.run(
            state_kernel, 1, [h.arg(), h.arg()], [h.states(), h.inside()], [states, inside],
            (key_in, value),
        )

    send, pre_theirs = local_states(theirs)
    extra = nearby(send, False)
    keep, pre_mine = local_states(mine)

    def inner_of(h, pre):
        return lambda message: h.run(
            inner_kernel, 5,
            [h.arg(), h.arg(), h.arg(), h.inside(), h.anywhere()],
            [h.own(), h.turned()], [part_wide, part_turned],
            (query, key_in, value, pre, message),
        )

    state_mine, state_theirs, made = scan_states(
        keep, extra, False, [inner_of(mine, pre_mine), inner_of(theirs, pre_theirs)]
    )
    (inner_mine, turned_mine), (inner_theirs, turned_theirs) = made

    def attn_of(h, inner, state, *sums):
        last = bool(sums)
        return h.run(
            functools.partial(attn_kernel, last), 1,
            [h.arg(), h.arg(), h.gain(), h.own(), h.states()] + [h.own(HEAD_DIM)] * len(sums),
            [h.own()] + ([h.turned(8)] if last else [h.own(HEAD_DIM)] * 2),
            [part_wide] + ([shape((8, rows), F32)] if last else [lane_sums] * 2),
            (query, out_grad, gain, inner, state, *sums),
        )

    attn_mine, square, cross = attn_of(mine, inner_mine, state_mine)
    attn_theirs, sums = attn_of(theirs, inner_theirs, state_theirs, square, cross)

    peers = lax.axis_size("head")
    parts = [sums] + [
        lax.ppermute(sums, "head", [(r, (r + shift) % peers) for r in range(peers)])
        for shift in range(1, peers)
    ]

    def grad_of(same, attn, turned):
        h = Half(odd, same, rows, width, reverse=True)
        return h.run(
            functools.partial(grad_kernel, full, peers), 1,
            [h.turned(8)] * peers + [h.own(), h.arg(), h.gain(), h.turned()],
            [h.own(), h.states(), h.inside()],
            [part_thin, states, inside],
            (*parts, attn, out_grad, gain, turned),
        )

    g_mine, gsend, post_mine = grad_of(True, attn_mine, turned_mine)
    gextra = nearby(gsend, True)
    g_theirs, gkeep, post_theirs = grad_of(False, attn_theirs, turned_theirs)

    def local_of(h, g, state, pre, post, out=None):
        def work(message):
            args = (query, key_in, value, g, state, pre, post, message)
            specs = [h.arg()] * 3 + [h.own(), h.states(), h.inside(), h.inside(), h.anywhere()]
            aliases = None
            if out is not None:
                args, specs, aliases = args + (out[0],), specs + [h.anywhere()], {len(args) + 1: 0}
            made = h.run(
                local_kernel, 10, specs, [h.arg(), h.own(), h.own()], [thin, part_wide, part_wide],
                args, aliases,
            )
            if out is None:
                qgrad_parts.append(made[0])
            return made

        return work

    qgrad_parts = []
    state_g_theirs, state_g_mine, made = scan_states(
        gkeep, gextra, True,
        [
            local_of(theirs, g_theirs, state_theirs, pre_theirs, post_theirs),
            local_of(mine, g_mine, state_mine, pre_mine, post_mine, qgrad_parts),
        ],
    )
    (_, kpart_theirs, vpart_theirs), (qgrad, kpart_mine, vpart_mine) = made

    def final_of(h, kpart, vpart, state, outs=()):
        return h.run(
            final_kernel, 2,
            [h.arg(), h.arg(), h.own(), h.own(), h.states()] + [h.anywhere()] * len(outs),
            [h.arg(), h.arg()], [thin, thin],
            (key_in, value, kpart, vpart, state, *outs),
            {6: 0, 7: 1} if outs else None,
        )

    outs = final_of(theirs, kpart_theirs, vpart_theirs, state_g_theirs)
    kgrad, vgrad = final_of(mine, kpart_mine, vpart_mine, state_g_mine, outs)
    return qgrad, kgrad, vgrad


def solution(mesh):
    spec = P("seq", "head")
    return jax.shard_map(
        shards,
        mesh=mesh,
        in_specs=(spec, spec, spec, spec, P("head")),
        out_specs=(spec, spec, spec),
        check_vma=False,
    )
```

```python
import functools

import jax
import jax.numpy as jnp
from jax import lax
from jax.experimental import pallas as pl
from jax.experimental.pallas import tpu as pltpu
from jax.sharding import PartitionSpec as P

HEAD_DIM = 128
CHUNK = 256
VMEM_BYTES = 16 * 2**20
F32 = jnp.float32
BF16 = jnp.bfloat16


def dot(a, b, contract_a=1, contract_b=0):
    dims = (((contract_a,), (contract_b,)), ((), ()))
    return lax.dot_general(a, b, dims, preferred_element_type=F32)


def chunk_of(rows):
    return CHUNK if rows % CHUNK == 0 else rows


def shape(dims, dtype):
    return jax.ShapeDtypeStruct(dims, dtype)


def lanes_of(j):
    return slice(j * HEAD_DIM, (j + 1) * HEAD_DIM)


def lower(chunk):
    row = lax.broadcasted_iota(jnp.int32, (chunk, chunk), 0)
    return row >= lax.broadcasted_iota(jnp.int32, (chunk, chunk), 1)


def upper(chunk):
    row = lax.broadcasted_iota(jnp.int32, (chunk, chunk), 0)
    return row <= lax.broadcasted_iota(jnp.int32, (chunk, chunk), 1)


def state_kernel(odd_ref, k_ref, v_ref, sum_ref, pre_ref):
    @pl.when(pl.program_id(0) == 0)
    def _():
        sum_ref[...] = jnp.zeros_like(sum_ref)

    for j in range(sum_ref.shape[0]):
        total = sum_ref[j]
        pre_ref[0, j] = total.astype(BF16)
        sum_ref[j] = total + dot(k_ref[:, lanes_of(j)], v_ref[:, lanes_of(j)], 0, 0)


def inner_kernel(odd_ref, q_ref, k_ref, v_ref, pre_ref, after_ref, inner_ref, turned_ref):
    keep = lower(q_ref.shape[0])
    for j in range(pre_ref.shape[1]):
        lanes = lanes_of(j)
        q = q_ref[:, lanes]
        scores = jnp.where(keep, dot(q, k_ref[:, lanes], 1, 1), 0.0).astype(BF16)
        inner_ref[:, lanes] = dot(scores, v_ref[:, lanes]) + dot(q, pre_ref[0, j])
        turned_ref[lanes, :] = q.T


def attn_kernel(last, odd_ref, q_ref, og_ref, gain_ref, inner_ref, state_ref, *refs):
    if last:
        square_in, cross_in, attn_ref, sums_ref = refs
        square, cross = square_in[...], cross_in[...]
    else:
        attn_ref, square_ref, cross_ref = refs
        square = cross = None
    for j in range(state_ref.shape[0]):
        lanes = lanes_of(j)
        attn = inner_ref[:, lanes] + dot(q_ref[:, lanes], state_ref[j].astype(BF16))
        attn_ref[:, lanes] = attn
        more = attn * attn
        crossed = gain_ref[:, lanes] * og_ref[:, lanes].astype(F32) * attn
        square = more if square is None else square + more
        cross = crossed if cross is None else cross + crossed
    if last:
        square = jnp.sum(square.T, axis=0, keepdims=True)
        cross = jnp.sum(cross.T, axis=0, keepdims=True)
        row = lax.broadcasted_iota(jnp.int32, sums_ref.shape, 0)
        sums_ref[...] = jnp.where(row == 0, square, cross)
    else:
        square_ref[...] = square
        cross_ref[...] = cross


def grad_kernel(full, parts, odd_ref, *refs):
    sums = refs[:parts]
    attn_ref, og_ref, gain_ref, turned_ref, g_ref, sum_ref, post_ref = refs[parts:]

    @pl.when(pl.program_id(0) == 0)
    def _():
        sum_ref[...] = jnp.zeros_like(sum_ref)

    total = sums[0][...]
    for ref in sums[1:]:
        total = total + ref[...]
    inv = lax.rsqrt(total[0:1] / full + 1e-6)
    slope = inv * inv * inv * (total[1:2] / full)
    row = lax.broadcasted_iota(jnp.int32, total.shape, 0)
    both = jnp.where(row == 0, inv, slope)
    both = jnp.concatenate([both] * 4, axis=0).T
    inv = jnp.broadcast_to(both[:, 0:1], (both.shape[0], HEAD_DIM))
    slope = jnp.broadcast_to(both[:, 1:2], (both.shape[0], HEAD_DIM))
    for j in range(sum_ref.shape[0]):
        lanes = lanes_of(j)
        scaled = gain_ref[:, lanes] * og_ref[:, lanes].astype(F32)
        grad = (inv * scaled - attn_ref[:, lanes] * slope).astype(BF16)
        g_ref[:, lanes] = grad
        total = sum_ref[j]
        post_ref[0, j] = total.astype(BF16)
        sum_ref[j] = total + dot(turned_ref[lanes, :], grad)


def local_kernel(odd_ref, q_ref, k_ref, v_ref, g_ref, state_ref, pre_ref, post_ref, after_ref, *refs):
    qgrad_ref, kpart_ref, vpart_ref = refs[-3:]
    low, up = lower(q_ref.shape[0]), upper(q_ref.shape[0])
    for j in range(state_ref.shape[0]):
        lanes = lanes_of(j)
        q, k, v, g = (ref[:, lanes] for ref in (q_ref, k_ref, v_ref, g_ref))
        gscores = jnp.where(low, dot(g, v, 1, 1), 0.0).astype(BF16)
        gturned = jnp.where(up, dot(v, g, 1, 1), 0.0).astype(BF16)
        turned = jnp.where(up, dot(k, q, 1, 1), 0.0).astype(BF16)
        qgrad = dot(gscores, k) + dot(g, state_ref[j].astype(BF16), 1, 1) + dot(g, pre_ref[0, j], 1, 1)
        qgrad_ref[:, lanes] = qgrad.astype(BF16)
        kpart_ref[:, lanes] = dot(gturned, q) + dot(v, post_ref[0, j], 1, 1)
        vpart_ref[:, lanes] = dot(turned, g) + dot(k, post_ref[0, j])


def final_kernel(odd_ref, k_ref, v_ref, kpart_ref, vpart_ref, state_ref, *refs):
    kgrad_ref, vgrad_ref = refs[-2:]
    for j in range(state_ref.shape[0]):
        lanes = lanes_of(j)
        state = state_ref[j].astype(BF16)
        kgrad_ref[:, lanes] = (kpart_ref[:, lanes] + dot(v_ref[:, lanes], state, 1, 1)).astype(BF16)
        vgrad_ref[:, lanes] = (vpart_ref[:, lanes] + dot(k_ref[:, lanes], state)).astype(BF16)


class Half:
    def __init__(self, odd, same, rows, width, reverse=False):
        self.odd, self.same, self.reverse = odd, same, reverse
        self.rows, self.width = rows, width // 2
        self.chunk = chunk_of(rows)
        self.steps = rows // self.chunk
        self.heads = self.width // HEAD_DIM

    def at(self, i):
        return self.steps - 1 - i if self.reverse else i

    def pick(self, odd_ref):
        return odd_ref[0] if self.same else 1 - odd_ref[0]

    def arg(self):
        return pl.BlockSpec((self.chunk, self.width), lambda i, odd: (self.at(i), self.pick(odd)))

    def gain(self):
        return pl.BlockSpec((1, self.width), lambda i, odd: (0, self.pick(odd)))

    def own(self, width=None):
        return pl.BlockSpec((self.chunk, width or self.width), lambda i, odd: (self.at(i), 0))

    def turned(self, height=None):
        return pl.BlockSpec((height or self.width, self.chunk), lambda i, odd: (0, self.at(i)))

    def states(self):
        return pl.BlockSpec((self.heads, HEAD_DIM, HEAD_DIM), lambda i, odd: (0, 0, 0))

    def inside(self):
        return pl.BlockSpec(
            (1, self.heads, HEAD_DIM, HEAD_DIM), lambda i, odd: (self.at(i), 0, 0, 0)
        )

    def anywhere(self):
        return pl.BlockSpec(memory_space=pl.ANY)

    def run(self, kernel, units, in_specs, out_specs, out_shape, args, aliases=None):
        flops = units * 2 * self.rows * self.width * HEAD_DIM
        nbytes = sum(a.size * a.dtype.itemsize for a in args) // 2
        return pl.pallas_call(
            kernel,
            grid_spec=pltpu.PrefetchScalarGridSpec(
                num_scalar_prefetch=1,
                grid=(self.steps,),
                in_specs=in_specs,
                out_specs=out_specs,
            ),
            out_shape=out_shape,
            input_output_aliases=aliases or {},
            cost_estimate=pl.CostEstimate(flops=flops, bytes_accessed=nbytes, transcendentals=0),
            compiler_params=pltpu.CompilerParams(vmem_limit_bytes=VMEM_BYTES),
        )(self.odd, *args)


def scan_plan(count):
    distances = [2 << i for i in range(max(count // 2 - 1, 0).bit_length())]
    stages = []
    for up, down in zip(distances, distances[::-1]):
        steps = [(r, r + (down if r & 1 else up)) for r in range(count)]
        stages.append([(a, b) for a, b in steps if b < count])
    return stages


def join_kernel(backward, done, final, *refs):
    rank = lax.axis_index("seq")
    if backward:
        rank = lax.axis_size("seq") - 1 - rank
    odd = (rank & 1) == 1
    keep_ref, extra_ref = refs[:2]
    before = jnp.zeros_like(keep_ref)
    for ref in refs[2:2 + done]:
        before = before + ref[...]
    if final:
        message_ref, state_ref = refs[-2:]
        message_ref[...] = before + jnp.where(odd, 0.0, keep_ref[...])
        state_ref[...] = before + jnp.where(odd, extra_ref[...], 0.0)
    else:
        refs[-1][...] = keep_ref[...] + extra_ref[...] + before


def join(backward, keep, extra, came, final, after=()):
    vmem = pl.BlockSpec(memory_space=pltpu.VMEM)
    anywhere = pl.BlockSpec(memory_space=pl.ANY)
    like = shape(keep.shape, F32)
    return pl.pallas_call(
        functools.partial(join_kernel, backward, len(came), final),
        in_specs=[vmem] * (2 + len(came)) + [anywhere] * len(after),
        out_specs=[vmem, vmem] if final else vmem,
        out_shape=[like, like] if final else like,
        cost_estimate=pl.CostEstimate(
            flops=4 * keep.size, bytes_accessed=16 * keep.size, transcendentals=0
        ),
        compiler_params=pltpu.CompilerParams(vmem_limit_bytes=VMEM_BYTES),
    )(keep, extra, *came, *after)


def scan_states(keep, extra, backward, beside):
    count = lax.axis_size("seq")
    plan = scan_plan(count)
    came, results = [], []
    message = join(backward, keep, extra, came, not plan)
    for stage, pairs in enumerate(plan):
        arrived = move(message, pairs, backward)
        mine = beside[stage::len(plan)] if stage < len(beside) else []
        made = [work(message) for work in mine]
        results += made
        came = came + [arrived]
        after = [leaf for item in made for leaf in item[-1:]]
        message = join(backward, keep, extra, came, stage == len(plan) - 1, after)
    message, state = message
    return state, nearby(message, backward), results


def move(value, pairs, backward):
    count = lax.axis_size("seq")
    if backward:
        pairs = [(count - 1 - a, count - 1 - b) for a, b in pairs]
    return lax.ppermute(value, "seq", pairs)


def nearby(value, backward):
    return move(value, [(r, r ^ 1) for r in range(lax.axis_size("seq"))], backward)


def add_kernel(left_ref, right_ref, out_ref):
    out_ref[...] = left_ref[...] + right_ref[...]


def head_sums(sums):
    peers = lax.axis_size("head")
    vmem = pl.BlockSpec(memory_space=pltpu.VMEM)
    distance, parts = 1, [sums]
    while distance < peers:
        if len(parts) == 2:
            sums = pl.pallas_call(
                add_kernel, in_specs=[vmem, vmem], out_specs=vmem,
                out_shape=shape(sums.shape, F32),
            )(*parts)
        pairs = [(r, (r + distance) % peers) for r in range(peers)]
        parts = [sums, lax.ppermute(sums, "head", pairs)]
        distance *= 2
    return parts


def shards(query, key_in, value, out_grad, gain):
    rows, width = query.shape
    full = width * lax.axis_size("head")
    gain = gain.reshape(1, width)
    pin = lambda x: pltpu.with_memory_space_constraint(x, pltpu.HBM)
    query, key_in, value, out_grad = (pin(x) for x in (query, key_in, value, out_grad))
    odd = lax.rem(lax.axis_index("seq"), 2).astype(jnp.int32).reshape(1)

    mine = Half(odd, True, rows, width)
    theirs = Half(odd, False, rows, width)
    heads = mine.heads
    states = shape((heads, HEAD_DIM, HEAD_DIM), F32)
    inside = shape((mine.steps, heads, HEAD_DIM, HEAD_DIM), BF16)
    part_wide = shape((rows, mine.width), F32)
    part_thin = shape((rows, mine.width), BF16)
    part_turned = shape((mine.width, rows), BF16)
    lane_sums = shape((rows, HEAD_DIM), F32)
    thin = shape((rows, width), BF16)

    def local_states(h):
        return h.run(
            state_kernel, 1, [h.arg(), h.arg()], [h.states(), h.inside()], [states, inside],
            (key_in, value),
        )

    send, pre_theirs = local_states(theirs)
    extra = nearby(send, False)
    keep, pre_mine = local_states(mine)

    def inner_of(h, pre):
        return lambda message: h.run(
            inner_kernel, 5,
            [h.arg(), h.arg(), h.arg(), h.inside(), h.anywhere()],
            [h.own(), h.turned()], [part_wide, part_turned],
            (query, key_in, value, pre, message),
        )

    state_mine, state_theirs, made = scan_states(
        keep, extra, False, [inner_of(mine, pre_mine), inner_of(theirs, pre_theirs)]
    )
    (inner_mine, turned_mine), (inner_theirs, turned_theirs) = made

    def attn_of(h, inner, state, *sums):
        last = bool(sums)
        return h.run(
            functools.partial(attn_kernel, last), 1,
            [h.arg(), h.arg(), h.gain(), h.own(), h.states()] + [h.own(HEAD_DIM)] * len(sums),
            [h.own()] + ([h.turned(2)] if last else [h.own(HEAD_DIM)] * 2),
            [part_wide] + ([shape((2, rows), F32)] if last else [lane_sums] * 2),
            (query, out_grad, gain, inner, state, *sums),
        )

    attn_mine, square, cross = attn_of(mine, inner_mine, state_mine)
    attn_theirs, sums = attn_of(theirs, inner_theirs, state_theirs, square, cross)

    parts = head_sums(sums)

    def grad_of(same, attn, turned):
        h = Half(odd, same, rows, width, reverse=True)
        return h.run(
            functools.partial(grad_kernel, full, len(parts)), 1,
            [h.turned(2)] * len(parts) + [h.own(), h.arg(), h.gain(), h.turned()],
            [h.own(), h.states(), h.inside()],
            [part_thin, states, inside],
            (*parts, attn, out_grad, gain, turned),
        )

    g_mine, gsend, post_mine = grad_of(True, attn_mine, turned_mine)
    gextra = nearby(gsend, True)
    g_theirs, gkeep, post_theirs = grad_of(False, attn_theirs, turned_theirs)

    def local_of(h, g, state, pre, post, out=None):
        def work(message):
            args = (query, key_in, value, g, state, pre, post, message)
            specs = [h.arg()] * 3 + [h.own(), h.states(), h.inside(), h.inside(), h.anywhere()]
            aliases = None
            if out is not None:
                args, specs, aliases = args + (out[0],), specs + [h.anywhere()], {len(args) + 1: 0}
            made = h.run(
                local_kernel, 10, specs, [h.arg(), h.own(), h.own()], [thin, part_wide, part_wide],
                args, aliases,
            )
            if out is None:
                qgrad_parts.append(made[0])
            return made

        return work

    qgrad_parts = []
    state_g_theirs, state_g_mine, made = scan_states(
        gkeep, gextra, True,
        [
            local_of(theirs, g_theirs, state_theirs, pre_theirs, post_theirs),
            local_of(mine, g_mine, state_mine, pre_mine, post_mine, qgrad_parts),
        ],
    )
    (_, kpart_theirs, vpart_theirs), (qgrad, kpart_mine, vpart_mine) = made

    def final_of(h, kpart, vpart, state, outs=()):
        return h.run(
            final_kernel, 2,
            [h.arg(), h.arg(), h.own(), h.own(), h.states()] + [h.anywhere()] * len(outs),
            [h.arg(), h.arg()], [thin, thin],
            (key_in, value, kpart, vpart, state, *outs),
            {6: 0, 7: 1} if outs else None,
        )

    outs = final_of(theirs, kpart_theirs, vpart_theirs, state_g_theirs)
    kgrad, vgrad = final_of(mine, kpart_mine, vpart_mine, state_g_mine, outs)
    return qgrad, kgrad, vgrad


def solution(mesh):
    spec = P("seq", "head")
    return jax.shard_map(
        shards,
        mesh=mesh,
        in_specs=(spec, spec, spec, spec, P("head")),
        out_specs=(spec, spec, spec),
        check_vma=False,
    )
```

```python
import functools

import jax
import jax.numpy as jnp
from jax import lax
from jax.experimental import pallas as pl
from jax.experimental.pallas import tpu as pltpu
from jax.sharding import PartitionSpec as P

HEAD_DIM = 128
CHUNK = 256
VMEM_BYTES = 12 * 2**20
F32 = jnp.float32
BF16 = jnp.bfloat16
VMEM = pl.BlockSpec(memory_space=pltpu.VMEM)
HBM = pl.BlockSpec(memory_space=pltpu.HBM)
ANYWHERE = pl.BlockSpec(memory_space=pl.ANY)


def dot(a, b, contract_a=1, contract_b=0):
    dims = (((contract_a,), (contract_b,)), ((), ()))
    return lax.dot_general(a, b, dims, preferred_element_type=F32)


def chunks_of(rows):
    size = CHUNK if rows % CHUNK == 0 else rows
    return [slice(i, i + size) for i in range(0, rows, size)]


def shape(dims, dtype):
    return jax.ShapeDtypeStruct(dims, dtype)


def lanes_of(j):
    return slice(j * HEAD_DIM, (j + 1) * HEAD_DIM)


def lower(size):
    row = lax.broadcasted_iota(jnp.int32, (size, size), 0)
    return row >= lax.broadcasted_iota(jnp.int32, (size, size), 1)


def upper(size):
    row = lax.broadcasted_iota(jnp.int32, (size, size), 0)
    return row <= lax.broadcasted_iota(jnp.int32, (size, size), 1)


def run(kernel, flops, in_specs, out_specs, out_shape, args, scratch=(), aliases=None):
    nbytes = sum(a.size * a.dtype.itemsize for a in args)
    return pl.pallas_call(
        kernel,
        in_specs=in_specs,
        out_specs=out_specs,
        out_shape=out_shape,
        scratch_shapes=list(scratch),
        input_output_aliases=aliases or {},
        cost_estimate=pl.CostEstimate(flops=flops, bytes_accessed=nbytes, transcendentals=0),
        compiler_params=pltpu.CompilerParams(vmem_limit_bytes=VMEM_BYTES),
    )(*args)


def columns(same, width):
    odd = lax.rem(lax.axis_index("seq"), 2)
    half = odd if same else 1 - odd
    return pl.ds(pl.multiple_of(half * width, width), width)


def fetches(sources, targets, sems, same):
    rows, width = targets[0].shape
    lanes = columns(same, width)
    copies = []
    for part in chunks_of(rows):
        for source, target in zip(sources, targets):
            sem = sems.at[len(copies)]
            copies.append(pltpu.make_async_copy(source.at[part, lanes], target.at[part], sem))
    return copies


def sum_states(k_ref, v_ref, sum_ref, pre_ref, copies=None):
    heads = sum_ref.shape[0]
    totals = [None] * heads
    for i, part in enumerate(chunks_of(k_ref.shape[0])):
        if copies:
            for copy in copies[2 * i:2 * i + 2]:
                copy.wait()
        for j in range(heads):
            term = dot(k_ref[part, lanes_of(j)], v_ref[part, lanes_of(j)], 0, 0)
            if i:
                pre_ref[i, j] = totals[j].astype(BF16)
            else:
                pre_ref[i, j] = jnp.zeros_like(pre_ref[i, j])
            totals[j] = totals[j] + term if i else term
    for j in range(heads):
        sum_ref[j] = totals[j]


def first_kernel(k_hbm, v_hbm, k1, v1, k2, v2, sum_ref, pre_ref, sems1, sems2):
    now = fetches((k_hbm, v_hbm), (k1, v1), sems1, False)
    later = fetches((k_hbm, v_hbm), (k2, v2), sems2, True)
    for copy in now + later:
        copy.start()
    sum_states(k1, v1, sum_ref, pre_ref, now)
    for copy in later:
        copy.wait()


def second_kernel(k2, v2, q_hbm, og_hbm, q1, og1, q2, og2, sum_ref, pre_ref, sems1, sems2):
    copies = fetches((q_hbm, og_hbm), (q2, og2), sems2, True)
    copies += fetches((q_hbm, og_hbm), (q1, og1), sems1, False)
    for copy in copies:
        copy.start()
    sum_states(k2, v2, sum_ref, pre_ref)
    for copy in copies:
        copy.wait()


def inner_kernel(same, q_ref, k_ref, v_ref, og_ref, gain_ref, pre_ref, after_ref, *outs):
    inner_ref, scaled_ref, qturned_ref, turned_ref = outs
    rows, width = q_ref.shape
    gain = gain_ref[:, columns(same, width)]
    for j in range(width // HEAD_DIM):
        lanes = lanes_of(j)
        for i, part in enumerate(chunks_of(rows)):
            q, k = q_ref[part, lanes], k_ref[part, lanes]
            size = q.shape[0]
            scores = jnp.where(lower(size), dot(q, k, 1, 1), 0.0).astype(BF16)
            turned_ref[j, part] = jnp.where(upper(size), dot(k, q, 1, 1), 0.0).astype(BF16)
            inner = dot(scores, v_ref[part, lanes])
            inner_ref[part, lanes] = inner + dot(q, pre_ref[i, j]) if i else inner
            scaled_ref[part, lanes] = gain[:, lanes] * og_ref[part, lanes].astype(F32)
            qturned_ref[lanes, part] = q.T


def attn_kernel(last, q_ref, inner_ref, scaled_ref, state_ref, *refs):
    attn_ref = refs[-3] if not last else refs[-2]
    rows, width = q_ref.shape
    states = [state_ref[j].astype(BF16) for j in range(width // HEAD_DIM)]
    for part in chunks_of(rows):
        square, cross = (refs[0][part], refs[1][part]) if last else (None, None)
        for j, state in enumerate(states):
            lanes = lanes_of(j)
            attn = inner_ref[part, lanes] + dot(q_ref[part, lanes], state)
            attn_ref[part, lanes] = attn
            more, crossed = attn * attn, scaled_ref[part, lanes] * attn
            square = more if square is None else square + more
            cross = crossed if cross is None else cross + crossed
        if last:
            square = jnp.sum(square.T, axis=0, keepdims=True)
            cross = jnp.sum(cross.T, axis=0, keepdims=True)
            row = lax.broadcasted_iota(jnp.int32, (8, square.shape[1]), 0)
            refs[-1][:, part] = jnp.where(row == 0, square, jnp.where(row == 1, cross, 0.0))
        else:
            refs[-2][part] = square
            refs[-1][part] = cross


def factors_kernel(full, parts, refs):
    total = refs[0][...]
    for ref in refs[1:parts]:
        total = total + ref[...]
    inv = lax.rsqrt(total[0:1] / full + 1e-6)
    slope = inv * inv * inv * (total[1:2] / full)
    row = lax.broadcasted_iota(jnp.int32, total.shape, 0)
    both = jnp.where(row == 0, inv, slope).T
    wide = (both.shape[0], HEAD_DIM)
    return jnp.broadcast_to(both[:, 0:1], wide), jnp.broadcast_to(both[:, 1:2], wide)


def grad_kernel(full, parts, *refs):
    if parts:
        inv, slope = factors_kernel(full, parts, refs)
        refs[-2][...] = inv
        refs[-1][...] = slope
        inv_ref, slope_ref = refs[-2:]
        attn_ref, scaled_ref, qturned_ref, g_ref, sum_ref, post_ref = refs[parts:-2]
    else:
        inv_ref, slope_ref, attn_ref, scaled_ref, qturned_ref, g_ref, sum_ref, post_ref = refs
    heads = sum_ref.shape[0]
    totals = [None] * heads
    for i, part in reversed(list(enumerate(chunks_of(g_ref.shape[0])))):
        for j in range(heads):
            lanes = lanes_of(j)
            grad = inv_ref[part] * scaled_ref[part, lanes] - attn_ref[part, lanes] * slope_ref[part]
            grad = grad.astype(BF16)
            g_ref[part, lanes] = grad
            term = dot(qturned_ref[lanes, part], grad)
            if totals[j] is None:
                post_ref[i, j] = jnp.zeros_like(post_ref[i, j])
                totals[j] = term
            else:
                post_ref[i, j] = totals[j].astype(BF16)
                totals[j] = totals[j] + term
    for j in range(heads):
        sum_ref[j] = totals[j]


def local_kernel(same, q_ref, k_ref, v_ref, g_ref, turned_ref, state_ref, pre_ref, post_ref, *refs):
    qgrad_hbm, kpart_ref, vpart_ref, qgrad_ref, sems = refs[-5:]
    rows, width = q_ref.shape
    target = columns(same, width)
    parts = chunks_of(rows)
    copies = []
    for i, part in enumerate(parts):
        for j in range(width // HEAD_DIM):
            lanes = lanes_of(j)
            q, k, v, g = (ref[part, lanes] for ref in (q_ref, k_ref, v_ref, g_ref))
            size = q.shape[0]
            gscores = jnp.where(lower(size), dot(g, v, 1, 1), 0.0).astype(BF16)
            gturned = jnp.where(upper(size), dot(v, g, 1, 1), 0.0).astype(BF16)
            qgrad = dot(gscores, k) + dot(g, state_ref[j].astype(BF16), 1, 1)
            kgrad = dot(gturned, q)
            vgrad = dot(turned_ref[j, part], g)
            if i:
                qgrad = qgrad + dot(g, pre_ref[i, j], 1, 1)
            if i < len(parts) - 1:
                kgrad = kgrad + dot(v, post_ref[i, j], 1, 1)
                vgrad = vgrad + dot(k, post_ref[i, j])
            qgrad_ref[part, lanes] = qgrad.astype(BF16)
            kpart_ref[part, lanes] = kgrad
            vpart_ref[part, lanes] = vgrad
        copy = pltpu.make_async_copy(qgrad_ref.at[part], qgrad_hbm.at[part, target], sems.at[i])
        copy.start()
        copies.append(copy)
    for copy in copies:
        copy.wait()


def final_kernel(same, k_ref, v_ref, kpart_ref, vpart_ref, state_ref, *refs):
    kgrad_hbm, vgrad_hbm, kgrad_ref, vgrad_ref, sems = refs[-5:]
    rows, width = k_ref.shape
    target = columns(same, width)
    states = [state_ref[j].astype(BF16) for j in range(width // HEAD_DIM)]
    copies = []
    for part in chunks_of(rows):
        for j, state in enumerate(states):
            lanes = lanes_of(j)
            kgrad = kpart_ref[part, lanes] + dot(v_ref[part, lanes], state, 1, 1)
            vgrad = vpart_ref[part, lanes] + dot(k_ref[part, lanes], state)
            kgrad_ref[part, lanes] = kgrad.astype(BF16)
            vgrad_ref[part, lanes] = vgrad.astype(BF16)
        for source, out in ((kgrad_ref, kgrad_hbm), (vgrad_ref, vgrad_hbm)):
            sem = sems.at[len(copies)]
            copy = pltpu.make_async_copy(source.at[part], out.at[part, target], sem)
            copy.start()
            copies.append(copy)
    for copy in copies:
        copy.wait()


def scan_plan(count):
    bits = count.bit_length() - 1
    stages = []
    for stage in range(bits - 1):
        rising, falling = 1 + stage, bits - 1 - stage
        pairs = []
        for r in range(count):
            bit = falling if r & 1 else rising
            useless = stage == 0 if r & 1 else stage == bits - 2
            if not ((r >> bit) & 1 and useless):
                pairs.append((r, r ^ (1 << bit)))
        stages.append((rising, falling, pairs))
    return stages


def join_kernel(backward, done, final, *refs):
    count = lax.axis_size("seq")
    rank = lax.axis_index("seq")
    if backward:
        rank = count - 1 - rank
    odd = (rank & 1) == 1
    plan = scan_plan(count)
    keep_ref, extra_ref = refs[:2]
    came = refs[2:2 + done]
    total = keep_ref[...] + extra_ref[...]
    before = jnp.zeros_like(total)
    for (rising, falling, _), ref in zip(plan, came):
        high = (jnp.where(odd, rank >> falling, rank >> rising) & 1) == 1
        value = ref[...]
        before = before + jnp.where(odd | high, value, 0.0)
        total = total + jnp.where(odd, 0.0, value)
    if final:
        message_ref, state_ref = refs[-2:]
        message_ref[...] = before + jnp.where(odd, 0.0, keep_ref[...])
        state_ref[...] = before + jnp.where(odd, extra_ref[...], 0.0)
    else:
        rising, falling, _ = plan[done]
        high = (jnp.where(odd, rank >> falling, rank >> rising) & 1) == 1
        refs[-1][...] = jnp.where(odd, before + jnp.where(high, 0.0, total), total)


def join(backward, keep, extra, came, final, after=()):
    like = shape(keep.shape, F32)
    return run(
        functools.partial(join_kernel, backward, len(came), final), 4 * keep.size,
        [VMEM] * (2 + len(came)) + [ANYWHERE] * len(after),
        [VMEM, VMEM] if final else VMEM,
        [like, like] if final else like,
        (keep, extra, *came, *after),
    )


def scan_states(keep, extra, backward, beside):
    count = lax.axis_size("seq")
    plan = scan_plan(count)
    came, results = [], []
    message = join(backward, keep, extra, came, not plan)
    for stage, (_, _, pairs) in enumerate(plan):
        arrived = move(message, pairs, backward)
        mine = beside[stage::len(plan)] if stage < len(beside) else []
        made = [work(message) for work in mine]
        results += made
        came = came + [arrived]
        after = [leaf for item in made for leaf in item[-1:]]
        message = join(backward, keep, extra, came, stage == len(plan) - 1, after)
    message, state = message
    return state, nearby(message, backward), results


def move(value, pairs, backward):
    count = lax.axis_size("seq")
    if backward:
        pairs = [(count - 1 - a, count - 1 - b) for a, b in pairs]
    return lax.ppermute(value, "seq", pairs)


def nearby(value, backward):
    return move(value, [(r, r ^ 1) for r in range(lax.axis_size("seq"))], backward)


def add_kernel(left_ref, right_ref, out_ref):
    out_ref[...] = left_ref[...] + right_ref[...]


def head_sums(sums):
    peers = lax.axis_size("head")
    distance, parts = 1, [sums]
    while distance < peers:
        if len(parts) == 2:
            sums = run(add_kernel, sums.size, [VMEM, VMEM], VMEM, shape(sums.shape, F32), parts)
        pairs = [(r, (r + distance) % peers) for r in range(peers)]
        parts = [sums, lax.ppermute(sums, "head", pairs)]
        distance *= 2
    return parts


def shards(query, key_in, value, out_grad, gain):
    rows, width = query.shape
    half = width // 2
    heads = half // HEAD_DIM
    chunks = len(chunks_of(rows))
    full = width * lax.axis_size("head")
    gain = gain.reshape(1, width)
    pin = lambda x: pltpu.with_memory_space_constraint(x, pltpu.HBM)
    query, key_in, value, out_grad = (pin(x) for x in (query, key_in, value, out_grad))
    unit = 2 * rows * half * HEAD_DIM
    partial = functools.partial

    states = shape((heads, HEAD_DIM, HEAD_DIM), F32)
    inside = shape((chunks, heads, HEAD_DIM, HEAD_DIM), BF16)
    wide = shape((rows, half), F32)
    thin = shape((rows, half), BF16)
    lane_sums = shape((rows, HEAD_DIM), F32)
    whole = shape((rows, width), BF16)
    sems = pltpu.SemaphoreType.DMA((2 * chunks,))

    k1, v1, k2, v2, send, pre1 = run(
        first_kernel, unit, [HBM, HBM], [VMEM] * 6, [thin] * 4 + [states, inside],
        (key_in, value), [sems, sems],
    )
    extra = nearby(send, False)
    q1, og1, q2, og2, keep, pre2 = run(
        second_kernel, unit, [VMEM, VMEM, HBM, HBM], [VMEM] * 6, [thin] * 4 + [states, inside],
        (k2, v2, query, out_grad), [sems, sems],
    )

    def inner_of(same, q, k, v, og, pre):
        return lambda message: run(
            partial(inner_kernel, same), 6 * unit,
            [VMEM] * 6 + [ANYWHERE], [VMEM] * 4,
            [wide, wide, shape((half, rows), BF16), shape((heads, rows, rows // chunks), BF16)],
            (q, k, v, og, gain, pre, message),
        )

    state2, state1, made = scan_states(
        keep, extra, False,
        [inner_of(True, q2, k2, v2, og2, pre2), inner_of(False, q1, k1, v1, og1, pre1)],
    )
    (inner2, scaled2, qturned2, turned2), (inner1, scaled1, qturned1, turned1) = made

    attn2, square, cross = run(
        partial(attn_kernel, False), unit, [VMEM] * 4, [VMEM] * 3, [wide, lane_sums, lane_sums],
        (q2, inner2, scaled2, state2),
    )
    attn1, sums = run(
        partial(attn_kernel, True), unit, [VMEM] * 6, [VMEM] * 2, [wide, shape((8, rows), F32)],
        (q1, inner1, scaled1, state1, square, cross),
    )
    parts = head_sums(sums)

    g2, gsend, post2, inv, slope = run(
        partial(grad_kernel, full, len(parts)), unit,
        [VMEM] * (len(parts) + 3), [VMEM] * 5, [thin, states, inside, lane_sums, lane_sums],
        (*parts, attn2, scaled2, qturned2),
    )
    gextra = nearby(gsend, True)
    g1, gkeep, post1 = run(
        partial(grad_kernel, full, 0), unit, [VMEM] * 5, [VMEM] * 3, [thin, states, inside],
        (inv, slope, attn1, scaled1, qturned1),
    )

    qgrads = []

    def local_of(same, *args):
        def work(message):
            more = [message] + qgrads
            qgrad, kpart, vpart = run(
                partial(local_kernel, same), 9 * unit,
                [VMEM] * len(args) + [ANYWHERE] + [HBM] * len(qgrads), [HBM, VMEM, VMEM],
                [whole, wide, wide], (*args, *more),
                [pltpu.VMEM((rows, half), BF16), sems],
                {len(args) + 1: 0} if qgrads else None,
            )
            qgrads[:] = [qgrad]
            return kpart, vpart

        return work

    gstate1, gstate2, made = scan_states(
        gkeep, gextra, True,
        [
            local_of(False, q1, k1, v1, g1, turned1, state1, pre1, post1),
            local_of(True, q2, k2, v2, g2, turned2, state2, pre2, post2),
        ],
    )
    (kpart1, vpart1), (kpart2, vpart2) = made

    def final_of(same, *args, outs=()):
        scratch = [pltpu.VMEM((rows, half), BF16)] * 2 + [sems]
        aliases = {len(args) + i: i for i in range(len(outs))}
        return run(
            partial(final_kernel, same), 2 * unit, [VMEM] * len(args) + [HBM] * len(outs),
            [HBM, HBM], [whole, whole], (*args, *outs), scratch, aliases,
        )

    outs = final_of(False, k1, v1, kpart1, vpart1, gstate1)
    kgrad, vgrad = final_of(True, k2, v2, kpart2, vpart2, gstate2, outs=outs)
    return qgrads[0], kgrad, vgrad


def solution(mesh):
    spec = P("seq", "head")
    return jax.shard_map(
        shards,
        mesh=mesh,
        in_specs=(spec, spec, spec, spec, P("head")),
        out_specs=(spec, spec, spec),
        check_vma=False,
    )
```

```python
import functools

import jax
import jax.numpy as jnp
from jax import lax
from jax.experimental import pallas as pl
from jax.experimental.pallas import tpu as pltpu
from jax.sharding import PartitionSpec as P

HEAD_DIM = 128
CHUNK = 256
VMEM_BYTES = 12 * 2**20
F32 = jnp.float32
BF16 = jnp.bfloat16
VMEM = pl.BlockSpec(memory_space=pltpu.VMEM)
HBM = pl.BlockSpec(memory_space=pltpu.HBM)
ANYWHERE = pl.BlockSpec(memory_space=pl.ANY)


def dot(a, b, contract_a=1, contract_b=0):
    dims = (((contract_a,), (contract_b,)), ((), ()))
    return lax.dot_general(a, b, dims, preferred_element_type=F32)


def chunks_of(rows):
    size = CHUNK if rows % CHUNK == 0 else rows
    return [slice(i, i + size) for i in range(0, rows, size)]


def shape(dims, dtype):
    return jax.ShapeDtypeStruct(dims, dtype)


def lanes_of(j):
    return slice(j * HEAD_DIM, (j + 1) * HEAD_DIM)


def lower(size):
    row = lax.broadcasted_iota(jnp.int32, (size, size), 0)
    return row >= lax.broadcasted_iota(jnp.int32, (size, size), 1)


def upper(size):
    row = lax.broadcasted_iota(jnp.int32, (size, size), 0)
    return row <= lax.broadcasted_iota(jnp.int32, (size, size), 1)


def run(kernel, flops, in_specs, out_specs, out_shape, args, scratch=(), aliases=None):
    nbytes = sum(a.size * a.dtype.itemsize for a in args)
    return pl.pallas_call(
        kernel,
        in_specs=in_specs,
        out_specs=out_specs,
        out_shape=out_shape,
        scratch_shapes=list(scratch),
        input_output_aliases=aliases or {},
        cost_estimate=pl.CostEstimate(flops=flops, bytes_accessed=nbytes, transcendentals=0),
        compiler_params=pltpu.CompilerParams(vmem_limit_bytes=VMEM_BYTES),
    )(*args)


def columns(same, width):
    odd = lax.rem(lax.axis_index("seq"), 2)
    half = odd if same else 1 - odd
    return pl.ds(pl.multiple_of(half * width, width), width)


def fetches(sources, targets, sems, same):
    rows, width = targets[0].shape
    lanes = columns(same, width)
    copies = []
    for part in chunks_of(rows):
        for source, target in zip(sources, targets):
            sem = sems.at[len(copies)]
            copies.append(pltpu.make_async_copy(source.at[part, lanes], target.at[part], sem))
    return copies


def sum_states(k_ref, v_ref, sum_ref, pre_ref, copies=None):
    heads = sum_ref.shape[0]
    totals = [None] * heads
    for i, part in enumerate(chunks_of(k_ref.shape[0])):
        if copies:
            for copy in copies[2 * i:2 * i + 2]:
                copy.wait()
        for j in range(heads):
            term = dot(k_ref[part, lanes_of(j)], v_ref[part, lanes_of(j)], 0, 0)
            if i:
                pre_ref[i, j] = totals[j].astype(BF16)
            else:
                pre_ref[i, j] = jnp.zeros_like(pre_ref[i, j])
            totals[j] = totals[j] + term if i else term
    for j in range(heads):
        sum_ref[j] = totals[j]


def first_kernel(k_hbm, v_hbm, k1, v1, k2, v2, sum_ref, pre_ref, sems1, sems2):
    now = fetches((k_hbm, v_hbm), (k1, v1), sems1, False)
    later = fetches((k_hbm, v_hbm), (k2, v2), sems2, True)
    for copy in now + later:
        copy.start()
    sum_states(k1, v1, sum_ref, pre_ref, now)
    for copy in later:
        copy.wait()


def second_kernel(k2, v2, sum_ref, pre_ref):
    sum_states(k2, v2, sum_ref, pre_ref)


def inner_kernel(same, q_hbm, og_hbm, k_ref, v_ref, gain_ref, pre_ref, after_ref, *outs):
    q_ref, inner_ref, scaled_ref, qturned_ref, turned_ref, og_ref, sems = outs
    rows, width = q_ref.shape
    copies = fetches((q_hbm, og_hbm), (q_ref, og_ref), sems, same)
    for copy in copies:
        copy.start()
    gain = gain_ref[:, columns(same, width)]
    for i, part in enumerate(chunks_of(rows)):
        for copy in copies[2 * i:2 * i + 2]:
            copy.wait()
        for j in range(width // HEAD_DIM):
            lanes = lanes_of(j)
            q, k = q_ref[part, lanes], k_ref[part, lanes]
            size = q.shape[0]
            scores = jnp.where(lower(size), dot(q, k, 1, 1), 0.0).astype(BF16)
            turned_ref[j, part] = jnp.where(upper(size), dot(k, q, 1, 1), 0.0).astype(BF16)
            inner = dot(scores, v_ref[part, lanes])
            inner_ref[part, lanes] = inner + dot(q, pre_ref[i, j]) if i else inner
            scaled_ref[part, lanes] = gain[:, lanes] * og_ref[part, lanes].astype(F32)
            qturned_ref[lanes, part] = q.T


def attn_kernel(last, q_ref, inner_ref, scaled_ref, state_ref, *refs):
    attn_ref = refs[-3] if not last else refs[-2]
    rows, width = q_ref.shape
    states = [state_ref[j].astype(BF16) for j in range(width // HEAD_DIM)]
    for part in chunks_of(rows):
        square, cross = (refs[0][part], refs[1][part]) if last else (None, None)
        for j, state in enumerate(states):
            lanes = lanes_of(j)
            attn = inner_ref[part, lanes] + dot(q_ref[part, lanes], state)
            attn_ref[part, lanes] = attn
            more, crossed = attn * attn, scaled_ref[part, lanes] * attn
            square = more if square is None else square + more
            cross = crossed if cross is None else cross + crossed
        if last:
            square = jnp.sum(square.T, axis=0, keepdims=True)
            cross = jnp.sum(cross.T, axis=0, keepdims=True)
            row = lax.broadcasted_iota(jnp.int32, (8, square.shape[1]), 0)
            sums = jnp.where(row == 0, square, jnp.where(row == 1, cross, 0.0))
            for peer in range(refs[-1].shape[0]):
                refs[-1][peer, :, part] = sums
        else:
            refs[-2][part] = square
            refs[-1][part] = cross


def factors_kernel(full, parts, refs):
    total = refs[0][0]
    for peer in range(1, parts):
        total = total + refs[0][peer]
    inv = lax.rsqrt(total[0:1] / full + 1e-6)
    slope = inv * inv * inv * (total[1:2] / full)
    row = lax.broadcasted_iota(jnp.int32, total.shape, 0)
    both = jnp.where(row == 0, inv, slope).T
    wide = (both.shape[0], HEAD_DIM)
    return jnp.broadcast_to(both[:, 0:1], wide), jnp.broadcast_to(both[:, 1:2], wide)


def grad_kernel(full, parts, *refs):
    if parts:
        inv, slope = factors_kernel(full, parts, refs)
        refs[-2][...] = inv
        refs[-1][...] = slope
        inv_ref, slope_ref = refs[-2:]
        attn_ref, scaled_ref, qturned_ref, g_ref, sum_ref, post_ref = refs[1:-2]
    else:
        inv_ref, slope_ref, attn_ref, scaled_ref, qturned_ref, g_ref, sum_ref, post_ref = refs
    heads = sum_ref.shape[0]
    totals = [None] * heads
    for i, part in reversed(list(enumerate(chunks_of(g_ref.shape[0])))):
        for j in range(heads):
            lanes = lanes_of(j)
            grad = inv_ref[part] * scaled_ref[part, lanes] - attn_ref[part, lanes] * slope_ref[part]
            grad = grad.astype(BF16)
            g_ref[part, lanes] = grad
            term = dot(qturned_ref[lanes, part], grad)
            if totals[j] is None:
                post_ref[i, j] = jnp.zeros_like(post_ref[i, j])
                totals[j] = term
            else:
                post_ref[i, j] = totals[j].astype(BF16)
                totals[j] = totals[j] + term
    for j in range(heads):
        sum_ref[j] = totals[j]


def local_kernel(same, q_ref, k_ref, v_ref, g_ref, turned_ref, state_ref, pre_ref, post_ref, *refs):
    qgrad_hbm, kpart_ref, vpart_ref, qgrad_ref, sems = refs[-5:]
    rows, width = q_ref.shape
    target = columns(same, width)
    parts = chunks_of(rows)
    copies = []
    for i, part in enumerate(parts):
        for j in range(width // HEAD_DIM):
            lanes = lanes_of(j)
            q, k, v, g = (ref[part, lanes] for ref in (q_ref, k_ref, v_ref, g_ref))
            size = q.shape[0]
            gscores = jnp.where(lower(size), dot(g, v, 1, 1), 0.0).astype(BF16)
            gturned = jnp.where(upper(size), dot(v, g, 1, 1), 0.0).astype(BF16)
            qgrad = dot(gscores, k) + dot(g, state_ref[j].astype(BF16), 1, 1)
            kgrad = dot(gturned, q)
            vgrad = dot(turned_ref[j, part], g)
            if i:
                qgrad = qgrad + dot(g, pre_ref[i, j], 1, 1)
            if i < len(parts) - 1:
                kgrad = kgrad + dot(v, post_ref[i, j], 1, 1)
                vgrad = vgrad + dot(k, post_ref[i, j])
            qgrad_ref[part, lanes] = qgrad.astype(BF16)
            kpart_ref[part, lanes] = kgrad
            vpart_ref[part, lanes] = vgrad
        copy = pltpu.make_async_copy(qgrad_ref.at[part], qgrad_hbm.at[part, target], sems.at[i])
        copy.start()
        copies.append(copy)
    for copy in copies:
        copy.wait()


def final_kernel(same, k_ref, v_ref, kpart_ref, vpart_ref, state_ref, *refs):
    kgrad_hbm, vgrad_hbm, kgrad_ref, vgrad_ref, sems = refs[-5:]
    rows, width = k_ref.shape
    target = columns(same, width)
    states = [state_ref[j].astype(BF16) for j in range(width // HEAD_DIM)]
    copies = []
    for part in chunks_of(rows):
        for j, state in enumerate(states):
            lanes = lanes_of(j)
            kgrad = kpart_ref[part, lanes] + dot(v_ref[part, lanes], state, 1, 1)
            vgrad = vpart_ref[part, lanes] + dot(k_ref[part, lanes], state)
            kgrad_ref[part, lanes] = kgrad.astype(BF16)
            vgrad_ref[part, lanes] = vgrad.astype(BF16)
        for source, out in ((kgrad_ref, kgrad_hbm), (vgrad_ref, vgrad_hbm)):
            sem = sems.at[len(copies)]
            copy = pltpu.make_async_copy(source.at[part], out.at[part, target], sem)
            copy.start()
            copies.append(copy)
    for copy in copies:
        copy.wait()


def scan_plan(count):
    bits = count.bit_length() - 1
    stages = []
    for stage in range(bits - 1):
        rising, falling = 1 + stage, bits - 1 - stage
        pairs = []
        for r in range(count):
            bit = falling if r & 1 else rising
            useless = stage == 0 if r & 1 else stage == bits - 2
            if not ((r >> bit) & 1 and useless):
                pairs.append((r, r ^ (1 << bit)))
        stages.append((rising, falling, pairs))
    return stages


def join_kernel(backward, done, final, *refs):
    count = lax.axis_size("seq")
    rank = lax.axis_index("seq")
    if backward:
        rank = count - 1 - rank
    odd = (rank & 1) == 1
    plan = scan_plan(count)
    keep_ref, extra_ref = refs[:2]
    came = refs[2:2 + done]
    total = keep_ref[...] + extra_ref[...]
    before = jnp.zeros_like(total)
    for (rising, falling, _), ref in zip(plan, came):
        high = (jnp.where(odd, rank >> falling, rank >> rising) & 1) == 1
        value = ref[...]
        before = before + jnp.where(odd | high, value, 0.0)
        total = total + jnp.where(odd, 0.0, value)
    if final:
        message_ref, state_ref = refs[-2:]
        message_ref[...] = before + jnp.where(odd, 0.0, keep_ref[...])
        state_ref[...] = before + jnp.where(odd, extra_ref[...], 0.0)
    else:
        rising, falling, _ = plan[done]
        high = (jnp.where(odd, rank >> falling, rank >> rising) & 1) == 1
        refs[-1][...] = jnp.where(odd, before + jnp.where(high, 0.0, total), total)


def join(backward, keep, extra, came, final, after=()):
    like = shape(keep.shape, F32)
    return run(
        functools.partial(join_kernel, backward, len(came), final), 4 * keep.size,
        [VMEM] * (2 + len(came)) + [ANYWHERE] * len(after),
        [VMEM, VMEM] if final else VMEM,
        [like, like] if final else like,
        (keep, extra, *came, *after),
    )


def scan_states(keep, extra, backward, beside):
    count = lax.axis_size("seq")
    plan = scan_plan(count)
    came, results = [], []
    message = join(backward, keep, extra, came, not plan)
    for stage, (_, _, pairs) in enumerate(plan):
        arrived = move(message, pairs, backward)
        mine = beside[stage::len(plan)] if stage < len(beside) else []
        made = [work(message) for work in mine]
        results += made
        came = came + [arrived]
        after = [leaf for item in made for leaf in item[-1:]]
        message = join(backward, keep, extra, came, stage == len(plan) - 1, after)
    message, state = message
    return state, nearby(message, backward), results


def move(value, pairs, backward):
    count = lax.axis_size("seq")
    if backward:
        pairs = [(count - 1 - a, count - 1 - b) for a, b in pairs]
    return lax.ppermute(value, "seq", pairs)


def nearby(value, backward):
    return move(value, [(r, r ^ 1) for r in range(lax.axis_size("seq"))], backward)


def shards(query, key_in, value, out_grad, gain):
    rows, width = query.shape
    half = width // 2
    heads = half // HEAD_DIM
    chunks = len(chunks_of(rows))
    peers = lax.axis_size("head")
    full = width * peers
    gain = gain.reshape(1, width)
    pin = lambda x: pltpu.with_memory_space_constraint(x, pltpu.HBM)
    query, key_in, value, out_grad = (pin(x) for x in (query, key_in, value, out_grad))
    unit = 2 * rows * half * HEAD_DIM
    partial = functools.partial

    states = shape((heads, HEAD_DIM, HEAD_DIM), F32)
    inside = shape((chunks, heads, HEAD_DIM, HEAD_DIM), BF16)
    wide = shape((rows, half), F32)
    thin = shape((rows, half), BF16)
    lane_sums = shape((rows, HEAD_DIM), F32)
    whole = shape((rows, width), BF16)
    sems = pltpu.SemaphoreType.DMA((2 * chunks,))

    k1, v1, k2, v2, send, pre1 = run(
        first_kernel, unit, [HBM, HBM], [VMEM] * 6, [thin] * 4 + [states, inside],
        (key_in, value), [sems, sems],
    )
    extra = nearby(send, False)
    keep, pre2 = run(
        second_kernel, unit, [VMEM, VMEM], [VMEM] * 2, [states, inside], (k2, v2),
    )

    def inner_of(same, k, v, pre):
        return lambda message: run(
            partial(inner_kernel, same), 6 * unit,
            [HBM, HBM, VMEM, VMEM, VMEM, VMEM, ANYWHERE], [VMEM] * 5,
            [
                thin, wide, wide,
                shape((half, rows), BF16), shape((heads, rows, rows // chunks), BF16),
            ],
            (query, out_grad, k, v, gain, pre, message),
            [pltpu.VMEM((rows, half), BF16), sems],
        )

    state2, state1, made = scan_states(
        keep, extra, False,
        [inner_of(True, k2, v2, pre2), inner_of(False, k1, v1, pre1)],
    )
    (q2, inner2, scaled2, qturned2, turned2), (q1, inner1, scaled1, qturned1, turned1) = made

    attn2, square, cross = run(
        partial(attn_kernel, False), unit, [VMEM] * 4, [VMEM] * 3, [wide, lane_sums, lane_sums],
        (q2, inner2, scaled2, state2),
    )
    attn1, sums = run(
        partial(attn_kernel, True), unit, [VMEM] * 6, [VMEM] * 2, [wide, shape((peers, 8, rows), F32)],
        (q1, inner1, scaled1, state1, square, cross),
    )
    sums = lax.all_to_all(sums, "head", 0, 0)

    g2, gsend, post2, inv, slope = run(
        partial(grad_kernel, full, peers), unit,
        [VMEM] * 4, [VMEM] * 5, [thin, states, inside, lane_sums, lane_sums],
        (sums, attn2, scaled2, qturned2),
    )
    gextra = nearby(gsend, True)
    g1, gkeep, post1 = run(
        partial(grad_kernel, full, 0), unit, [VMEM] * 5, [VMEM] * 3, [thin, states, inside],
        (inv, slope, attn1, scaled1, qturned1),
    )

    qgrads = []

    def local_of(same, *args):
        def work(message):
            more = [message] + qgrads
            qgrad, kpart, vpart = run(
                partial(local_kernel, same), 9 * unit,
                [VMEM] * len(args) + [ANYWHERE] + [HBM] * len(qgrads), [HBM, VMEM, VMEM],
                [whole, wide, wide], (*args, *more),
                [pltpu.VMEM((rows, half), BF16), sems],
                {len(args) + 1: 0} if qgrads else None,
            )
            qgrads[:] = [qgrad]
            return kpart, vpart

        return work

    gstate1, gstate2, made = scan_states(
        gkeep, gextra, True,
        [
            local_of(False, q1, k1, v1, g1, turned1, state1, pre1, post1),
            local_of(True, q2, k2, v2, g2, turned2, state2, pre2, post2),
        ],
    )
    (kpart1, vpart1), (kpart2, vpart2) = made

    def final_of(same, *args, outs=()):
        scratch = [pltpu.VMEM((rows, half), BF16)] * 2 + [sems]
        aliases = {len(args) + i: i for i in range(len(outs))}
        return run(
            partial(final_kernel, same), 2 * unit, [VMEM] * len(args) + [HBM] * len(outs),
            [HBM, HBM], [whole, whole], (*args, *outs), scratch, aliases,
        )

    outs = final_of(False, k1, v1, kpart1, vpart1, gstate1)
    kgrad, vgrad = final_of(True, k2, v2, kpart2, vpart2, gstate2, outs=outs)
    return qgrads[0], kgrad, vgrad


def solution(mesh):
    spec = P("seq", "head")
    return jax.shard_map(
        shards,
        mesh=mesh,
        in_specs=(spec, spec, spec, spec, P("head")),
        out_specs=(spec, spec, spec),
        check_vma=False,
    )
```

```python
import functools

import jax
import jax.numpy as jnp
from jax import lax
from jax.experimental import pallas as pl
from jax.experimental.pallas import tpu as pltpu
from jax.sharding import PartitionSpec as P

HEAD_DIM = 128
CHUNK = 256
VMEM_BYTES = 12 * 2**20
F32 = jnp.float32
BF16 = jnp.bfloat16
VMEM = pl.BlockSpec(memory_space=pltpu.VMEM)
HBM = pl.BlockSpec(memory_space=pltpu.HBM)
ANYWHERE = pl.BlockSpec(memory_space=pl.ANY)


def dot(a, b, contract_a=1, contract_b=0):
    dims = (((contract_a,), (contract_b,)), ((), ()))
    return lax.dot_general(a, b, dims, preferred_element_type=F32)


def chunks_of(rows):
    size = CHUNK if rows % CHUNK == 0 else rows
    return [slice(i, i + size) for i in range(0, rows, size)]


def shape(dims, dtype):
    return jax.ShapeDtypeStruct(dims, dtype)


def lanes_of(j):
    return slice(j * HEAD_DIM, (j + 1) * HEAD_DIM)


def lower(size):
    row = lax.broadcasted_iota(jnp.int32, (size, size), 0)
    return row >= lax.broadcasted_iota(jnp.int32, (size, size), 1)


def upper(size):
    row = lax.broadcasted_iota(jnp.int32, (size, size), 0)
    return row <= lax.broadcasted_iota(jnp.int32, (size, size), 1)


def run(kernel, flops, in_specs, out_specs, out_shape, args, scratch=(), aliases=None):
    nbytes = sum(a.size * a.dtype.itemsize for a in args)
    return pl.pallas_call(
        kernel,
        in_specs=in_specs,
        out_specs=out_specs,
        out_shape=out_shape,
        scratch_shapes=list(scratch),
        input_output_aliases=aliases or {},
        cost_estimate=pl.CostEstimate(flops=flops, bytes_accessed=nbytes, transcendentals=0),
        compiler_params=pltpu.CompilerParams(vmem_limit_bytes=VMEM_BYTES),
    )(*args)


def columns(same, width):
    odd = lax.rem(lax.axis_index("seq"), 2)
    half = odd if same else 1 - odd
    return pl.ds(pl.multiple_of(half * width, width), width)


def fetches(sources, targets, sems, same):
    rows, width = targets[0].shape
    lanes = columns(same, width)
    copies = []
    for part in chunks_of(rows):
        for source, target in zip(sources, targets):
            sem = sems.at[len(copies)]
            copies.append(pltpu.make_async_copy(source.at[part, lanes], target.at[part], sem))
    return copies


def state_kernel(same, k_hbm, v_hbm, k_ref, v_ref, sum_ref, pre_ref, sems):
    copies = fetches((k_hbm, v_hbm), (k_ref, v_ref), sems, same)
    for copy in copies:
        copy.start()
    heads = sum_ref.shape[0]
    totals = [None] * heads
    for i, part in enumerate(chunks_of(k_ref.shape[0])):
        for copy in copies[2 * i:2 * i + 2]:
            copy.wait()
        for j in range(heads):
            term = dot(k_ref[part, lanes_of(j)], v_ref[part, lanes_of(j)], 0, 0)
            if i:
                pre_ref[i, j] = totals[j].astype(BF16)
            else:
                pre_ref[i, j] = jnp.zeros_like(pre_ref[i, j])
            totals[j] = totals[j] + term if i else term
    for j in range(heads):
        sum_ref[j] = totals[j]


def inner_kernel(same, q_hbm, og_hbm, k_ref, v_ref, gain_ref, pre_ref, after_ref, *outs):
    q_ref, inner_ref, scaled_ref, qturned_ref, turned_ref, og_ref, sems = outs
    rows, width = q_ref.shape
    copies = fetches((q_hbm, og_hbm), (q_ref, og_ref), sems, same)
    for copy in copies:
        copy.start()
    gain = gain_ref[:, columns(same, width)]
    for i, part in enumerate(chunks_of(rows)):
        for copy in copies[2 * i:2 * i + 2]:
            copy.wait()
        for j in range(width // HEAD_DIM):
            lanes = lanes_of(j)
            q, k = q_ref[part, lanes], k_ref[part, lanes]
            size = q.shape[0]
            scores = jnp.where(lower(size), dot(q, k, 1, 1), 0.0).astype(BF16)
            turned_ref[j, part] = jnp.where(upper(size), dot(k, q, 1, 1), 0.0).astype(BF16)
            inner = dot(scores, v_ref[part, lanes])
            inner_ref[part, lanes] = inner + dot(q, pre_ref[i, j]) if i else inner
            scaled_ref[part, lanes] = gain[:, lanes] * og_ref[part, lanes].astype(F32)
            qturned_ref[lanes, part] = q.T


def attn_kernel(last, q_ref, inner_ref, scaled_ref, state_ref, *refs):
    attn_ref = refs[-3] if not last else refs[-2]
    rows, width = q_ref.shape
    states = [state_ref[j].astype(BF16) for j in range(width // HEAD_DIM)]
    for part in chunks_of(rows):
        square, cross = (refs[0][part], refs[1][part]) if last else (None, None)
        for j, state in enumerate(states):
            lanes = lanes_of(j)
            attn = inner_ref[part, lanes] + dot(q_ref[part, lanes], state)
            attn_ref[part, lanes] = attn
            more, crossed = attn * attn, scaled_ref[part, lanes] * attn
            square = more if square is None else square + more
            cross = crossed if cross is None else cross + crossed
        if last:
            square = jnp.sum(square.T, axis=0, keepdims=True)
            cross = jnp.sum(cross.T, axis=0, keepdims=True)
            row = lax.broadcasted_iota(jnp.int32, (8, square.shape[1]), 0)
            sums = jnp.where(row == 0, square, jnp.where(row == 1, cross, 0.0))
            refs[-1][:, part] = sums
        else:
            refs[-2][part] = square
            refs[-1][part] = cross


def factors_kernel(full, parts, refs):
    total = refs[0][...]
    for ref in refs[1:parts]:
        total = total + ref[...]
    inv = lax.rsqrt(total[0:1] / full + 1e-6)
    slope = inv * inv * inv * (total[1:2] / full)
    row = lax.broadcasted_iota(jnp.int32, total.shape, 0)
    both = jnp.where(row == 0, inv, slope).T
    wide = (both.shape[0], HEAD_DIM)
    return jnp.broadcast_to(both[:, 0:1], wide), jnp.broadcast_to(both[:, 1:2], wide)


def grad_kernel(full, parts, *refs):
    if parts:
        inv, slope = factors_kernel(full, parts, refs)
        refs[-2][...] = inv
        refs[-1][...] = slope
        inv_ref, slope_ref = refs[-2:]
        attn_ref, scaled_ref, qturned_ref, g_ref, sum_ref, post_ref = refs[parts:-2]
    else:
        inv_ref, slope_ref, attn_ref, scaled_ref, qturned_ref, g_ref, sum_ref, post_ref = refs
    heads = sum_ref.shape[0]
    totals = [None] * heads
    for i, part in reversed(list(enumerate(chunks_of(g_ref.shape[0])))):
        for j in range(heads):
            lanes = lanes_of(j)
            grad = inv_ref[part] * scaled_ref[part, lanes] - attn_ref[part, lanes] * slope_ref[part]
            grad = grad.astype(BF16)
            g_ref[part, lanes] = grad
            term = dot(qturned_ref[lanes, part], grad)
            if totals[j] is None:
                post_ref[i, j] = jnp.zeros_like(post_ref[i, j])
                totals[j] = term
            else:
                post_ref[i, j] = totals[j].astype(BF16)
                totals[j] = totals[j] + term
    for j in range(heads):
        sum_ref[j] = totals[j]


def local_kernel(same, q_ref, k_ref, v_ref, g_ref, turned_ref, state_ref, pre_ref, post_ref, *refs):
    qgrad_hbm, kpart_ref, vpart_ref, qgrad_ref, sems = refs[-5:]
    rows, width = q_ref.shape
    target = columns(same, width)
    parts = chunks_of(rows)
    copies = []
    for i, part in enumerate(parts):
        for j in range(width // HEAD_DIM):
            lanes = lanes_of(j)
            q, k, v, g = (ref[part, lanes] for ref in (q_ref, k_ref, v_ref, g_ref))
            size = q.shape[0]
            gscores = jnp.where(lower(size), dot(g, v, 1, 1), 0.0).astype(BF16)
            gturned = jnp.where(upper(size), dot(v, g, 1, 1), 0.0).astype(BF16)
            qgrad = dot(gscores, k) + dot(g, state_ref[j].astype(BF16), 1, 1)
            kgrad = dot(gturned, q)
            vgrad = dot(turned_ref[j, part], g)
            if i:
                qgrad = qgrad + dot(g, pre_ref[i, j], 1, 1)
            if i < len(parts) - 1:
                kgrad = kgrad + dot(v, post_ref[i, j], 1, 1)
                vgrad = vgrad + dot(k, post_ref[i, j])
            qgrad_ref[part, lanes] = qgrad.astype(BF16)
            kpart_ref[part, lanes] = kgrad
            vpart_ref[part, lanes] = vgrad
        copy = pltpu.make_async_copy(qgrad_ref.at[part], qgrad_hbm.at[part, target], sems.at[i])
        copy.start()
        copies.append(copy)
    for copy in copies:
        copy.wait()


def final_parts(k_ref, v_ref, kpart_ref, vpart_ref, state_ref, kgrad_ref, vgrad_ref, part):
    for j in range(state_ref.shape[0]):
        lanes = lanes_of(j)
        state = state_ref[j].astype(BF16)
        kgrad = kpart_ref[part, lanes] + dot(v_ref[part, lanes], state, 1, 1)
        vgrad = vpart_ref[part, lanes] + dot(k_ref[part, lanes], state)
        kgrad_ref[part, lanes] = kgrad.astype(BF16)
        vgrad_ref[part, lanes] = vgrad.astype(BF16)


def near_kernel(*refs):
    for part in chunks_of(refs[0].shape[0]):
        final_parts(*refs, part)


def last_kernel(same, *refs):
    kdone_ref, vdone_ref, kgrad_hbm, vgrad_hbm, kgrad_ref, vgrad_ref, sems = refs[5:]
    rows, width = kgrad_ref.shape
    copies = []

    def send(source, out, part, half):
        sem = sems.at[len(copies)]
        target = out.at[part, columns(half, width)]
        copy = pltpu.make_async_copy(source.at[part], target, sem)
        copy.start()
        copies.append(copy)

    send(kdone_ref, kgrad_hbm, slice(0, rows), not same)
    send(vdone_ref, vgrad_hbm, slice(0, rows), not same)
    for part in chunks_of(rows):
        final_parts(*refs[:5], kgrad_ref, vgrad_ref, part)
        send(kgrad_ref, kgrad_hbm, part, same)
        send(vgrad_ref, vgrad_hbm, part, same)
    for copy in copies:
        copy.wait()


def scan_plan(count):
    bits = count.bit_length() - 1
    stages = []
    for stage in range(bits - 1):
        rising, falling = 1 + stage, bits - 1 - stage
        pairs = [(r, r ^ (1 << (falling if r & 1 else rising))) for r in range(count)]
        stages.append((rising, falling, pairs))
    return stages


def join_kernel(backward, done, final, *refs):
    count = lax.axis_size("seq")
    rank = lax.axis_index("seq")
    if backward:
        rank = count - 1 - rank
    odd = (rank & 1) == 1
    plan = scan_plan(count)
    keep_ref, extra_ref = refs[:2]
    came = refs[2:2 + done]
    total = keep_ref[...] + extra_ref[...]
    before = jnp.zeros_like(total)
    for (rising, falling, _), ref in zip(plan, came):
        high = (jnp.where(odd, rank >> falling, rank >> rising) & 1) == 1
        value = ref[...]
        before = before + jnp.where(odd | high, value, 0.0)
        total = total + jnp.where(odd, 0.0, value)
    if final:
        message_ref, state_ref = refs[-2:]
        message_ref[...] = before + jnp.where(odd, 0.0, keep_ref[...])
        state_ref[...] = before + jnp.where(odd, extra_ref[...], 0.0)
    else:
        rising, falling, _ = plan[done]
        high = (jnp.where(odd, rank >> falling, rank >> rising) & 1) == 1
        refs[-1][...] = jnp.where(odd, before + jnp.where(high, 0.0, total), total)


def join(backward, keep, extra, came, final, after=()):
    like = shape(keep.shape, F32)
    return run(
        functools.partial(join_kernel, backward, len(came), final), 4 * keep.size,
        [VMEM] * (2 + len(came)) + [ANYWHERE] * len(after),
        [VMEM, VMEM] if final else VMEM,
        [like, like] if final else like,
        (keep, extra, *came, *after),
    )


def scan_states(keep, extra, backward, beside):
    count = lax.axis_size("seq")
    plan = scan_plan(count)
    came, results = [], []
    message = join(backward, keep, extra, came, not plan)
    for stage, (_, _, pairs) in enumerate(plan):
        arrived = move(message, pairs, backward)
        mine = beside[stage::len(plan)] if stage < len(beside) else []
        made = [work(message) for work in mine]
        results += made
        came = came + [arrived]
        after = [leaf for item in made for leaf in item[-1:]]
        message = join(backward, keep, extra, came, stage == len(plan) - 1, after)
    message, state = message
    return state, nearby(message, backward), results


def move(value, pairs, backward):
    count = lax.axis_size("seq")
    if backward:
        pairs = [(count - 1 - a, count - 1 - b) for a, b in pairs]
    return lax.ppermute(value, "seq", pairs)


def nearby(value, backward):
    return move(value, [(r, r ^ 1) for r in range(lax.axis_size("seq"))], backward)


def shards(query, key_in, value, out_grad, gain):
    rows, width = query.shape
    half = width // 2
    heads = half // HEAD_DIM
    chunks = len(chunks_of(rows))
    peers = lax.axis_size("head")
    full = width * peers
    gain = gain.reshape(1, width)
    pin = lambda x: pltpu.with_memory_space_constraint(x, pltpu.HBM)
    query, key_in, value, out_grad = (pin(x) for x in (query, key_in, value, out_grad))
    unit = 2 * rows * half * HEAD_DIM
    partial = functools.partial

    states = shape((heads, HEAD_DIM, HEAD_DIM), F32)
    inside = shape((chunks, heads, HEAD_DIM, HEAD_DIM), BF16)
    wide = shape((rows, half), F32)
    thin = shape((rows, half), BF16)
    lane_sums = shape((rows, HEAD_DIM), F32)
    whole = shape((rows, width), BF16)
    sems = pltpu.SemaphoreType.DMA((2 * chunks,))

    def states_of(same):
        return run(
            partial(state_kernel, same), unit, [HBM, HBM], [VMEM] * 4, [thin, thin, states, inside],
            (key_in, value), [sems],
        )

    k1, v1, send, pre1 = states_of(False)
    extra = nearby(send, False)
    k2, v2, keep, pre2 = states_of(True)

    def inner_of(same, k, v, pre):
        return lambda message: run(
            partial(inner_kernel, same), 6 * unit,
            [HBM, HBM, VMEM, VMEM, VMEM, VMEM, ANYWHERE], [VMEM] * 5,
            [
                thin, wide, wide,
                shape((half, rows), BF16), shape((heads, rows, rows // chunks), BF16),
            ],
            (query, out_grad, k, v, gain, pre, message),
            [pltpu.VMEM((rows, half), BF16), sems],
        )

    state2, state1, made = scan_states(
        keep, extra, False,
        [inner_of(True, k2, v2, pre2), inner_of(False, k1, v1, pre1)],
    )
    (q2, inner2, scaled2, qturned2, turned2), (q1, inner1, scaled1, qturned1, turned1) = made

    attn2, square, cross = run(
        partial(attn_kernel, False), unit, [VMEM] * 4, [VMEM] * 3, [wide, lane_sums, lane_sums],
        (q2, inner2, scaled2, state2),
    )
    attn1, sums = run(
        partial(attn_kernel, True), unit, [VMEM] * 6, [VMEM] * 2, [wide, shape((8, rows), F32)],
        (q1, inner1, scaled1, state1, square, cross),
    )
    parts = [sums] + [
        lax.ppermute(sums, "head", [(r, (r + shift) % peers) for r in range(peers)])
        for shift in range(1, peers)
    ]

    g2, gsend, post2, inv, slope = run(
        partial(grad_kernel, full, peers), unit,
        [VMEM] * (peers + 3), [VMEM] * 5, [thin, states, inside, lane_sums, lane_sums],
        (*parts, attn2, scaled2, qturned2),
    )
    gextra = nearby(gsend, True)
    g1, gkeep, post1 = run(
        partial(grad_kernel, full, 0), unit, [VMEM] * 5, [VMEM] * 3, [thin, states, inside],
        (inv, slope, attn1, scaled1, qturned1),
    )

    qgrads = []

    def local_of(same, *args):
        def work(message):
            more = [message] + qgrads
            qgrad, kpart, vpart = run(
                partial(local_kernel, same), 9 * unit,
                [VMEM] * len(args) + [ANYWHERE] + [HBM] * len(qgrads), [HBM, VMEM, VMEM],
                [whole, wide, wide], (*args, *more),
                [pltpu.VMEM((rows, half), BF16), sems],
                {len(args) + 1: 0} if qgrads else None,
            )
            qgrads[:] = [qgrad]
            return kpart, vpart

        return work

    gstate1, gstate2, made = scan_states(
        gkeep, gextra, True,
        [
            local_of(False, q1, k1, v1, g1, turned1, state1, pre1, post1),
            local_of(True, q2, k2, v2, g2, turned2, state2, pre2, post2),
        ],
    )
    (kpart1, vpart1), (kpart2, vpart2) = made

    done = run(
        near_kernel, 2 * unit, [VMEM] * 5, [VMEM] * 2, [thin, thin],
        (k1, v1, kpart1, vpart1, gstate1),
    )
    kgrad, vgrad = run(
        partial(last_kernel, True), 2 * unit, [VMEM] * 7, [HBM, HBM], [whole, whole],
        (k2, v2, kpart2, vpart2, gstate2, *done),
        [pltpu.VMEM((rows, half), BF16)] * 2 + [pltpu.SemaphoreType.DMA((2 * chunks + 2,))],
    )
    return qgrads[0], kgrad, vgrad


def solution(mesh):
    spec = P("seq", "head")
    return jax.shard_map(
        shards,
        mesh=mesh,
        in_specs=(spec, spec, spec, spec, P("head")),
        out_specs=(spec, spec, spec),
        check_vma=False,
    )
```

```python
import functools

import jax
import jax.numpy as jnp
from jax import lax
from jax.experimental import pallas as pl
from jax.experimental.pallas import tpu as pltpu
from jax.sharding import PartitionSpec as P

HEAD_DIM = 128
CHUNK = 256
VMEM_BYTES = 12 * 2**20
F32 = jnp.float32
BF16 = jnp.bfloat16
VMEM = pl.BlockSpec(memory_space=pltpu.VMEM)
HBM = pl.BlockSpec(memory_space=pltpu.HBM)
ANYWHERE = pl.BlockSpec(memory_space=pl.ANY)


def dot(a, b, contract_a=1, contract_b=0):
    dims = (((contract_a,), (contract_b,)), ((), ()))
    return lax.dot_general(a, b, dims, preferred_element_type=F32)


def chunks_of(rows):
    size = CHUNK if rows % CHUNK == 0 else rows
    return [slice(i, i + size) for i in range(0, rows, size)]


def shape(dims, dtype):
    return jax.ShapeDtypeStruct(dims, dtype)


def lanes_of(j):
    return slice(j * HEAD_DIM, (j + 1) * HEAD_DIM)


def lower(size):
    row = lax.broadcasted_iota(jnp.int32, (size, size), 0)
    return row >= lax.broadcasted_iota(jnp.int32, (size, size), 1)


def upper(size):
    row = lax.broadcasted_iota(jnp.int32, (size, size), 0)
    return row <= lax.broadcasted_iota(jnp.int32, (size, size), 1)


def run(kernel, flops, in_specs, out_specs, out_shape, args, scratch=(), aliases=None):
    nbytes = sum(a.size * a.dtype.itemsize for a in args)
    return pl.pallas_call(
        kernel,
        in_specs=in_specs,
        out_specs=out_specs,
        out_shape=out_shape,
        scratch_shapes=list(scratch),
        input_output_aliases=aliases or {},
        cost_estimate=pl.CostEstimate(flops=flops, bytes_accessed=nbytes, transcendentals=0),
        compiler_params=pltpu.CompilerParams(vmem_limit_bytes=VMEM_BYTES),
    )(*args)


def columns(same, width):
    odd = lax.rem(lax.axis_index("seq"), 2)
    half = odd if same else 1 - odd
    return pl.ds(pl.multiple_of(half * width, width), width)


def fetches(sources, targets, sems, same):
    rows, width = targets[0].shape
    lanes = columns(same, width)
    copies = []
    for part in chunks_of(rows):
        for source, target in zip(sources, targets):
            sem = sems.at[len(copies)]
            copies.append(pltpu.make_async_copy(source.at[part, lanes], target.at[part], sem))
    return copies


def state_kernel(same, k_hbm, v_hbm, k_ref, v_ref, sum_ref, pre_ref, sems):
    copies = fetches((k_hbm, v_hbm), (k_ref, v_ref), sems, same)
    for copy in copies:
        copy.start()
    heads = sum_ref.shape[0]
    totals = [None] * heads
    for i, part in enumerate(chunks_of(k_ref.shape[0])):
        for copy in copies[2 * i:2 * i + 2]:
            copy.wait()
        for j in range(heads):
            term = dot(k_ref[part, lanes_of(j)], v_ref[part, lanes_of(j)], 0, 0)
            if i:
                pre_ref[i, j] = totals[j].astype(BF16)
            else:
                pre_ref[i, j] = jnp.zeros_like(pre_ref[i, j])
            totals[j] = totals[j] + term if i else term
    for j in range(heads):
        sum_ref[j] = totals[j]


def inner_kernel(same, q_hbm, og_hbm, k_ref, v_ref, gain_ref, pre_ref, after_ref, *outs):
    q_ref, inner_ref, scaled_ref, qturned_ref, turned_ref, og_ref, sems = outs
    rows, width = q_ref.shape
    copies = fetches((q_hbm, og_hbm), (q_ref, og_ref), sems, same)
    for copy in copies:
        copy.start()
    gain = gain_ref[:, columns(same, width)]
    for i, part in enumerate(chunks_of(rows)):
        for copy in copies[2 * i:2 * i + 2]:
            copy.wait()
        for j in range(width // HEAD_DIM):
            lanes = lanes_of(j)
            q, k = q_ref[part, lanes], k_ref[part, lanes]
            size = q.shape[0]
            scores = jnp.where(lower(size), dot(q, k, 1, 1), 0.0).astype(BF16)
            turned_ref[j, part] = jnp.where(upper(size), dot(k, q, 1, 1), 0.0).astype(BF16)
            inner = dot(scores, v_ref[part, lanes])
            inner_ref[part, lanes] = inner + dot(q, pre_ref[i, j]) if i else inner
            scaled_ref[part, lanes] = gain[:, lanes] * og_ref[part, lanes].astype(F32)
            qturned_ref[lanes, part] = q.T


def attn_kernel(last, q_ref, inner_ref, scaled_ref, state_ref, *refs):
    attn_ref = refs[-3] if not last else refs[-2]
    rows, width = q_ref.shape
    states = [state_ref[j].astype(BF16) for j in range(width // HEAD_DIM)]
    for part in chunks_of(rows):
        square, cross = (refs[0][part], refs[1][part]) if last else (None, None)
        for j, state in enumerate(states):
            lanes = lanes_of(j)
            attn = inner_ref[part, lanes] + dot(q_ref[part, lanes], state)
            attn_ref[part, lanes] = attn
            more, crossed = attn * attn, scaled_ref[part, lanes] * attn
            square = more if square is None else square + more
            cross = crossed if cross is None else cross + crossed
        if last:
            square = jnp.sum(square.T, axis=0, keepdims=True)
            cross = jnp.sum(cross.T, axis=0, keepdims=True)
            row = lax.broadcasted_iota(jnp.int32, (8, square.shape[1]), 0)
            sums = jnp.where(row == 0, square, jnp.where(row == 1, cross, 0.0))
            refs[-1][:, part] = sums
        else:
            refs[-2][part] = square
            refs[-1][part] = cross


def factors_kernel(full, parts, refs):
    total = refs[0][...]
    for ref in refs[1:parts]:
        total = total + ref[...]
    inv = lax.rsqrt(total[0:1] / full + 1e-6)
    slope = inv * inv * inv * (total[1:2] / full)
    row = lax.broadcasted_iota(jnp.int32, total.shape, 0)
    both = jnp.where(row == 0, inv, slope).T
    wide = (both.shape[0], HEAD_DIM)
    return jnp.broadcast_to(both[:, 0:1], wide), jnp.broadcast_to(both[:, 1:2], wide)


def grad_kernel(full, parts, *refs):
    if parts:
        inv, slope = factors_kernel(full, parts, refs)
        refs[-2][...] = inv
        refs[-1][...] = slope
        inv_ref, slope_ref = refs[-2:]
        attn_ref, scaled_ref, qturned_ref, g_ref, sum_ref, post_ref = refs[parts:-2]
    else:
        inv_ref, slope_ref, attn_ref, scaled_ref, qturned_ref, g_ref, sum_ref, post_ref = refs
    heads = sum_ref.shape[0]
    totals = [None] * heads
    for i, part in reversed(list(enumerate(chunks_of(g_ref.shape[0])))):
        for j in range(heads):
            lanes = lanes_of(j)
            grad = inv_ref[part] * scaled_ref[part, lanes] - attn_ref[part, lanes] * slope_ref[part]
            grad = grad.astype(BF16)
            g_ref[part, lanes] = grad
            term = dot(qturned_ref[lanes, part], grad)
            if totals[j] is None:
                post_ref[i, j] = jnp.zeros_like(post_ref[i, j])
                totals[j] = term
            else:
                post_ref[i, j] = totals[j].astype(BF16)
                totals[j] = totals[j] + term
    for j in range(heads):
        sum_ref[j] = totals[j]


def local_kernel(same, q_ref, k_ref, v_ref, g_ref, turned_ref, state_ref, pre_ref, post_ref, *refs):
    qgrad_hbm, kpart_ref, vpart_ref, qgrad_ref, sems = refs[-5:]
    rows, width = q_ref.shape
    target = columns(same, width)
    parts = chunks_of(rows)
    copies = []
    for i, part in enumerate(parts):
        for j in range(width // HEAD_DIM):
            lanes = lanes_of(j)
            q, k, v, g = (ref[part, lanes] for ref in (q_ref, k_ref, v_ref, g_ref))
            size = q.shape[0]
            gscores = jnp.where(lower(size), dot(g, v, 1, 1), 0.0).astype(BF16)
            gturned = jnp.where(upper(size), dot(v, g, 1, 1), 0.0).astype(BF16)
            qgrad = dot(gscores, k) + dot(g, state_ref[j].astype(BF16), 1, 1)
            kgrad = dot(gturned, q)
            vgrad = dot(turned_ref[j, part], g)
            if i:
                qgrad = qgrad + dot(g, pre_ref[i, j], 1, 1)
            if i < len(parts) - 1:
                kgrad = kgrad + dot(v, post_ref[i, j], 1, 1)
                vgrad = vgrad + dot(k, post_ref[i, j])
            qgrad_ref[part, lanes] = qgrad.astype(BF16)
            kpart_ref[part, lanes] = kgrad
            vpart_ref[part, lanes] = vgrad
        copy = pltpu.make_async_copy(qgrad_ref.at[part], qgrad_hbm.at[part, target], sems.at[i])
        copy.start()
        copies.append(copy)
    for copy in copies:
        copy.wait()


def final_parts(k_ref, v_ref, kpart_ref, vpart_ref, state_ref, kgrad_ref, vgrad_ref, part):
    for j in range(state_ref.shape[0]):
        lanes = lanes_of(j)
        state = state_ref[j].astype(BF16)
        kgrad = kpart_ref[part, lanes] + dot(v_ref[part, lanes], state, 1, 1)
        vgrad = vpart_ref[part, lanes] + dot(k_ref[part, lanes], state)
        kgrad_ref[part, lanes] = kgrad.astype(BF16)
        vgrad_ref[part, lanes] = vgrad.astype(BF16)


def near_kernel(*refs):
    for part in chunks_of(refs[0].shape[0]):
        final_parts(*refs, part)


def last_kernel(same, *refs):
    kdone_ref, vdone_ref, kgrad_hbm, vgrad_hbm, kgrad_ref, vgrad_ref, sems = refs[5:]
    rows, width = kgrad_ref.shape
    copies = []

    def send(source, out, part, half):
        sem = sems.at[len(copies)]
        target = out.at[part, columns(half, width)]
        copy = pltpu.make_async_copy(source.at[part], target, sem)
        copy.start()
        copies.append(copy)

    send(kdone_ref, kgrad_hbm, slice(0, rows), not same)
    send(vdone_ref, vgrad_hbm, slice(0, rows), not same)
    for part in chunks_of(rows):
        final_parts(*refs[:5], kgrad_ref, vgrad_ref, part)
        send(kgrad_ref, kgrad_hbm, part, same)
        send(vgrad_ref, vgrad_hbm, part, same)
    for copy in copies:
        copy.wait()


def scan_plan(count):
    bits = count.bit_length() - 1
    stages = []
    for stage in range(bits - 1):
        rising, falling = 1 + stage, bits - 1 - stage
        pairs = [(r, r ^ (1 << (falling if r & 1 else rising))) for r in range(count)]
        stages.append((rising, falling, pairs))
    return stages


def join_kernel(backward, done, final, *refs):
    count = lax.axis_size("seq")
    rank = lax.axis_index("seq")
    if backward:
        rank = count - 1 - rank
    odd = (rank & 1) == 1
    plan = scan_plan(count)
    keep_ref, extra_ref = refs[:2]
    came = refs[2:2 + done]
    total = keep_ref[...] + extra_ref[...]
    before = jnp.zeros_like(total)
    for (rising, falling, _), ref in zip(plan, came):
        high = (jnp.where(odd, rank >> falling, rank >> rising) & 1) == 1
        value = ref[...]
        before = before + jnp.where(odd | high, value, 0.0)
        total = total + jnp.where(odd, 0.0, value)
    if final:
        message_ref, state_ref = refs[-2:]
        message_ref[...] = before + jnp.where(odd, 0.0, keep_ref[...])
        state_ref[...] = before + jnp.where(odd, extra_ref[...], 0.0)
    else:
        rising, falling, _ = plan[done]
        high = (jnp.where(odd, rank >> falling, rank >> rising) & 1) == 1
        refs[-1][...] = jnp.where(odd, before + jnp.where(high, 0.0, total), total)


def join(backward, keep, extra, came, final, after=()):
    like = shape(keep.shape, F32)
    return run(
        functools.partial(join_kernel, backward, len(came), final), 4 * keep.size,
        [VMEM] * (2 + len(came)) + [ANYWHERE] * len(after),
        [VMEM, VMEM] if final else VMEM,
        [like, like] if final else like,
        (keep, extra, *came, *after),
    )


def scan_states(keep, extra, backward, beside):
    count = lax.axis_size("seq")
    plan = scan_plan(count)
    came, results = [], []
    message = join(backward, keep, extra, came, not plan)
    for stage, (_, _, pairs) in enumerate(plan):
        arrived = move(message, pairs, backward)
        mine = beside[stage::len(plan)] if stage < len(beside) else []
        made = [work(message) for work in mine]
        results += made
        came = came + [arrived]
        after = [leaf for item in made for leaf in item[-1:]]
        message = join(backward, keep, extra, came, stage == len(plan) - 1, after)
    message, state = message
    return state, nearby(message, backward), results


def move(value, pairs, backward):
    count = lax.axis_size("seq")
    if backward:
        pairs = [(count - 1 - a, count - 1 - b) for a, b in pairs]
    return lax.ppermute(value, "seq", pairs)


def nearby(value, backward):
    return move(value, [(r, r ^ 1) for r in range(lax.axis_size("seq"))], backward)


def shards(query, key_in, value, out_grad, gain):
    rows, width = query.shape
    half = width // 2
    heads = half // HEAD_DIM
    chunks = len(chunks_of(rows))
    peers = lax.axis_size("head")
    full = width * peers
    gain = gain.reshape(1, width)
    pin = lambda x: pltpu.with_memory_space_constraint(x, pltpu.HBM)
    query, key_in, value, out_grad = (pin(x) for x in (query, key_in, value, out_grad))
    unit = 2 * rows * half * HEAD_DIM
    partial = functools.partial

    states = shape((heads, HEAD_DIM, HEAD_DIM), F32)
    inside = shape((chunks, heads, HEAD_DIM, HEAD_DIM), BF16)
    wide = shape((rows, half), F32)
    thin = shape((rows, half), BF16)
    lane_sums = shape((rows, HEAD_DIM), F32)
    whole = shape((rows, width), BF16)
    sems = pltpu.SemaphoreType.DMA((2 * chunks,))

    def states_of(same):
        return run(
            partial(state_kernel, same), unit, [HBM, HBM], [VMEM] * 4, [thin, thin, states, inside],
            (key_in, value), [sems],
        )

    k1, v1, send, pre1 = states_of(False)
    extra = nearby(send, False)
    k2, v2, keep, pre2 = states_of(True)

    def inner_of(same, k, v, pre):
        return lambda message: run(
            partial(inner_kernel, same), 6 * unit,
            [HBM, HBM, VMEM, VMEM, VMEM, VMEM, ANYWHERE], [VMEM] * 5,
            [
                thin, wide, wide,
                shape((half, rows), BF16), shape((heads, rows, rows // chunks), BF16),
            ],
            (query, out_grad, k, v, gain, pre, message),
            [pltpu.VMEM((rows, half), BF16), sems],
        )

    state2, state1, made = scan_states(
        keep, extra, False,
        [inner_of(True, k2, v2, pre2), inner_of(False, k1, v1, pre1)],
    )
    (q2, inner2, scaled2, qturned2, turned2), (q1, inner1, scaled1, qturned1, turned1) = made

    attn2, square, cross = run(
        partial(attn_kernel, False), unit, [VMEM] * 4, [VMEM] * 3, [wide, lane_sums, lane_sums],
        (q2, inner2, scaled2, state2),
    )
    attn1, sums = run(
        partial(attn_kernel, True), unit, [VMEM] * 6, [VMEM] * 2, [wide, shape((8, rows), F32)],
        (q1, inner1, scaled1, state1, square, cross),
    )
    parts = [sums] + [
        lax.ppermute(sums, "head", [(r, r ^ other) for r in range(peers)])
        for other in range(1, peers)
    ]

    g2, gsend, post2, inv, slope = run(
        partial(grad_kernel, full, peers), unit,
        [VMEM] * (peers + 3), [VMEM] * 5, [thin, states, inside, lane_sums, lane_sums],
        (*parts, attn2, scaled2, qturned2),
    )
    gextra = nearby(gsend, True)
    g1, gkeep, post1 = run(
        partial(grad_kernel, full, 0), unit, [VMEM] * 5, [VMEM] * 3, [thin, states, inside],
        (inv, slope, attn1, scaled1, qturned1),
    )

    qgrads = []

    def local_of(same, *args):
        def work(message):
            more = [message] + qgrads
            qgrad, kpart, vpart = run(
                partial(local_kernel, same), 9 * unit,
                [VMEM] * len(args) + [ANYWHERE] + [HBM] * len(qgrads), [HBM, VMEM, VMEM],
                [whole, wide, wide], (*args, *more),
                [pltpu.VMEM((rows, half), BF16), sems],
                {len(args) + 1: 0} if qgrads else None,
            )
            qgrads[:] = [qgrad]
            return kpart, vpart

        return work

    gstate1, gstate2, made = scan_states(
        gkeep, gextra, True,
        [
            local_of(False, q1, k1, v1, g1, turned1, state1, pre1, post1),
            local_of(True, q2, k2, v2, g2, turned2, state2, pre2, post2),
        ],
    )
    (kpart1, vpart1), (kpart2, vpart2) = made

    done = run(
        near_kernel, 2 * unit, [VMEM] * 5, [VMEM] * 2, [thin, thin],
        (k1, v1, kpart1, vpart1, gstate1),
    )
    kgrad, vgrad = run(
        partial(last_kernel, True), 2 * unit, [VMEM] * 7, [HBM, HBM], [whole, whole],
        (k2, v2, kpart2, vpart2, gstate2, *done),
        [pltpu.VMEM((rows, half), BF16)] * 2 + [pltpu.SemaphoreType.DMA((2 * chunks + 2,))],
    )
    return qgrads[0], kgrad, vgrad


def solution(mesh):
    spec = P("seq", "head")
    return jax.shard_map(
        shards,
        mesh=mesh,
        in_specs=(spec, spec, spec, spec, P("head")),
        out_specs=(spec, spec, spec),
        check_vma=False,
    )
```

```python
import functools

import jax
import jax.numpy as jnp
from jax import lax
from jax.experimental import pallas as pl
from jax.experimental.pallas import tpu as pltpu
from jax.sharding import PartitionSpec as P

HEAD_DIM = 128
CHUNK = 256
VMEM_BYTES = 12 * 2**20
F32 = jnp.float32
BF16 = jnp.bfloat16
VMEM = pl.BlockSpec(memory_space=pltpu.VMEM)
HBM = pl.BlockSpec(memory_space=pltpu.HBM)
ANYWHERE = pl.BlockSpec(memory_space=pl.ANY)


def dot(a, b, contract_a=1, contract_b=0):
    dims = (((contract_a,), (contract_b,)), ((), ()))
    return lax.dot_general(a, b, dims, preferred_element_type=F32)


def chunks_of(rows):
    size = CHUNK if rows % CHUNK == 0 else rows
    return [slice(i, i + size) for i in range(0, rows, size)]


def shape(dims, dtype):
    return jax.ShapeDtypeStruct(dims, dtype)


def lanes_of(j):
    return slice(j * HEAD_DIM, (j + 1) * HEAD_DIM)


def lower(size):
    row = lax.broadcasted_iota(jnp.int32, (size, size), 0)
    return row >= lax.broadcasted_iota(jnp.int32, (size, size), 1)


def upper(size):
    row = lax.broadcasted_iota(jnp.int32, (size, size), 0)
    return row <= lax.broadcasted_iota(jnp.int32, (size, size), 1)


def run(kernel, flops, in_specs, out_specs, out_shape, args, scratch=(), aliases=None):
    nbytes = sum(a.size * a.dtype.itemsize for a in args)
    return pl.pallas_call(
        kernel,
        in_specs=in_specs,
        out_specs=out_specs,
        out_shape=out_shape,
        scratch_shapes=list(scratch),
        input_output_aliases=aliases or {},
        cost_estimate=pl.CostEstimate(flops=flops, bytes_accessed=nbytes, transcendentals=0),
        compiler_params=pltpu.CompilerParams(vmem_limit_bytes=VMEM_BYTES),
    )(*args)


def is_hub():
    return lax.rem(lax.axis_index("seq"), 2) == 1


def columns(half, width):
    return slice(half * width, (half + 1) * width)


def fetches(sources, targets, sems, half):
    rows, width = targets[0].shape
    lanes = columns(half, width)
    copies = []
    for part in chunks_of(rows):
        for source, target in zip(sources, targets):
            sem = sems.at[len(copies)]
            copies.append(pltpu.make_async_copy(source.at[part, lanes], target.at[part], sem))
    return copies


def sum_states(k_ref, v_ref, sum_ref, pre_ref, copies=()):
    heads = sum_ref.shape[0]
    totals = [None] * heads
    for i, part in enumerate(chunks_of(k_ref.shape[0])):
        for copy in copies[2 * i:2 * i + 2]:
            copy.wait()
        for j in range(heads):
            term = dot(k_ref[part, lanes_of(j)], v_ref[part, lanes_of(j)], 0, 0)
            if i:
                pre_ref[i, j] = totals[j].astype(BF16)
            else:
                pre_ref[i, j] = jnp.zeros_like(pre_ref[i, j])
            totals[j] = totals[j] + term if i else term
    for j in range(heads):
        sum_ref[j] = totals[j]


def first_kernel(k_hbm, v_hbm, k0, v0, k1, v1, sum_ref, pre_ref, sems0, sems1):
    now = fetches((k_hbm, v_hbm), (k0, v0), sems0, 0)
    later = fetches((k_hbm, v_hbm), (k1, v1), sems1, 1)
    for copy in now + later:
        copy.start()
    sum_states(k0, v0, sum_ref, pre_ref, now)
    for copy in later:
        copy.wait()


def inner_kernel(half, q_hbm, og_hbm, k_ref, v_ref, gain_ref, pre_ref, *refs):
    q_ref, inner_ref, scaled_ref, qturned_ref, turned_ref, og_ref, sems = refs[-7:]
    rows, width = q_ref.shape
    copies = fetches((q_hbm, og_hbm), (q_ref, og_ref), sems, half)
    for copy in copies:
        copy.start()
    gain = gain_ref[:, columns(half, width)]
    for i, part in enumerate(chunks_of(rows)):
        for copy in copies[2 * i:2 * i + 2]:
            copy.wait()
        for j in range(width // HEAD_DIM):
            lanes = lanes_of(j)
            q, k = q_ref[part, lanes], k_ref[part, lanes]
            size = q.shape[0]
            scores = jnp.where(lower(size), dot(q, k, 1, 1), 0.0).astype(BF16)
            turned_ref[j, part] = jnp.where(upper(size), dot(k, q, 1, 1), 0.0).astype(BF16)
            inner = dot(scores, v_ref[part, lanes])
            inner_ref[part, lanes] = inner + dot(q, pre_ref[i, j]) if i else inner
            scaled_ref[part, lanes] = gain[:, lanes] * og_ref[part, lanes].astype(F32)
            qturned_ref[lanes, part] = q.T


def chosen_states(own_ref, came_ref):
    hub = is_hub()
    heads = range(own_ref.shape[0])
    return [jnp.where(hub, own_ref[j], came_ref[j]).astype(BF16) for j in heads]


def attn_kernel(last, q_ref, inner_ref, scaled_ref, own_ref, came_ref, *refs):
    attn_ref, state_ref = refs[2:4] if last else refs[:2]
    rows, width = q_ref.shape
    states = chosen_states(own_ref, came_ref)
    for j, state in enumerate(states):
        state_ref[j] = state
    for part in chunks_of(rows):
        square, cross = (refs[0][part], refs[1][part]) if last else (None, None)
        for j, state in enumerate(states):
            lanes = lanes_of(j)
            attn = inner_ref[part, lanes] + dot(q_ref[part, lanes], state)
            attn_ref[part, lanes] = attn
            more, crossed = attn * attn, scaled_ref[part, lanes] * attn
            square = more if square is None else square + more
            cross = crossed if cross is None else cross + crossed
        if last:
            square = jnp.sum(square.T, axis=0, keepdims=True)
            cross = jnp.sum(cross.T, axis=0, keepdims=True)
            row = lax.broadcasted_iota(jnp.int32, (8, square.shape[1]), 0)
            sums = jnp.where(row == 0, square, jnp.where(row == 1, cross, 0.0))
            refs[-1][:, part] = sums
        else:
            refs[-2][part] = square
            refs[-1][part] = cross


def factors_kernel(full, parts, refs):
    total = refs[0][...]
    for ref in refs[1:parts]:
        total = total + ref[...]
    inv = lax.rsqrt(total[0:1] / full + 1e-6)
    slope = inv * inv * inv * (total[1:2] / full)
    row = lax.broadcasted_iota(jnp.int32, total.shape, 0)
    both = jnp.where(row == 0, inv, slope).T
    wide = (both.shape[0], HEAD_DIM)
    return jnp.broadcast_to(both[:, 0:1], wide), jnp.broadcast_to(both[:, 1:2], wide)


def grad_kernel(full, parts, *refs):
    if parts:
        inv, slope = factors_kernel(full, parts, refs)
        refs[-2][...] = inv
        refs[-1][...] = slope
        inv_ref, slope_ref = refs[-2:]
        attn_ref, scaled_ref, qturned_ref, g_ref, sum_ref, post_ref = refs[parts:-2]
    else:
        inv_ref, slope_ref, attn_ref, scaled_ref, qturned_ref, g_ref, sum_ref, post_ref = refs
    heads = sum_ref.shape[0]
    totals = [None] * heads
    for i, part in reversed(list(enumerate(chunks_of(g_ref.shape[0])))):
        for j in range(heads):
            lanes = lanes_of(j)
            grad = inv_ref[part] * scaled_ref[part, lanes] - attn_ref[part, lanes] * slope_ref[part]
            grad = grad.astype(BF16)
            g_ref[part, lanes] = grad
            term = dot(qturned_ref[lanes, part], grad)
            if totals[j] is None:
                post_ref[i, j] = jnp.zeros_like(post_ref[i, j])
                totals[j] = term
            else:
                post_ref[i, j] = totals[j].astype(BF16)
                totals[j] = totals[j] + term
    for j in range(heads):
        sum_ref[j] = totals[j]


def local_kernel(half, q_ref, k_ref, v_ref, g_ref, turned_ref, state_ref, pre_ref, post_ref, *refs):
    qgrad_hbm, kpart_ref, vpart_ref, qgrad_ref, sems = refs[-5:]
    rows, width = q_ref.shape
    target = columns(half, width)
    parts = chunks_of(rows)
    copies = []
    for i, part in enumerate(parts):
        for j in range(width // HEAD_DIM):
            lanes = lanes_of(j)
            q, k, v, g = (ref[part, lanes] for ref in (q_ref, k_ref, v_ref, g_ref))
            size = q.shape[0]
            gscores = jnp.where(lower(size), dot(g, v, 1, 1), 0.0).astype(BF16)
            gturned = jnp.where(upper(size), dot(v, g, 1, 1), 0.0).astype(BF16)
            qgrad = dot(gscores, k) + dot(g, state_ref[j], 1, 1)
            kgrad = dot(gturned, q)
            vgrad = dot(turned_ref[j, part], g)
            if i:
                qgrad = qgrad + dot(g, pre_ref[i, j], 1, 1)
            if i < len(parts) - 1:
                kgrad = kgrad + dot(v, post_ref[i, j], 1, 1)
                vgrad = vgrad + dot(k, post_ref[i, j])
            qgrad_ref[part, lanes] = qgrad.astype(BF16)
            kpart_ref[part, lanes] = kgrad
            vpart_ref[part, lanes] = vgrad
        copy = pltpu.make_async_copy(qgrad_ref.at[part], qgrad_hbm.at[part, target], sems.at[i])
        copy.start()
        copies.append(copy)
    for copy in copies:
        copy.wait()


def final_parts(k_ref, v_ref, kpart_ref, vpart_ref, states, kgrad_ref, vgrad_ref, part):
    for j, state in enumerate(states):
        lanes = lanes_of(j)
        kgrad = kpart_ref[part, lanes] + dot(v_ref[part, lanes], state, 1, 1)
        vgrad = vpart_ref[part, lanes] + dot(k_ref[part, lanes], state)
        kgrad_ref[part, lanes] = kgrad.astype(BF16)
        vgrad_ref[part, lanes] = vgrad.astype(BF16)


def near_kernel(*refs):
    states = chosen_states(*refs[4:6])
    for part in chunks_of(refs[0].shape[0]):
        final_parts(*refs[:4], states, *refs[6:], part)


def last_kernel(*refs):
    kdone_ref, vdone_ref, kgrad_hbm, vgrad_hbm, kgrad_ref, vgrad_ref, sems = refs[6:]
    rows, width = kgrad_ref.shape
    copies = []

    def send(source, out, part, half):
        sem = sems.at[len(copies)]
        target = out.at[part, columns(half, width)]
        copy = pltpu.make_async_copy(source.at[part], target, sem)
        copy.start()
        copies.append(copy)

    send(kdone_ref, kgrad_hbm, slice(0, rows), 0)
    send(vdone_ref, vgrad_hbm, slice(0, rows), 0)
    states = chosen_states(*refs[4:6])
    for part in chunks_of(rows):
        final_parts(*refs[:4], states, kgrad_ref, vgrad_ref, part)
        send(kgrad_ref, kgrad_hbm, part, 1)
        send(vgrad_ref, vgrad_hbm, part, 1)
    for copy in copies:
        copy.wait()


def stage_bits(half):
    bits = (lax.axis_size("seq") // 2).bit_length() - 1
    return list(range(bits)) if half == 0 else list(range(bits))[::-1]


def join_kernel(backward, half, done, *refs):
    pairs = lax.axis_size("seq") // 2
    place = lax.axis_index("seq") // 2
    if backward:
        place = pairs - 1 - place
    bits = stage_bits(half)
    highs = [((place >> bit) & 1) == 1 for bit in bits]
    keep_ref, extra_ref = refs[:2]
    total = keep_ref[...] + extra_ref[...]
    before = jnp.zeros_like(total)
    for high, ref in zip(highs, refs[2:2 + done]):
        value = ref[...]
        if half == 0:
            before = before + jnp.where(high, value, 0.0)
            total = total + value
        else:
            before = before + value
    if done == len(bits):
        message_ref, own_ref = refs[-2:]
        message_ref[...] = before + keep_ref[...] if backward else before
        own_ref[...] = before if backward else before + extra_ref[...]
    elif half == 0:
        refs[-1][...] = total
    else:
        refs[-1][...] = before + jnp.where(highs[done], 0.0, total)


def join(backward, half, keep, extra, came, after):
    final = len(came) == len(stage_bits(half))
    like = shape(keep.shape, F32)
    return run(
        functools.partial(join_kernel, backward, half, len(came)), 4 * keep.size,
        [VMEM] * (2 + len(came)) + [ANYWHERE] * len(after),
        [VMEM, VMEM] if final else VMEM,
        [like, like] if final else like,
        (keep, extra, *came, *after),
    )


def scan_states(keeps, extras, backward, beside):
    stages = len(stage_bits(0))
    came, results, after = ([], []), [], []
    for stage in range(stages):
        messages = []
        for half in (0, 1):
            message = join(backward, half, keeps[half], extras[half], came[half], after + messages)
            messages.append(message)
            flip = 1 << stage_bits(half)[stage]
            pairs = [(2 * p + 1, 2 * (p ^ flip) + 1) for p in range(lax.axis_size("seq") // 2)]
            came[half].append(lax.ppermute(message, "seq", pairs))
        mine = beside[stage:] if stage == stages - 1 else beside[stage:stage + 1]
        made = [work(messages) for work in mine]
        after = [item[-1] for item in made]
        results += made
    states, last = [], []
    for half in (0, 1):
        message, own = join(backward, half, keeps[half], extras[half], came[half], after + last)
        last = [message]
        states.append((own, nearby(message)))
    return states, results


def nearby(value):
    return lax.ppermute(value, "seq", [(r, r ^ 1) for r in range(lax.axis_size("seq"))])


def shards(query, key_in, value, out_grad, gain):
    rows, width = query.shape
    half = width // 2
    heads = half // HEAD_DIM
    chunks = len(chunks_of(rows))
    peers = lax.axis_size("head")
    full = width * peers
    gain = gain.reshape(1, width)
    pin = lambda x: pltpu.with_memory_space_constraint(x, pltpu.HBM)
    query, key_in, value, out_grad = (pin(x) for x in (query, key_in, value, out_grad))
    unit = 2 * rows * half * HEAD_DIM
    partial = functools.partial

    states = shape((heads, HEAD_DIM, HEAD_DIM), F32)
    inside = shape((chunks, heads, HEAD_DIM, HEAD_DIM), BF16)
    wide = shape((rows, half), F32)
    thin = shape((rows, half), BF16)
    lane_sums = shape((rows, HEAD_DIM), F32)
    whole = shape((rows, width), BF16)
    sems = pltpu.SemaphoreType.DMA((2 * chunks,))

    k0, v0, k1, v1, sum0, pre0 = run(
        first_kernel, unit, [HBM, HBM], [VMEM] * 6, [thin] * 4 + [states, inside],
        (key_in, value), [sems, sems],
    )
    extra0 = nearby(sum0)
    sum1, pre1 = run(sum_states, unit, [VMEM, VMEM], [VMEM] * 2, [states, inside], (k1, v1))
    extra1 = nearby(sum1)

    def inner_of(half_number, k, v, pre):
        return lambda messages: run(
            partial(inner_kernel, half_number), 6 * unit,
            [HBM, HBM, VMEM, VMEM, VMEM, VMEM] + [ANYWHERE] * len(messages), [VMEM] * 5,
            [
                thin, wide, wide,
                shape((half, rows), BF16), shape((heads, rows, rows // chunks), BF16),
            ],
            (query, out_grad, k, v, gain, pre, *messages),
            [pltpu.VMEM((rows, half), BF16), sems],
        )

    (before0, before1), made = scan_states(
        (sum0, sum1), (extra0, extra1), False,
        [inner_of(0, k0, v0, pre0), inner_of(1, k1, v1, pre1)],
    )
    (q0, inner0, scaled0, qturned0, turned0), (q1, inner1, scaled1, qturned1, turned1) = made

    bf_states = shape((heads, HEAD_DIM, HEAD_DIM), BF16)
    attn0, state0, square, cross = run(
        partial(attn_kernel, False), unit, [VMEM] * 5, [VMEM] * 4,
        [wide, bf_states, lane_sums, lane_sums], (q0, inner0, scaled0, *before0),
    )
    attn1, state1, sums = run(
        partial(attn_kernel, True), unit, [VMEM] * 7, [VMEM] * 3,
        [wide, bf_states, shape((8, rows), F32)], (q1, inner1, scaled1, *before1, square, cross),
    )
    parts = [sums] + [
        lax.ppermute(sums, "head", [(r, r ^ other) for r in range(peers)])
        for other in range(1, peers)
    ]

    g0, gsum0, post0, inv, slope = run(
        partial(grad_kernel, full, len(parts)), unit,
        [VMEM] * (peers + 3), [VMEM] * 5, [thin, states, inside, lane_sums, lane_sums],
        (*parts, attn0, scaled0, qturned0),
    )
    gextra0 = nearby(gsum0)
    g1, gsum1, post1 = run(
        partial(grad_kernel, full, 0), unit, [VMEM] * 5, [VMEM] * 3, [thin, states, inside],
        (inv, slope, attn1, scaled1, qturned1),
    )
    gextra1 = nearby(gsum1)

    qgrads = []

    def local_of(half_number, *args):
        def work(messages):
            more = list(messages) + qgrads
            qgrad, kpart, vpart = run(
                partial(local_kernel, half_number), 9 * unit,
                [VMEM] * len(args) + [ANYWHERE] * len(messages) + [HBM] * len(qgrads),
                [HBM, VMEM, VMEM], [whole, wide, wide], (*args, *more),
                [pltpu.VMEM((rows, half), BF16), sems],
                {len(args) + len(messages): 0} if qgrads else None,
            )
            qgrads[:] = [qgrad]
            return kpart, vpart

        return work

    (after0, after1), made = scan_states(
        (gsum0, gsum1), (gextra0, gextra1), True,
        [
            local_of(0, q0, k0, v0, g0, turned0, state0, pre0, post0),
            local_of(1, q1, k1, v1, g1, turned1, state1, pre1, post1),
        ],
    )
    (kpart0, vpart0), (kpart1, vpart1) = made

    done = run(
        near_kernel, 2 * unit, [VMEM] * 6, [VMEM] * 2, [thin, thin],
        (k0, v0, kpart0, vpart0, *after0),
    )
    kgrad, vgrad = run(
        last_kernel, 2 * unit, [VMEM] * 8, [HBM, HBM], [whole, whole],
        (k1, v1, kpart1, vpart1, *after1, *done),
        [pltpu.VMEM((rows, half), BF16)] * 2 + [pltpu.SemaphoreType.DMA((2 * chunks + 2,))],
    )
    return qgrads[0], kgrad, vgrad


def solution(mesh):
    spec = P("seq", "head")
    return jax.shard_map(
        shards,
        mesh=mesh,
        in_specs=(spec, spec, spec, spec, P("head")),
        out_specs=(spec, spec, spec),
        check_vma=False,
    )
```

```python
import functools

import jax
import jax.numpy as jnp
from jax import lax
from jax.experimental import pallas as pl
from jax.experimental.pallas import tpu as pltpu
from jax.sharding import PartitionSpec as P

HEAD_DIM = 128
CHUNK = 256
VMEM_BYTES = 12 * 2**20
F32 = jnp.float32
BF16 = jnp.bfloat16
VMEM = pl.BlockSpec(memory_space=pltpu.VMEM)
HBM = pl.BlockSpec(memory_space=pltpu.HBM)
ANYWHERE = pl.BlockSpec(memory_space=pl.ANY)


def dot(a, b, contract_a=1, contract_b=0):
    dims = (((contract_a,), (contract_b,)), ((), ()))
    return lax.dot_general(a, b, dims, preferred_element_type=F32)


def chunks_of(rows):
    size = CHUNK if rows % CHUNK == 0 else rows
    return [slice(i, i + size) for i in range(0, rows, size)]


def shape(dims, dtype):
    return jax.ShapeDtypeStruct(dims, dtype)


def lanes_of(j):
    return slice(j * HEAD_DIM, (j + 1) * HEAD_DIM)


def lower(size):
    row = lax.broadcasted_iota(jnp.int32, (size, size), 0)
    return row >= lax.broadcasted_iota(jnp.int32, (size, size), 1)


def upper(size):
    row = lax.broadcasted_iota(jnp.int32, (size, size), 0)
    return row <= lax.broadcasted_iota(jnp.int32, (size, size), 1)


def run(kernel, flops, in_specs, out_specs, out_shape, args, scratch=(), aliases=None):
    nbytes = sum(a.size * a.dtype.itemsize for a in args)
    return pl.pallas_call(
        kernel,
        in_specs=in_specs,
        out_specs=out_specs,
        out_shape=out_shape,
        scratch_shapes=list(scratch),
        input_output_aliases=aliases or {},
        cost_estimate=pl.CostEstimate(flops=flops, bytes_accessed=nbytes, transcendentals=0),
        compiler_params=pltpu.CompilerParams(vmem_limit_bytes=VMEM_BYTES),
    )(*args)


def is_hub():
    return lax.rem(lax.axis_index("seq"), 2) == 1


def columns(half, width):
    return slice(half * width, (half + 1) * width)


def fetches(sources, targets, sems, half):
    rows, width = targets[0].shape
    lanes = columns(half, width)
    copies = []
    for part in chunks_of(rows):
        for source, target in zip(sources, targets):
            sem = sems.at[len(copies)]
            copies.append(pltpu.make_async_copy(source.at[part, lanes], target.at[part], sem))
    return copies


def sum_states(k_ref, v_ref, sum_ref, pre_ref, copies=()):
    heads = sum_ref.shape[0]
    totals = [None] * heads
    for i, part in enumerate(chunks_of(k_ref.shape[0])):
        for copy in copies[2 * i:2 * i + 2]:
            copy.wait()
        for j in range(heads):
            term = dot(k_ref[part, lanes_of(j)], v_ref[part, lanes_of(j)], 0, 0)
            if i:
                pre_ref[i, j] = totals[j].astype(BF16)
            else:
                pre_ref[i, j] = jnp.zeros_like(pre_ref[i, j])
            totals[j] = totals[j] + term if i else term
    for j in range(heads):
        sum_ref[j] = totals[j]


def first_kernel(k_hbm, v_hbm, k0, v0, k1, v1, sum_ref, pre_ref, sems0, sems1):
    now = fetches((k_hbm, v_hbm), (k0, v0), sems0, 0)
    later = fetches((k_hbm, v_hbm), (k1, v1), sems1, 1)
    for copy in now + later:
        copy.start()
    sum_states(k0, v0, sum_ref, pre_ref, now)
    for copy in later:
        copy.wait()


def inner_kernel(half, q_hbm, og_hbm, k_ref, v_ref, gain_ref, pre_ref, *refs):
    q_ref, inner_ref, scaled_ref, qturned_ref, turned_ref, og_ref, sems = refs[-7:]
    rows, width = q_ref.shape
    copies = fetches((q_hbm, og_hbm), (q_ref, og_ref), sems, half)
    for copy in copies:
        copy.start()
    gain = gain_ref[:, columns(half, width)]
    for i, part in enumerate(chunks_of(rows)):
        for copy in copies[2 * i:2 * i + 2]:
            copy.wait()
        for j in range(width // HEAD_DIM):
            lanes = lanes_of(j)
            q, k = q_ref[part, lanes], k_ref[part, lanes]
            size = q.shape[0]
            scores = jnp.where(lower(size), dot(q, k, 1, 1), 0.0).astype(BF16)
            turned_ref[j, part] = jnp.where(upper(size), dot(k, q, 1, 1), 0.0).astype(BF16)
            inner = dot(scores, v_ref[part, lanes])
            inner_ref[part, lanes] = inner + dot(q, pre_ref[i, j]) if i else inner
            scaled_ref[part, lanes] = gain[:, lanes] * og_ref[part, lanes].astype(F32)
            qturned_ref[lanes, part] = q.T


def chosen_states(own_ref, came_ref):
    hub = is_hub()
    heads = range(own_ref.shape[0])
    return [jnp.where(hub, own_ref[j], came_ref[j]).astype(BF16) for j in heads]


def attn_kernel(last, q_ref, inner_ref, scaled_ref, own_ref, came_ref, *refs):
    attn_ref, state_ref = refs[2:4] if last else refs[:2]
    rows, width = q_ref.shape
    states = chosen_states(own_ref, came_ref)
    for j, state in enumerate(states):
        state_ref[j] = state
    for part in chunks_of(rows):
        square, cross = (refs[0][part], refs[1][part]) if last else (None, None)
        for j, state in enumerate(states):
            lanes = lanes_of(j)
            attn = inner_ref[part, lanes] + dot(q_ref[part, lanes], state)
            attn_ref[part, lanes] = attn
            more, crossed = attn * attn, scaled_ref[part, lanes] * attn
            square = more if square is None else square + more
            cross = crossed if cross is None else cross + crossed
        if last:
            square = jnp.sum(square.T, axis=0, keepdims=True)
            cross = jnp.sum(cross.T, axis=0, keepdims=True)
            row = lax.broadcasted_iota(jnp.int32, (8, square.shape[1]), 0)
            sums = jnp.where(row == 0, square, jnp.where(row == 1, cross, 0.0))
            refs[-1][:, part] = sums
        else:
            refs[-2][part] = square
            refs[-1][part] = cross


def factors_kernel(full, parts, refs):
    total = refs[0][...]
    for ref in refs[1:parts]:
        total = total + ref[...]
    inv = lax.rsqrt(total[0:1] / full + 1e-6)
    slope = inv * inv * inv * (total[1:2] / full)
    row = lax.broadcasted_iota(jnp.int32, total.shape, 0)
    both = jnp.where(row == 0, inv, slope).T
    wide = (both.shape[0], HEAD_DIM)
    return jnp.broadcast_to(both[:, 0:1], wide), jnp.broadcast_to(both[:, 1:2], wide)


def grad_kernel(full, parts, *refs):
    if parts:
        inv, slope = factors_kernel(full, parts, refs)
        refs[-2][...] = inv
        refs[-1][...] = slope
        inv_ref, slope_ref = refs[-2:]
        attn_ref, scaled_ref, qturned_ref, g_ref, sum_ref, post_ref = refs[parts:-2]
    else:
        inv_ref, slope_ref, attn_ref, scaled_ref, qturned_ref, g_ref, sum_ref, post_ref = refs
    heads = sum_ref.shape[0]
    totals = [None] * heads
    for i, part in reversed(list(enumerate(chunks_of(g_ref.shape[0])))):
        for j in range(heads):
            lanes = lanes_of(j)
            grad = inv_ref[part] * scaled_ref[part, lanes] - attn_ref[part, lanes] * slope_ref[part]
            grad = grad.astype(BF16)
            g_ref[part, lanes] = grad
            term = dot(qturned_ref[lanes, part], grad)
            if totals[j] is None:
                post_ref[i, j] = jnp.zeros_like(post_ref[i, j])
                totals[j] = term
            else:
                post_ref[i, j] = totals[j].astype(BF16)
                totals[j] = totals[j] + term
    for j in range(heads):
        sum_ref[j] = totals[j]


def local_kernel(half, q_ref, k_ref, v_ref, g_ref, turned_ref, state_ref, pre_ref, post_ref, *refs):
    qgrad_hbm, kpart_ref, vpart_ref, qgrad_ref, sems = refs[-5:]
    rows, width = q_ref.shape
    target = columns(half, width)
    parts = chunks_of(rows)
    copies = []
    for i, part in enumerate(parts):
        for j in range(width // HEAD_DIM):
            lanes = lanes_of(j)
            q, k, v, g = (ref[part, lanes] for ref in (q_ref, k_ref, v_ref, g_ref))
            size = q.shape[0]
            gscores = jnp.where(lower(size), dot(g, v, 1, 1), 0.0).astype(BF16)
            gturned = jnp.where(upper(size), dot(v, g, 1, 1), 0.0).astype(BF16)
            qgrad = dot(gscores, k) + dot(g, state_ref[j], 1, 1)
            kgrad = dot(gturned, q)
            vgrad = dot(turned_ref[j, part], g)
            if i:
                qgrad = qgrad + dot(g, pre_ref[i, j], 1, 1)
            if i < len(parts) - 1:
                kgrad = kgrad + dot(v, post_ref[i, j], 1, 1)
                vgrad = vgrad + dot(k, post_ref[i, j])
            qgrad_ref[part, lanes] = qgrad.astype(BF16)
            kpart_ref[part, lanes] = kgrad
            vpart_ref[part, lanes] = vgrad
        copy = pltpu.make_async_copy(qgrad_ref.at[part], qgrad_hbm.at[part, target], sems.at[i])
        copy.start()
        copies.append(copy)
    for copy in copies:
        copy.wait()


def final_parts(k_ref, v_ref, kpart_ref, vpart_ref, states, kgrad_ref, vgrad_ref, part):
    for j, state in enumerate(states):
        lanes = lanes_of(j)
        kgrad = kpart_ref[part, lanes] + dot(v_ref[part, lanes], state, 1, 1)
        vgrad = vpart_ref[part, lanes] + dot(k_ref[part, lanes], state)
        kgrad_ref[part, lanes] = kgrad.astype(BF16)
        vgrad_ref[part, lanes] = vgrad.astype(BF16)


def near_kernel(*refs):
    states = chosen_states(*refs[4:6])
    for part in chunks_of(refs[0].shape[0]):
        final_parts(*refs[:4], states, *refs[6:], part)


def last_kernel(*refs):
    kdone_ref, vdone_ref, kgrad_hbm, vgrad_hbm, kgrad_ref, vgrad_ref, sems = refs[6:]
    rows, width = kgrad_ref.shape
    copies = []

    def send(source, out, part, half):
        sem = sems.at[len(copies)]
        target = out.at[part, columns(half, width)]
        copy = pltpu.make_async_copy(source.at[part], target, sem)
        copy.start()
        copies.append(copy)

    send(kdone_ref, kgrad_hbm, slice(0, rows), 0)
    send(vdone_ref, vgrad_hbm, slice(0, rows), 0)
    states = chosen_states(*refs[4:6])
    for part in chunks_of(rows):
        final_parts(*refs[:4], states, kgrad_ref, vgrad_ref, part)
        send(kgrad_ref, kgrad_hbm, part, 1)
        send(vgrad_ref, vgrad_hbm, part, 1)
    for copy in copies:
        copy.wait()


def stage_bits(half):
    bits = (lax.axis_size("seq") // 2).bit_length() - 1
    return list(range(bits)) if half == 0 else list(range(bits))[::-1]


def join_kernel(backward, half, done, *refs):
    pairs = lax.axis_size("seq") // 2
    place = lax.axis_index("seq") // 2
    if backward:
        place = pairs - 1 - place
    bits = stage_bits(half)
    highs = [((place >> bit) & 1) == 1 for bit in bits]
    keep_ref, extra_ref = refs[:2]
    total = keep_ref[...] + extra_ref[...]
    before = jnp.zeros_like(total)
    for high, ref in zip(highs, refs[2:2 + done]):
        value = ref[...]
        if half == 0:
            before = before + jnp.where(high, value, 0.0)
            total = total + value
        else:
            before = before + value
    if done == len(bits):
        message_ref, own_ref = refs[-2:]
        message_ref[...] = before + keep_ref[...] if backward else before
        own_ref[...] = before if backward else before + extra_ref[...]
    elif half == 0:
        refs[-1][...] = total
    else:
        refs[-1][...] = before + jnp.where(highs[done], 0.0, total)


def join(backward, half, keep, extra, came, after):
    final = len(came) == len(stage_bits(half))
    like = shape(keep.shape, F32)
    return run(
        functools.partial(join_kernel, backward, half, len(came)), 4 * keep.size,
        [VMEM] * (2 + len(came)) + [ANYWHERE] * len(after),
        [VMEM, VMEM] if final else VMEM,
        [like, like] if final else like,
        (keep, extra, *came, *after),
    )


def scan_states(keeps, extras, backward, beside):
    stages = len(stage_bits(0))
    came, results, after = ([], []), [], []
    for stage in range(stages):
        messages = []
        for half in (0, 1):
            message = join(backward, half, keeps[half], extras[half], came[half], after + messages)
            messages.append(message)
            flip = 1 << stage_bits(half)[stage]
            pairs = [(r, r ^ (2 * flip) if r & 1 else r) for r in range(lax.axis_size("seq"))]
            came[half].append(lax.ppermute(message, "seq", pairs))
        mine = beside[stage:] if stage == stages - 1 else beside[stage:stage + 1]
        made = [work(messages) for work in mine]
        after = [item[-1] for item in made]
        results += made
    states, last = [], []
    for half in (0, 1):
        message, own = join(backward, half, keeps[half], extras[half], came[half], after + last)
        last = [message]
        states.append((own, nearby(message)))
    return states, results


def nearby(value):
    return lax.ppermute(value, "seq", [(r, r ^ 1) for r in range(lax.axis_size("seq"))])


def shards(query, key_in, value, out_grad, gain):
    rows, width = query.shape
    half = width // 2
    heads = half // HEAD_DIM
    chunks = len(chunks_of(rows))
    peers = lax.axis_size("head")
    full = width * peers
    gain = gain.reshape(1, width)
    pin = lambda x: pltpu.with_memory_space_constraint(x, pltpu.HBM)
    query, key_in, value, out_grad = (pin(x) for x in (query, key_in, value, out_grad))
    unit = 2 * rows * half * HEAD_DIM
    partial = functools.partial

    states = shape((heads, HEAD_DIM, HEAD_DIM), F32)
    inside = shape((chunks, heads, HEAD_DIM, HEAD_DIM), BF16)
    wide = shape((rows, half), F32)
    thin = shape((rows, half), BF16)
    lane_sums = shape((rows, HEAD_DIM), F32)
    whole = shape((rows, width), BF16)
    sems = pltpu.SemaphoreType.DMA((2 * chunks,))

    k0, v0, k1, v1, sum0, pre0 = run(
        first_kernel, unit, [HBM, HBM], [VMEM] * 6, [thin] * 4 + [states, inside],
        (key_in, value), [sems, sems],
    )
    extra0 = nearby(sum0)
    sum1, pre1 = run(sum_states, unit, [VMEM, VMEM], [VMEM] * 2, [states, inside], (k1, v1))
    extra1 = nearby(sum1)

    def inner_of(half_number, k, v, pre):
        return lambda messages: run(
            partial(inner_kernel, half_number), 6 * unit,
            [HBM, HBM, VMEM, VMEM, VMEM, VMEM] + [ANYWHERE] * len(messages), [VMEM] * 5,
            [
                thin, wide, wide,
                shape((half, rows), BF16), shape((heads, rows, rows // chunks), BF16),
            ],
            (query, out_grad, k, v, gain, pre, *messages),
            [pltpu.VMEM((rows, half), BF16), sems],
        )

    (before0, before1), made = scan_states(
        (sum0, sum1), (extra0, extra1), False,
        [inner_of(0, k0, v0, pre0), inner_of(1, k1, v1, pre1)],
    )
    (q0, inner0, scaled0, qturned0, turned0), (q1, inner1, scaled1, qturned1, turned1) = made

    bf_states = shape((heads, HEAD_DIM, HEAD_DIM), BF16)
    attn0, state0, square, cross = run(
        partial(attn_kernel, False), unit, [VMEM] * 5, [VMEM] * 4,
        [wide, bf_states, lane_sums, lane_sums], (q0, inner0, scaled0, *before0),
    )
    attn1, state1, sums = run(
        partial(attn_kernel, True), unit, [VMEM] * 7, [VMEM] * 3,
        [wide, bf_states, shape((8, rows), F32)], (q1, inner1, scaled1, *before1, square, cross),
    )
    parts = [sums] + [
        lax.ppermute(sums, "head", [(r, r ^ other) for r in range(peers)])
        for other in range(1, peers)
    ]

    g0, gsum0, post0, inv, slope = run(
        partial(grad_kernel, full, len(parts)), unit,
        [VMEM] * (peers + 3), [VMEM] * 5, [thin, states, inside, lane_sums, lane_sums],
        (*parts, attn0, scaled0, qturned0),
    )
    gextra0 = nearby(gsum0)
    g1, gsum1, post1 = run(
        partial(grad_kernel, full, 0), unit, [VMEM] * 5, [VMEM] * 3, [thin, states, inside],
        (inv, slope, attn1, scaled1, qturned1),
    )
    gextra1 = nearby(gsum1)

    qgrads = []

    def local_of(half_number, *args):
        def work(messages):
            more = list(messages) + qgrads
            qgrad, kpart, vpart = run(
                partial(local_kernel, half_number), 9 * unit,
                [VMEM] * len(args) + [ANYWHERE] * len(messages) + [HBM] * len(qgrads),
                [HBM, VMEM, VMEM], [whole, wide, wide], (*args, *more),
                [pltpu.VMEM((rows, half), BF16), sems],
                {len(args) + len(messages): 0} if qgrads else None,
            )
            qgrads[:] = [qgrad]
            return kpart, vpart

        return work

    (after0, after1), made = scan_states(
        (gsum0, gsum1), (gextra0, gextra1), True,
        [
            local_of(0, q0, k0, v0, g0, turned0, state0, pre0, post0),
            local_of(1, q1, k1, v1, g1, turned1, state1, pre1, post1),
        ],
    )
    (kpart0, vpart0), (kpart1, vpart1) = made

    done = run(
        near_kernel, 2 * unit, [VMEM] * 6, [VMEM] * 2, [thin, thin],
        (k0, v0, kpart0, vpart0, *after0),
    )
    kgrad, vgrad = run(
        last_kernel, 2 * unit, [VMEM] * 8, [HBM, HBM], [whole, whole],
        (k1, v1, kpart1, vpart1, *after1, *done),
        [pltpu.VMEM((rows, half), BF16)] * 2 + [pltpu.SemaphoreType.DMA((2 * chunks + 2,))],
    )
    return qgrads[0], kgrad, vgrad


def solution(mesh):
    spec = P("seq", "head")
    return jax.shard_map(
        shards,
        mesh=mesh,
        in_specs=(spec, spec, spec, spec, P("head")),
        out_specs=(spec, spec, spec),
        check_vma=False,
    )
```

```python
import functools

import jax
import jax.numpy as jnp
from jax import lax
from jax.experimental import pallas as pl
from jax.experimental.pallas import tpu as pltpu
from jax.sharding import PartitionSpec as P

HEAD_DIM = 128
CHUNK = 256
VMEM_BYTES = 12 * 2**20
F32 = jnp.float32
BF16 = jnp.bfloat16
VMEM = pl.BlockSpec(memory_space=pltpu.VMEM)
HBM = pl.BlockSpec(memory_space=pltpu.HBM)
ANYWHERE = pl.BlockSpec(memory_space=pl.ANY)


def dot(a, b, contract_a=1, contract_b=0):
    dims = (((contract_a,), (contract_b,)), ((), ()))
    return lax.dot_general(a, b, dims, preferred_element_type=F32)


def chunks_of(rows):
    size = CHUNK if rows % CHUNK == 0 else rows
    return [slice(i, i + size) for i in range(0, rows, size)]


def shape(dims, dtype):
    return jax.ShapeDtypeStruct(dims, dtype)


def lanes_of(j):
    return slice(j * HEAD_DIM, (j + 1) * HEAD_DIM)


def pairs_of(width):
    return [slice(i, i + 2 * HEAD_DIM) for i in range(0, width, 2 * HEAD_DIM)]


def diagonal(first, second):
    zero = jnp.zeros_like(first)
    top = jnp.concatenate([first, zero], axis=1)
    return jnp.concatenate([top, jnp.concatenate([zero, second], axis=1)], axis=0)


def diagonals(states):
    states = [state.astype(BF16) for state in states]
    return [diagonal(*states[i:i + 2]) for i in range(0, len(states), 2)]


def heads_in(pieces):
    return [ref[j] for ref in pieces for j in range(ref.shape[0])]


def lower(size):
    row = lax.broadcasted_iota(jnp.int32, (size, size), 0)
    return row >= lax.broadcasted_iota(jnp.int32, (size, size), 1)


def upper(size):
    row = lax.broadcasted_iota(jnp.int32, (size, size), 0)
    return row <= lax.broadcasted_iota(jnp.int32, (size, size), 1)


def run(kernel, flops, in_specs, out_specs, out_shape, args, scratch=(), aliases=None):
    nbytes = sum(a.size * a.dtype.itemsize for a in args)
    return pl.pallas_call(
        kernel,
        in_specs=in_specs,
        out_specs=out_specs,
        out_shape=out_shape,
        scratch_shapes=list(scratch),
        input_output_aliases=aliases or {},
        cost_estimate=pl.CostEstimate(flops=flops, bytes_accessed=nbytes, transcendentals=0),
        compiler_params=pltpu.CompilerParams(vmem_limit_bytes=VMEM_BYTES),
    )(*args)


def columns(same, width):
    odd = lax.rem(lax.axis_index("seq"), 2)
    half = odd if same else 1 - odd
    return pl.ds(pl.multiple_of(half * width, width), width)


def fetches(sources, targets, sems, same):
    rows, width = targets[0].shape
    lanes = columns(same, width)
    copies = []
    for part in chunks_of(rows):
        for source, target in zip(sources, targets):
            sem = sems.at[len(copies)]
            copies.append(pltpu.make_async_copy(source.at[part, lanes], target.at[part], sem))
    return copies


def state_kernel(same, k_hbm, v_hbm, k_ref, v_ref, sum_ref, pre_ref, sems):
    copies = fetches((k_hbm, v_hbm), (k_ref, v_ref), sems, same)
    for copy in copies:
        copy.start()
    heads = sum_ref.shape[0]
    totals = [None] * heads
    for i, part in enumerate(chunks_of(k_ref.shape[0])):
        for copy in copies[2 * i:2 * i + 2]:
            copy.wait()
        for j in range(heads):
            term = dot(k_ref[part, lanes_of(j)], v_ref[part, lanes_of(j)], 0, 0)
            if i:
                pre_ref[i, j] = totals[j].astype(BF16)
            else:
                pre_ref[i, j] = jnp.zeros_like(pre_ref[i, j])
            totals[j] = totals[j] + term if i else term
    for j in range(heads):
        sum_ref[j] = totals[j]


def inner_kernel(same, q_hbm, og_hbm, k_ref, v_ref, gain_ref, pre_ref, *refs):
    q_ref, inner_ref, scaled_ref, qturned_ref, turned_ref, og_ref, sems = refs[-7:]
    rows, width = q_ref.shape
    copies = fetches((q_hbm, og_hbm), (q_ref, og_ref), sems, same)
    for copy in copies:
        copy.start()
    gain = gain_ref[:, columns(same, width)]
    for i, part in enumerate(chunks_of(rows)):
        for copy in copies[2 * i:2 * i + 2]:
            copy.wait()
        if i:
            earlier = diagonals([pre_ref[i, j] for j in range(width // HEAD_DIM)])
            for lanes, states in zip(pairs_of(width), earlier):
                inner_ref[part, lanes] = dot(q_ref[part, lanes], states)
        for j in range(width // HEAD_DIM):
            lanes = lanes_of(j)
            q, k = q_ref[part, lanes], k_ref[part, lanes]
            size = q.shape[0]
            scores = jnp.where(lower(size), dot(q, k, 1, 1), 0.0).astype(BF16)
            turned_ref[j, part] = jnp.where(upper(size), dot(k, q, 1, 1), 0.0).astype(BF16)
            inner = dot(scores, v_ref[part, lanes])
            inner_ref[part, lanes] = inner_ref[part, lanes] + inner if i else inner
            scaled_ref[part, lanes] = gain[:, lanes] * og_ref[part, lanes].astype(F32)
            qturned_ref[lanes, part] = q.T


def attn_kernel(last, pieces, q_ref, inner_ref, scaled_ref, *refs):
    states = diagonals(heads_in(refs[:pieces]))
    refs = refs[pieces:]
    attn_ref = refs[2] if last else refs[0]
    rows, width = q_ref.shape
    for part in chunks_of(rows):
        square, cross = (refs[0][part], refs[1][part]) if last else (None, None)
        for lanes, state in zip(pairs_of(width), states):
            attn = inner_ref[part, lanes] + dot(q_ref[part, lanes], state)
            attn_ref[part, lanes] = attn
            more, crossed = attn * attn, scaled_ref[part, lanes] * attn
            for i in range(2):
                square = more[:, lanes_of(i)] if square is None else square + more[:, lanes_of(i)]
                cross = crossed[:, lanes_of(i)] if cross is None else cross + crossed[:, lanes_of(i)]
        if last:
            square = jnp.sum(square.T, axis=0, keepdims=True)
            cross = jnp.sum(cross.T, axis=0, keepdims=True)
            row = lax.broadcasted_iota(jnp.int32, (8, square.shape[1]), 0)
            sums = jnp.where(row == 0, square, jnp.where(row == 1, cross, 0.0))
            refs[-1][:, part] = sums
        else:
            refs[-2][part] = square
            refs[-1][part] = cross


def factors_kernel(full, parts, refs):
    total = refs[0][...]
    for ref in refs[1:parts]:
        total = total + ref[...]
    inv = lax.rsqrt(total[0:1] / full + 1e-6)
    slope = inv * inv * inv * (total[1:2] / full)
    row = lax.broadcasted_iota(jnp.int32, total.shape, 0)
    both = jnp.where(row == 0, inv, slope).T
    wide = (both.shape[0], HEAD_DIM)
    return jnp.broadcast_to(both[:, 0:1], wide), jnp.broadcast_to(both[:, 1:2], wide)


def grad_kernel(full, parts, *refs):
    if parts:
        inv, slope = factors_kernel(full, parts, refs)
        refs[-2][...] = inv
        refs[-1][...] = slope
        inv_ref, slope_ref = refs[-2:]
        attn_ref, scaled_ref, qturned_ref, g_ref, sum_ref, post_ref = refs[parts:-2]
    else:
        inv_ref, slope_ref, attn_ref, scaled_ref, qturned_ref, g_ref, sum_ref, post_ref = refs
    heads = sum_ref.shape[0]
    totals = [None] * heads
    for i, part in reversed(list(enumerate(chunks_of(g_ref.shape[0])))):
        for j in range(heads):
            lanes = lanes_of(j)
            grad = inv_ref[part] * scaled_ref[part, lanes] - attn_ref[part, lanes] * slope_ref[part]
            grad = grad.astype(BF16)
            g_ref[part, lanes] = grad
            term = dot(qturned_ref[lanes, part], grad)
            if totals[j] is None:
                post_ref[i, j] = jnp.zeros_like(post_ref[i, j])
                totals[j] = term
            else:
                post_ref[i, j] = totals[j].astype(BF16)
                totals[j] = totals[j] + term
    for j in range(heads):
        sum_ref[j] = totals[j]


def local_kernel(same, pieces, q_ref, k_ref, v_ref, g_ref, turned_ref, pre_ref, post_ref, *refs):
    qgrad_hbm, kpart_ref, vpart_ref, qgrad_ref, out_ref, sems = refs[-6:]
    state = heads_in(refs[:pieces])
    rows, width = q_ref.shape
    target = columns(same, width)
    parts = chunks_of(rows)
    copies = []
    for i, part in enumerate(parts):
        heads = range(width // HEAD_DIM)
        before = [state[j] + pre_ref[i, j].astype(F32) if i else state[j] for j in heads]
        for lanes, both in zip(pairs_of(width), diagonals(before)):
            qgrad_ref[part, lanes] = dot(g_ref[part, lanes], both, 1, 1)
        last = i == len(parts) - 1
        if not last:
            later = diagonals([post_ref[i, j] for j in heads])
            for lanes, both in zip(pairs_of(width), later):
                kpart_ref[part, lanes] = dot(v_ref[part, lanes], both, 1, 1)
                vpart_ref[part, lanes] = dot(k_ref[part, lanes], both)
        for j in heads:
            lanes = lanes_of(j)
            q, k, v, g = (ref[part, lanes] for ref in (q_ref, k_ref, v_ref, g_ref))
            size = q.shape[0]
            gscores = jnp.where(lower(size), dot(g, v, 1, 1), 0.0).astype(BF16)
            gturned = jnp.where(upper(size), dot(v, g, 1, 1), 0.0).astype(BF16)
            kgrad, vgrad = dot(gturned, q), dot(turned_ref[j, part], g)
            out_ref[part, lanes] = (qgrad_ref[part, lanes] + dot(gscores, k)).astype(BF16)
            kpart_ref[part, lanes] = kgrad if last else kpart_ref[part, lanes] + kgrad
            vpart_ref[part, lanes] = vgrad if last else vpart_ref[part, lanes] + vgrad
        copy = pltpu.make_async_copy(out_ref.at[part], qgrad_hbm.at[part, target], sems.at[i])
        copy.start()
        copies.append(copy)
    for copy in copies:
        copy.wait()


def final_parts(k_ref, v_ref, kpart_ref, vpart_ref, states, kgrad_ref, vgrad_ref, part):
    for lanes, state in zip(pairs_of(k_ref.shape[1]), states):
        kgrad = kpart_ref[part, lanes] + dot(v_ref[part, lanes], state, 1, 1)
        vgrad = vpart_ref[part, lanes] + dot(k_ref[part, lanes], state)
        kgrad_ref[part, lanes] = kgrad.astype(BF16)
        vgrad_ref[part, lanes] = vgrad.astype(BF16)


def near_kernel(pieces, *refs):
    states = diagonals(heads_in(refs[4:4 + pieces]))
    for part in chunks_of(refs[0].shape[0]):
        final_parts(*refs[:4], states, *refs[4 + pieces:], part)


def last_kernel(same, pieces, *refs):
    states = diagonals(heads_in(refs[4:4 + pieces]))
    kdone_ref, vdone_ref, kgrad_hbm, vgrad_hbm, kgrad_ref, vgrad_ref, sems = refs[4 + pieces:]
    rows, width = kgrad_ref.shape
    copies = []

    def send(source, out, part, half):
        sem = sems.at[len(copies)]
        target = out.at[part, columns(half, width)]
        copy = pltpu.make_async_copy(source.at[part], target, sem)
        copy.start()
        copies.append(copy)

    send(kdone_ref, kgrad_hbm, slice(0, rows), not same)
    send(vdone_ref, vgrad_hbm, slice(0, rows), not same)
    for part in chunks_of(rows):
        final_parts(*refs[:4], states, kgrad_ref, vgrad_ref, part)
        send(kgrad_ref, kgrad_hbm, part, same)
        send(vgrad_ref, vgrad_hbm, part, same)
    for copy in copies:
        copy.wait()


def scan_plan(count):
    bits = count.bit_length() - 1
    stages = []
    for stage in range(bits - 1):
        rising, falling = 1 + stage, bits - 1 - stage
        pairs = [(r, r ^ (1 << (falling if r & 1 else rising))) for r in range(count)]
        stages.append((rising, falling, pairs))
    return stages


def join_kernel(backward, piece, done, final, *refs):
    count = lax.axis_size("seq")
    rank = lax.axis_index("seq")
    if backward:
        rank = count - 1 - rank
    odd = (rank & 1) == 1
    plan = scan_plan(count)
    keep, extra = (ref[piece] for ref in refs[:2])
    came = refs[2:2 + done]
    total = keep + extra
    before = jnp.zeros_like(total)
    for (rising, falling, _), ref in zip(plan, came):
        high = (jnp.where(odd, rank >> falling, rank >> rising) & 1) == 1
        value = ref[...]
        before = before + jnp.where(odd | high, value, 0.0)
        total = total + jnp.where(odd, 0.0, value)
    if final:
        message_ref, state_ref = refs[-2:]
        message_ref[...] = before + jnp.where(odd, 0.0, keep)
        state_ref[...] = before + jnp.where(odd, extra, 0.0)
    else:
        rising, falling, _ = plan[done]
        high = (jnp.where(odd, rank >> falling, rank >> rising) & 1) == 1
        refs[-1][...] = jnp.where(odd, before + jnp.where(high, 0.0, total), total)


def join(backward, piece, keep, extra, came, final, after):
    like = shape((piece.stop - piece.start,) + keep.shape[1:], F32)
    return run(
        functools.partial(join_kernel, backward, piece, len(came), final), 4 * like.size,
        [VMEM] * (2 + len(came)) + [ANYWHERE] * len(after),
        [VMEM, VMEM] if final else VMEM,
        [like, like] if final else like,
        (keep, extra, *came, *after),
    )


def scan_states(keep, extra, backward, beside):
    plan = scan_plan(lax.axis_size("seq"))
    pieces = [slice(i, i + 2) for i in range(0, keep.shape[0], 2)]
    came = [[] for _ in pieces]
    results, after = [], []
    for stage, (_, _, pairs) in enumerate(plan):
        messages = []
        for piece, arrived in zip(pieces, came):
            message = join(backward, piece, keep, extra, arrived, False, after + messages)
            messages.append(message)
            arrived.append(move(message, pairs, backward))
        mine = beside[stage:] if stage == len(plan) - 1 else beside[stage:stage + 1]
        made = [work(messages) for work in mine]
        after = [item[-1] for item in made]
        results += made
    states, others, last = [], [], []
    for piece, arrived in zip(pieces, came):
        message, state = join(backward, piece, keep, extra, arrived, True, after + last)
        last = [message]
        states.append(state)
        others.append(nearby(message, backward))
    return states, others, results


def move(value, pairs, backward):
    count = lax.axis_size("seq")
    if backward:
        pairs = [(count - 1 - a, count - 1 - b) for a, b in pairs]
    return lax.ppermute(value, "seq", pairs)


def nearby(value, backward):
    return move(value, [(r, r ^ 1) for r in range(lax.axis_size("seq"))], backward)


def shards(query, key_in, value, out_grad, gain):
    rows, width = query.shape
    half = width // 2
    heads = half // HEAD_DIM
    chunks = len(chunks_of(rows))
    peers = lax.axis_size("head")
    full = width * peers
    gain = gain.reshape(1, width)
    pin = lambda x: pltpu.with_memory_space_constraint(x, pltpu.HBM)
    query, key_in, value, out_grad = (pin(x) for x in (query, key_in, value, out_grad))
    unit = 2 * rows * half * HEAD_DIM
    partial = functools.partial

    states = shape((heads, HEAD_DIM, HEAD_DIM), F32)
    inside = shape((chunks, heads, HEAD_DIM, HEAD_DIM), BF16)
    wide = shape((rows, half), F32)
    thin = shape((rows, half), BF16)
    lane_sums = shape((rows, HEAD_DIM), F32)
    whole = shape((rows, width), BF16)
    sems = pltpu.SemaphoreType.DMA((2 * chunks,))

    def states_of(same):
        return run(
            partial(state_kernel, same), unit, [HBM, HBM], [VMEM] * 4, [thin, thin, states, inside],
            (key_in, value), [sems],
        )

    k1, v1, send, pre1 = states_of(False)
    extra = nearby(send, False)
    k2, v2, keep, pre2 = states_of(True)

    def inner_of(same, k, v, pre):
        return lambda messages: run(
            partial(inner_kernel, same), 6 * unit,
            [HBM, HBM, VMEM, VMEM, VMEM, VMEM] + [ANYWHERE] * len(messages), [VMEM] * 5,
            [
                thin, wide, wide,
                shape((half, rows), BF16), shape((heads, rows, rows // chunks), BF16),
            ],
            (query, out_grad, k, v, gain, pre, *messages),
            [pltpu.VMEM((rows, half), BF16), sems],
        )

    state2, state1, made = scan_states(
        keep, extra, False,
        [inner_of(True, k2, v2, pre2), inner_of(False, k1, v1, pre1)],
    )
    (q2, inner2, scaled2, qturned2, turned2), (q1, inner1, scaled1, qturned1, turned1) = made

    count = len(state2)
    attn2, square, cross = run(
        partial(attn_kernel, False, count), unit, [VMEM] * (3 + count), [VMEM] * 3,
        [wide, lane_sums, lane_sums], (q2, inner2, scaled2, *state2),
    )
    attn1, sums = run(
        partial(attn_kernel, True, count), unit, [VMEM] * (5 + count), [VMEM] * 2,
        [wide, shape((8, rows), F32)], (q1, inner1, scaled1, *state1, square, cross),
    )
    parts = [sums] + [
        lax.ppermute(sums, "head", [(r, r ^ other) for r in range(peers)])
        for other in range(1, peers)
    ]

    g2, gsend, post2, inv, slope = run(
        partial(grad_kernel, full, peers), unit,
        [VMEM] * (peers + 3), [VMEM] * 5, [thin, states, inside, lane_sums, lane_sums],
        (*parts, attn2, scaled2, qturned2),
    )
    gextra = nearby(gsend, True)
    g1, gkeep, post1 = run(
        partial(grad_kernel, full, 0), unit, [VMEM] * 5, [VMEM] * 3, [thin, states, inside],
        (inv, slope, attn1, scaled1, qturned1),
    )

    qgrads = []

    def local_of(same, *args):
        def work(messages):
            more = list(messages) + qgrads
            qgrad, kpart, vpart = run(
                partial(local_kernel, same, count), 9 * unit,
                [VMEM] * len(args) + [ANYWHERE] * len(messages) + [HBM] * len(qgrads),
                [HBM, VMEM, VMEM], [whole, wide, wide], (*args, *more),
                [pltpu.VMEM((rows, half), F32), pltpu.VMEM((rows, half), BF16), sems],
                {len(args) + len(messages): 0} if qgrads else None,
            )
            qgrads[:] = [qgrad]
            return kpart, vpart

        return work

    gstate1, gstate2, made = scan_states(
        gkeep, gextra, True,
        [
            local_of(False, q1, k1, v1, g1, turned1, pre1, post1, *state1),
            local_of(True, q2, k2, v2, g2, turned2, pre2, post2, *state2),
        ],
    )
    (kpart1, vpart1), (kpart2, vpart2) = made

    done = run(
        partial(near_kernel, count), 2 * unit, [VMEM] * (4 + count), [VMEM] * 2, [thin, thin],
        (k1, v1, kpart1, vpart1, *gstate1),
    )
    kgrad, vgrad = run(
        partial(last_kernel, True, count), 2 * unit, [VMEM] * (6 + count), [HBM, HBM],
        [whole, whole], (k2, v2, kpart2, vpart2, *gstate2, *done),
        [pltpu.VMEM((rows, half), BF16)] * 2 + [pltpu.SemaphoreType.DMA((2 * chunks + 2,))],
    )
    return qgrads[0], kgrad, vgrad


def solution(mesh):
    spec = P("seq", "head")
    return jax.shard_map(
        shards,
        mesh=mesh,
        in_specs=(spec, spec, spec, spec, P("head")),
        out_specs=(spec, spec, spec),
        check_vma=False,
    )
```

```python
import functools

import jax
import jax.numpy as jnp
from jax import lax
from jax.experimental import pallas as pl
from jax.experimental.pallas import tpu as pltpu
from jax.sharding import PartitionSpec as P

HEAD_DIM = 128
CHUNK = 128
VMEM_BYTES = 12 * 2**20
F32 = jnp.float32
BF16 = jnp.bfloat16
VMEM = pl.BlockSpec(memory_space=pltpu.VMEM)
HBM = pl.BlockSpec(memory_space=pltpu.HBM)
ANYWHERE = pl.BlockSpec(memory_space=pl.ANY)


def dot(a, b, contract_a=1, contract_b=0):
    dims = (((contract_a,), (contract_b,)), ((), ()))
    return lax.dot_general(a, b, dims, preferred_element_type=F32)


def chunks_of(rows):
    size = CHUNK if rows % CHUNK == 0 else rows
    return [slice(i, i + size) for i in range(0, rows, size)]


def shape(dims, dtype):
    return jax.ShapeDtypeStruct(dims, dtype)


def lanes_of(j):
    return slice(j * HEAD_DIM, (j + 1) * HEAD_DIM)


def heads_in(pieces):
    return [ref[j] for ref in pieces for j in range(ref.shape[0])]


def lower(size):
    row = lax.broadcasted_iota(jnp.int32, (size, size), 0)
    return row >= lax.broadcasted_iota(jnp.int32, (size, size), 1)


def upper(size):
    row = lax.broadcasted_iota(jnp.int32, (size, size), 0)
    return row <= lax.broadcasted_iota(jnp.int32, (size, size), 1)


def run(kernel, flops, in_specs, out_specs, out_shape, args, scratch=(), aliases=None):
    nbytes = sum(a.size * a.dtype.itemsize for a in args)
    return pl.pallas_call(
        kernel,
        in_specs=in_specs,
        out_specs=out_specs,
        out_shape=out_shape,
        scratch_shapes=list(scratch),
        input_output_aliases=aliases or {},
        cost_estimate=pl.CostEstimate(flops=flops, bytes_accessed=nbytes, transcendentals=0),
        compiler_params=pltpu.CompilerParams(vmem_limit_bytes=VMEM_BYTES),
    )(*args)


def columns(same, width):
    odd = lax.rem(lax.axis_index("seq"), 2)
    half = odd if same else 1 - odd
    return pl.ds(pl.multiple_of(half * width, width), width)


def fetches(sources, targets, sems, same):
    rows, width = targets[0].shape
    lanes = columns(same, width)
    copies = []
    for part in chunks_of(rows):
        for source, target in zip(sources, targets):
            sem = sems.at[len(copies)]
            copies.append(pltpu.make_async_copy(source.at[part, lanes], target.at[part], sem))
    return copies


def state_kernel(same, k_hbm, v_hbm, k_ref, v_ref, sum_ref, pre_ref, sems):
    copies = fetches((k_hbm, v_hbm), (k_ref, v_ref), sems, same)
    for copy in copies:
        copy.start()
    heads = sum_ref.shape[0]
    totals = [None] * heads
    for i, part in enumerate(chunks_of(k_ref.shape[0])):
        for copy in copies[2 * i:2 * i + 2]:
            copy.wait()
        for j in range(heads):
            term = dot(k_ref[part, lanes_of(j)], v_ref[part, lanes_of(j)], 0, 0)
            if i:
                pre_ref[i, j] = totals[j].astype(BF16)
            else:
                pre_ref[i, j] = jnp.zeros_like(pre_ref[i, j])
            totals[j] = totals[j] + term if i else term
    for j in range(heads):
        sum_ref[j] = totals[j]


def inner_kernel(same, q_hbm, og_hbm, k_ref, v_ref, gain_ref, pre_ref, *refs):
    q_ref, inner_ref, scaled_ref, qturned_ref, turned_ref, og_ref, sems = refs[-7:]
    rows, width = q_ref.shape
    copies = fetches((q_hbm, og_hbm), (q_ref, og_ref), sems, same)
    for copy in copies:
        copy.start()
    gain = gain_ref[:, columns(same, width)]
    for i, part in enumerate(chunks_of(rows)):
        for copy in copies[2 * i:2 * i + 2]:
            copy.wait()
        for j in range(width // HEAD_DIM):
            lanes = lanes_of(j)
            q, k = q_ref[part, lanes], k_ref[part, lanes]
            size = q.shape[0]
            scores = jnp.where(lower(size), dot(q, k, 1, 1), 0.0).astype(BF16)
            turned_ref[j, part] = jnp.where(upper(size), dot(k, q, 1, 1), 0.0).astype(BF16)
            inner = dot(scores, v_ref[part, lanes])
            inner_ref[part, lanes] = inner + dot(q, pre_ref[i, j]) if i else inner
            scaled_ref[part, lanes] = gain[:, lanes] * og_ref[part, lanes].astype(F32)
            qturned_ref[lanes, part] = q.T


def attn_kernel(last, pieces, q_ref, inner_ref, scaled_ref, *refs):
    states = [state.astype(BF16) for state in heads_in(refs[:pieces])]
    refs = refs[pieces:]
    attn_ref = refs[2] if last else refs[0]
    rows, width = q_ref.shape
    for part in chunks_of(rows):
        square, cross = (refs[0][part], refs[1][part]) if last else (None, None)
        for j, state in enumerate(states):
            lanes = lanes_of(j)
            attn = inner_ref[part, lanes] + dot(q_ref[part, lanes], state)
            attn_ref[part, lanes] = attn
            more, crossed = attn * attn, scaled_ref[part, lanes] * attn
            square = more if square is None else square + more
            cross = crossed if cross is None else cross + crossed
        if last:
            square = jnp.sum(square.T, axis=0, keepdims=True)
            cross = jnp.sum(cross.T, axis=0, keepdims=True)
            row = lax.broadcasted_iota(jnp.int32, (8, square.shape[1]), 0)
            sums = jnp.where(row == 0, square, jnp.where(row == 1, cross, 0.0))
            refs[-1][:, part] = sums
        else:
            refs[-2][part] = square
            refs[-1][part] = cross


def factors_kernel(full, parts, refs):
    total = refs[0][...]
    for ref in refs[1:parts]:
        total = total + ref[...]
    inv = lax.rsqrt(total[0:1] / full + 1e-6)
    slope = inv * inv * inv * (total[1:2] / full)
    row = lax.broadcasted_iota(jnp.int32, total.shape, 0)
    both = jnp.where(row == 0, inv, slope).T
    wide = (both.shape[0], HEAD_DIM)
    return jnp.broadcast_to(both[:, 0:1], wide), jnp.broadcast_to(both[:, 1:2], wide)


def grad_kernel(full, parts, *refs):
    if parts:
        inv, slope = factors_kernel(full, parts, refs)
        refs[-2][...] = inv
        refs[-1][...] = slope
        inv_ref, slope_ref = refs[-2:]
        attn_ref, scaled_ref, qturned_ref, g_ref, sum_ref, post_ref = refs[parts:-2]
    else:
        inv_ref, slope_ref, attn_ref, scaled_ref, qturned_ref, g_ref, sum_ref, post_ref = refs
    heads = sum_ref.shape[0]
    totals = [None] * heads
    for i, part in reversed(list(enumerate(chunks_of(g_ref.shape[0])))):
        for j in range(heads):
            lanes = lanes_of(j)
            grad = inv_ref[part] * scaled_ref[part, lanes] - attn_ref[part, lanes] * slope_ref[part]
            grad = grad.astype(BF16)
            g_ref[part, lanes] = grad
            term = dot(qturned_ref[lanes, part], grad)
            if totals[j] is None:
                post_ref[i, j] = jnp.zeros_like(post_ref[i, j])
                totals[j] = term
            else:
                post_ref[i, j] = totals[j].astype(BF16)
                totals[j] = totals[j] + term
    for j in range(heads):
        sum_ref[j] = totals[j]


def local_kernel(same, pieces, q_ref, k_ref, v_ref, g_ref, turned_ref, pre_ref, post_ref, *refs):
    qgrad_hbm, kpart_ref, vpart_ref, qgrad_ref, sems = refs[-5:]
    state = heads_in(refs[:pieces])
    rows, width = q_ref.shape
    target = columns(same, width)
    parts = chunks_of(rows)
    copies = []
    for i, part in enumerate(parts):
        for j in range(width // HEAD_DIM):
            lanes = lanes_of(j)
            q, k, v, g = (ref[part, lanes] for ref in (q_ref, k_ref, v_ref, g_ref))
            size = q.shape[0]
            gscores = jnp.where(lower(size), dot(g, v, 1, 1), 0.0).astype(BF16)
            gturned = jnp.where(upper(size), dot(v, g, 1, 1), 0.0).astype(BF16)
            before = state[j] + pre_ref[i, j].astype(F32) if i else state[j]
            qgrad = dot(gscores, k) + dot(g, before.astype(BF16), 1, 1)
            kgrad = dot(gturned, q)
            vgrad = dot(turned_ref[j, part], g)
            if i < len(parts) - 1:
                kgrad = kgrad + dot(v, post_ref[i, j], 1, 1)
                vgrad = vgrad + dot(k, post_ref[i, j])
            qgrad_ref[part, lanes] = qgrad.astype(BF16)
            kpart_ref[part, lanes] = kgrad
            vpart_ref[part, lanes] = vgrad
        copy = pltpu.make_async_copy(qgrad_ref.at[part], qgrad_hbm.at[part, target], sems.at[i])
        copy.start()
        copies.append(copy)
    for copy in copies:
        copy.wait()


def final_parts(k_ref, v_ref, kpart_ref, vpart_ref, states, kgrad_ref, vgrad_ref, part):
    for j, state in enumerate(states):
        lanes = lanes_of(j)
        kgrad = kpart_ref[part, lanes] + dot(v_ref[part, lanes], state, 1, 1)
        vgrad = vpart_ref[part, lanes] + dot(k_ref[part, lanes], state)
        kgrad_ref[part, lanes] = kgrad.astype(BF16)
        vgrad_ref[part, lanes] = vgrad.astype(BF16)


def near_kernel(pieces, *refs):
    states = [state.astype(BF16) for state in heads_in(refs[4:4 + pieces])]
    for part in chunks_of(refs[0].shape[0]):
        final_parts(*refs[:4], states, *refs[4 + pieces:], part)


def last_kernel(same, pieces, *refs):
    states = [state.astype(BF16) for state in heads_in(refs[4:4 + pieces])]
    kdone_ref, vdone_ref, kgrad_hbm, vgrad_hbm, kgrad_ref, vgrad_ref, sems = refs[4 + pieces:]
    rows, width = kgrad_ref.shape
    copies = []

    def send(source, out, part, half):
        sem = sems.at[len(copies)]
        target = out.at[part, columns(half, width)]
        copy = pltpu.make_async_copy(source.at[part], target, sem)
        copy.start()
        copies.append(copy)

    send(kdone_ref, kgrad_hbm, slice(0, rows), not same)
    send(vdone_ref, vgrad_hbm, slice(0, rows), not same)
    for part in chunks_of(rows):
        final_parts(*refs[:4], states, kgrad_ref, vgrad_ref, part)
        send(kgrad_ref, kgrad_hbm, part, same)
        send(vgrad_ref, vgrad_hbm, part, same)
    for copy in copies:
        copy.wait()


def scan_plan(count):
    bits = count.bit_length() - 1
    stages = []
    for stage in range(bits - 1):
        rising, falling = 1 + stage, bits - 1 - stage
        pairs = [(r, r ^ (1 << (falling if r & 1 else rising))) for r in range(count)]
        stages.append((rising, falling, pairs))
    return stages


def join_kernel(backward, piece, done, final, *refs):
    count = lax.axis_size("seq")
    rank = lax.axis_index("seq")
    if backward:
        rank = count - 1 - rank
    odd = (rank & 1) == 1
    plan = scan_plan(count)
    keep, extra = (ref[piece] for ref in refs[:2])
    came = refs[2:2 + done]
    total = keep + extra
    before = jnp.zeros_like(total)
    for (rising, falling, _), ref in zip(plan, came):
        high = (jnp.where(odd, rank >> falling, rank >> rising) & 1) == 1
        value = ref[...]
        before = before + jnp.where(odd | high, value, 0.0)
        total = total + jnp.where(odd, 0.0, value)
    if final:
        message_ref, state_ref = refs[-2:]
        message_ref[...] = before + jnp.where(odd, 0.0, keep)
        state_ref[...] = before + jnp.where(odd, extra, 0.0)
    else:
        rising, falling, _ = plan[done]
        high = (jnp.where(odd, rank >> falling, rank >> rising) & 1) == 1
        refs[-1][...] = jnp.where(odd, before + jnp.where(high, 0.0, total), total)


def join(backward, piece, keep, extra, came, final, after):
    like = shape((piece.stop - piece.start,) + keep.shape[1:], F32)
    return run(
        functools.partial(join_kernel, backward, piece, len(came), final), 4 * like.size,
        [VMEM] * (2 + len(came)) + [ANYWHERE] * len(after),
        [VMEM, VMEM] if final else VMEM,
        [like, like] if final else like,
        (keep, extra, *came, *after),
    )


def scan_states(keep, extra, backward, beside):
    plan = scan_plan(lax.axis_size("seq"))
    pieces = [slice(i, i + 2) for i in range(0, keep.shape[0], 2)]
    came = [[] for _ in pieces]
    results, after = [], []
    for stage, (_, _, pairs) in enumerate(plan):
        messages = []
        for piece, arrived in zip(pieces, came):
            message = join(backward, piece, keep, extra, arrived, False, after + messages)
            messages.append(message)
            arrived.append(move(message, pairs, backward))
        mine = beside[stage:] if stage == len(plan) - 1 else beside[stage:stage + 1]
        made = [work(messages) for work in mine]
        after = [item[-1] for item in made]
        results += made
    states, others, last = [], [], []
    for piece, arrived in zip(pieces, came):
        message, state = join(backward, piece, keep, extra, arrived, True, after + last)
        last = [message]
        states.append(state)
        others.append(nearby(message, backward))
    return states, others, results


def move(value, pairs, backward):
    count = lax.axis_size("seq")
    if backward:
        pairs = [(count - 1 - a, count - 1 - b) for a, b in pairs]
    return lax.ppermute(value, "seq", pairs)


def nearby(value, backward):
    return move(value, [(r, r ^ 1) for r in range(lax.axis_size("seq"))], backward)


def shards(query, key_in, value, out_grad, gain):
    rows, width = query.shape
    half = width // 2
    heads = half // HEAD_DIM
    chunks = len(chunks_of(rows))
    peers = lax.axis_size("head")
    full = width * peers
    gain = gain.reshape(1, width)
    pin = lambda x: pltpu.with_memory_space_constraint(x, pltpu.HBM)
    query, key_in, value, out_grad = (pin(x) for x in (query, key_in, value, out_grad))
    unit = 2 * rows * half * HEAD_DIM
    partial = functools.partial

    states = shape((heads, HEAD_DIM, HEAD_DIM), F32)
    inside = shape((chunks, heads, HEAD_DIM, HEAD_DIM), BF16)
    wide = shape((rows, half), F32)
    thin = shape((rows, half), BF16)
    lane_sums = shape((rows, HEAD_DIM), F32)
    whole = shape((rows, width), BF16)
    sems = pltpu.SemaphoreType.DMA((2 * chunks,))

    def states_of(same):
        return run(
            partial(state_kernel, same), unit, [HBM, HBM], [VMEM] * 4, [thin, thin, states, inside],
            (key_in, value), [sems],
        )

    k1, v1, send, pre1 = states_of(False)
    extra = nearby(send, False)
    k2, v2, keep, pre2 = states_of(True)

    def inner_of(same, k, v, pre):
        return lambda messages: run(
            partial(inner_kernel, same), 6 * unit,
            [HBM, HBM, VMEM, VMEM, VMEM, VMEM] + [ANYWHERE] * len(messages), [VMEM] * 5,
            [
                thin, wide, wide,
                shape((half, rows), BF16), shape((heads, rows, rows // chunks), BF16),
            ],
            (query, out_grad, k, v, gain, pre, *messages),
            [pltpu.VMEM((rows, half), BF16), sems],
        )

    state2, state1, made = scan_states(
        keep, extra, False,
        [inner_of(True, k2, v2, pre2), inner_of(False, k1, v1, pre1)],
    )
    (q2, inner2, scaled2, qturned2, turned2), (q1, inner1, scaled1, qturned1, turned1) = made

    count = len(state2)
    attn2, square, cross = run(
        partial(attn_kernel, False, count), unit, [VMEM] * (3 + count), [VMEM] * 3,
        [wide, lane_sums, lane_sums], (q2, inner2, scaled2, *state2),
    )
    attn1, sums = run(
        partial(attn_kernel, True, count), unit, [VMEM] * (5 + count), [VMEM] * 2,
        [wide, shape((8, rows), F32)], (q1, inner1, scaled1, *state1, square, cross),
    )
    parts = [sums] + [
        lax.ppermute(sums, "head", [(r, r ^ other) for r in range(peers)])
        for other in range(1, peers)
    ]

    g2, gsend, post2, inv, slope = run(
        partial(grad_kernel, full, peers), unit,
        [VMEM] * (peers + 3), [VMEM] * 5, [thin, states, inside, lane_sums, lane_sums],
        (*parts, attn2, scaled2, qturned2),
    )
    gextra = nearby(gsend, True)
    g1, gkeep, post1 = run(
        partial(grad_kernel, full, 0), unit, [VMEM] * 5, [VMEM] * 3, [thin, states, inside],
        (inv, slope, attn1, scaled1, qturned1),
    )

    qgrads = []

    def local_of(same, *args):
        def work(messages):
            more = list(messages) + qgrads
            qgrad, kpart, vpart = run(
                partial(local_kernel, same, count), 9 * unit,
                [VMEM] * len(args) + [ANYWHERE] * len(messages) + [HBM] * len(qgrads),
                [HBM, VMEM, VMEM], [whole, wide, wide], (*args, *more),
                [pltpu.VMEM((rows, half), BF16), sems],
                {len(args) + len(messages): 0} if qgrads else None,
            )
            qgrads[:] = [qgrad]
            return kpart, vpart

        return work

    gstate1, gstate2, made = scan_states(
        gkeep, gextra, True,
        [
            local_of(False, q1, k1, v1, g1, turned1, pre1, post1, *state1),
            local_of(True, q2, k2, v2, g2, turned2, pre2, post2, *state2),
        ],
    )
    (kpart1, vpart1), (kpart2, vpart2) = made

    done = run(
        partial(near_kernel, count), 2 * unit, [VMEM] * (4 + count), [VMEM] * 2, [thin, thin],
        (k1, v1, kpart1, vpart1, *gstate1),
    )
    kgrad, vgrad = run(
        partial(last_kernel, True, count), 2 * unit, [VMEM] * (6 + count), [HBM, HBM],
        [whole, whole], (k2, v2, kpart2, vpart2, *gstate2, *done),
        [pltpu.VMEM((rows, half), BF16)] * 2 + [pltpu.SemaphoreType.DMA((2 * chunks + 2,))],
    )
    return qgrads[0], kgrad, vgrad


def solution(mesh):
    spec = P("seq", "head")
    return jax.shard_map(
        shards,
        mesh=mesh,
        in_specs=(spec, spec, spec, spec, P("head")),
        out_specs=(spec, spec, spec),
        check_vma=False,
    )
```

```python
import functools

import jax
import jax.numpy as jnp
from jax import lax
from jax.experimental import pallas as pl
from jax.experimental.pallas import tpu as pltpu
from jax.sharding import PartitionSpec as P

HEAD_DIM = 128
CHUNK = 256
VMEM_BYTES = 12 * 2**20
F32 = jnp.float32
BF16 = jnp.bfloat16
VMEM = pl.BlockSpec(memory_space=pltpu.VMEM)
HBM = pl.BlockSpec(memory_space=pltpu.HBM)
ANYWHERE = pl.BlockSpec(memory_space=pl.ANY)


def dot(a, b, contract_a=1, contract_b=0):
    dims = (((contract_a,), (contract_b,)), ((), ()))
    return lax.dot_general(a, b, dims, preferred_element_type=F32)


def chunks_of(rows):
    size = CHUNK if rows % CHUNK == 0 else rows
    return [slice(i, i + size) for i in range(0, rows, size)]


def shape(dims, dtype):
    return jax.ShapeDtypeStruct(dims, dtype)


def lanes_of(j):
    return slice(j * HEAD_DIM, (j + 1) * HEAD_DIM)


def heads_in(pieces):
    return [ref[j] for ref in pieces for j in range(ref.shape[0])]


def lower(size):
    row = lax.broadcasted_iota(jnp.int32, (size, size), 0)
    return row >= lax.broadcasted_iota(jnp.int32, (size, size), 1)


def upper(size):
    row = lax.broadcasted_iota(jnp.int32, (size, size), 0)
    return row <= lax.broadcasted_iota(jnp.int32, (size, size), 1)


def run(kernel, flops, in_specs, out_specs, out_shape, args, scratch=(), aliases=None):
    nbytes = sum(a.size * a.dtype.itemsize for a in args)
    return pl.pallas_call(
        kernel,
        in_specs=in_specs,
        out_specs=out_specs,
        out_shape=out_shape,
        scratch_shapes=list(scratch),
        input_output_aliases=aliases or {},
        cost_estimate=pl.CostEstimate(flops=flops, bytes_accessed=nbytes, transcendentals=0),
        compiler_params=pltpu.CompilerParams(vmem_limit_bytes=VMEM_BYTES),
    )(*args)


def columns(same, width):
    odd = lax.rem(lax.axis_index("seq"), 2)
    half = odd if same else 1 - odd
    return pl.ds(pl.multiple_of(half * width, width), width)


def fetches(sources, targets, sems, same):
    rows, width = targets[0].shape
    lanes = columns(same, width)
    copies = []
    for part in chunks_of(rows):
        for source, target in zip(sources, targets):
            sem = sems.at[len(copies)]
            copies.append(pltpu.make_async_copy(source.at[part, lanes], target.at[part], sem))
    return copies


def sum_states(k_ref, v_ref, sum_ref, pre_ref, copies=()):
    heads = sum_ref.shape[0]
    totals = [None] * heads
    for i, part in enumerate(chunks_of(k_ref.shape[0])):
        for copy in copies[2 * i:2 * i + 2]:
            copy.wait()
        for j in range(heads):
            term = dot(k_ref[part, lanes_of(j)], v_ref[part, lanes_of(j)], 0, 0)
            if i:
                pre_ref[i, j] = totals[j].astype(BF16)
            else:
                pre_ref[i, j] = jnp.zeros_like(pre_ref[i, j])
            totals[j] = totals[j] + term if i else term
    for j in range(heads):
        sum_ref[j] = totals[j]


def first_kernel(k_hbm, v_hbm, k1, v1, k2, v2, sum_ref, pre_ref, sems1, sems2):
    now = fetches((k_hbm, v_hbm), (k1, v1), sems1, False)
    later = fetches((k_hbm, v_hbm), (k2, v2), sems2, True)
    for copy in now + later:
        copy.start()
    sum_states(k1, v1, sum_ref, pre_ref, now)
    for copy in later:
        copy.wait()


def inner_kernel(same, q_hbm, og_hbm, k_ref, v_ref, gain_ref, pre_ref, *refs):
    q_ref, inner_ref, scaled_ref, qturned_ref, turned_ref, og_ref, sems = refs[-7:]
    rows, width = q_ref.shape
    copies = fetches((q_hbm, og_hbm), (q_ref, og_ref), sems, same)
    for copy in copies:
        copy.start()
    gain = gain_ref[:, columns(same, width)]
    for i, part in enumerate(chunks_of(rows)):
        for copy in copies[2 * i:2 * i + 2]:
            copy.wait()
        for j in range(width // HEAD_DIM):
            lanes = lanes_of(j)
            q, k = q_ref[part, lanes], k_ref[part, lanes]
            size = q.shape[0]
            scores = jnp.where(lower(size), dot(q, k, 1, 1), 0.0).astype(BF16)
            turned_ref[j, part] = jnp.where(upper(size), dot(k, q, 1, 1), 0.0).astype(BF16)
            inner = dot(scores, v_ref[part, lanes])
            inner_ref[part, lanes] = inner + dot(q, pre_ref[i, j]) if i else inner
            scaled_ref[part, lanes] = gain[:, lanes] * og_ref[part, lanes].astype(F32)
            qturned_ref[lanes, part] = q.T


def attn_kernel(last, pieces, q_ref, inner_ref, scaled_ref, *refs):
    states = [state.astype(BF16) for state in heads_in(refs[:pieces])]
    refs = refs[pieces:]
    attn_ref = refs[2] if last else refs[0]
    rows, width = q_ref.shape
    for part in chunks_of(rows):
        square, cross = (refs[0][part], refs[1][part]) if last else (None, None)
        for j, state in enumerate(states):
            lanes = lanes_of(j)
            attn = inner_ref[part, lanes] + dot(q_ref[part, lanes], state)
            attn_ref[part, lanes] = attn
            more, crossed = attn * attn, scaled_ref[part, lanes] * attn
            square = more if square is None else square + more
            cross = crossed if cross is None else cross + crossed
        if last:
            square = jnp.sum(square.T, axis=0, keepdims=True)
            cross = jnp.sum(cross.T, axis=0, keepdims=True)
            row = lax.broadcasted_iota(jnp.int32, (8, square.shape[1]), 0)
            sums = jnp.where(row == 0, square, jnp.where(row == 1, cross, 0.0))
            refs[-1][:, part] = sums
        else:
            refs[-2][part] = square
            refs[-1][part] = cross


def factors_kernel(full, parts, refs):
    total = refs[0][...]
    for ref in refs[1:parts]:
        total = total + ref[...]
    inv = lax.rsqrt(total[0:1] / full + 1e-6)
    slope = inv * inv * inv * (total[1:2] / full)
    row = lax.broadcasted_iota(jnp.int32, total.shape, 0)
    both = jnp.where(row == 0, inv, slope).T
    wide = (both.shape[0], HEAD_DIM)
    return jnp.broadcast_to(both[:, 0:1], wide), jnp.broadcast_to(both[:, 1:2], wide)


def grad_kernel(full, parts, *refs):
    if parts:
        inv, slope = factors_kernel(full, parts, refs)
        refs[-2][...] = inv
        refs[-1][...] = slope
        inv_ref, slope_ref = refs[-2:]
        attn_ref, scaled_ref, qturned_ref, g_ref, sum_ref, post_ref = refs[parts:-2]
    else:
        inv_ref, slope_ref, attn_ref, scaled_ref, qturned_ref, g_ref, sum_ref, post_ref = refs
    heads = sum_ref.shape[0]
    totals = [None] * heads
    for i, part in reversed(list(enumerate(chunks_of(g_ref.shape[0])))):
        for j in range(heads):
            lanes = lanes_of(j)
            grad = inv_ref[part] * scaled_ref[part, lanes] - attn_ref[part, lanes] * slope_ref[part]
            grad = grad.astype(BF16)
            g_ref[part, lanes] = grad
            term = dot(qturned_ref[lanes, part], grad)
            if totals[j] is None:
                post_ref[i, j] = jnp.zeros_like(post_ref[i, j])
                totals[j] = term
            else:
                post_ref[i, j] = totals[j].astype(BF16)
                totals[j] = totals[j] + term
    for j in range(heads):
        sum_ref[j] = totals[j]


def local_kernel(same, pieces, q_ref, k_ref, v_ref, g_ref, turned_ref, pre_ref, post_ref, *refs):
    qgrad_hbm, kpart_ref, vpart_ref, qgrad_ref, sems = refs[-5:]
    state = heads_in(refs[:pieces])
    rows, width = q_ref.shape
    target = columns(same, width)
    parts = chunks_of(rows)
    copies = []

    def scores(i, j):
        part, lanes = parts[i], lanes_of(j)
        v, g = v_ref[part, lanes], g_ref[part, lanes]
        size = g.shape[0]
        gscores = jnp.where(lower(size), dot(g, v, 1, 1), 0.0).astype(BF16)
        gturned = jnp.where(upper(size), dot(v, g, 1, 1), 0.0).astype(BF16)
        return gscores, gturned

    def products(i, j, gscores, gturned):
        part, lanes = parts[i], lanes_of(j)
        q, k, v, g = (ref[part, lanes] for ref in (q_ref, k_ref, v_ref, g_ref))
        before = state[j] + pre_ref[i, j].astype(F32) if i else state[j]
        qgrad = dot(g, before.astype(BF16), 1, 1) + dot(gscores, k)
        kgrad = dot(gturned, q)
        vgrad = dot(turned_ref[j, part], g)
        if i < len(parts) - 1:
            kgrad = kgrad + dot(v, post_ref[i, j], 1, 1)
            vgrad = vgrad + dot(k, post_ref[i, j])
        qgrad_ref[part, lanes] = qgrad.astype(BF16)
        kpart_ref[part, lanes] = kgrad
        vpart_ref[part, lanes] = vgrad

    places = [(i, j) for i in range(len(parts)) for j in range(width // HEAD_DIM)]
    ready = scores(*places[0])
    for place, following in zip(places, places[1:] + [None]):
        coming = scores(*following) if following else None
        products(*place, *ready)
        ready = coming
        i = place[0]
        if following is None or following[0] != i:
            source, out = qgrad_ref.at[parts[i]], qgrad_hbm.at[parts[i], target]
            copies.append(pltpu.make_async_copy(source, out, sems.at[i]))
            copies[-1].start()
    for copy in copies:
        copy.wait()


def final_parts(k_ref, v_ref, kpart_ref, vpart_ref, states, kgrad_ref, vgrad_ref, part):
    for j, state in enumerate(states):
        lanes = lanes_of(j)
        kgrad = kpart_ref[part, lanes] + dot(v_ref[part, lanes], state, 1, 1)
        vgrad = vpart_ref[part, lanes] + dot(k_ref[part, lanes], state)
        kgrad_ref[part, lanes] = kgrad.astype(BF16)
        vgrad_ref[part, lanes] = vgrad.astype(BF16)


def near_kernel(pieces, *refs):
    states = [state.astype(BF16) for state in heads_in(refs[4:4 + pieces])]
    for part in chunks_of(refs[0].shape[0]):
        final_parts(*refs[:4], states, *refs[4 + pieces:], part)


def last_kernel(same, pieces, *refs):
    states = [state.astype(BF16) for state in heads_in(refs[4:4 + pieces])]
    kdone_ref, vdone_ref, kgrad_hbm, vgrad_hbm, kgrad_ref, vgrad_ref, sems = refs[4 + pieces:]
    rows, width = kgrad_ref.shape
    copies = []

    def send(source, out, part, half):
        sem = sems.at[len(copies)]
        target = out.at[part, columns(half, width)]
        copy = pltpu.make_async_copy(source.at[part], target, sem)
        copy.start()
        copies.append(copy)

    send(kdone_ref, kgrad_hbm, slice(0, rows), not same)
    send(vdone_ref, vgrad_hbm, slice(0, rows), not same)
    for part in chunks_of(rows):
        final_parts(*refs[:4], states, kgrad_ref, vgrad_ref, part)
        send(kgrad_ref, kgrad_hbm, part, same)
        send(vgrad_ref, vgrad_hbm, part, same)
    for copy in copies:
        copy.wait()


def scan_plan(count):
    bits = count.bit_length() - 1
    stages = []
    for stage in range(bits - 1):
        rising, falling = 1 + stage, bits - 1 - stage
        pairs = [(r, r ^ (1 << (falling if r & 1 else rising))) for r in range(count)]
        stages.append((rising, falling, pairs))
    return stages


def join_kernel(backward, piece, done, final, *refs):
    count = lax.axis_size("seq")
    rank = lax.axis_index("seq")
    if backward:
        rank = count - 1 - rank
    odd = (rank & 1) == 1
    plan = scan_plan(count)
    keep, extra = (ref[piece] for ref in refs[:2])
    came = refs[2:2 + done]
    total = keep + extra
    before = jnp.zeros_like(total)
    for (rising, falling, _), ref in zip(plan, came):
        high = (jnp.where(odd, rank >> falling, rank >> rising) & 1) == 1
        value = ref[...]
        before = before + jnp.where(odd | high, value, 0.0)
        total = total + jnp.where(odd, 0.0, value)
    if final:
        message_ref, state_ref = refs[-2:]
        message_ref[...] = before + jnp.where(odd, 0.0, keep)
        state_ref[...] = before + jnp.where(odd, extra, 0.0)
    else:
        rising, falling, _ = plan[done]
        high = (jnp.where(odd, rank >> falling, rank >> rising) & 1) == 1
        refs[-1][...] = jnp.where(odd, before + jnp.where(high, 0.0, total), total)


def join(backward, piece, keep, extra, came, final, after):
    like = shape((piece.stop - piece.start,) + keep.shape[1:], F32)
    return run(
        functools.partial(join_kernel, backward, piece, len(came), final), 4 * like.size,
        [VMEM] * (2 + len(came)) + [ANYWHERE] * len(after),
        [VMEM, VMEM] if final else VMEM,
        [like, like] if final else like,
        (keep, extra, *came, *after),
    )


def scan_states(keep, extra, backward, beside):
    plan = scan_plan(lax.axis_size("seq"))
    pieces = [slice(i, i + 2) for i in range(0, keep.shape[0], 2)]
    came = [[] for _ in pieces]
    results, after = [], []
    for stage, (_, _, pairs) in enumerate(plan):
        messages = []
        for piece, arrived in zip(pieces, came):
            message = join(backward, piece, keep, extra, arrived, False, after + messages)
            messages.append(message)
            arrived.append(move(message, pairs, backward))
        mine = beside[stage:] if stage == len(plan) - 1 else beside[stage:stage + 1]
        made = [work(messages) for work in mine]
        after = [item[-1] for item in made]
        results += made
    states, others, last = [], [], []
    for piece, arrived in zip(pieces, came):
        message, state = join(backward, piece, keep, extra, arrived, True, after + last)
        last = [message]
        states.append(state)
        others.append(nearby(message, backward))
    return states, others, results


def move(value, pairs, backward):
    count = lax.axis_size("seq")
    if backward:
        pairs = [(count - 1 - a, count - 1 - b) for a, b in pairs]
    return lax.ppermute(value, "seq", pairs)


def nearby(value, backward):
    return move(value, [(r, r ^ 1) for r in range(lax.axis_size("seq"))], backward)


def shards(query, key_in, value, out_grad, gain):
    rows, width = query.shape
    half = width // 2
    heads = half // HEAD_DIM
    chunks = len(chunks_of(rows))
    peers = lax.axis_size("head")
    full = width * peers
    gain = gain.reshape(1, width)
    pin = lambda x: pltpu.with_memory_space_constraint(x, pltpu.HBM)
    query, key_in, value, out_grad = (pin(x) for x in (query, key_in, value, out_grad))
    unit = 2 * rows * half * HEAD_DIM
    partial = functools.partial

    states = shape((heads, HEAD_DIM, HEAD_DIM), F32)
    inside = shape((chunks, heads, HEAD_DIM, HEAD_DIM), BF16)
    wide = shape((rows, half), F32)
    thin = shape((rows, half), BF16)
    lane_sums = shape((rows, HEAD_DIM), F32)
    whole = shape((rows, width), BF16)
    sems = pltpu.SemaphoreType.DMA((2 * chunks,))

    k1, v1, k2, v2, send, pre1 = run(
        first_kernel, unit, [HBM, HBM], [VMEM] * 6, [thin] * 4 + [states, inside],
        (key_in, value), [sems, sems],
    )
    extra = nearby(send, False)
    keep, pre2 = run(sum_states, unit, [VMEM, VMEM], [VMEM] * 2, [states, inside], (k2, v2))

    def inner_of(same, k, v, pre):
        return lambda messages: run(
            partial(inner_kernel, same), 6 * unit,
            [HBM, HBM, VMEM, VMEM, VMEM, VMEM] + [ANYWHERE] * len(messages), [VMEM] * 5,
            [
                thin, wide, wide,
                shape((half, rows), BF16), shape((heads, rows, rows // chunks), BF16),
            ],
            (query, out_grad, k, v, gain, pre, *messages),
            [pltpu.VMEM((rows, half), BF16), sems],
        )

    state2, state1, made = scan_states(
        keep, extra, False,
        [inner_of(True, k2, v2, pre2), inner_of(False, k1, v1, pre1)],
    )
    (q2, inner2, scaled2, qturned2, turned2), (q1, inner1, scaled1, qturned1, turned1) = made

    count = len(state2)
    attn2, square, cross = run(
        partial(attn_kernel, False, count), unit, [VMEM] * (3 + count), [VMEM] * 3,
        [wide, lane_sums, lane_sums], (q2, inner2, scaled2, *state2),
    )
    attn1, sums = run(
        partial(attn_kernel, True, count), unit, [VMEM] * (5 + count), [VMEM] * 2,
        [wide, shape((8, rows), F32)], (q1, inner1, scaled1, *state1, square, cross),
    )
    parts = [sums] + [
        lax.ppermute(sums, "head", [(r, r ^ other) for r in range(peers)])
        for other in range(1, peers)
    ]

    g2, gsend, post2, inv, slope = run(
        partial(grad_kernel, full, peers), unit,
        [VMEM] * (peers + 3), [VMEM] * 5, [thin, states, inside, lane_sums, lane_sums],
        (*parts, attn2, scaled2, qturned2),
    )
    gextra = nearby(gsend, True)
    g1, gkeep, post1 = run(
        partial(grad_kernel, full, 0), unit, [VMEM] * 5, [VMEM] * 3, [thin, states, inside],
        (inv, slope, attn1, scaled1, qturned1),
    )

    qgrads = []

    def local_of(same, *args):
        def work(messages):
            more = list(messages) + qgrads
            qgrad, kpart, vpart = run(
                partial(local_kernel, same, count), 9 * unit,
                [VMEM] * len(args) + [ANYWHERE] * len(messages) + [HBM] * len(qgrads),
                [HBM, VMEM, VMEM], [whole, wide, wide], (*args, *more),
                [pltpu.VMEM((rows, half), BF16), sems],
                {len(args) + len(messages): 0} if qgrads else None,
            )
            qgrads[:] = [qgrad]
            return kpart, vpart

        return work

    gstate1, gstate2, made = scan_states(
        gkeep, gextra, True,
        [
            local_of(False, q1, k1, v1, g1, turned1, pre1, post1, *state1),
            local_of(True, q2, k2, v2, g2, turned2, pre2, post2, *state2),
        ],
    )
    (kpart1, vpart1), (kpart2, vpart2) = made

    done = run(
        partial(near_kernel, count), 2 * unit, [VMEM] * (4 + count), [VMEM] * 2, [thin, thin],
        (k1, v1, kpart1, vpart1, *gstate1),
    )
    kgrad, vgrad = run(
        partial(last_kernel, True, count), 2 * unit, [VMEM] * (6 + count), [HBM, HBM],
        [whole, whole], (k2, v2, kpart2, vpart2, *gstate2, *done),
        [pltpu.VMEM((rows, half), BF16)] * 2 + [pltpu.SemaphoreType.DMA((2 * chunks + 2,))],
    )
    return qgrads[0], kgrad, vgrad


def solution(mesh):
    spec = P("seq", "head")
    return jax.shard_map(
        shards,
        mesh=mesh,
        in_specs=(spec, spec, spec, spec, P("head")),
        out_specs=(spec, spec, spec),
        check_vma=False,
    )
```

```python
import functools

import jax
import jax.numpy as jnp
from jax import lax
from jax.experimental import pallas as pl
from jax.experimental.pallas import tpu as pltpu
from jax.sharding import PartitionSpec as P

HEAD_DIM = 128
CHUNK = 256
PIECE = 2
VMEM_BYTES = 12 * 2**20
F32 = jnp.float32
BF16 = jnp.bfloat16
VMEM = pl.BlockSpec(memory_space=pltpu.VMEM)
HBM = pl.BlockSpec(memory_space=pltpu.HBM)
ANYWHERE = pl.BlockSpec(memory_space=pl.ANY)


def dot(a, b, contract_a=1, contract_b=0):
    dims = (((contract_a,), (contract_b,)), ((), ()))
    return lax.dot_general(a, b, dims, preferred_element_type=F32)


def chunks_of(rows):
    size = CHUNK if rows % CHUNK == 0 else rows
    return [slice(i, i + size) for i in range(0, rows, size)]


def shape(dims, dtype):
    return jax.ShapeDtypeStruct(dims, dtype)


def lanes_of(j):
    return slice(j * HEAD_DIM, (j + 1) * HEAD_DIM)


def heads_in(pieces):
    return [ref[j] for ref in pieces for j in range(ref.shape[0])]


def lower(size):
    row = lax.broadcasted_iota(jnp.int32, (size, size), 0)
    return row >= lax.broadcasted_iota(jnp.int32, (size, size), 1)


def upper(size):
    row = lax.broadcasted_iota(jnp.int32, (size, size), 0)
    return row <= lax.broadcasted_iota(jnp.int32, (size, size), 1)


def run(kernel, flops, in_specs, out_specs, out_shape, args, scratch=(), aliases=None):
    nbytes = sum(a.size * a.dtype.itemsize for a, spec in zip(args, in_specs) if spec is HBM)
    return pl.pallas_call(
        kernel,
        in_specs=in_specs,
        out_specs=out_specs,
        out_shape=out_shape,
        scratch_shapes=list(scratch),
        input_output_aliases=aliases or {},
        cost_estimate=pl.CostEstimate(flops=flops, bytes_accessed=nbytes, transcendentals=0),
        compiler_params=pltpu.CompilerParams(vmem_limit_bytes=VMEM_BYTES),
    )(*args)


def columns(same, width, piece=None):
    odd = lax.rem(lax.axis_index("seq"), 2)
    half = odd if same else 1 - odd
    if piece is None:
        return pl.ds(pl.multiple_of(half * width, width), width)
    size = PIECE * HEAD_DIM
    return pl.ds(pl.multiple_of(half * width + piece * size, size), size)


def fetches(sources, targets, sems, same):
    rows, width = targets[0].shape
    lanes = columns(same, width)
    copies = []
    for part in chunks_of(rows):
        for source, target in zip(sources, targets):
            sem = sems.at[len(copies)]
            copies.append(pltpu.make_async_copy(source.at[part, lanes], target.at[part], sem))
    return copies


def sum_states(k_ref, v_ref, pre_ref, *sum_refs, copies=()):
    heads = pre_ref.shape[1]
    totals = [None] * heads
    for i, part in enumerate(chunks_of(k_ref.shape[0])):
        for copy in copies[2 * i:2 * i + 2]:
            copy.wait()
        for j in range(heads):
            term = dot(k_ref[part, lanes_of(j)], v_ref[part, lanes_of(j)], 0, 0)
            if i:
                pre_ref[i, j] = totals[j].astype(BF16)
            else:
                pre_ref[i, j] = jnp.zeros_like(pre_ref[i, j])
            totals[j] = totals[j] + term if i else term
    for j in range(heads):
        sum_refs[j // PIECE][j % PIECE] = totals[j]


def first_kernel(k_hbm, v_hbm, k1, v1, k2, v2, pre_ref, *refs):
    *sum_refs, sems1, sems2 = refs
    now = fetches((k_hbm, v_hbm), (k1, v1), sems1, False)
    later = fetches((k_hbm, v_hbm), (k2, v2), sems2, True)
    for copy in now + later:
        copy.start()
    sum_states(k1, v1, pre_ref, *sum_refs, copies=now)
    for copy in later:
        copy.wait()


def inner_kernel(same, q_hbm, og_hbm, k_ref, v_ref, gain_ref, pre_ref, *refs):
    q_ref, inner_ref, scaled_ref, qturned_ref, turned_ref, og_ref, sems = refs[-7:]
    rows, width = q_ref.shape
    copies = fetches((q_hbm, og_hbm), (q_ref, og_ref), sems, same)
    for copy in copies:
        copy.start()
    gain = gain_ref[:, columns(same, width)]
    for i, part in enumerate(chunks_of(rows)):
        for copy in copies[2 * i:2 * i + 2]:
            copy.wait()
        for j in range(width // HEAD_DIM):
            lanes = lanes_of(j)
            q, k = q_ref[part, lanes], k_ref[part, lanes]
            size = q.shape[0]
            scores = jnp.where(lower(size), dot(q, k, 1, 1), 0.0).astype(BF16)
            turned_ref[j, part] = jnp.where(upper(size), dot(k, q, 1, 1), 0.0).astype(BF16)
            inner = dot(scores, v_ref[part, lanes])
            inner_ref[part, lanes] = inner + dot(q, pre_ref[i, j]) if i else inner
            scaled_ref[part, lanes] = gain[:, lanes] * og_ref[part, lanes].astype(F32)
            qturned_ref[lanes, part] = q.T


def attn_kernel(piece, first, last, q_ref, inner_ref, scaled_ref, state_ref, *refs):
    attn_ref = refs[0] if first else refs[2]
    for part in chunks_of(q_ref.shape[0]):
        square, cross = (None, None) if first else (refs[0][part], refs[1][part])
        for j in range(PIECE):
            lanes = lanes_of(piece * PIECE + j)
            state = state_ref[j].astype(BF16)
            attn = inner_ref[part, lanes] + dot(q_ref[part, lanes], state)
            attn_ref[part, lanes_of(j)] = attn
            more, crossed = attn * attn, scaled_ref[part, lanes] * attn
            square = more if square is None else square + more
            cross = crossed if cross is None else cross + crossed
        if last:
            square = jnp.sum(square.T, axis=0, keepdims=True)
            cross = jnp.sum(cross.T, axis=0, keepdims=True)
            row = lax.broadcasted_iota(jnp.int32, (8, square.shape[1]), 0)
            sums = jnp.where(row == 0, square, jnp.where(row == 1, cross, 0.0))
            refs[-1][:, part] = sums
        else:
            refs[-2][part] = square
            refs[-1][part] = cross


def factors_kernel(full, parts, refs):
    total = refs[0][...]
    for ref in refs[1:parts]:
        total = total + ref[...]
    inv = lax.rsqrt(total[0:1] / full + 1e-6)
    slope = inv * inv * inv * (total[1:2] / full)
    row = lax.broadcasted_iota(jnp.int32, total.shape, 0)
    both = jnp.where(row == 0, inv, slope).T
    wide = (both.shape[0], HEAD_DIM)
    return jnp.broadcast_to(both[:, 0:1], wide), jnp.broadcast_to(both[:, 1:2], wide)


def grad_kernel(piece, full, parts, *refs):
    if parts:
        inv, slope = factors_kernel(full, parts, refs)
        refs[-2][...] = inv
        refs[-1][...] = slope
        inv_ref, slope_ref = refs[-2:]
        attn_ref, scaled_ref, qturned_ref, g_ref, post_ref, sum_ref = refs[parts:-2]
    else:
        inv_ref, slope_ref, attn_ref, scaled_ref, qturned_ref, g_ref, post_ref, sum_ref = refs
    totals = [None] * PIECE
    for i, part in reversed(list(enumerate(chunks_of(g_ref.shape[0])))):
        for j in range(PIECE):
            lanes = lanes_of(piece * PIECE + j)
            attn = attn_ref[part, lanes_of(j)]
            grad = inv_ref[part] * scaled_ref[part, lanes] - attn * slope_ref[part]
            grad = grad.astype(BF16)
            g_ref[part, lanes_of(j)] = grad
            term = dot(qturned_ref[lanes, part], grad)
            if totals[j] is None:
                post_ref[i, j] = jnp.zeros_like(post_ref[i, j])
                totals[j] = term
            else:
                post_ref[i, j] = totals[j].astype(BF16)
                totals[j] = totals[j] + term
    for j in range(PIECE):
        sum_ref[j] = totals[j]


def local_kernel(same, pieces, q_ref, k_ref, v_ref, turned_ref, pre_ref, *refs):
    qgrad_hbm, kpart_ref, vpart_ref, qgrad_ref, sems = refs[-5:]
    state = heads_in(refs[:pieces])
    g_refs, post_refs = refs[pieces:2 * pieces], refs[2 * pieces:3 * pieces]
    rows, width = q_ref.shape
    target = columns(same, width)
    parts = chunks_of(rows)
    copies = []

    def scores(i, j):
        part, lanes = parts[i], lanes_of(j)
        v, g = v_ref[part, lanes], g_refs[j // PIECE][part, lanes_of(j % PIECE)]
        size = g.shape[0]
        gscores = jnp.where(lower(size), dot(g, v, 1, 1), 0.0).astype(BF16)
        gturned = jnp.where(upper(size), dot(v, g, 1, 1), 0.0).astype(BF16)
        return gscores, gturned

    def products(i, j, gscores, gturned):
        part, lanes = parts[i], lanes_of(j)
        q, k, v = (ref[part, lanes] for ref in (q_ref, k_ref, v_ref))
        g = g_refs[j // PIECE][part, lanes_of(j % PIECE)]
        before = state[j] + pre_ref[i, j].astype(F32) if i else state[j]
        qgrad = dot(g, before.astype(BF16), 1, 1) + dot(gscores, k)
        kgrad = dot(gturned, q)
        vgrad = dot(turned_ref[j, part], g)
        if i < len(parts) - 1:
            post = post_refs[j // PIECE][i, j % PIECE]
            kgrad = kgrad + dot(v, post, 1, 1)
            vgrad = vgrad + dot(k, post)
        qgrad_ref[part, lanes] = qgrad.astype(BF16)
        kpart_ref[part, lanes] = kgrad
        vpart_ref[part, lanes] = vgrad

    places = [(i, j) for i in range(len(parts)) for j in range(width // HEAD_DIM)]
    ready = scores(*places[0])
    for place, following in zip(places, places[1:] + [None]):
        coming = scores(*following) if following else None
        products(*place, *ready)
        ready = coming
        i = place[0]
        if following is None or following[0] != i:
            source, out = qgrad_ref.at[parts[i]], qgrad_hbm.at[parts[i], target]
            copies.append(pltpu.make_async_copy(source, out, sems.at[i]))
            copies[-1].start()
    for copy in copies:
        copy.wait()


def final_part(piece, part, k_ref, v_ref, kpart_ref, vpart_ref, state_ref, kgrad_ref, vgrad_ref):
    for j in range(PIECE):
        lanes = lanes_of(piece * PIECE + j)
        state = state_ref[j].astype(BF16)
        kgrad = kpart_ref[part, lanes] + dot(v_ref[part, lanes], state, 1, 1)
        vgrad = vpart_ref[part, lanes] + dot(k_ref[part, lanes], state)
        kgrad_ref[part, lanes_of(j)] = kgrad.astype(BF16)
        vgrad_ref[part, lanes_of(j)] = vgrad.astype(BF16)


def final_kernel(piece, *refs):
    for part in chunks_of(refs[0].shape[0]):
        final_part(piece, part, *refs)


def write_kernel(same, piece, *refs):
    kgrad_hbm, vgrad_hbm, kgrad_ref, vgrad_ref, sems = refs[-5:]
    done = refs[5:5 + 2 * piece]
    rows, width = refs[0].shape
    copies = []

    def send(source, out, part, number):
        target = out.at[part, columns(same, width, number)]
        copies.append(pltpu.make_async_copy(source.at[part], target, sems.at[len(copies)]))
        copies[-1].start()

    for number in range(piece):
        send(done[2 * number], kgrad_hbm, slice(0, rows), number)
        send(done[2 * number + 1], vgrad_hbm, slice(0, rows), number)
    for part in chunks_of(rows):
        final_part(piece, part, *refs[:5], kgrad_ref, vgrad_ref)
        send(kgrad_ref, kgrad_hbm, part, piece)
        send(vgrad_ref, vgrad_hbm, part, piece)
    for copy in copies:
        copy.wait()


def scan_plan(count):
    bits = count.bit_length() - 1
    stages = []
    for stage in range(bits - 1):
        rising, falling = 1 + stage, bits - 1 - stage
        pairs = [(r, r ^ (1 << (falling if r & 1 else rising))) for r in range(count)]
        stages.append((rising, falling, pairs))
    return stages


def join_kernel(backward, done, final, *refs):
    count = lax.axis_size("seq")
    rank = lax.axis_index("seq")
    if backward:
        rank = count - 1 - rank
    odd = (rank & 1) == 1
    plan = scan_plan(count)
    keep, extra = (ref[...] for ref in refs[:2])
    came = refs[2:2 + done]
    total = keep + extra
    before = jnp.zeros_like(total)
    for (rising, falling, _), ref in zip(plan, came):
        high = (jnp.where(odd, rank >> falling, rank >> rising) & 1) == 1
        value = ref[...]
        before = before + jnp.where(odd | high, value, 0.0)
        total = total + jnp.where(odd, 0.0, value)
    if final:
        message_ref, state_ref = refs[-2:]
        message_ref[...] = before + jnp.where(odd, 0.0, keep)
        state_ref[...] = before + jnp.where(odd, extra, 0.0)
    else:
        rising, falling, _ = plan[done]
        high = (jnp.where(odd, rank >> falling, rank >> rising) & 1) == 1
        refs[-1][...] = jnp.where(odd, before + jnp.where(high, 0.0, total), total)


def join(backward, keep, extra, came, final, after):
    like = shape(keep.shape, F32)
    return run(
        functools.partial(join_kernel, backward, len(came), final), 4 * like.size,
        [VMEM] * (2 + len(came)) + [ANYWHERE] * len(after),
        [VMEM, VMEM] if final else VMEM,
        [like, like] if final else like,
        (keep, extra, *came, *after),
    )


def scan_states(keeps, extras, backward, beside):
    plan = scan_plan(lax.axis_size("seq"))
    came = [[] for _ in keeps]
    results, after = [], []
    for stage, (_, _, pairs) in enumerate(plan):
        messages = []
        for keep, extra, arrived in zip(keeps, extras, came):
            message = join(backward, keep, extra, arrived, False, after + messages)
            messages.append(message)
            arrived.append(move(message, pairs, backward))
        mine = beside[stage:] if stage == len(plan) - 1 else beside[stage:stage + 1]
        made = [work(messages) for work in mine]
        after = [item[-1] for item in made]
        results += made
    states, messages = [], []
    for keep, extra, arrived in zip(keeps, extras, came):
        message, state = join(backward, keep, extra, arrived, True, after + messages)
        states.append(state)
        messages.append(message)
    others = [nearby(message, backward) for message in messages[::-1]][::-1]
    return states, others, results


def move(value, pairs, backward):
    count = lax.axis_size("seq")
    if backward:
        pairs = [(count - 1 - a, count - 1 - b) for a, b in pairs]
    return lax.ppermute(value, "seq", pairs)


def nearby(value, backward):
    return move(value, [(r, r ^ 1) for r in range(lax.axis_size("seq"))], backward)


def shards(query, key_in, value, out_grad, gain):
    rows, width = query.shape
    half = width // 2
    heads = half // HEAD_DIM
    chunks = len(chunks_of(rows))
    peers = lax.axis_size("head")
    full = width * peers
    gain = gain.reshape(1, width)
    pin = lambda x: pltpu.with_memory_space_constraint(x, pltpu.HBM)
    query, key_in, value, out_grad = (pin(x) for x in (query, key_in, value, out_grad))
    unit = 2 * rows * half * HEAD_DIM
    partial = functools.partial

    count = heads // PIECE
    states = shape((PIECE, HEAD_DIM, HEAD_DIM), F32)
    inside = shape((chunks, heads, HEAD_DIM, HEAD_DIM), BF16)
    wide = shape((rows, half), F32)
    thin = shape((rows, half), BF16)
    lane_sums = shape((rows, HEAD_DIM), F32)
    whole = shape((rows, width), BF16)
    sems = pltpu.SemaphoreType.DMA((2 * chunks,))

    k1, v1, k2, v2, pre1, *sends = run(
        first_kernel, unit, [HBM, HBM], [VMEM] * (5 + count), [thin] * 4 + [inside] + [states] * count,
        (key_in, value), [sems, sems],
    )
    extras = [nearby(send, False) for send in sends]
    pre2, *keeps = run(
        sum_states, unit, [VMEM, VMEM], [VMEM] * (1 + count), [inside] + [states] * count, (k2, v2)
    )

    def inner_of(same, k, v, pre):
        return lambda messages: run(
            partial(inner_kernel, same), 6 * unit,
            [HBM, HBM, VMEM, VMEM, VMEM, VMEM] + [ANYWHERE] * len(messages), [VMEM] * 5,
            [
                thin, wide, wide,
                shape((half, rows), BF16), shape((heads, rows, rows // chunks), BF16),
            ],
            (query, out_grad, k, v, gain, pre, *messages),
            [pltpu.VMEM((rows, half), BF16), sems],
        )

    state2, state1, made = scan_states(
        keeps, extras, False,
        [inner_of(True, k2, v2, pre2), inner_of(False, k1, v1, pre1)],
    )
    (q2, inner2, scaled2, qturned2, turned2), (q1, inner1, scaled1, qturned1, turned1) = made

    attns, sums = [], ()
    piece_wide = shape((rows, PIECE * HEAD_DIM), F32)
    for number, state in enumerate([*state2, *state1]):
        args = (q2, inner2, scaled2) if number < count else (q1, inner1, scaled1)
        last = number == 2 * count - 1
        attn, *sums = run(
            partial(attn_kernel, number % count, number == 0, last), unit // count,
            [VMEM] * (4 + len(sums)), [VMEM] * (2 if last else 3),
            [piece_wide] + ([shape((8, rows), F32)] if last else [lane_sums] * 2),
            (*args, state, *sums),
        )
        attns.append(attn)
    sums = sums[0]
    parts = [sums] + [
        lax.ppermute(sums, "head", [(r, r ^ other) for r in range(peers)])
        for other in range(1, peers)
    ]

    factors = []

    def grads_of(attns, scaled, qturned):
        made = []
        for piece, attn in enumerate(attns):
            peers_in = 0 if factors else len(parts)
            first = factors or parts
            g, post, total, *more = run(
                partial(grad_kernel, piece, full, peers_in), unit // count,
                [VMEM] * (len(first) + 3), [VMEM] * (3 if factors else 5),
                [shape((rows, PIECE * HEAD_DIM), BF16), posts, states]
                + ([] if factors else [lane_sums] * 2),
                (*first, attn, scaled, qturned),
            )
            factors.extend(more)
            made.append((g, post, total))
        return zip(*made)

    posts = shape((chunks, PIECE, HEAD_DIM, HEAD_DIM), BF16)
    gs2, posts2, gsends = grads_of(attns[:count], scaled2, qturned2)
    gextras = [nearby(gsend, True) for gsend in gsends]
    gs1, posts1, gkeeps = grads_of(attns[count:], scaled1, qturned1)

    qgrads = []

    def local_of(same, *args):
        def work(messages):
            more = list(messages) + qgrads
            qgrad, kpart, vpart = run(
                partial(local_kernel, same, count), 9 * unit,
                [VMEM] * len(args) + [ANYWHERE] * len(messages) + [HBM] * len(qgrads),
                [HBM, VMEM, VMEM], [whole, wide, wide], (*args, *more),
                [pltpu.VMEM((rows, half), BF16), sems],
                {len(args) + len(messages): 0} if qgrads else None,
            )
            qgrads[:] = [qgrad]
            return kpart, vpart

        return work

    gstate1, gstate2, made = scan_states(
        gkeeps, gextras, True,
        [
            local_of(False, q1, k1, v1, turned1, pre1, *state1, *gs1, *posts1),
            local_of(True, q2, k2, v2, turned2, pre2, *state2, *gs2, *posts2),
        ],
    )
    (kpart1, vpart1), (kpart2, vpart2) = made

    piece_thin = shape((rows, PIECE * HEAD_DIM), BF16)

    def finals_of(same, k, v, kpart, vpart, found, outs):
        done = []
        for piece, state in enumerate(found[:-1]):
            done += run(
                partial(final_kernel, piece), 2 * unit // count, [VMEM] * 5, [VMEM] * 2,
                [piece_thin] * 2, (k, v, kpart, vpart, state),
            )
        args = (k, v, kpart, vpart, found[-1], *done)
        return run(
            partial(write_kernel, same, count - 1), 2 * unit // count,
            [VMEM] * len(args) + [HBM] * len(outs), [HBM, HBM], [whole, whole], (*args, *outs),
            [pltpu.VMEM(piece_thin.shape, BF16)] * 2
            + [pltpu.SemaphoreType.DMA((2 * (chunks + count - 1),))],
            {len(args) + i: i for i in range(len(outs))},
        )

    outs = finals_of(False, k1, v1, kpart1, vpart1, gstate1, ())
    kgrad, vgrad = finals_of(True, k2, v2, kpart2, vpart2, gstate2, outs)
    return qgrads[0], kgrad, vgrad


def solution(mesh):
    spec = P("seq", "head")
    return jax.shard_map(
        shards,
        mesh=mesh,
        in_specs=(spec, spec, spec, spec, P("head")),
        out_specs=(spec, spec, spec),
        check_vma=False,
    )
```

```python
import functools

import jax
import jax.numpy as jnp
from jax import lax
from jax.experimental import pallas as pl
from jax.experimental.pallas import tpu as pltpu
from jax.sharding import PartitionSpec as P

HEAD_DIM = 128
CHUNK = 256
PIECE = 2
VMEM_BYTES = 12 * 2**20
F32 = jnp.float32
BF16 = jnp.bfloat16
VMEM = pl.BlockSpec(memory_space=pltpu.VMEM)
HBM = pl.BlockSpec(memory_space=pltpu.HBM)
ANYWHERE = pl.BlockSpec(memory_space=pl.ANY)


def dot(a, b, contract_a=1, contract_b=0):
    dims = (((contract_a,), (contract_b,)), ((), ()))
    return lax.dot_general(a, b, dims, preferred_element_type=F32)


def chunks_of(rows):
    size = CHUNK if rows % CHUNK == 0 else rows
    return [slice(i, i + size) for i in range(0, rows, size)]


def shape(dims, dtype):
    return jax.ShapeDtypeStruct(dims, dtype)


def lanes_of(j):
    return slice(j * HEAD_DIM, (j + 1) * HEAD_DIM)


def heads_in(pieces):
    return [ref[j] for ref in pieces for j in range(ref.shape[0])]


def lower(size):
    row = lax.broadcasted_iota(jnp.int32, (size, size), 0)
    return row >= lax.broadcasted_iota(jnp.int32, (size, size), 1)


def upper(size):
    row = lax.broadcasted_iota(jnp.int32, (size, size), 0)
    return row <= lax.broadcasted_iota(jnp.int32, (size, size), 1)


def run(kernel, flops, in_specs, out_specs, out_shape, args, scratch=(), aliases=None):
    nbytes = sum(a.size * a.dtype.itemsize for a, spec in zip(args, in_specs) if spec is HBM)
    return pl.pallas_call(
        kernel,
        in_specs=in_specs,
        out_specs=out_specs,
        out_shape=out_shape,
        scratch_shapes=list(scratch),
        input_output_aliases=aliases or {},
        cost_estimate=pl.CostEstimate(flops=flops, bytes_accessed=nbytes, transcendentals=0),
        compiler_params=pltpu.CompilerParams(vmem_limit_bytes=VMEM_BYTES),
    )(*args)


def columns(same, width, piece=None):
    odd = lax.rem(lax.axis_index("seq"), 2)
    half = odd if same else 1 - odd
    if piece is None:
        return pl.ds(pl.multiple_of(half * width, width), width)
    size = PIECE * HEAD_DIM
    return pl.ds(pl.multiple_of(half * width + piece * size, size), size)


def fetches(sources, targets, sems, same):
    rows, width = targets[0].shape
    lanes = columns(same, width)
    copies = []
    for part in chunks_of(rows):
        for source, target in zip(sources, targets):
            sem = sems.at[len(copies)]
            copies.append(pltpu.make_async_copy(source.at[part, lanes], target.at[part], sem))
    return copies


def sum_states(k_ref, v_ref, pre_ref, *sum_refs, copies=()):
    heads = pre_ref.shape[1]
    totals = [None] * heads
    for i, part in enumerate(chunks_of(k_ref.shape[0])):
        for copy in copies[2 * i:2 * i + 2]:
            copy.wait()
        for j in range(heads):
            term = dot(k_ref[part, lanes_of(j)], v_ref[part, lanes_of(j)], 0, 0)
            if i:
                pre_ref[i, j] = totals[j].astype(BF16)
            else:
                pre_ref[i, j] = jnp.zeros_like(pre_ref[i, j])
            totals[j] = totals[j] + term if i else term
    for j in range(heads):
        sum_refs[j // PIECE][j % PIECE] = totals[j]


def first_kernel(k_hbm, v_hbm, k1, v1, k2, v2, pre_ref, *refs):
    *sum_refs, sems1, sems2 = refs
    now = fetches((k_hbm, v_hbm), (k1, v1), sems1, False)
    later = fetches((k_hbm, v_hbm), (k2, v2), sems2, True)
    for copy in now + later:
        copy.start()
    sum_states(k1, v1, pre_ref, *sum_refs, copies=now)
    for copy in later:
        copy.wait()


def inner_kernel(same, q_hbm, og_hbm, k_ref, v_ref, gain_ref, pre_ref, *refs):
    q_ref, inner_ref, scaled_ref, qturned_ref, turned_ref, og_ref, sems = refs[-7:]
    rows, width = q_ref.shape
    copies = fetches((q_hbm, og_hbm), (q_ref, og_ref), sems, same)
    for copy in copies:
        copy.start()
    gain = gain_ref[:, columns(same, width)]
    for i, part in enumerate(chunks_of(rows)):
        for copy in copies[2 * i:2 * i + 2]:
            copy.wait()
        for j in range(width // HEAD_DIM):
            lanes = lanes_of(j)
            q, k = q_ref[part, lanes], k_ref[part, lanes]
            size = q.shape[0]
            scores = jnp.where(lower(size), dot(q, k, 1, 1), 0.0).astype(BF16)
            turned_ref[j, part] = jnp.where(upper(size), dot(k, q, 1, 1), 0.0).astype(BF16)
            inner = dot(scores, v_ref[part, lanes])
            inner_ref[part, lanes] = inner + dot(q, pre_ref[i, j]) if i else inner
            scaled_ref[part, lanes] = gain[:, lanes] * og_ref[part, lanes].astype(F32)
            qturned_ref[lanes, part] = q.T


def attn_kernel(piece, first, last, q_ref, inner_ref, scaled_ref, state_ref, *refs):
    attn_ref = refs[0] if first else refs[2]
    for part in chunks_of(q_ref.shape[0]):
        square, cross = (None, None) if first else (refs[0][part], refs[1][part])
        for j in range(PIECE):
            lanes = lanes_of(piece * PIECE + j)
            state = state_ref[j].astype(BF16)
            attn = inner_ref[part, lanes] + dot(q_ref[part, lanes], state)
            attn_ref[part, lanes_of(j)] = attn
            more, crossed = attn * attn, scaled_ref[part, lanes] * attn
            square = more if square is None else square + more
            cross = crossed if cross is None else cross + crossed
        if last:
            square = jnp.sum(square.T, axis=0, keepdims=True)
            cross = jnp.sum(cross.T, axis=0, keepdims=True)
            row = lax.broadcasted_iota(jnp.int32, (8, square.shape[1]), 0)
            sums = jnp.where(row == 0, square, jnp.where(row == 1, cross, 0.0))
            refs[-1][:, part] = sums
        else:
            refs[-2][part] = square
            refs[-1][part] = cross


def factors_kernel(full, parts, refs):
    total = refs[0][...]
    for ref in refs[1:parts]:
        total = total + ref[...]
    inv = lax.rsqrt(total[0:1] / full + 1e-6)
    slope = inv * inv * inv * (total[1:2] / full)
    row = lax.broadcasted_iota(jnp.int32, total.shape, 0)
    both = jnp.where(row == 0, inv, slope).T
    wide = (both.shape[0], HEAD_DIM)
    return jnp.broadcast_to(both[:, 0:1], wide), jnp.broadcast_to(both[:, 1:2], wide)


def grad_kernel(piece, full, parts, *refs):
    if parts:
        inv, slope = factors_kernel(full, parts, refs)
        refs[-2][...] = inv
        refs[-1][...] = slope
        inv_ref, slope_ref = refs[-2:]
        attn_ref, scaled_ref, qturned_ref, g_ref, post_ref, sum_ref = refs[parts:-2]
    else:
        inv_ref, slope_ref, attn_ref, scaled_ref, qturned_ref, g_ref, post_ref, sum_ref = refs
    totals = [None] * PIECE
    for i, part in reversed(list(enumerate(chunks_of(g_ref.shape[0])))):
        for j in range(PIECE):
            lanes = lanes_of(piece * PIECE + j)
            attn = attn_ref[part, lanes_of(j)]
            grad = inv_ref[part] * scaled_ref[part, lanes] - attn * slope_ref[part]
            grad = grad.astype(BF16)
            g_ref[part, lanes_of(j)] = grad
            term = dot(qturned_ref[lanes, part], grad)
            if totals[j] is None:
                post_ref[i, j] = jnp.zeros_like(post_ref[i, j])
                totals[j] = term
            else:
                post_ref[i, j] = totals[j].astype(BF16)
                totals[j] = totals[j] + term
    for j in range(PIECE):
        sum_ref[j] = totals[j]


def local_kernel(pieces, second, q_ref, k_ref, v_ref, turned_ref, pre_ref, *refs):
    if second:
        qgrad_hbm, tail_ref, kpart_ref, vpart_ref, qgrad_ref, sems = refs[-6:]
        first_ref = refs[3 * pieces]
    else:
        qgrad_ref, kpart_ref, vpart_ref = refs[-3:]
    state = heads_in(refs[:pieces])
    g_refs, post_refs = refs[pieces:2 * pieces], refs[2 * pieces:3 * pieces]
    rows, width = q_ref.shape
    parts = chunks_of(rows)
    copies = []

    def send(source, lanes, part):
        copies.append(pltpu.make_async_copy(source, qgrad_hbm.at[part, lanes], sems.at[len(copies)]))
        copies[-1].start()

    if second:
        send(first_ref, columns(False, width), slice(0, rows))

    def scores(i, j):
        part, lanes = parts[i], lanes_of(j)
        v, g = v_ref[part, lanes], g_refs[j // PIECE][part, lanes_of(j % PIECE)]
        size = g.shape[0]
        gscores = jnp.where(lower(size), dot(g, v, 1, 1), 0.0).astype(BF16)
        gturned = jnp.where(upper(size), dot(v, g, 1, 1), 0.0).astype(BF16)
        return gscores, gturned

    def products(i, j, gscores, gturned):
        part, lanes = parts[i], lanes_of(j)
        q, k, v = (ref[part, lanes] for ref in (q_ref, k_ref, v_ref))
        g = g_refs[j // PIECE][part, lanes_of(j % PIECE)]
        before = state[j] + pre_ref[i, j].astype(F32) if i else state[j]
        qgrad = dot(g, before.astype(BF16), 1, 1) + dot(gscores, k)
        kgrad = dot(gturned, q)
        vgrad = dot(turned_ref[j, part], g)
        if i < len(parts) - 1:
            post = post_refs[j // PIECE][i, j % PIECE]
            kgrad = kgrad + dot(v, post, 1, 1)
            vgrad = vgrad + dot(k, post)
        if second and i == len(parts) - 1:
            tail_ref[:, lanes] = qgrad.astype(BF16)
        else:
            qgrad_ref[part, lanes] = qgrad.astype(BF16)
        kpart_ref[part, lanes] = kgrad
        vpart_ref[part, lanes] = vgrad

    places = [(i, j) for i in range(len(parts)) for j in range(width // HEAD_DIM)]
    ready = scores(*places[0])
    for place, following in zip(places, places[1:] + [None]):
        coming = scores(*following) if following else None
        products(*place, *ready)
        ready = coming
        if second and following and following[0] != place[0]:
            part = parts[place[0]]
            send(qgrad_ref.at[part], columns(True, width), part)
    for copy in copies:
        copy.wait()


def final_part(piece, part, k_ref, v_ref, kpart_ref, vpart_ref, state_ref, kgrad_ref, vgrad_ref):
    for j in range(PIECE):
        lanes = lanes_of(piece * PIECE + j)
        state = state_ref[j].astype(BF16)
        kgrad = kpart_ref[part, lanes] + dot(v_ref[part, lanes], state, 1, 1)
        vgrad = vpart_ref[part, lanes] + dot(k_ref[part, lanes], state)
        kgrad_ref[part, lanes_of(j)] = kgrad.astype(BF16)
        vgrad_ref[part, lanes_of(j)] = vgrad.astype(BF16)


def final_kernel(piece, *refs):
    for part in chunks_of(refs[0].shape[0]):
        final_part(piece, part, *refs)


def last_kernel(count, *refs):
    qgrad_hbm, kgrad_hbm, vgrad_hbm, kgrad_ref, vgrad_ref, sems = refs[-6:]
    near, far, tail_ref = refs[5:5 + 2 * count], refs[5 + 2 * count:3 + 4 * count], refs[3 + 4 * count]
    rows, width = refs[0].shape
    everything, copies = slice(0, rows), []

    def send(source, out, part, lanes):
        copies.append(pltpu.make_async_copy(source, out.at[part, lanes], sems.at[len(copies)]))
        copies[-1].start()

    for same, done in ((False, near), (True, far)):
        for i, source in enumerate(done):
            out = vgrad_hbm if i % 2 else kgrad_hbm
            send(source, out, everything, columns(same, width, i // 2))
    send(tail_ref, qgrad_hbm, chunks_of(rows)[-1], columns(True, width))
    for part in chunks_of(rows):
        final_part(count - 1, part, *refs[:5], kgrad_ref, vgrad_ref)
        lanes = columns(True, width, count - 1)
        send(kgrad_ref.at[part], kgrad_hbm, part, lanes)
        send(vgrad_ref.at[part], vgrad_hbm, part, lanes)
    for copy in copies:
        copy.wait()


def scan_plan(count):
    bits = count.bit_length() - 1
    stages = []
    for stage in range(bits - 1):
        rising, falling = 1 + stage, bits - 1 - stage
        pairs = [(r, r ^ (1 << (falling if r & 1 else rising))) for r in range(count)]
        stages.append((rising, falling, pairs))
    return stages


def join_kernel(backward, done, final, *refs):
    count = lax.axis_size("seq")
    rank = lax.axis_index("seq")
    if backward:
        rank = count - 1 - rank
    odd = (rank & 1) == 1
    plan = scan_plan(count)
    keep, extra = (ref[...] for ref in refs[:2])
    came = refs[2:2 + done]
    total = keep + extra
    before = jnp.zeros_like(total)
    for (rising, falling, _), ref in zip(plan, came):
        high = (jnp.where(odd, rank >> falling, rank >> rising) & 1) == 1
        value = ref[...]
        before = before + jnp.where(odd | high, value, 0.0)
        total = total + jnp.where(odd, 0.0, value)
    if final:
        message_ref, state_ref = refs[-2:]
        message_ref[...] = before + jnp.where(odd, 0.0, keep)
        state_ref[...] = before + jnp.where(odd, extra, 0.0)
    else:
        rising, falling, _ = plan[done]
        high = (jnp.where(odd, rank >> falling, rank >> rising) & 1) == 1
        refs[-1][...] = jnp.where(odd, before + jnp.where(high, 0.0, total), total)


def join(backward, keep, extra, came, final, after):
    like = shape(keep.shape, F32)
    return run(
        functools.partial(join_kernel, backward, len(came), final), 4 * like.size,
        [VMEM] * (2 + len(came)) + [ANYWHERE] * len(after),
        [VMEM, VMEM] if final else VMEM,
        [like, like] if final else like,
        (keep, extra, *came, *after),
    )


def scan_states(keeps, extras, backward, beside, between):
    plan = scan_plan(lax.axis_size("seq"))
    came = [[] for _ in keeps]
    results, after = [], []
    for stage, (_, _, pairs) in enumerate(plan):
        messages = []
        for keep, extra, arrived in zip(keeps, extras, came):
            message = join(backward, keep, extra, arrived, False, after + messages)
            messages.append(message)
            arrived.append(move(message, pairs, backward))
        mine = beside[stage:] if stage == len(plan) - 1 else beside[stage:stage + 1]
        made = [work(messages) for work in mine]
        after = [item[-1] for item in made]
        results += made
    states, messages, early = [], [], ()
    for keep, extra, arrived in zip(keeps, extras, came):
        token = [*after, *messages, *early[-1:]]
        message, state = join(backward, keep, extra, arrived, True, token)
        states.append(state)
        messages.append(message)
        early = early or between(state, results)
    others = [nearby(message, backward) for message in messages[::-1]][::-1]
    return states, others, results, early


def move(value, pairs, backward):
    count = lax.axis_size("seq")
    if backward:
        pairs = [(count - 1 - a, count - 1 - b) for a, b in pairs]
    return lax.ppermute(value, "seq", pairs)


def nearby(value, backward):
    return move(value, [(r, r ^ 1) for r in range(lax.axis_size("seq"))], backward)


def shards(query, key_in, value, out_grad, gain):
    rows, width = query.shape
    half = width // 2
    heads = half // HEAD_DIM
    chunks = len(chunks_of(rows))
    peers = lax.axis_size("head")
    full = width * peers
    gain = gain.reshape(1, width)
    pin = lambda x: pltpu.with_memory_space_constraint(x, pltpu.HBM)
    query, key_in, value, out_grad = (pin(x) for x in (query, key_in, value, out_grad))
    unit = 2 * rows * half * HEAD_DIM
    partial = functools.partial

    count = heads // PIECE
    states = shape((PIECE, HEAD_DIM, HEAD_DIM), F32)
    inside = shape((chunks, heads, HEAD_DIM, HEAD_DIM), BF16)
    wide = shape((rows, half), F32)
    thin = shape((rows, half), BF16)
    lane_sums = shape((rows, HEAD_DIM), F32)
    whole = shape((rows, width), BF16)
    sems = pltpu.SemaphoreType.DMA((2 * chunks,))

    k1, v1, k2, v2, pre1, *sends = run(
        first_kernel, unit, [HBM, HBM], [VMEM] * (5 + count), [thin] * 4 + [inside] + [states] * count,
        (key_in, value), [sems, sems],
    )
    extras = [nearby(send, False) for send in sends]
    pre2, *keeps = run(
        sum_states, unit, [VMEM, VMEM], [VMEM] * (1 + count), [inside] + [states] * count, (k2, v2)
    )

    def inner_of(same, k, v, pre):
        return lambda messages: run(
            partial(inner_kernel, same), 6 * unit,
            [HBM, HBM, VMEM, VMEM, VMEM, VMEM] + [ANYWHERE] * len(messages), [VMEM] * 5,
            [
                thin, wide, wide,
                shape((half, rows), BF16), shape((heads, rows, rows // chunks), BF16),
            ],
            (query, out_grad, k, v, gain, pre, *messages),
            [pltpu.VMEM((rows, half), BF16), sems],
        )

    piece_wide = shape((rows, PIECE * HEAD_DIM), F32)

    def attn_of(number, inner, state, sums):
        last = number == 2 * count - 1
        return run(
            partial(attn_kernel, number % count, number == 0, last), unit // count,
            [VMEM] * (4 + len(sums)), [VMEM] * (2 if last else 3),
            [piece_wide] + ([shape((8, rows), F32)] if last else [lane_sums] * 2),
            (*inner, state, *sums),
        )

    state2, state1, made, early = scan_states(
        keeps, extras, False,
        [inner_of(True, k2, v2, pre2), inner_of(False, k1, v1, pre1)],
        lambda state, made: attn_of(0, made[0][:3], state, ()),
    )
    (q2, inner2, scaled2, qturned2, turned2), (q1, inner1, scaled1, qturned1, turned1) = made

    attn, *sums = early
    attns = [attn]
    for number, state in list(enumerate([*state2, *state1]))[1:]:
        inner = (q2, inner2, scaled2) if number < count else (q1, inner1, scaled1)
        attn, *sums = attn_of(number, inner, state, sums)
        attns.append(attn)
    sums = sums[0]
    parts = [sums] + [
        lax.ppermute(sums, "head", [(r, r ^ other) for r in range(peers)])
        for other in [*range(2, peers), 1][:peers - 1]
    ]

    factors = []

    def grads_of(attns, scaled, qturned):
        made = []
        for piece, attn in enumerate(attns):
            peers_in = 0 if factors else len(parts)
            first = factors or parts
            g, post, total, *more = run(
                partial(grad_kernel, piece, full, peers_in), unit // count,
                [VMEM] * (len(first) + 3), [VMEM] * (3 if factors else 5),
                [shape((rows, PIECE * HEAD_DIM), BF16), posts, states]
                + ([] if factors else [lane_sums] * 2),
                (*first, attn, scaled, qturned),
            )
            factors.extend(more)
            made.append((g, post, total))
        return zip(*made)

    posts = shape((chunks, PIECE, HEAD_DIM, HEAD_DIM), BF16)
    gs2, posts2, gsends = grads_of(attns[:count], scaled2, qturned2)
    gextras = [nearby(gsend, True) for gsend in gsends]
    gs1, posts1, gkeeps = grads_of(attns[count:], scaled1, qturned1)

    def local_of(second, *args):
        def work(messages):
            more = (*first_grads, *messages)
            outs = [VMEM] * 3, [thin, wide, wide], ()
            if second:
                tail = shape((rows // chunks, half), BF16)
                outs = (
                    [HBM] + [VMEM] * 3, [whole, tail, wide, wide],
                    [pltpu.VMEM((rows, half), BF16), sems],
                )
            qgrad, *others = run(
                partial(local_kernel, count, second), 9 * unit,
                [VMEM] * (len(args) + len(first_grads)) + [ANYWHERE] * len(messages), outs[0], outs[1],
                (*args, *more), outs[2],
            )
            first_grads.append(qgrad)
            return (qgrad, *others)

        return work

    piece_thin = shape((rows, PIECE * HEAD_DIM), BF16)

    def final_of(piece, args, state):
        return run(
            partial(final_kernel, piece), 2 * unit // count, [VMEM] * 5, [VMEM] * 2,
            [piece_thin] * 2, (*args, state),
        )

    first_grads = []
    gstate1, gstate2, made, early = scan_states(
        gkeeps, gextras, True,
        [
            local_of(False, q1, k1, v1, turned1, pre1, *state1, *gs1, *posts1),
            local_of(True, q2, k2, v2, turned2, pre2, *state2, *gs2, *posts2),
        ],
        lambda state, made: final_of(0, (k1, v1, *made[0][1:]), state),
    )
    (_, kpart1, vpart1), (qgrad, tail, kpart2, vpart2) = made

    done = list(early)
    for piece in range(1, count):
        done += final_of(piece, (k1, v1, kpart1, vpart1), gstate1[piece])
    for piece in range(count - 1):
        done += final_of(piece, (k2, v2, kpart2, vpart2), gstate2[piece])
    args = (k2, v2, kpart2, vpart2, gstate2[-1], *done, tail)
    qgrad, kgrad, vgrad = run(
        partial(last_kernel, count), 2 * unit // count, [VMEM] * len(args) + [HBM],
        [HBM] * 3, [whole] * 3, (*args, qgrad),
        [pltpu.VMEM(piece_thin.shape, BF16)] * 2
        + [pltpu.SemaphoreType.DMA((2 * (chunks + 2 * count - 1) + 1,))],
        {len(args): 0},
    )
    return qgrad, kgrad, vgrad


def solution(mesh):
    spec = P("seq", "head")
    return jax.shard_map(
        shards,
        mesh=mesh,
        in_specs=(spec, spec, spec, spec, P("head")),
        out_specs=(spec, spec, spec),
        check_vma=False,
    )
```

```python
import functools

import jax
import jax.numpy as jnp
from jax import lax
from jax.experimental import pallas as pl
from jax.experimental.pallas import tpu as pltpu
from jax.sharding import PartitionSpec as P

HEAD_DIM = 128
CHUNK = 256
PIECE = 2
VMEM_BYTES = 12 * 2**20
F32 = jnp.float32
BF16 = jnp.bfloat16
VMEM = pl.BlockSpec(memory_space=pltpu.VMEM)
HBM = pl.BlockSpec(memory_space=pltpu.HBM)
ANYWHERE = pl.BlockSpec(memory_space=pl.ANY)


def dot(a, b, contract_a=1, contract_b=0):
    dims = (((contract_a,), (contract_b,)), ((), ()))
    return lax.dot_general(a, b, dims, preferred_element_type=F32)


def chunks_of(rows):
    size = CHUNK if rows % CHUNK == 0 else rows
    return [slice(i, i + size) for i in range(0, rows, size)]


def shape(dims, dtype):
    return jax.ShapeDtypeStruct(dims, dtype)


def lanes_of(j):
    return slice(j * HEAD_DIM, (j + 1) * HEAD_DIM)


def heads_in(pieces):
    return [ref[j] for ref in pieces for j in range(ref.shape[0])]


def lower(size):
    row = lax.broadcasted_iota(jnp.int32, (size, size), 0)
    return row >= lax.broadcasted_iota(jnp.int32, (size, size), 1)


def upper(size):
    row = lax.broadcasted_iota(jnp.int32, (size, size), 0)
    return row <= lax.broadcasted_iota(jnp.int32, (size, size), 1)


def run(kernel, flops, in_specs, out_specs, out_shape, args, scratch=(), aliases=None):
    nbytes = sum(a.size * a.dtype.itemsize for a, spec in zip(args, in_specs) if spec is HBM)
    return pl.pallas_call(
        kernel,
        in_specs=in_specs,
        out_specs=out_specs,
        out_shape=out_shape,
        scratch_shapes=list(scratch),
        input_output_aliases=aliases or {},
        cost_estimate=pl.CostEstimate(flops=flops, bytes_accessed=nbytes, transcendentals=0),
        compiler_params=pltpu.CompilerParams(vmem_limit_bytes=VMEM_BYTES),
    )(*args)


def columns(same, width, piece=None):
    odd = lax.rem(lax.axis_index("seq"), 2)
    half = odd if same else 1 - odd
    if piece is None:
        return pl.ds(pl.multiple_of(half * width, width), width)
    size = PIECE * HEAD_DIM
    return pl.ds(pl.multiple_of(half * width + piece * size, size), size)


def fetches(sources, targets, sems, same):
    rows, width = targets[0].shape
    lanes = columns(same, width)
    copies = []
    for part in chunks_of(rows):
        for source, target in zip(sources, targets):
            sem = sems.at[len(copies)]
            copies.append(pltpu.make_async_copy(source.at[part, lanes], target.at[part], sem))
    return copies


def sum_states(k_ref, v_ref, pre_ref, *sum_refs, copies=()):
    heads = pre_ref.shape[1]
    totals = [None] * heads
    for i, part in enumerate(chunks_of(k_ref.shape[0])):
        for copy in copies[2 * i:2 * i + 2]:
            copy.wait()
        for j in range(heads):
            term = dot(k_ref[part, lanes_of(j)], v_ref[part, lanes_of(j)], 0, 0)
            if i:
                pre_ref[i, j] = totals[j].astype(BF16)
            else:
                pre_ref[i, j] = jnp.zeros_like(pre_ref[i, j])
            totals[j] = totals[j] + term if i else term
    for j in range(heads):
        sum_refs[j // PIECE][j % PIECE] = totals[j]


def first_kernel(k_hbm, v_hbm, k1, v1, k2, v2, pre_ref, *refs):
    *sum_refs, sems1, sems2 = refs
    now = fetches((k_hbm, v_hbm), (k1, v1), sems1, False)
    later = fetches((k_hbm, v_hbm), (k2, v2), sems2, True)
    for copy in now + later:
        copy.start()
    sum_states(k1, v1, pre_ref, *sum_refs, copies=now)
    for copy in later:
        copy.wait()


def inner_kernel(same, q_hbm, og_hbm, k_ref, v_ref, gain_ref, pre_ref, *refs):
    q_ref, inner_ref, scaled_ref, qturned_ref, turned_ref, og_ref, sems = refs[-7:]
    rows, width = q_ref.shape
    copies = fetches((q_hbm, og_hbm), (q_ref, og_ref), sems, same)
    for copy in copies:
        copy.start()
    gain = gain_ref[:, columns(same, width)]
    for i, part in enumerate(chunks_of(rows)):
        for copy in copies[2 * i:2 * i + 2]:
            copy.wait()
        for j in range(width // HEAD_DIM):
            lanes = lanes_of(j)
            q, k = q_ref[part, lanes], k_ref[part, lanes]
            size = q.shape[0]
            scores = jnp.where(lower(size), dot(q, k, 1, 1), 0.0).astype(BF16)
            turned_ref[j, part] = jnp.where(upper(size), dot(k, q, 1, 1), 0.0).astype(BF16)
            inner = dot(scores, v_ref[part, lanes])
            inner_ref[part, lanes] = inner + dot(q, pre_ref[i, j]) if i else inner
            scaled_ref[part, lanes] = gain[:, lanes] * og_ref[part, lanes].astype(F32)
            qturned_ref[lanes, part] = q.T


def attn_kernel(piece, first, last, q_ref, inner_ref, scaled_ref, state_ref, *refs):
    attn_ref = refs[0] if first else refs[2]
    for part in chunks_of(q_ref.shape[0]):
        square, cross = (None, None) if first else (refs[0][part], refs[1][part])
        for j in range(PIECE):
            lanes = lanes_of(piece * PIECE + j)
            state = state_ref[j].astype(BF16)
            attn = inner_ref[part, lanes] + dot(q_ref[part, lanes], state)
            attn_ref[part, lanes_of(j)] = attn
            more, crossed = attn * attn, scaled_ref[part, lanes] * attn
            square = more if square is None else square + more
            cross = crossed if cross is None else cross + crossed
        if last:
            square = jnp.sum(square.T, axis=0, keepdims=True)
            cross = jnp.sum(cross.T, axis=0, keepdims=True)
            row = lax.broadcasted_iota(jnp.int32, (8, square.shape[1]), 0)
            sums = jnp.where(row == 0, square, jnp.where(row == 1, cross, 0.0))
            refs[-1][:, part] = sums
        else:
            refs[-2][part] = square
            refs[-1][part] = cross


def factors_kernel(full, parts, refs):
    total = refs[0][...]
    for ref in refs[1:parts]:
        total = total + ref[...]
    inv = lax.rsqrt(total[0:1] / full + 1e-6)
    slope = inv * inv * inv * (total[1:2] / full)
    row = lax.broadcasted_iota(jnp.int32, total.shape, 0)
    both = jnp.where(row == 0, inv, slope).T
    wide = (both.shape[0], HEAD_DIM)
    return jnp.broadcast_to(both[:, 0:1], wide), jnp.broadcast_to(both[:, 1:2], wide)


def grad_kernel(pieces, full, parts, *refs):
    if parts:
        inv, slope = factors_kernel(full, parts, refs)
        refs[-2][...] = inv
        refs[-1][...] = slope
        inv_ref, slope_ref = refs[-2:]
        refs = refs[parts:-2]
    else:
        inv_ref, slope_ref = refs[:2]
        refs = refs[2:]
    scaled_ref, qturned_ref = refs[:2]
    count = len(pieces)
    attns, outs = refs[2:2 + count], refs[2 + count:]
    for attn_ref, piece, at in zip(attns, pieces, range(0, 3 * count, 3)):
        g_ref, post_ref, sum_ref = outs[at:at + 3]
        totals = [None] * PIECE
        for i, part in reversed(list(enumerate(chunks_of(g_ref.shape[0])))):
            for j in range(PIECE):
                lanes = lanes_of(piece * PIECE + j)
                attn = attn_ref[part, lanes_of(j)]
                grad = inv_ref[part] * scaled_ref[part, lanes] - attn * slope_ref[part]
                grad = grad.astype(BF16)
                g_ref[part, lanes_of(j)] = grad
                term = dot(qturned_ref[lanes, part], grad)
                if totals[j] is None:
                    post_ref[i, j] = jnp.zeros_like(post_ref[i, j])
                    totals[j] = term
                else:
                    post_ref[i, j] = totals[j].astype(BF16)
                    totals[j] = totals[j] + term
        for j in range(PIECE):
            sum_ref[j] = totals[j]


def local_kernel(pieces, second, q_ref, k_ref, v_ref, turned_ref, pre_ref, *refs):
    if second:
        qgrad_hbm, qgrad_ref, kpart_ref, vpart_ref, sem = refs[-5:]
    else:
        qgrad_ref, kpart_ref, vpart_ref = refs[-3:]
    state = heads_in(refs[:pieces])
    g_refs, post_refs = refs[pieces:2 * pieces], refs[2 * pieces:3 * pieces]
    rows, width = q_ref.shape
    parts = chunks_of(rows)
    if second:
        target = qgrad_hbm.at[slice(0, rows), columns(False, width)]
        copy = pltpu.make_async_copy(refs[3 * pieces], target, sem)
        copy.start()

    def scores(i, j):
        part, lanes = parts[i], lanes_of(j)
        v, g = v_ref[part, lanes], g_refs[j // PIECE][part, lanes_of(j % PIECE)]
        size = g.shape[0]
        gscores = jnp.where(lower(size), dot(g, v, 1, 1), 0.0).astype(BF16)
        gturned = jnp.where(upper(size), dot(v, g, 1, 1), 0.0).astype(BF16)
        return gscores, gturned

    def products(i, j, gscores, gturned):
        part, lanes = parts[i], lanes_of(j)
        q, k, v = (ref[part, lanes] for ref in (q_ref, k_ref, v_ref))
        g = g_refs[j // PIECE][part, lanes_of(j % PIECE)]
        before = state[j] + pre_ref[i, j].astype(F32) if i else state[j]
        qgrad = dot(g, before.astype(BF16), 1, 1) + dot(gscores, k)
        kgrad = dot(gturned, q)
        vgrad = dot(turned_ref[j, part], g)
        if i < len(parts) - 1:
            post = post_refs[j // PIECE][i, j % PIECE]
            kgrad = kgrad + dot(v, post, 1, 1)
            vgrad = vgrad + dot(k, post)
        qgrad_ref[part, lanes] = qgrad.astype(BF16)
        kpart_ref[part, lanes] = kgrad
        vpart_ref[part, lanes] = vgrad

    places = [(i, j) for i in range(len(parts)) for j in range(width // HEAD_DIM)]
    ready = scores(*places[0])
    for place, following in zip(places, places[1:] + [None]):
        coming = scores(*following) if following else None
        products(*place, *ready)
        ready = coming
    if second:
        copy.wait()


def final_part(piece, part, k_ref, v_ref, kpart_ref, vpart_ref, state_ref, kgrad_ref, vgrad_ref):
    for j in range(PIECE):
        lanes = lanes_of(piece * PIECE + j)
        state = state_ref[j].astype(BF16)
        kgrad = kpart_ref[part, lanes] + dot(v_ref[part, lanes], state, 1, 1)
        vgrad = vpart_ref[part, lanes] + dot(k_ref[part, lanes], state)
        kgrad_ref[part, lanes_of(j)] = kgrad.astype(BF16)
        vgrad_ref[part, lanes_of(j)] = vgrad.astype(BF16)


def final_kernel(piece, own, wholes, plan, *refs):
    sources = refs[5:5 + len(plan)]
    *outs, kgrad_ref, vgrad_ref, sems = refs[5 + len(plan):]
    outs = outs[len(outs) - wholes:]
    rows, copies = refs[0].shape[0], []

    def send(source, out, part, place):
        target = outs[out].at[part, columns(*place)]
        copies.append(pltpu.make_async_copy(source, target, sems.at[len(copies)]))
        copies[-1].start()

    for source, (out, place) in zip(sources, plan):
        send(source, out, slice(0, rows), place)
    for part in chunks_of(rows):
        final_part(piece, part, *refs[:5], kgrad_ref, vgrad_ref)
        if own:
            send(kgrad_ref.at[part], 0, part, own)
            send(vgrad_ref.at[part], 1, part, own)
    for copy in copies:
        copy.wait()


def scan_plan(count):
    bits = count.bit_length() - 1
    stages = []
    for stage in range(bits - 1):
        rising, falling = 1 + stage, bits - 1 - stage
        pairs = [(r, r ^ (1 << (falling if r & 1 else rising))) for r in range(count)]
        stages.append((rising, falling, pairs))
    return stages


def join_kernel(backward, done, final, *refs):
    count = lax.axis_size("seq")
    rank = lax.axis_index("seq")
    if backward:
        rank = count - 1 - rank
    odd = (rank & 1) == 1
    plan = scan_plan(count)
    keep, extra = (ref[...] for ref in refs[:2])
    came = refs[2:2 + done]
    total = keep + extra
    before = jnp.zeros_like(total)
    for (rising, falling, _), ref in zip(plan, came):
        high = (jnp.where(odd, rank >> falling, rank >> rising) & 1) == 1
        value = ref[...]
        before = before + jnp.where(odd | high, value, 0.0)
        total = total + jnp.where(odd, 0.0, value)
    if final:
        message_ref, state_ref = refs[-2:]
        message_ref[...] = before + jnp.where(odd, 0.0, keep)
        state_ref[...] = before + jnp.where(odd, extra, 0.0)
    else:
        rising, falling, _ = plan[done]
        high = (jnp.where(odd, rank >> falling, rank >> rising) & 1) == 1
        refs[-1][...] = jnp.where(odd, before + jnp.where(high, 0.0, total), total)


def join(backward, keep, extra, came, final, after):
    like = shape(keep.shape, F32)
    return run(
        functools.partial(join_kernel, backward, len(came), final), 4 * like.size,
        [VMEM] * (2 + len(came)) + [ANYWHERE] * len(after),
        [VMEM, VMEM] if final else VMEM,
        [like, like] if final else like,
        (keep, extra, *came, *after),
    )


def scan_states(keeps, extras, backward, beside, between):
    plan = scan_plan(lax.axis_size("seq"))
    came = [[] for _ in keeps]
    results, after = [], []
    for stage, (_, _, pairs) in enumerate(plan):
        messages = []
        for keep, extra, arrived in zip(keeps, extras, came):
            message = join(backward, keep, extra, arrived, False, after + messages)
            messages.append(message)
            arrived.append(move(message, pairs, backward))
        mine = beside[stage:] if stage == len(plan) - 1 else beside[stage:stage + 1]
        made = [work(messages) for work in mine]
        after = [item[-1] for item in made]
        results += made
    states, messages, early = [], [], ()
    for keep, extra, arrived in zip(keeps, extras, came):
        token = [*after, *messages, *early[-1:]]
        message, state = join(backward, keep, extra, arrived, True, token)
        states.append(state)
        messages.append(message)
        early = early or between(state, results)
    others = [nearby(message, backward) for message in messages[::-1]][::-1]
    return states, others, results, early


def move(value, pairs, backward):
    count = lax.axis_size("seq")
    if backward:
        pairs = [(count - 1 - a, count - 1 - b) for a, b in pairs]
    return lax.ppermute(value, "seq", pairs)


def nearby(value, backward):
    return move(value, [(r, r ^ 1) for r in range(lax.axis_size("seq"))], backward)


def shards(query, key_in, value, out_grad, gain):
    rows, width = query.shape
    half = width // 2
    heads = half // HEAD_DIM
    chunks = len(chunks_of(rows))
    peers = lax.axis_size("head")
    full = width * peers
    gain = gain.reshape(1, width)
    pin = lambda x: pltpu.with_memory_space_constraint(x, pltpu.HBM)
    query, key_in, value, out_grad = (pin(x) for x in (query, key_in, value, out_grad))
    unit = 2 * rows * half * HEAD_DIM
    partial = functools.partial

    count = heads // PIECE
    states = shape((PIECE, HEAD_DIM, HEAD_DIM), F32)
    inside = shape((chunks, heads, HEAD_DIM, HEAD_DIM), BF16)
    wide = shape((rows, half), F32)
    thin = shape((rows, half), BF16)
    lane_sums = shape((rows, HEAD_DIM), F32)
    whole = shape((rows, width), BF16)
    sems = pltpu.SemaphoreType.DMA((2 * chunks,))

    k1, v1, k2, v2, pre1, *sends = run(
        first_kernel, unit, [HBM, HBM], [VMEM] * (5 + count), [thin] * 4 + [inside] + [states] * count,
        (key_in, value), [sems, sems],
    )
    extras = [nearby(send, False) for send in sends]
    pre2, *keeps = run(
        sum_states, unit, [VMEM, VMEM], [VMEM] * (1 + count), [inside] + [states] * count, (k2, v2)
    )

    def inner_of(same, k, v, pre):
        return lambda messages: run(
            partial(inner_kernel, same), 6 * unit,
            [HBM, HBM, VMEM, VMEM, VMEM, VMEM] + [ANYWHERE] * len(messages), [VMEM] * 5,
            [
                thin, wide, wide,
                shape((half, rows), BF16), shape((heads, rows, rows // chunks), BF16),
            ],
            (query, out_grad, k, v, gain, pre, *messages),
            [pltpu.VMEM((rows, half), BF16), sems],
        )

    piece_wide = shape((rows, PIECE * HEAD_DIM), F32)

    def attn_of(number, inner, state, sums):
        last = number == 2 * count - 1
        return run(
            partial(attn_kernel, number % count, number == 0, last), unit // count,
            [VMEM] * (4 + len(sums)), [VMEM] * (2 if last else 3),
            [piece_wide] + ([shape((8, rows), F32)] if last else [lane_sums] * 2),
            (*inner, state, *sums),
        )

    state2, state1, made, early = scan_states(
        keeps, extras, False,
        [inner_of(True, k2, v2, pre2), inner_of(False, k1, v1, pre1)],
        lambda state, made: attn_of(0, made[0][:3], state, ()),
    )
    (q2, inner2, scaled2, qturned2, turned2), (q1, inner1, scaled1, qturned1, turned1) = made

    attn, *sums = early
    attns = [attn]
    for number, state in list(enumerate([*state2, *state1]))[1:]:
        inner = (q2, inner2, scaled2) if number < count else (q1, inner1, scaled1)
        attn, *sums = attn_of(number, inner, state, sums)
        attns.append(attn)
    sums = sums[0]
    parts = [sums] + [
        lax.ppermute(sums, "head", [(r, r ^ other) for r in range(peers)])
        for other in range(1, peers)
    ]

    posts = shape((chunks, PIECE, HEAD_DIM, HEAD_DIM), BF16)
    piece_out = [shape((rows, PIECE * HEAD_DIM), BF16), posts, states]

    def grads_of(pieces, first, attns, scaled, qturned):
        fresh = len(first) if first is parts else 0
        shapes = piece_out * len(pieces) + [lane_sums] * (2 if fresh else 0)
        made = run(
            partial(grad_kernel, pieces, full, fresh), unit * len(pieces) // count,
            [VMEM] * (len(first) + 2 + len(pieces)), [VMEM] * len(shapes), shapes,
            (*first, scaled, qturned, *attns),
        )
        return [made[i:i + 3] for i in range(0, 3 * len(pieces), 3)], made[3 * len(pieces):]

    made, factors = grads_of([0], parts, attns[:1], scaled2, qturned2)
    for piece in range(1, count):
        made += grads_of([piece], factors, attns[piece:piece + 1], scaled2, qturned2)[0]
    gs2, posts2, gsends = zip(*made)
    gextras = [nearby(gsend, True) for gsend in gsends]
    made = grads_of(list(range(count)), factors, attns[count:], scaled1, qturned1)[0]
    gs1, posts1, gkeeps = zip(*made)

    first_grads = []

    def local_of(second, *args):
        def work(messages):
            made = run(
                partial(local_kernel, count, second), 9 * unit,
                [VMEM] * (len(args) + len(first_grads)) + [ANYWHERE] * len(messages),
                [HBM] * second + [VMEM] * 3, [whole] * second + [thin, wide, wide],
                (*args, *first_grads, *messages), [pltpu.SemaphoreType.DMA(())] * second,
            )
            first_grads.append(made[0])
            return made

        return work

    piece_thin = shape((rows, PIECE * HEAD_DIM), BF16)

    def final_of(piece, args, state, ready=(), outs=(), fresh=0, own=None):
        sources = [source for source, _, _ in ready]
        plan = [(out, place) for _, out, place in ready]
        args = (*args, state, *sources)
        wholes = len(outs) + fresh
        last = [pltpu.VMEM(piece_thin.shape, BF16)] * 2 if own else []
        return run(
            partial(final_kernel, piece, own, wholes, plan), 2 * unit // count,
            [VMEM] * len(args) + [HBM] * len(outs),
            [HBM] * wholes + ([] if own else [VMEM] * 2),
            [whole] * wholes + ([] if own else [piece_thin] * 2), (*args, *outs),
            last + [pltpu.SemaphoreType.DMA((len(plan) + 2 * chunks,))],
            {len(args) + i: i for i in range(len(outs))},
        )

    gstate1, gstate2, made, early = scan_states(
        gkeeps, gextras, True,
        [
            local_of(0, q1, k1, v1, turned1, pre1, *state1, *gs1, *posts1),
            local_of(1, q2, k2, v2, turned2, pre2, *state2, *gs2, *posts2),
        ],
        lambda state, made: final_of(
            0, (k1, v1, *made[0][1:]), state, [(made[1][1], 0, (True, half))], made[1][:1]
        ),
    )
    near = (k1, v1, *made[0][1:])
    far = (k2, v2, *made[1][2:])
    qgrad, *done = early
    for piece in range(1, count):
        done += final_of(piece, near, gstate1[piece])
    ready = [(array, i % 2, (False, half, i // 2)) for i, array in enumerate(done)]
    outs, done = [], []
    for piece in range(count - 1):
        *outs, kdone, vdone = final_of(
            piece, far, gstate2[piece], ready, outs, 0 if outs else 2
        )
        ready = [(kdone, 0, (True, half, piece)), (vdone, 1, (True, half, piece))]
    kgrad, vgrad = final_of(
        count - 1, far, gstate2[-1], ready, outs, 0 if outs else 2, (True, half, count - 1)
    )
    return qgrad, kgrad, vgrad


def solution(mesh):
    spec = P("seq", "head")
    return jax.shard_map(
        shards,
        mesh=mesh,
        in_specs=(spec, spec, spec, spec, P("head")),
        out_specs=(spec, spec, spec),
        check_vma=False,
    )
```

```python
import functools

import jax
import jax.numpy as jnp
from jax import lax
from jax.experimental import pallas as pl
from jax.experimental.pallas import tpu as pltpu
from jax.sharding import PartitionSpec as P

HEAD_DIM = 128
CHUNK = 256
PIECE = 2
VMEM_BYTES = 12 * 2**20
F32 = jnp.float32
BF16 = jnp.bfloat16
VMEM = pl.BlockSpec(memory_space=pltpu.VMEM)
HBM = pl.BlockSpec(memory_space=pltpu.HBM)
ANYWHERE = pl.BlockSpec(memory_space=pl.ANY)


def dot(a, b, contract_a=1, contract_b=0):
    dims = (((contract_a,), (contract_b,)), ((), ()))
    return lax.dot_general(a, b, dims, preferred_element_type=F32)


def chunks_of(rows):
    size = CHUNK if rows % CHUNK == 0 else rows
    return [slice(i, i + size) for i in range(0, rows, size)]


def shape(dims, dtype):
    return jax.ShapeDtypeStruct(dims, dtype)


def lanes_of(j):
    return slice(j * HEAD_DIM, (j + 1) * HEAD_DIM)


def heads_in(pieces):
    return [ref[j] for ref in pieces for j in range(ref.shape[0])]


def lower(size):
    row = lax.broadcasted_iota(jnp.int32, (size, size), 0)
    return row >= lax.broadcasted_iota(jnp.int32, (size, size), 1)


def upper(size):
    row = lax.broadcasted_iota(jnp.int32, (size, size), 0)
    return row <= lax.broadcasted_iota(jnp.int32, (size, size), 1)


def run(kernel, flops, in_specs, out_specs, out_shape, args, scratch=(), aliases=None):
    nbytes = sum(a.size * a.dtype.itemsize for a, spec in zip(args, in_specs) if spec is HBM)
    return pl.pallas_call(
        kernel,
        in_specs=in_specs,
        out_specs=out_specs,
        out_shape=out_shape,
        scratch_shapes=list(scratch),
        input_output_aliases=aliases or {},
        cost_estimate=pl.CostEstimate(flops=flops, bytes_accessed=nbytes, transcendentals=0),
        compiler_params=pltpu.CompilerParams(vmem_limit_bytes=VMEM_BYTES),
    )(*args)


def columns(same, width, piece=None):
    odd = lax.rem(lax.axis_index("seq"), 2)
    half = odd if same else 1 - odd
    if piece is None:
        return pl.ds(pl.multiple_of(half * width, width), width)
    size = PIECE * HEAD_DIM
    return pl.ds(pl.multiple_of(half * width + piece * size, size), size)


def fetches(sources, targets, sems, same):
    rows, width = targets[0].shape
    lanes = columns(same, width)
    copies = []
    for part in chunks_of(rows):
        for source, target in zip(sources, targets):
            sem = sems.at[len(copies)]
            copies.append(pltpu.make_async_copy(source.at[part, lanes], target.at[part], sem))
    return copies


def sum_states(k_ref, v_ref, pre_ref, *sum_refs, copies=()):
    heads = pre_ref.shape[1]
    totals = [None] * heads
    for i, part in enumerate(chunks_of(k_ref.shape[0])):
        for copy in copies[2 * i:2 * i + 2]:
            copy.wait()
        for j in range(heads):
            term = dot(k_ref[part, lanes_of(j)], v_ref[part, lanes_of(j)], 0, 0)
            if i:
                pre_ref[i, j] = totals[j].astype(BF16)
            else:
                pre_ref[i, j] = jnp.zeros_like(pre_ref[i, j])
            totals[j] = totals[j] + term if i else term
    for j in range(heads):
        sum_refs[j // PIECE][j % PIECE] = totals[j]


def first_kernel(k_hbm, v_hbm, k1, v1, k2, v2, pre_ref, *refs):
    *sum_refs, sems1, sems2 = refs
    now = fetches((k_hbm, v_hbm), (k1, v1), sems1, False)
    later = fetches((k_hbm, v_hbm), (k2, v2), sems2, True)
    for copy in now + later:
        copy.start()
    sum_states(k1, v1, pre_ref, *sum_refs, copies=now)
    for copy in later:
        copy.wait()


def inner_kernel(same, q_hbm, og_hbm, k_ref, v_ref, gain_ref, pre_ref, *refs):
    q_ref, inner_ref, scaled_ref, qturned_ref, turned_ref, og_ref, sems = refs[-7:]
    rows, width = q_ref.shape
    copies = fetches((q_hbm, og_hbm), (q_ref, og_ref), sems, same)
    for copy in copies:
        copy.start()
    gain = gain_ref[:, columns(same, width)]
    for i, part in enumerate(chunks_of(rows)):
        for copy in copies[2 * i:2 * i + 2]:
            copy.wait()
        for j in range(width // HEAD_DIM):
            lanes = lanes_of(j)
            q, k = q_ref[part, lanes], k_ref[part, lanes]
            size = q.shape[0]
            scores = jnp.where(lower(size), dot(q, k, 1, 1), 0.0).astype(BF16)
            turned_ref[j, part] = jnp.where(upper(size), dot(k, q, 1, 1), 0.0).astype(BF16)
            inner = dot(scores, v_ref[part, lanes])
            inner_ref[part, lanes] = inner + dot(q, pre_ref[i, j]) if i else inner
            scaled_ref[part, lanes] = gain[:, lanes] * og_ref[part, lanes].astype(F32)
            qturned_ref[lanes, part] = q.T


def attn_kernel(piece, first, last, q_ref, inner_ref, scaled_ref, state_ref, *refs):
    attn_ref = refs[0] if first else refs[2]
    for part in chunks_of(q_ref.shape[0]):
        square, cross = (None, None) if first else (refs[0][part], refs[1][part])
        for j in range(PIECE):
            lanes = lanes_of(piece * PIECE + j)
            state = state_ref[j].astype(BF16)
            attn = inner_ref[part, lanes] + dot(q_ref[part, lanes], state)
            attn_ref[part, lanes_of(j)] = attn
            more, crossed = attn * attn, scaled_ref[part, lanes] * attn
            square = more if square is None else square + more
            cross = crossed if cross is None else cross + crossed
        if last:
            square = jnp.sum(square.T, axis=0, keepdims=True)
            cross = jnp.sum(cross.T, axis=0, keepdims=True)
            row = lax.broadcasted_iota(jnp.int32, (8, square.shape[1]), 0)
            sums = jnp.where(row == 0, square, jnp.where(row == 1, cross, 0.0))
            refs[-1][:, part] = sums
        else:
            refs[-2][part] = square
            refs[-1][part] = cross


def factors_kernel(full, parts, refs):
    total = refs[0][...]
    for ref in refs[1:parts]:
        total = total + ref[...]
    inv = lax.rsqrt(total[0:1] / full + 1e-6)
    slope = inv * inv * inv * (total[1:2] / full)
    row = lax.broadcasted_iota(jnp.int32, total.shape, 0)
    both = jnp.where(row == 0, inv, slope).T
    wide = (both.shape[0], HEAD_DIM)
    return jnp.broadcast_to(both[:, 0:1], wide), jnp.broadcast_to(both[:, 1:2], wide)


def grad_kernel(pieces, full, parts, *refs):
    if parts:
        inv, slope = factors_kernel(full, parts, refs)
        refs[-2][...] = inv
        refs[-1][...] = slope
        inv_ref, slope_ref = refs[-2:]
        refs = refs[parts:-2]
    else:
        inv_ref, slope_ref = refs[:2]
        refs = refs[2:]
    scaled_ref, qturned_ref = refs[:2]
    count = len(pieces)
    attns, outs = refs[2:2 + count], refs[2 + count:]
    for attn_ref, piece, at in zip(attns, pieces, range(0, 3 * count, 3)):
        g_ref, post_ref, sum_ref = outs[at:at + 3]
        totals = [None] * PIECE
        for i, part in reversed(list(enumerate(chunks_of(g_ref.shape[0])))):
            for j in range(PIECE):
                lanes = lanes_of(piece * PIECE + j)
                attn = attn_ref[part, lanes_of(j)]
                grad = inv_ref[part] * scaled_ref[part, lanes] - attn * slope_ref[part]
                grad = grad.astype(BF16)
                g_ref[part, lanes_of(j)] = grad
                term = dot(qturned_ref[lanes, part], grad)
                if totals[j] is None:
                    post_ref[i, j] = jnp.zeros_like(post_ref[i, j])
                    totals[j] = term
                else:
                    post_ref[i, j] = totals[j].astype(BF16)
                    totals[j] = totals[j] + term
        for j in range(PIECE):
            sum_ref[j] = totals[j]


def local_kernel(pieces, second, q_ref, k_ref, v_ref, turned_ref, pre_ref, *refs):
    if second:
        qgrad_hbm, tail_ref, kpart_ref, vpart_ref, qgrad_ref, sems = refs[-6:]
    else:
        qgrad_ref, kpart_ref, vpart_ref = refs[-3:]
    state = heads_in(refs[:pieces])
    g_refs, post_refs = refs[pieces:2 * pieces], refs[2 * pieces:3 * pieces]
    rows, width = q_ref.shape
    parts = chunks_of(rows)
    copies = []

    def send(source, same, part):
        target = qgrad_hbm.at[part, columns(same, width)]
        copies.append(pltpu.make_async_copy(source, target, sems.at[len(copies)]))
        copies[-1].start()

    if second:
        send(refs[3 * pieces], False, slice(0, rows))

    def scores(i, j):
        part, lanes = parts[i], lanes_of(j)
        v, g = v_ref[part, lanes], g_refs[j // PIECE][part, lanes_of(j % PIECE)]
        size = g.shape[0]
        gscores = jnp.where(lower(size), dot(g, v, 1, 1), 0.0).astype(BF16)
        gturned = jnp.where(upper(size), dot(v, g, 1, 1), 0.0).astype(BF16)
        return gscores, gturned

    def products(i, j, gscores, gturned):
        part, lanes = parts[i], lanes_of(j)
        q, k, v = (ref[part, lanes] for ref in (q_ref, k_ref, v_ref))
        g = g_refs[j // PIECE][part, lanes_of(j % PIECE)]
        before = state[j] + pre_ref[i, j].astype(F32) if i else state[j]
        qgrad = dot(g, before.astype(BF16), 1, 1) + dot(gscores, k)
        kgrad = dot(gturned, q)
        vgrad = dot(turned_ref[j, part], g)
        if i < len(parts) - 1:
            post = post_refs[j // PIECE][i, j % PIECE]
            kgrad = kgrad + dot(v, post, 1, 1)
            vgrad = vgrad + dot(k, post)
        if second and i == len(parts) - 1:
            tail_ref[:, lanes] = qgrad.astype(BF16)
        else:
            qgrad_ref[part, lanes] = qgrad.astype(BF16)
        kpart_ref[part, lanes] = kgrad
        vpart_ref[part, lanes] = vgrad

    places = [(i, j) for i in range(len(parts)) for j in range(width // HEAD_DIM)]
    ready = scores(*places[0])
    for place, following in zip(places, places[1:] + [None]):
        coming = scores(*following) if following else None
        products(*place, *ready)
        ready = coming
        if second and following and following[0] != place[0]:
            part = parts[place[0]]
            send(qgrad_ref.at[part], True, part)
    for copy in copies:
        copy.wait()


def final_part(piece, part, k_ref, v_ref, kpart_ref, vpart_ref, state_ref, kgrad_ref, vgrad_ref):
    for j in range(PIECE):
        lanes = lanes_of(piece * PIECE + j)
        state = state_ref[j].astype(BF16)
        kgrad = kpart_ref[part, lanes] + dot(v_ref[part, lanes], state, 1, 1)
        vgrad = vpart_ref[part, lanes] + dot(k_ref[part, lanes], state)
        kgrad_ref[part, lanes_of(j)] = kgrad.astype(BF16)
        vgrad_ref[part, lanes_of(j)] = vgrad.astype(BF16)


def final_kernel(piece, own, wholes, plan, *refs):
    sources = refs[5:5 + len(plan)]
    *outs, kgrad_ref, vgrad_ref, sems = refs[5 + len(plan):]
    outs = outs[len(outs) - wholes:]
    rows, copies = refs[0].shape[0], []

    def send(source, out, part, place):
        target = outs[out].at[part, columns(*place)]
        copies.append(pltpu.make_async_copy(source, target, sems.at[len(copies)]))
        copies[-1].start()

    for source, (out, part, place) in zip(sources, plan):
        send(source, out, part, place)
    for part in chunks_of(rows):
        final_part(piece, part, *refs[:5], kgrad_ref, vgrad_ref)
        if own:
            send(kgrad_ref.at[part], -2, part, own)
            send(vgrad_ref.at[part], -1, part, own)
    for copy in copies:
        copy.wait()


def scan_plan(count):
    bits = count.bit_length() - 1
    stages = []
    for stage in range(bits - 1):
        rising, falling = 1 + stage, bits - 1 - stage
        pairs = [(r, r ^ (1 << (falling if r & 1 else rising))) for r in range(count)]
        stages.append((rising, falling, pairs))
    return stages


def join_kernel(backward, done, final, *refs):
    count = lax.axis_size("seq")
    rank = lax.axis_index("seq")
    if backward:
        rank = count - 1 - rank
    odd = (rank & 1) == 1
    plan = scan_plan(count)
    keep, extra = (ref[...] for ref in refs[:2])
    came = refs[2:2 + done]
    total = keep + extra
    before = jnp.zeros_like(total)
    for (rising, falling, _), ref in zip(plan, came):
        high = (jnp.where(odd, rank >> falling, rank >> rising) & 1) == 1
        value = ref[...]
        before = before + jnp.where(odd | high, value, 0.0)
        total = total + jnp.where(odd, 0.0, value)
    if final:
        message_ref, state_ref = refs[-2:]
        message_ref[...] = before + jnp.where(odd, 0.0, keep)
        state_ref[...] = before + jnp.where(odd, extra, 0.0)
    else:
        rising, falling, _ = plan[done]
        high = (jnp.where(odd, rank >> falling, rank >> rising) & 1) == 1
        refs[-1][...] = jnp.where(odd, before + jnp.where(high, 0.0, total), total)


def join(backward, keep, extra, came, final, after):
    like = shape(keep.shape, F32)
    return run(
        functools.partial(join_kernel, backward, len(came), final), 4 * like.size,
        [VMEM] * (2 + len(came)) + [ANYWHERE] * len(after),
        [VMEM, VMEM] if final else VMEM,
        [like, like] if final else like,
        (keep, extra, *came, *after),
    )


def scan_states(keeps, extras, backward, beside, between):
    plan = scan_plan(lax.axis_size("seq"))
    came = [[] for _ in keeps]
    results, after = [], []
    for stage, (_, _, pairs) in enumerate(plan):
        messages = []
        for keep, extra, arrived in zip(keeps, extras, came):
            message = join(backward, keep, extra, arrived, False, after + messages)
            messages.append(message)
            arrived.append(move(message, pairs, backward))
        mine = beside[stage:] if stage == len(plan) - 1 else beside[stage:stage + 1]
        made = [work(messages) for work in mine]
        after = [item[-1] for item in made]
        results += made
    states, messages, early = [], [], ()
    for keep, extra, arrived in zip(keeps, extras, came):
        token = [*after, *messages, *early[-1:]]
        message, state = join(backward, keep, extra, arrived, True, token)
        states.append(state)
        messages.append(message)
        early = early or between(state, results)
    others = [nearby(message, backward) for message in messages[::-1]][::-1]
    return states, others, results, early


def move(value, pairs, backward):
    count = lax.axis_size("seq")
    if backward:
        pairs = [(count - 1 - a, count - 1 - b) for a, b in pairs]
    return lax.ppermute(value, "seq", pairs)


def nearby(value, backward):
    return move(value, [(r, r ^ 1) for r in range(lax.axis_size("seq"))], backward)


def shards(query, key_in, value, out_grad, gain):
    rows, width = query.shape
    half = width // 2
    heads = half // HEAD_DIM
    chunks = len(chunks_of(rows))
    peers = lax.axis_size("head")
    full = width * peers
    gain = gain.reshape(1, width)
    pin = lambda x: pltpu.with_memory_space_constraint(x, pltpu.HBM)
    query, key_in, value, out_grad = (pin(x) for x in (query, key_in, value, out_grad))
    unit = 2 * rows * half * HEAD_DIM
    partial = functools.partial

    count = heads // PIECE
    states = shape((PIECE, HEAD_DIM, HEAD_DIM), F32)
    inside = shape((chunks, heads, HEAD_DIM, HEAD_DIM), BF16)
    wide = shape((rows, half), F32)
    thin = shape((rows, half), BF16)
    lane_sums = shape((rows, HEAD_DIM), F32)
    whole = shape((rows, width), BF16)
    sems = pltpu.SemaphoreType.DMA((2 * chunks,))

    k1, v1, k2, v2, pre1, *sends = run(
        first_kernel, unit, [HBM, HBM], [VMEM] * (5 + count), [thin] * 4 + [inside] + [states] * count,
        (key_in, value), [sems, sems],
    )
    extras = [nearby(send, False) for send in sends]
    pre2, *keeps = run(
        sum_states, unit, [VMEM, VMEM], [VMEM] * (1 + count), [inside] + [states] * count, (k2, v2)
    )

    def inner_of(same, k, v, pre):
        return lambda messages: run(
            partial(inner_kernel, same), 6 * unit,
            [HBM, HBM, VMEM, VMEM, VMEM, VMEM] + [ANYWHERE] * len(messages), [VMEM] * 5,
            [
                thin, wide, wide,
                shape((half, rows), BF16), shape((heads, rows, rows // chunks), BF16),
            ],
            (query, out_grad, k, v, gain, pre, *messages),
            [pltpu.VMEM((rows, half), BF16), sems],
        )

    piece_wide = shape((rows, PIECE * HEAD_DIM), F32)

    def attn_of(number, inner, state, sums):
        last = number == 2 * count - 1
        return run(
            partial(attn_kernel, number % count, number == 0, last), unit // count,
            [VMEM] * (4 + len(sums)), [VMEM] * (2 if last else 3),
            [piece_wide] + ([shape((8, rows), F32)] if last else [lane_sums] * 2),
            (*inner, state, *sums),
        )

    state2, state1, made, early = scan_states(
        keeps, extras, False,
        [inner_of(True, k2, v2, pre2), inner_of(False, k1, v1, pre1)],
        lambda state, made: attn_of(0, made[0][:3], state, ()),
    )
    (q2, inner2, scaled2, qturned2, turned2), (q1, inner1, scaled1, qturned1, turned1) = made

    attn, *sums = early
    attns = [attn]
    for number, state in list(enumerate([*state2, *state1]))[1:]:
        inner = (q2, inner2, scaled2) if number < count else (q1, inner1, scaled1)
        attn, *sums = attn_of(number, inner, state, sums)
        attns.append(attn)
    sums = sums[0]
    parts = [sums] + [
        lax.ppermute(sums, "head", [(r, r ^ other) for r in range(peers)])
        for other in range(1, peers)
    ]

    posts = shape((chunks, PIECE, HEAD_DIM, HEAD_DIM), BF16)
    piece_out = [shape((rows, PIECE * HEAD_DIM), BF16), posts, states]

    def grads_of(pieces, first, attns, scaled, qturned):
        fresh = len(first) if first is parts else 0
        shapes = piece_out * len(pieces) + [lane_sums] * (2 if fresh else 0)
        made = run(
            partial(grad_kernel, pieces, full, fresh), unit * len(pieces) // count,
            [VMEM] * (len(first) + 2 + len(pieces)), [VMEM] * len(shapes), shapes,
            (*first, scaled, qturned, *attns),
        )
        return [made[i:i + 3] for i in range(0, 3 * len(pieces), 3)], made[3 * len(pieces):]

    made, factors = grads_of([0], parts, attns[:1], scaled2, qturned2)
    for piece in range(1, count):
        made += grads_of([piece], factors, attns[piece:piece + 1], scaled2, qturned2)[0]
    gs2, posts2, gsends = zip(*made)
    gextras = [nearby(gsend, True) for gsend in gsends]
    made = grads_of(list(range(count)), factors, attns[count:], scaled1, qturned1)[0]
    gs1, posts1, gkeeps = zip(*made)

    first_grads = []

    def local_of(second, *args):
        def work(messages):
            if second:
                specs, scratch = [HBM] + [VMEM] * 3, [pltpu.VMEM((rows, half), BF16), sems]
                shapes = [whole, shape((rows // chunks, half), BF16), wide, wide]
            else:
                specs, scratch, shapes = [VMEM] * 3, [], [thin, wide, wide]
            made = run(
                partial(local_kernel, count, second), 9 * unit,
                [VMEM] * (len(args) + len(first_grads)) + [ANYWHERE] * len(messages),
                specs, shapes, (*args, *first_grads, *messages), scratch,
            )
            first_grads.append(made[0])
            return made

        return work

    piece_thin = shape((rows, PIECE * HEAD_DIM), BF16)

    def final_of(piece, args, state, ready=(), outs=(), fresh=0, own=None):
        sources = [item[0] for item in ready]
        plan = [item[1:] for item in ready]
        args = (*args, state, *sources)
        wholes = len(outs) + fresh
        last = [pltpu.VMEM(piece_thin.shape, BF16)] * 2 if own else []
        return run(
            partial(final_kernel, piece, own, wholes, plan), 2 * unit // count,
            [VMEM] * len(args) + [HBM] * len(outs),
            [HBM] * wholes + ([] if own else [VMEM] * 2),
            [whole] * wholes + ([] if own else [piece_thin] * 2), (*args, *outs),
            last + [pltpu.SemaphoreType.DMA((len(plan) + 2 * chunks,))],
            {len(args) + i: i for i in range(len(outs))},
        )

    gstate1, gstate2, made, early = scan_states(
        gkeeps, gextras, True,
        [
            local_of(0, q1, k1, v1, turned1, pre1, *state1, *gs1, *posts1),
            local_of(1, q2, k2, v2, turned2, pre2, *state2, *gs2, *posts2),
        ],
        lambda state, made: final_of(0, (k1, v1, *made[0][1:]), state),
    )
    near = (k1, v1, *made[0][1:])
    qgrad, tail, *far = made[1]
    far = (k2, v2, *far)
    every = slice(0, rows)
    ready, outs, done = [], [], list(early)
    for piece in range(1, count):
        done += final_of(piece, near, gstate1[piece])
    for i, array in enumerate(done):
        ready.append((array, i % 2, every, (False, half, i // 2)))
    for piece in range(count - 1):
        now, ready = ready[:2], ready[2:]
        fresh = 0 if outs else 2
        *outs, kdone, vdone = final_of(piece, far, gstate2[piece], now, outs, fresh)
        ready.append((kdone, 0, every, (True, half, piece)))
        ready.append((vdone, 1, every, (True, half, piece)))
    ready = [(array, out + 1, part, place) for array, out, part, place in ready]
    ready.append((tail, 0, chunks_of(rows)[-1], (True, half)))
    qgrad, kgrad, vgrad = final_of(
        count - 1, far, gstate2[-1], ready, [qgrad, *outs], 0 if outs else 2,
        (True, half, count - 1),
    )
    return qgrad, kgrad, vgrad


def solution(mesh):
    spec = P("seq", "head")
    return jax.shard_map(
        shards,
        mesh=mesh,
        in_specs=(spec, spec, spec, spec, P("head")),
        out_specs=(spec, spec, spec),
        check_vma=False,
    )
```

```python
import functools

import jax
import jax.numpy as jnp
from jax import lax
from jax.experimental import pallas as pl
from jax.experimental.pallas import tpu as pltpu
from jax.sharding import PartitionSpec as P

HEAD_DIM = 128
CHUNK = 256
PIECE = 2
VMEM_BYTES = 12 * 2**20
F32 = jnp.float32
BF16 = jnp.bfloat16
VMEM = pl.BlockSpec(memory_space=pltpu.VMEM)
HBM = pl.BlockSpec(memory_space=pltpu.HBM)
ANYWHERE = pl.BlockSpec(memory_space=pl.ANY)


def dot(a, b, contract_a=1, contract_b=0):
    dims = (((contract_a,), (contract_b,)), ((), ()))
    return lax.dot_general(a, b, dims, preferred_element_type=F32)


def chunks_of(rows):
    size = CHUNK if rows % CHUNK == 0 else rows
    return [slice(i, i + size) for i in range(0, rows, size)]


def shape(dims, dtype):
    return jax.ShapeDtypeStruct(dims, dtype)


def lanes_of(j):
    return slice(j * HEAD_DIM, (j + 1) * HEAD_DIM)


def heads_in(pieces):
    return [ref[j] for ref in pieces for j in range(ref.shape[0])]


def lower(size):
    row = lax.broadcasted_iota(jnp.int32, (size, size), 0)
    return row >= lax.broadcasted_iota(jnp.int32, (size, size), 1)


def upper(size):
    row = lax.broadcasted_iota(jnp.int32, (size, size), 0)
    return row <= lax.broadcasted_iota(jnp.int32, (size, size), 1)


def run(kernel, flops, in_specs, out_specs, out_shape, args, scratch=(), aliases=None):
    nbytes = sum(a.size * a.dtype.itemsize for a, spec in zip(args, in_specs) if spec is HBM)
    return pl.pallas_call(
        kernel,
        in_specs=in_specs,
        out_specs=out_specs,
        out_shape=out_shape,
        scratch_shapes=list(scratch),
        input_output_aliases=aliases or {},
        cost_estimate=pl.CostEstimate(flops=flops, bytes_accessed=nbytes, transcendentals=0),
        compiler_params=pltpu.CompilerParams(vmem_limit_bytes=VMEM_BYTES),
    )(*args)


def columns(same, width, piece=None):
    odd = lax.rem(lax.axis_index("seq"), 2)
    half = odd if same else 1 - odd
    if piece is None:
        return pl.ds(pl.multiple_of(half * width, width), width)
    size = PIECE * HEAD_DIM
    return pl.ds(pl.multiple_of(half * width + piece * size, size), size)


def fetches(sources, targets, sems, same):
    rows, width = targets[0].shape
    lanes = columns(same, width)
    copies = []
    for part in chunks_of(rows):
        for source, target in zip(sources, targets):
            sem = sems.at[len(copies)]
            copies.append(pltpu.make_async_copy(source.at[part, lanes], target.at[part], sem))
    return copies


def sum_states(k_ref, v_ref, pre_ref, *sum_refs, copies=()):
    heads = pre_ref.shape[1]
    totals = [None] * heads
    for i, part in enumerate(chunks_of(k_ref.shape[0])):
        for copy in copies[2 * i:2 * i + 2]:
            copy.wait()
        for j in range(heads):
            term = dot(k_ref[part, lanes_of(j)], v_ref[part, lanes_of(j)], 0, 0)
            if i:
                pre_ref[i, j] = totals[j].astype(BF16)
            else:
                pre_ref[i, j] = jnp.zeros_like(pre_ref[i, j])
            totals[j] = totals[j] + term if i else term
    for j in range(heads):
        sum_refs[j // PIECE][j % PIECE] = totals[j]


def first_kernel(k_hbm, v_hbm, k1, v1, k2, v2, pre_ref, *refs):
    *sum_refs, sems1, sems2 = refs
    now = fetches((k_hbm, v_hbm), (k1, v1), sems1, False)
    later = fetches((k_hbm, v_hbm), (k2, v2), sems2, True)
    for copy in now + later:
        copy.start()
    sum_states(k1, v1, pre_ref, *sum_refs, copies=now)
    for copy in later:
        copy.wait()


def inner_kernel(same, q_hbm, og_hbm, k_ref, v_ref, gain_ref, pre_ref, *refs):
    q_ref, inner_ref, scaled_ref, qturned_ref, turned_ref, og_ref, sems = refs[-7:]
    rows, width = q_ref.shape
    copies = fetches((q_hbm, og_hbm), (q_ref, og_ref), sems, same)
    for copy in copies:
        copy.start()
    gain = gain_ref[:, columns(same, width)]
    for i, part in enumerate(chunks_of(rows)):
        for copy in copies[2 * i:2 * i + 2]:
            copy.wait()
        for j in range(width // HEAD_DIM):
            lanes = lanes_of(j)
            q, k = q_ref[part, lanes], k_ref[part, lanes]
            size = q.shape[0]
            scores = jnp.where(lower(size), dot(q, k, 1, 1), 0.0).astype(BF16)
            turned_ref[j, part] = jnp.where(upper(size), dot(k, q, 1, 1), 0.0).astype(BF16)
            inner = dot(scores, v_ref[part, lanes])
            inner_ref[part, lanes] = inner + dot(q, pre_ref[i, j]) if i else inner
            scaled_ref[part, lanes] = gain[:, lanes] * og_ref[part, lanes].astype(F32)
            qturned_ref[lanes, part] = q.T


def attn_kernel(piece, first, last, q_ref, inner_ref, scaled_ref, state_ref, *refs):
    attn_ref = refs[0] if first else refs[2]
    for part in chunks_of(q_ref.shape[0]):
        square, cross = (None, None) if first else (refs[0][part], refs[1][part])
        for j in range(PIECE):
            lanes = lanes_of(piece * PIECE + j)
            state = state_ref[j].astype(BF16)
            attn = inner_ref[part, lanes] + dot(q_ref[part, lanes], state)
            attn_ref[part, lanes_of(j)] = attn
            more, crossed = attn * attn, scaled_ref[part, lanes] * attn
            square = more if square is None else square + more
            cross = crossed if cross is None else cross + crossed
        if last:
            square = jnp.sum(square.T, axis=0, keepdims=True)
            cross = jnp.sum(cross.T, axis=0, keepdims=True)
            row = lax.broadcasted_iota(jnp.int32, (8, square.shape[1]), 0)
            sums = jnp.where(row == 0, square, jnp.where(row == 1, cross, 0.0))
            refs[-1][:, part] = sums
        else:
            refs[-2][part] = square
            refs[-1][part] = cross


def factors_kernel(full, parts, refs):
    total = refs[0][...]
    for ref in refs[1:parts]:
        total = total + ref[...]
    inv = lax.rsqrt(total[0:1] / full + 1e-6)
    slope = inv * inv * inv * (total[1:2] / full)
    row = lax.broadcasted_iota(jnp.int32, total.shape, 0)
    both = jnp.where(row == 0, inv, slope).T
    wide = (both.shape[0], HEAD_DIM)
    return jnp.broadcast_to(both[:, 0:1], wide), jnp.broadcast_to(both[:, 1:2], wide)


def grad_kernel(pieces, full, parts, *refs):
    if parts:
        inv, slope = factors_kernel(full, parts, refs)
        refs[-2][...] = inv
        refs[-1][...] = slope
        inv_ref, slope_ref = refs[-2:]
        refs = refs[parts:-2]
    else:
        inv_ref, slope_ref = refs[:2]
        refs = refs[2:]
    scaled_ref, qturned_ref = refs[:2]
    count = len(pieces)
    attns, outs = refs[2:2 + count], refs[2 + count:]
    for attn_ref, piece, at in zip(attns, pieces, range(0, 3 * count, 3)):
        g_ref, post_ref, sum_ref = outs[at:at + 3]
        totals = [None] * PIECE
        for i, part in reversed(list(enumerate(chunks_of(g_ref.shape[0])))):
            for j in range(PIECE):
                lanes = lanes_of(piece * PIECE + j)
                attn = attn_ref[part, lanes_of(j)]
                grad = inv_ref[part] * scaled_ref[part, lanes] - attn * slope_ref[part]
                grad = grad.astype(BF16)
                g_ref[part, lanes_of(j)] = grad
                term = dot(qturned_ref[lanes, part], grad)
                if totals[j] is None:
                    post_ref[i, j] = jnp.zeros_like(post_ref[i, j])
                    totals[j] = term
                else:
                    post_ref[i, j] = totals[j].astype(BF16)
                    totals[j] = totals[j] + term
        for j in range(PIECE):
            sum_ref[j] = totals[j]


def local_kernel(pieces, second, q_ref, k_ref, v_ref, turned_ref, pre_ref, *refs):
    if second:
        qgrad_hbm, tail_ref, kpart_ref, vpart_ref, qgrad_ref, sems = refs[-6:]
    else:
        qgrad_ref, kpart_ref, vpart_ref = refs[-3:]
    state = heads_in(refs[:pieces])
    g_refs, post_refs = refs[pieces:2 * pieces], refs[2 * pieces:3 * pieces]
    rows, width = q_ref.shape
    parts = chunks_of(rows)
    copies = []

    def send(source, same, part):
        target = qgrad_hbm.at[part, columns(same, width)]
        copies.append(pltpu.make_async_copy(source, target, sems.at[len(copies)]))
        copies[-1].start()

    if second:
        send(refs[3 * pieces], False, slice(0, rows))

    def scores(i, j):
        part, lanes = parts[i], lanes_of(j)
        v, g = v_ref[part, lanes], g_refs[j // PIECE][part, lanes_of(j % PIECE)]
        size = g.shape[0]
        gscores = jnp.where(lower(size), dot(g, v, 1, 1), 0.0).astype(BF16)
        gturned = jnp.where(upper(size), dot(v, g, 1, 1), 0.0).astype(BF16)
        return gscores, gturned

    def products(i, j, gscores, gturned):
        part, lanes = parts[i], lanes_of(j)
        q, k, v = (ref[part, lanes] for ref in (q_ref, k_ref, v_ref))
        g = g_refs[j // PIECE][part, lanes_of(j % PIECE)]
        before = state[j] + pre_ref[i, j].astype(F32) if i else state[j]
        qgrad = dot(g, before.astype(BF16), 1, 1) + dot(gscores, k)
        kgrad = dot(gturned, q)
        vgrad = dot(turned_ref[j, part], g)
        if i < len(parts) - 1:
            post = post_refs[j // PIECE][i, j % PIECE]
            kgrad = kgrad + dot(v, post, 1, 1)
            vgrad = vgrad + dot(k, post)
        if second and i == len(parts) - 1:
            tail_ref[:, lanes] = qgrad.astype(BF16)
        else:
            qgrad_ref[part, lanes] = qgrad.astype(BF16)
        kpart_ref[part, lanes] = kgrad
        vpart_ref[part, lanes] = vgrad

    places = [(i, j) for i in range(len(parts)) for j in range(width // HEAD_DIM)]
    ready = scores(*places[0])
    for place, following in zip(places, places[1:] + [None]):
        coming = scores(*following) if following else None
        products(*place, *ready)
        ready = coming
        if second and following and following[0] != place[0]:
            part = parts[place[0]]
            send(qgrad_ref.at[part], True, part)
    for copy in copies:
        copy.wait()


def final_part(piece, part, k_ref, v_ref, kpart_ref, vpart_ref, state_ref, kgrad_ref, vgrad_ref):
    for j in range(PIECE):
        lanes = lanes_of(piece * PIECE + j)
        state = state_ref[j].astype(BF16)
        kgrad = kpart_ref[part, lanes] + dot(v_ref[part, lanes], state, 1, 1)
        vgrad = vpart_ref[part, lanes] + dot(k_ref[part, lanes], state)
        kgrad_ref[part, lanes_of(j)] = kgrad.astype(BF16)
        vgrad_ref[part, lanes_of(j)] = vgrad.astype(BF16)


def final_kernel(jobs, wholes, plan, *refs):
    inputs = [refs[5 * i:5 * i + 5] for i in range(len(jobs))]
    refs = refs[5 * len(jobs):]
    sources, refs = refs[:len(plan)], refs[len(plan):]
    results, sems = refs[-1 - 2 * len(jobs):-1], refs[-1]
    outs = refs[:-1 - 2 * len(jobs)]
    outs = outs[len(outs) - wholes:]
    rows, copies = inputs[0][0].shape[0], []

    def send(source, out, part, place):
        target = outs[out].at[part, columns(*place)]
        copies.append(pltpu.make_async_copy(source, target, sems.at[len(copies)]))
        copies[-1].start()

    for source, (out, part, place) in zip(sources, plan):
        send(source, out, part, place)
    kept = [i for i, (_, place) in enumerate(jobs) if place is None]
    order = kept + [i for i in range(len(jobs)) if i not in kept]
    for i, (piece, place) in enumerate(jobs):
        at = 2 * order.index(i)
        kgrad_ref, vgrad_ref = results[at:at + 2]
        for part in chunks_of(rows):
            final_part(piece, part, *inputs[i], kgrad_ref, vgrad_ref)
            if place:
                send(kgrad_ref.at[part], -2, part, place)
                send(vgrad_ref.at[part], -1, part, place)
    for copy in copies:
        copy.wait()


def scan_plan(count):
    bits = count.bit_length() - 1
    stages = []
    for stage in range(bits - 1):
        rising, falling = 1 + stage, bits - 1 - stage
        pairs = [(r, r ^ (1 << (falling if r & 1 else rising))) for r in range(count)]
        stages.append((rising, falling, pairs))
    return stages


def join_kernel(backward, done, final, *refs):
    count = lax.axis_size("seq")
    rank = lax.axis_index("seq")
    if backward:
        rank = count - 1 - rank
    odd = (rank & 1) == 1
    plan = scan_plan(count)
    keep, extra = (ref[...] for ref in refs[:2])
    came = refs[2:2 + done]
    total = keep + extra
    before = jnp.zeros_like(total)
    for (rising, falling, _), ref in zip(plan, came):
        high = (jnp.where(odd, rank >> falling, rank >> rising) & 1) == 1
        value = ref[...]
        before = before + jnp.where(odd | high, value, 0.0)
        total = total + jnp.where(odd, 0.0, value)
    if final:
        message_ref, state_ref = refs[-2:]
        message_ref[...] = before + jnp.where(odd, 0.0, keep)
        state_ref[...] = before + jnp.where(odd, extra, 0.0)
    else:
        rising, falling, _ = plan[done]
        high = (jnp.where(odd, rank >> falling, rank >> rising) & 1) == 1
        refs[-1][...] = jnp.where(odd, before + jnp.where(high, 0.0, total), total)


def join(backward, keep, extra, came, final, after):
    like = shape(keep.shape, F32)
    return run(
        functools.partial(join_kernel, backward, len(came), final), 4 * like.size,
        [VMEM] * (2 + len(came)) + [ANYWHERE] * len(after),
        [VMEM, VMEM] if final else VMEM,
        [like, like] if final else like,
        (keep, extra, *came, *after),
    )


def scan_states(keeps, extras, backward, beside, between):
    plan = scan_plan(lax.axis_size("seq"))
    came = [[] for _ in keeps]
    results, after = [], []
    for stage, (_, _, pairs) in enumerate(plan):
        messages = []
        for keep, extra, arrived in zip(keeps, extras, came):
            message = join(backward, keep, extra, arrived, False, after + messages)
            messages.append(message)
            arrived.append(move(message, pairs, backward))
        mine = beside[stage:] if stage == len(plan) - 1 else beside[stage:stage + 1]
        made = [work(messages) for work in mine]
        after = [item[-1] for item in made]
        results += made
    states, messages, early = [], [], ()
    for keep, extra, arrived in zip(keeps, extras, came):
        token = [*after, *messages, *early[-1:]]
        message, state = join(backward, keep, extra, arrived, True, token)
        states.append(state)
        messages.append(message)
        early = early or between(state, results)
    others = [nearby(message, backward) for message in messages[::-1]][::-1]
    return states, others, results, early


def move(value, pairs, backward):
    count = lax.axis_size("seq")
    if backward:
        pairs = [(count - 1 - a, count - 1 - b) for a, b in pairs]
    return lax.ppermute(value, "seq", pairs)


def nearby(value, backward):
    return move(value, [(r, r ^ 1) for r in range(lax.axis_size("seq"))], backward)


def shards(query, key_in, value, out_grad, gain):
    rows, width = query.shape
    half = width // 2
    heads = half // HEAD_DIM
    chunks = len(chunks_of(rows))
    peers = lax.axis_size("head")
    full = width * peers
    gain = gain.reshape(1, width)
    pin = lambda x: pltpu.with_memory_space_constraint(x, pltpu.HBM)
    query, key_in, value, out_grad = (pin(x) for x in (query, key_in, value, out_grad))
    unit = 2 * rows * half * HEAD_DIM
    partial = functools.partial

    count = heads // PIECE
    states = shape((PIECE, HEAD_DIM, HEAD_DIM), F32)
    inside = shape((chunks, heads, HEAD_DIM, HEAD_DIM), BF16)
    wide = shape((rows, half), F32)
    thin = shape((rows, half), BF16)
    lane_sums = shape((rows, HEAD_DIM), F32)
    whole = shape((rows, width), BF16)
    sems = pltpu.SemaphoreType.DMA((2 * chunks,))

    k1, v1, k2, v2, pre1, *sends = run(
        first_kernel, unit, [HBM, HBM], [VMEM] * (5 + count), [thin] * 4 + [inside] + [states] * count,
        (key_in, value), [sems, sems],
    )
    extras = [nearby(send, False) for send in sends]
    pre2, *keeps = run(
        sum_states, unit, [VMEM, VMEM], [VMEM] * (1 + count), [inside] + [states] * count, (k2, v2)
    )

    def inner_of(same, k, v, pre):
        return lambda messages: run(
            partial(inner_kernel, same), 6 * unit,
            [HBM, HBM, VMEM, VMEM, VMEM, VMEM] + [ANYWHERE] * len(messages), [VMEM] * 5,
            [
                thin, wide, wide,
                shape((half, rows), BF16), shape((heads, rows, rows // chunks), BF16),
            ],
            (query, out_grad, k, v, gain, pre, *messages),
            [pltpu.VMEM((rows, half), BF16), sems],
        )

    piece_wide = shape((rows, PIECE * HEAD_DIM), F32)

    def attn_of(number, inner, state, sums):
        last = number == 2 * count - 1
        return run(
            partial(attn_kernel, number % count, number == 0, last), unit // count,
            [VMEM] * (4 + len(sums)), [VMEM] * (2 if last else 3),
            [piece_wide] + ([shape((8, rows), F32)] if last else [lane_sums] * 2),
            (*inner, state, *sums),
        )

    state2, state1, made, early = scan_states(
        keeps, extras, False,
        [inner_of(True, k2, v2, pre2), inner_of(False, k1, v1, pre1)],
        lambda state, made: attn_of(0, made[0][:3], state, ()),
    )
    (q2, inner2, scaled2, qturned2, turned2), (q1, inner1, scaled1, qturned1, turned1) = made

    attn, *sums = early
    attns = [attn]
    for number, state in list(enumerate([*state2, *state1]))[1:]:
        inner = (q2, inner2, scaled2) if number < count else (q1, inner1, scaled1)
        attn, *sums = attn_of(number, inner, state, sums)
        attns.append(attn)
    sums = sums[0]
    parts = [sums] + [
        lax.ppermute(sums, "head", [(r, r ^ other) for r in range(peers)])
        for other in range(1, peers)
    ]

    posts = shape((chunks, PIECE, HEAD_DIM, HEAD_DIM), BF16)
    piece_out = [shape((rows, PIECE * HEAD_DIM), BF16), posts, states]

    def grads_of(pieces, first, attns, scaled, qturned):
        fresh = len(first) if first is parts else 0
        shapes = piece_out * len(pieces) + [lane_sums] * (2 if fresh else 0)
        made = run(
            partial(grad_kernel, pieces, full, fresh), unit * len(pieces) // count,
            [VMEM] * (len(first) + 2 + len(pieces)), [VMEM] * len(shapes), shapes,
            (*first, scaled, qturned, *attns),
        )
        return [made[i:i + 3] for i in range(0, 3 * len(pieces), 3)], made[3 * len(pieces):]

    made, factors = grads_of([0], parts, attns[:1], scaled2, qturned2)
    for piece in range(1, count):
        made += grads_of([piece], factors, attns[piece:piece + 1], scaled2, qturned2)[0]
    gs2, posts2, gsends = zip(*made)
    gextras = [nearby(gsend, True) for gsend in gsends]
    made = grads_of(list(range(count)), factors, attns[count:], scaled1, qturned1)[0]
    gs1, posts1, gkeeps = zip(*made)

    first_grads = []

    def local_of(second, *args):
        def work(messages):
            if second:
                specs, scratch = [HBM] + [VMEM] * 3, [pltpu.VMEM((rows, half), BF16), sems]
                shapes = [whole, shape((rows // chunks, half), BF16), wide, wide]
            else:
                specs, scratch, shapes = [VMEM] * 3, [], [thin, wide, wide]
            made = run(
                partial(local_kernel, count, second), 9 * unit,
                [VMEM] * (len(args) + len(first_grads)) + [ANYWHERE] * len(messages),
                specs, shapes, (*args, *first_grads, *messages), scratch,
            )
            first_grads.append(made[0])
            return made

        return work

    piece_thin = shape((rows, PIECE * HEAD_DIM), BF16)

    def final_of(jobs, ready=(), outs=(), fresh=0):
        plan = [item[1:] for item in ready]
        args = [leaf for job in jobs for leaf in job[2]] + [item[0] for item in ready]
        wholes = len(outs) + fresh
        kept = sum(job[1] is None for job in jobs)
        buffers = [pltpu.VMEM(piece_thin.shape, BF16)] * (2 * (len(jobs) - kept))
        return run(
            partial(final_kernel, [job[:2] for job in jobs], wholes, plan),
            2 * unit * len(jobs) // count, [VMEM] * len(args) + [HBM] * len(outs),
            [HBM] * wholes + [VMEM] * (2 * kept), [whole] * wholes + [piece_thin] * (2 * kept),
            (*args, *outs),
            buffers + [pltpu.SemaphoreType.DMA((len(plan) + 2 * chunks * (len(jobs) - kept) + 1,))],
            {len(args) + i: i for i in range(len(outs))},
        )

    gstate1, gstate2, made, early = scan_states(
        gkeeps, gextras, True,
        [
            local_of(0, q1, k1, v1, turned1, pre1, *state1, *gs1, *posts1),
            local_of(1, q2, k2, v2, turned2, pre2, *state2, *gs2, *posts2),
        ],
        lambda state, made: final_of([(0, None, (k1, v1, *made[0][1:], state))]),
    )
    near = (k1, v1, *made[0][1:])
    qgrad, tail, *far = made[1]
    far = (k2, v2, *far)
    every = slice(0, rows)
    jobs = [(i, (False, half, i), (*near, gstate1[i])) for i in range(1, count)]
    jobs += [(i, None, (*far, gstate2[i])) for i in range(count - 1)]
    ready = [(early[i], i, every, (False, half, 0)) for i in range(2)]
    kgrad, vgrad, *done = final_of(jobs, ready, (), 2)
    jobs = [(count - 1, (True, half, count - 1), (*far, gstate2[-1]))]
    ready = [(done[i], 1 + i % 2, every, (True, half, i // 2)) for i in range(len(done))]
    ready.append((tail, 0, chunks_of(rows)[-1], (True, half)))
    qgrad, kgrad, vgrad = final_of(jobs, ready, (qgrad, kgrad, vgrad))
    return qgrad, kgrad, vgrad


def solution(mesh):
    spec = P("seq", "head")
    return jax.shard_map(
        shards,
        mesh=mesh,
        in_specs=(spec, spec, spec, spec, P("head")),
        out_specs=(spec, spec, spec),
        check_vma=False,
    )
```

```python
import functools

import jax
import jax.numpy as jnp
from jax import lax
from jax.experimental import pallas as pl
from jax.experimental.pallas import tpu as pltpu
from jax.sharding import PartitionSpec as P

HEAD_DIM = 128
CHUNK = 256
PIECE = 2
VMEM_BYTES = 12 * 2**20
F32 = jnp.float32
BF16 = jnp.bfloat16
VMEM = pl.BlockSpec(memory_space=pltpu.VMEM)
HBM = pl.BlockSpec(memory_space=pltpu.HBM)
ANYWHERE = pl.BlockSpec(memory_space=pl.ANY)


def dot(a, b, contract_a=1, contract_b=0):
    dims = (((contract_a,), (contract_b,)), ((), ()))
    return lax.dot_general(a, b, dims, preferred_element_type=F32)


def chunks_of(rows):
    size = CHUNK if rows % CHUNK == 0 else rows
    return [slice(i, i + size) for i in range(0, rows, size)]


def shape(dims, dtype):
    return jax.ShapeDtypeStruct(dims, dtype)


def lanes_of(j):
    return slice(j * HEAD_DIM, (j + 1) * HEAD_DIM)


def heads_in(pieces):
    return [ref[j] for ref in pieces for j in range(ref.shape[0])]


def lower(size):
    row = lax.broadcasted_iota(jnp.int32, (size, size), 0)
    return row >= lax.broadcasted_iota(jnp.int32, (size, size), 1)


def upper(size):
    row = lax.broadcasted_iota(jnp.int32, (size, size), 0)
    return row <= lax.broadcasted_iota(jnp.int32, (size, size), 1)


def run(kernel, flops, in_specs, out_specs, out_shape, args, scratch=(), aliases=None):
    nbytes = sum(a.size * a.dtype.itemsize for a, spec in zip(args, in_specs) if spec is HBM)
    return pl.pallas_call(
        kernel,
        in_specs=in_specs,
        out_specs=out_specs,
        out_shape=out_shape,
        scratch_shapes=list(scratch),
        input_output_aliases=aliases or {},
        cost_estimate=pl.CostEstimate(flops=flops, bytes_accessed=nbytes, transcendentals=0),
        compiler_params=pltpu.CompilerParams(vmem_limit_bytes=VMEM_BYTES),
    )(*args)


def columns(same, width, piece=None):
    odd = lax.rem(lax.axis_index("seq"), 2)
    half = odd if same else 1 - odd
    if piece is None:
        return pl.ds(pl.multiple_of(half * width, width), width)
    size = PIECE * HEAD_DIM
    return pl.ds(pl.multiple_of(half * width + piece * size, size), size)


def fetches(sources, targets, sems, same):
    rows, width = targets[0].shape
    lanes = columns(same, width)
    copies = []
    for part in chunks_of(rows):
        for source, target in zip(sources, targets):
            sem = sems.at[len(copies)]
            copies.append(pltpu.make_async_copy(source.at[part, lanes], target.at[part], sem))
    return copies


def sum_states(k_ref, v_ref, pre_ref, *sum_refs, copies=()):
    heads = pre_ref.shape[1]
    totals = [None] * heads
    for i, part in enumerate(chunks_of(k_ref.shape[0])):
        for copy in copies[2 * i:2 * i + 2]:
            copy.wait()
        for j in range(heads):
            term = dot(k_ref[part, lanes_of(j)], v_ref[part, lanes_of(j)], 0, 0)
            if i:
                pre_ref[i, j] = totals[j].astype(BF16)
            else:
                pre_ref[i, j] = jnp.zeros_like(pre_ref[i, j])
            totals[j] = totals[j] + term if i else term
    for j in range(heads):
        sum_refs[j // PIECE][j % PIECE] = totals[j]


def first_kernel(k_hbm, v_hbm, k1, v1, k2, v2, pre_ref, *refs):
    *sum_refs, sems1, sems2 = refs
    now = fetches((k_hbm, v_hbm), (k1, v1), sems1, False)
    later = fetches((k_hbm, v_hbm), (k2, v2), sems2, True)
    for copy in now + later:
        copy.start()
    sum_states(k1, v1, pre_ref, *sum_refs, copies=now)
    for copy in later:
        copy.wait()


def inner_kernel(same, q_hbm, og_hbm, k_ref, v_ref, gain_ref, pre_ref, *refs):
    q_ref, inner_ref, scaled_ref, qturned_ref, turned_ref, og_ref, sems = refs[-7:]
    rows, width = q_ref.shape
    copies = fetches((q_hbm, og_hbm), (q_ref, og_ref), sems, same)
    for copy in copies:
        copy.start()
    gain = gain_ref[:, columns(same, width)]
    for i, part in enumerate(chunks_of(rows)):
        for copy in copies[2 * i:2 * i + 2]:
            copy.wait()
        for j in range(width // HEAD_DIM):
            lanes = lanes_of(j)
            q, k = q_ref[part, lanes], k_ref[part, lanes]
            size = q.shape[0]
            scores = jnp.where(lower(size), dot(q, k, 1, 1), 0.0).astype(BF16)
            turned_ref[j, part] = jnp.where(upper(size), dot(k, q, 1, 1), 0.0).astype(BF16)
            inner = dot(scores, v_ref[part, lanes])
            inner_ref[part, lanes] = inner + dot(q, pre_ref[i, j]) if i else inner
            scaled_ref[part, lanes] = gain[:, lanes] * og_ref[part, lanes].astype(F32)
            qturned_ref[lanes, part] = q.T


def attn_kernel(piece, first, last, q_ref, inner_ref, scaled_ref, state_ref, *refs):
    attn_ref = refs[0] if first else refs[2]
    for part in chunks_of(q_ref.shape[0]):
        square, cross = (None, None) if first else (refs[0][part], refs[1][part])
        for j in range(PIECE):
            lanes = lanes_of(piece * PIECE + j)
            state = state_ref[j].astype(BF16)
            attn = inner_ref[part, lanes] + dot(q_ref[part, lanes], state)
            attn_ref[part, lanes_of(j)] = attn
            more, crossed = attn * attn, scaled_ref[part, lanes] * attn
            square = more if square is None else square + more
            cross = crossed if cross is None else cross + crossed
        if last:
            square = jnp.sum(square.T, axis=0, keepdims=True)
            cross = jnp.sum(cross.T, axis=0, keepdims=True)
            row = lax.broadcasted_iota(jnp.int32, (8, square.shape[1]), 0)
            sums = jnp.where(row == 0, square, jnp.where(row == 1, cross, 0.0))
            refs[-1][:, part] = sums
        else:
            refs[-2][part] = square
            refs[-1][part] = cross


def factors_kernel(full, parts, refs):
    total = refs[0][...]
    for ref in refs[1:parts]:
        total = total + ref[...]
    inv = lax.rsqrt(total[0:1] / full + 1e-6)
    slope = inv * inv * inv * (total[1:2] / full)
    row = lax.broadcasted_iota(jnp.int32, total.shape, 0)
    both = jnp.where(row == 0, inv, slope).T
    wide = (both.shape[0], HEAD_DIM)
    return jnp.broadcast_to(both[:, 0:1], wide), jnp.broadcast_to(both[:, 1:2], wide)


def grad_kernel(pieces, full, parts, *refs):
    if parts:
        inv, slope = factors_kernel(full, parts, refs)
        refs[-2][...] = inv
        refs[-1][...] = slope
        inv_ref, slope_ref = refs[-2:]
        refs = refs[parts:-2]
    else:
        inv_ref, slope_ref = refs[:2]
        refs = refs[2:]
    scaled_ref, qturned_ref = refs[:2]
    count = len(pieces)
    attns, outs = refs[2:2 + count], refs[2 + count:]
    for attn_ref, piece, at in zip(attns, pieces, range(0, 3 * count, 3)):
        g_ref, post_ref, sum_ref = outs[at:at + 3]
        totals = [None] * PIECE
        for i, part in reversed(list(enumerate(chunks_of(g_ref.shape[0])))):
            for j in range(PIECE):
                lanes = lanes_of(piece * PIECE + j)
                attn = attn_ref[part, lanes_of(j)]
                grad = inv_ref[part] * scaled_ref[part, lanes] - attn * slope_ref[part]
                grad = grad.astype(BF16)
                g_ref[part, lanes_of(j)] = grad
                term = dot(qturned_ref[lanes, part], grad)
                if totals[j] is None:
                    post_ref[i, j] = jnp.zeros_like(post_ref[i, j])
                    totals[j] = term
                else:
                    post_ref[i, j] = totals[j].astype(BF16)
                    totals[j] = totals[j] + term
        for j in range(PIECE):
            sum_ref[j] = totals[j]


def local_kernel(pieces, second, q_ref, k_ref, v_ref, turned_ref, pre_ref, *refs):
    if second:
        qgrad_hbm, tail_ref, kpart_ref, vpart_ref, qgrad_ref, sems = refs[-6:]
    else:
        qgrad_ref, kpart_ref, vpart_ref = refs[-3:]
    state = heads_in(refs[:pieces])
    g_refs, post_refs = refs[pieces:2 * pieces], refs[2 * pieces:3 * pieces]
    rows, width = q_ref.shape
    parts = chunks_of(rows)
    copies = []

    def send(source, same, part):
        target = qgrad_hbm.at[part, columns(same, width)]
        copies.append(pltpu.make_async_copy(source, target, sems.at[len(copies)]))
        copies[-1].start()

    if second:
        send(refs[3 * pieces], False, slice(0, rows))

    def scores(i, j):
        part, lanes = parts[i], lanes_of(j)
        v, g = v_ref[part, lanes], g_refs[j // PIECE][part, lanes_of(j % PIECE)]
        size = g.shape[0]
        gscores = jnp.where(lower(size), dot(g, v, 1, 1), 0.0).astype(BF16)
        gturned = jnp.where(upper(size), dot(v, g, 1, 1), 0.0).astype(BF16)
        return gscores, gturned

    def products(i, j, gscores, gturned):
        part, lanes = parts[i], lanes_of(j)
        q, k, v = (ref[part, lanes] for ref in (q_ref, k_ref, v_ref))
        g = g_refs[j // PIECE][part, lanes_of(j % PIECE)]
        before = state[j] + pre_ref[i, j].astype(F32) if i else state[j]
        qgrad = dot(g, before.astype(BF16), 1, 1) + dot(gscores, k)
        kgrad = dot(gturned, q)
        vgrad = dot(turned_ref[j, part], g)
        if i < len(parts) - 1:
            post = post_refs[j // PIECE][i, j % PIECE]
            kgrad = kgrad + dot(v, post, 1, 1)
            vgrad = vgrad + dot(k, post)
        if second and i == len(parts) - 1:
            tail_ref[:, lanes] = qgrad.astype(BF16)
        else:
            qgrad_ref[part, lanes] = qgrad.astype(BF16)
        kpart_ref[part, lanes] = kgrad
        vpart_ref[part, lanes] = vgrad

    places = [(i, j) for i in range(len(parts)) for j in range(width // HEAD_DIM)]
    ready = scores(*places[0])
    for place, following in zip(places, places[1:] + [None]):
        coming = scores(*following) if following else None
        products(*place, *ready)
        ready = coming
        if second and following and following[0] != place[0]:
            part = parts[place[0]]
            send(qgrad_ref.at[part], True, part)
    for copy in copies:
        copy.wait()


def final_part(piece, part, k_ref, v_ref, kpart_ref, vpart_ref, state_ref, kgrad_ref, vgrad_ref):
    for j in range(PIECE):
        lanes = lanes_of(piece * PIECE + j)
        state = state_ref[j].astype(BF16)
        kgrad = kpart_ref[part, lanes] + dot(v_ref[part, lanes], state, 1, 1)
        vgrad = vpart_ref[part, lanes] + dot(k_ref[part, lanes], state)
        kgrad_ref[part, lanes_of(j)] = kgrad.astype(BF16)
        vgrad_ref[part, lanes_of(j)] = vgrad.astype(BF16)


def final_kernel(jobs, wholes, plan, *refs):
    inputs = [refs[5 * i:5 * i + 5] for i in range(len(jobs))]
    refs = refs[5 * len(jobs):]
    sources, refs = refs[:len(plan)], refs[len(plan):]
    results, sems = refs[-1 - 2 * len(jobs):-1], refs[-1]
    outs = refs[:-1 - 2 * len(jobs)]
    outs = outs[len(outs) - wholes:]
    rows, copies = inputs[0][0].shape[0], []

    def send(source, out, part, place):
        target = outs[out].at[part, columns(*place)]
        copies.append(pltpu.make_async_copy(source, target, sems.at[len(copies)]))
        copies[-1].start()

    for source, (out, part, place) in zip(sources, plan):
        send(source, out, part, place)
    kept = [i for i, (_, place) in enumerate(jobs) if place is None]
    order = kept + [i for i in range(len(jobs)) if i not in kept]
    for i, (piece, place) in enumerate(jobs):
        at = 2 * order.index(i)
        kgrad_ref, vgrad_ref = results[at:at + 2]
        for part in chunks_of(rows):
            final_part(piece, part, *inputs[i], kgrad_ref, vgrad_ref)
            if place:
                send(kgrad_ref.at[part], -2, part, place)
                send(vgrad_ref.at[part], -1, part, place)
    for copy in copies:
        copy.wait()


def scan_plan(count):
    bits = count.bit_length() - 1
    stages = []
    for stage in range(bits - 1):
        rising, falling = 1 + stage, bits - 1 - stage
        pairs = [(r, r ^ (1 << (falling if r & 1 else rising))) for r in range(count)]
        stages.append((rising, falling, pairs))
    return stages


def join_kernel(backward, done, final, *refs):
    count = lax.axis_size("seq")
    rank = lax.axis_index("seq")
    if backward:
        rank = count - 1 - rank
    odd = (rank & 1) == 1
    plan = scan_plan(count)
    keep, extra = (ref[...] for ref in refs[:2])
    came = refs[2:2 + done]
    total = keep + extra
    before = jnp.zeros_like(total)
    for (rising, falling, _), ref in zip(plan, came):
        high = (jnp.where(odd, rank >> falling, rank >> rising) & 1) == 1
        value = ref[...]
        before = before + jnp.where(odd | high, value, 0.0)
        total = total + jnp.where(odd, 0.0, value)
    if final:
        message_ref, state_ref = refs[-2:]
        message_ref[...] = before + jnp.where(odd, 0.0, keep)
        state_ref[...] = before + jnp.where(odd, extra, 0.0)
    else:
        rising, falling, _ = plan[done]
        high = (jnp.where(odd, rank >> falling, rank >> rising) & 1) == 1
        refs[-1][...] = jnp.where(odd, before + jnp.where(high, 0.0, total), total)


def join(backward, keep, extra, came, final, after):
    like = shape(keep.shape, F32)
    return run(
        functools.partial(join_kernel, backward, len(came), final), 4 * like.size,
        [VMEM] * (2 + len(came)) + [ANYWHERE] * len(after),
        [VMEM, VMEM] if final else VMEM,
        [like, like] if final else like,
        (keep, extra, *came, *after),
    )


def scan_states(keeps, extras, backward, beside, between):
    plan = scan_plan(lax.axis_size("seq"))
    came = [[] for _ in keeps]
    results, after = [], []
    for stage, (_, _, pairs) in enumerate(plan):
        messages = []
        for keep, extra, arrived in zip(keeps, extras, came):
            message = join(backward, keep, extra, arrived, False, after + messages)
            messages.append(message)
            arrived.append(move(message, pairs, backward))
        mine = beside[stage:] if stage == len(plan) - 1 else beside[stage:stage + 1]
        made = [work(messages) for work in mine]
        after = [item[-1] for item in made]
        results += made
    states, messages, early = [], [], ()
    for keep, extra, arrived in zip(keeps, extras, came):
        token = [*after, *messages, *early[-1:]]
        message, state = join(backward, keep, extra, arrived, True, token)
        states.append(state)
        messages.append(message)
        early = early or between(state, results)
    others = [nearby(message, backward) for message in messages[::-1]][::-1]
    return states, others, results, early


def move(value, pairs, backward):
    count = lax.axis_size("seq")
    if backward:
        pairs = [(count - 1 - a, count - 1 - b) for a, b in pairs]
    return lax.ppermute(value, "seq", pairs)


def nearby(value, backward):
    return move(value, [(r, r ^ 1) for r in range(lax.axis_size("seq"))], backward)


def add_kernel(left_ref, right_ref, out_ref):
    out_ref[...] = left_ref[...] + right_ref[...]


def head_sums(sums):
    peers = lax.axis_size("head")
    distance, parts = 1, [sums]
    while distance < peers:
        if len(parts) == 2:
            sums = run(add_kernel, sums.size, [VMEM] * 2, VMEM, shape(sums.shape, F32), parts)
        parts = [sums, lax.ppermute(sums, "head", [(r, r ^ distance) for r in range(peers)])]
        distance *= 2
    return parts


def shards(query, key_in, value, out_grad, gain):
    rows, width = query.shape
    half = width // 2
    heads = half // HEAD_DIM
    chunks = len(chunks_of(rows))
    peers = lax.axis_size("head")
    full = width * peers
    gain = gain.reshape(1, width)
    pin = lambda x: pltpu.with_memory_space_constraint(x, pltpu.HBM)
    query, key_in, value, out_grad = (pin(x) for x in (query, key_in, value, out_grad))
    unit = 2 * rows * half * HEAD_DIM
    partial = functools.partial

    count = heads // PIECE
    states = shape((PIECE, HEAD_DIM, HEAD_DIM), F32)
    inside = shape((chunks, heads, HEAD_DIM, HEAD_DIM), BF16)
    wide = shape((rows, half), F32)
    thin = shape((rows, half), BF16)
    lane_sums = shape((rows, HEAD_DIM), F32)
    whole = shape((rows, width), BF16)
    sems = pltpu.SemaphoreType.DMA((2 * chunks,))

    k1, v1, k2, v2, pre1, *sends = run(
        first_kernel, unit, [HBM, HBM], [VMEM] * (5 + count), [thin] * 4 + [inside] + [states] * count,
        (key_in, value), [sems, sems],
    )
    extras = [nearby(send, False) for send in sends]
    pre2, *keeps = run(
        sum_states, unit, [VMEM, VMEM], [VMEM] * (1 + count), [inside] + [states] * count, (k2, v2)
    )

    def inner_of(same, k, v, pre):
        return lambda messages: run(
            partial(inner_kernel, same), 6 * unit,
            [HBM, HBM, VMEM, VMEM, VMEM, VMEM] + [ANYWHERE] * len(messages), [VMEM] * 5,
            [
                thin, wide, wide,
                shape((half, rows), BF16), shape((heads, rows, rows // chunks), BF16),
            ],
            (query, out_grad, k, v, gain, pre, *messages),
            [pltpu.VMEM((rows, half), BF16), sems],
        )

    piece_wide = shape((rows, PIECE * HEAD_DIM), F32)

    def attn_of(number, inner, state, sums):
        last = number == 2 * count - 1
        return run(
            partial(attn_kernel, number % count, number == 0, last), unit // count,
            [VMEM] * (4 + len(sums)), [VMEM] * (2 if last else 3),
            [piece_wide] + ([shape((8, rows), F32)] if last else [lane_sums] * 2),
            (*inner, state, *sums),
        )

    state2, state1, made, early = scan_states(
        keeps, extras, False,
        [inner_of(True, k2, v2, pre2), inner_of(False, k1, v1, pre1)],
        lambda state, made: attn_of(0, made[0][:3], state, ()),
    )
    (q2, inner2, scaled2, qturned2, turned2), (q1, inner1, scaled1, qturned1, turned1) = made

    attn, *sums = early
    attns = [attn]
    for number, state in list(enumerate([*state2, *state1]))[1:]:
        inner = (q2, inner2, scaled2) if number < count else (q1, inner1, scaled1)
        attn, *sums = attn_of(number, inner, state, sums)
        attns.append(attn)
    sums = sums[0]
    parts = head_sums(sums)

    posts = shape((chunks, PIECE, HEAD_DIM, HEAD_DIM), BF16)
    piece_out = [shape((rows, PIECE * HEAD_DIM), BF16), posts, states]

    def grads_of(pieces, first, attns, scaled, qturned):
        fresh = len(first) if first is parts else 0
        shapes = piece_out * len(pieces) + [lane_sums] * (2 if fresh else 0)
        made = run(
            partial(grad_kernel, pieces, full, fresh), unit * len(pieces) // count,
            [VMEM] * (len(first) + 2 + len(pieces)), [VMEM] * len(shapes), shapes,
            (*first, scaled, qturned, *attns),
        )
        return [made[i:i + 3] for i in range(0, 3 * len(pieces), 3)], made[3 * len(pieces):]

    made, factors = grads_of([0], parts, attns[:1], scaled2, qturned2)
    for piece in range(1, count):
        made += grads_of([piece], factors, attns[piece:piece + 1], scaled2, qturned2)[0]
    gs2, posts2, gsends = zip(*made)
    gextras = [nearby(gsend, True) for gsend in gsends]
    made = grads_of(list(range(count)), factors, attns[count:], scaled1, qturned1)[0]
    gs1, posts1, gkeeps = zip(*made)

    first_grads = []

    def local_of(second, *args):
        def work(messages):
            if second:
                specs, scratch = [HBM] + [VMEM] * 3, [pltpu.VMEM((rows, half), BF16), sems]
                shapes = [whole, shape((rows // chunks, half), BF16), wide, wide]
            else:
                specs, scratch, shapes = [VMEM] * 3, [], [thin, wide, wide]
            made = run(
                partial(local_kernel, count, second), 9 * unit,
                [VMEM] * (len(args) + len(first_grads)) + [ANYWHERE] * len(messages),
                specs, shapes, (*args, *first_grads, *messages), scratch,
            )
            first_grads.append(made[0])
            return made

        return work

    piece_thin = shape((rows, PIECE * HEAD_DIM), BF16)

    def final_of(jobs, ready=(), outs=(), fresh=0):
        plan = [item[1:] for item in ready]
        args = [leaf for job in jobs for leaf in job[2]] + [item[0] for item in ready]
        wholes = len(outs) + fresh
        kept = sum(job[1] is None for job in jobs)
        buffers = [pltpu.VMEM(piece_thin.shape, BF16)] * (2 * (len(jobs) - kept))
        return run(
            partial(final_kernel, [job[:2] for job in jobs], wholes, plan),
            2 * unit * len(jobs) // count, [VMEM] * len(args) + [HBM] * len(outs),
            [HBM] * wholes + [VMEM] * (2 * kept), [whole] * wholes + [piece_thin] * (2 * kept),
            (*args, *outs),
            buffers + [pltpu.SemaphoreType.DMA((len(plan) + 2 * chunks * (len(jobs) - kept) + 1,))],
            {len(args) + i: i for i in range(len(outs))},
        )

    gstate1, gstate2, made, early = scan_states(
        gkeeps, gextras, True,
        [
            local_of(0, q1, k1, v1, turned1, pre1, *state1, *gs1, *posts1),
            local_of(1, q2, k2, v2, turned2, pre2, *state2, *gs2, *posts2),
        ],
        lambda state, made: final_of([(0, None, (k1, v1, *made[0][1:], state))]),
    )
    near = (k1, v1, *made[0][1:])
    qgrad, tail, *far = made[1]
    far = (k2, v2, *far)
    every = slice(0, rows)
    jobs = [(i, (False, half, i), (*near, gstate1[i])) for i in range(1, count)]
    jobs += [(i, None, (*far, gstate2[i])) for i in range(count - 1)]
    ready = [(early[i], i, every, (False, half, 0)) for i in range(2)]
    kgrad, vgrad, *done = final_of(jobs, ready, (), 2)
    jobs = [(count - 1, (True, half, count - 1), (*far, gstate2[-1]))]
    ready = [(done[i], 1 + i % 2, every, (True, half, i // 2)) for i in range(len(done))]
    ready.append((tail, 0, chunks_of(rows)[-1], (True, half)))
    qgrad, kgrad, vgrad = final_of(jobs, ready, (qgrad, kgrad, vgrad))
    return qgrad, kgrad, vgrad


def solution(mesh):
    spec = P("seq", "head")
    return jax.shard_map(
        shards,
        mesh=mesh,
        in_specs=(spec, spec, spec, spec, P("head")),
        out_specs=(spec, spec, spec),
        check_vma=False,
    )
```

```python
import functools

import jax
import jax.numpy as jnp
from jax import lax
from jax.experimental import pallas as pl
from jax.experimental.pallas import tpu as pltpu
from jax.sharding import PartitionSpec as P

HEAD_DIM = 128
CHUNK = 256
PIECE = 2
VMEM_BYTES = 12 * 2**20
F32 = jnp.float32
BF16 = jnp.bfloat16
VMEM = pl.BlockSpec(memory_space=pltpu.VMEM)
HBM = pl.BlockSpec(memory_space=pltpu.HBM)
ANYWHERE = pl.BlockSpec(memory_space=pl.ANY)


def dot(a, b, contract_a=1, contract_b=0):
    dims = (((contract_a,), (contract_b,)), ((), ()))
    return lax.dot_general(a, b, dims, preferred_element_type=F32)


def chunks_of(rows):
    size = CHUNK if rows % CHUNK == 0 else rows
    return [slice(i, i + size) for i in range(0, rows, size)]


def shape(dims, dtype):
    return jax.ShapeDtypeStruct(dims, dtype)


def lanes_of(j):
    return slice(j * HEAD_DIM, (j + 1) * HEAD_DIM)


def heads_in(pieces):
    return [ref[j] for ref in pieces for j in range(ref.shape[0])]


def lower(size):
    row = lax.broadcasted_iota(jnp.int32, (size, size), 0)
    return row >= lax.broadcasted_iota(jnp.int32, (size, size), 1)


def upper(size):
    row = lax.broadcasted_iota(jnp.int32, (size, size), 0)
    return row <= lax.broadcasted_iota(jnp.int32, (size, size), 1)


def run(kernel, flops, in_specs, out_specs, out_shape, args, scratch=(), aliases=None):
    nbytes = sum(a.size * a.dtype.itemsize for a, spec in zip(args, in_specs) if spec is HBM)
    return pl.pallas_call(
        kernel,
        in_specs=in_specs,
        out_specs=out_specs,
        out_shape=out_shape,
        scratch_shapes=list(scratch),
        input_output_aliases=aliases or {},
        cost_estimate=pl.CostEstimate(flops=flops, bytes_accessed=nbytes, transcendentals=0),
        compiler_params=pltpu.CompilerParams(vmem_limit_bytes=VMEM_BYTES),
    )(*args)


def columns(same, width, piece=None):
    odd = lax.rem(lax.axis_index("seq"), 2)
    half = odd if same else 1 - odd
    if piece is None:
        return pl.ds(pl.multiple_of(half * width, width), width)
    size = PIECE * HEAD_DIM
    return pl.ds(pl.multiple_of(half * width + piece * size, size), size)


def fetches(sources, targets, sems, same):
    rows, width = targets[0].shape
    lanes = columns(same, width)
    copies = []
    for part in chunks_of(rows):
        for source, target in zip(sources, targets):
            sem = sems.at[len(copies)]
            copies.append(pltpu.make_async_copy(source.at[part, lanes], target.at[part], sem))
    return copies


def sum_states(k_ref, v_ref, pre_ref, *sum_refs, copies=()):
    heads = pre_ref.shape[1]
    totals = [None] * heads
    for i, part in enumerate(chunks_of(k_ref.shape[0])):
        for copy in copies[2 * i:2 * i + 2]:
            copy.wait()
        for j in range(heads):
            term = dot(k_ref[part, lanes_of(j)], v_ref[part, lanes_of(j)], 0, 0)
            if i:
                pre_ref[i, j] = totals[j].astype(BF16)
            else:
                pre_ref[i, j] = jnp.zeros_like(pre_ref[i, j])
            totals[j] = totals[j] + term if i else term
    for j in range(heads):
        sum_refs[j // PIECE][j % PIECE] = totals[j]


def first_kernel(k_hbm, v_hbm, k1, v1, k2, v2, pre_ref, *refs):
    *sum_refs, sems1, sems2 = refs
    now = fetches((k_hbm, v_hbm), (k1, v1), sems1, False)
    later = fetches((k_hbm, v_hbm), (k2, v2), sems2, True)
    for copy in now + later:
        copy.start()
    sum_states(k1, v1, pre_ref, *sum_refs, copies=now)
    for copy in later:
        copy.wait()


def inner_kernel(same, q_hbm, og_hbm, k_ref, v_ref, gain_ref, pre_ref, *refs):
    q_ref, inner_ref, scaled_ref, qturned_ref, turned_ref, og_ref, sems = refs[-7:]
    rows, width = q_ref.shape
    copies = fetches((q_hbm, og_hbm), (q_ref, og_ref), sems, same)
    for copy in copies:
        copy.start()
    gain = gain_ref[:, columns(same, width)]
    for i, part in enumerate(chunks_of(rows)):
        for copy in copies[2 * i:2 * i + 2]:
            copy.wait()
        for j in range(width // HEAD_DIM):
            lanes = lanes_of(j)
            q, k = q_ref[part, lanes], k_ref[part, lanes]
            size = q.shape[0]
            scores = jnp.where(lower(size), dot(q, k, 1, 1), 0.0).astype(BF16)
            turned_ref[j, part] = jnp.where(upper(size), dot(k, q, 1, 1), 0.0).astype(BF16)
            inner = dot(scores, v_ref[part, lanes])
            inner_ref[part, lanes] = inner + dot(q, pre_ref[i, j]) if i else inner
            scaled_ref[part, lanes] = gain[:, lanes] * og_ref[part, lanes].astype(F32)
            qturned_ref[lanes, part] = q.T


def attn_kernel(piece, first, last, q_ref, inner_ref, scaled_ref, state_ref, *refs):
    attn_ref = refs[0] if first else refs[2]
    parts = chunks_of(q_ref.shape[0])
    if last:
        refs[-1][...] = jnp.zeros_like(refs[-1])
    for i, part in enumerate(parts):
        square, cross = (None, None) if first else (refs[0][part], refs[1][part])
        for j in range(PIECE):
            lanes = lanes_of(piece * PIECE + j)
            state = state_ref[j].astype(BF16)
            attn = inner_ref[part, lanes] + dot(q_ref[part, lanes], state)
            attn_ref[part, lanes_of(j)] = attn
            more, crossed = attn * attn, scaled_ref[part, lanes] * attn
            square = more if square is None else square + more
            cross = crossed if cross is None else cross + crossed
        if last:
            refs[-1][2 * i:2 * i + 1] = jnp.sum(square.T, axis=0, keepdims=True)
            refs[-1][2 * i + 1:2 * i + 2] = jnp.sum(cross.T, axis=0, keepdims=True)
        else:
            refs[-2][part] = square
            refs[-1][part] = cross


def factors_kernel(full, parts, inv_ref, slope_ref, refs):
    total = refs[0][...]
    for ref in refs[1:parts]:
        total = total + ref[...]
    rows = []
    for i, _ in enumerate(chunks_of(inv_ref.shape[0])):
        inv = lax.rsqrt(total[2 * i:2 * i + 1] / full + 1e-6)
        rows += [inv, inv * inv * inv * (total[2 * i + 1:2 * i + 2] / full)]
    both = jnp.concatenate(rows + [total[len(rows):]], axis=0).T
    for i, part in enumerate(chunks_of(inv_ref.shape[0])):
        wide = (both.shape[0], HEAD_DIM)
        inv_ref[part] = jnp.broadcast_to(both[:, 2 * i:2 * i + 1], wide)
        slope_ref[part] = jnp.broadcast_to(both[:, 2 * i + 1:2 * i + 2], wide)


def grad_kernel(pieces, full, parts, *refs):
    if parts:
        inv_ref, slope_ref = refs[-2:]
        factors_kernel(full, parts, inv_ref, slope_ref, refs)
        refs = refs[parts:-2]
    else:
        inv_ref, slope_ref = refs[:2]
        refs = refs[2:]
    scaled_ref, qturned_ref = refs[:2]
    count = len(pieces)
    attns, outs = refs[2:2 + count], refs[2 + count:]
    for attn_ref, piece, at in zip(attns, pieces, range(0, 3 * count, 3)):
        g_ref, post_ref, sum_ref = outs[at:at + 3]
        totals = [None] * PIECE
        for i, part in reversed(list(enumerate(chunks_of(g_ref.shape[0])))):
            for j in range(PIECE):
                lanes = lanes_of(piece * PIECE + j)
                attn = attn_ref[part, lanes_of(j)]
                grad = inv_ref[part] * scaled_ref[part, lanes] - attn * slope_ref[part]
                grad = grad.astype(BF16)
                g_ref[part, lanes_of(j)] = grad
                term = dot(qturned_ref[lanes, part], grad)
                if totals[j] is None:
                    post_ref[i, j] = jnp.zeros_like(post_ref[i, j])
                    totals[j] = term
                else:
                    post_ref[i, j] = totals[j].astype(BF16)
                    totals[j] = totals[j] + term
        for j in range(PIECE):
            sum_ref[j] = totals[j]


def local_kernel(pieces, second, q_ref, k_ref, v_ref, turned_ref, pre_ref, *refs):
    if second:
        qgrad_hbm, tail_ref, kpart_ref, vpart_ref, qgrad_ref, sems = refs[-6:]
    else:
        qgrad_ref, kpart_ref, vpart_ref = refs[-3:]
    state = heads_in(refs[:pieces])
    g_refs, post_refs = refs[pieces:2 * pieces], refs[2 * pieces:3 * pieces]
    rows, width = q_ref.shape
    parts = chunks_of(rows)
    copies = []

    def send(source, same, part):
        target = qgrad_hbm.at[part, columns(same, width)]
        copies.append(pltpu.make_async_copy(source, target, sems.at[len(copies)]))
        copies[-1].start()

    if second:
        send(refs[3 * pieces], False, slice(0, rows))

    def scores(i, j):
        part, lanes = parts[i], lanes_of(j)
        v, g = v_ref[part, lanes], g_refs[j // PIECE][part, lanes_of(j % PIECE)]
        size = g.shape[0]
        gscores = jnp.where(lower(size), dot(g, v, 1, 1), 0.0).astype(BF16)
        gturned = jnp.where(upper(size), dot(v, g, 1, 1), 0.0).astype(BF16)
        return gscores, gturned

    def products(i, j, gscores, gturned):
        part, lanes = parts[i], lanes_of(j)
        q, k, v = (ref[part, lanes] for ref in (q_ref, k_ref, v_ref))
        g = g_refs[j // PIECE][part, lanes_of(j % PIECE)]
        before = state[j] + pre_ref[i, j].astype(F32) if i else state[j]
        qgrad = dot(g, before.astype(BF16), 1, 1) + dot(gscores, k)
        kgrad = dot(gturned, q)
        vgrad = dot(turned_ref[j, part], g)
        if i < len(parts) - 1:
            post = post_refs[j // PIECE][i, j % PIECE]
            kgrad = kgrad + dot(v, post, 1, 1)
            vgrad = vgrad + dot(k, post)
        if second and i == len(parts) - 1:
            tail_ref[:, lanes] = qgrad.astype(BF16)
        else:
            qgrad_ref[part, lanes] = qgrad.astype(BF16)
        kpart_ref[part, lanes] = kgrad
        vpart_ref[part, lanes] = vgrad

    places = [(i, j) for i in range(len(parts)) for j in range(width // HEAD_DIM)]
    ready = scores(*places[0])
    for place, following in zip(places, places[1:] + [None]):
        coming = scores(*following) if following else None
        products(*place, *ready)
        ready = coming
        if second and following and following[0] != place[0]:
            part = parts[place[0]]
            send(qgrad_ref.at[part], True, part)
    for copy in copies:
        copy.wait()


def final_part(piece, part, k_ref, v_ref, kpart_ref, vpart_ref, state_ref, kgrad_ref, vgrad_ref):
    for j in range(PIECE):
        lanes = lanes_of(piece * PIECE + j)
        state = state_ref[j].astype(BF16)
        kgrad = kpart_ref[part, lanes] + dot(v_ref[part, lanes], state, 1, 1)
        vgrad = vpart_ref[part, lanes] + dot(k_ref[part, lanes], state)
        kgrad_ref[part, lanes_of(j)] = kgrad.astype(BF16)
        vgrad_ref[part, lanes_of(j)] = vgrad.astype(BF16)


def final_kernel(jobs, wholes, plan, *refs):
    inputs = [refs[5 * i:5 * i + 5] for i in range(len(jobs))]
    refs = refs[5 * len(jobs):]
    sources, refs = refs[:len(plan)], refs[len(plan):]
    results, sems = refs[-1 - 2 * len(jobs):-1], refs[-1]
    outs = refs[:-1 - 2 * len(jobs)]
    outs = outs[len(outs) - wholes:]
    rows, copies = inputs[0][0].shape[0], []

    def send(source, out, part, place):
        target = outs[out].at[part, columns(*place)]
        copies.append(pltpu.make_async_copy(source, target, sems.at[len(copies)]))
        copies[-1].start()

    for source, (out, part, place) in zip(sources, plan):
        send(source, out, part, place)
    kept = [i for i, (_, place) in enumerate(jobs) if place is None]
    order = kept + [i for i in range(len(jobs)) if i not in kept]
    for i, (piece, place) in enumerate(jobs):
        at = 2 * order.index(i)
        kgrad_ref, vgrad_ref = results[at:at + 2]
        for part in chunks_of(rows):
            final_part(piece, part, *inputs[i], kgrad_ref, vgrad_ref)
            if place:
                send(kgrad_ref.at[part], -2, part, place)
                send(vgrad_ref.at[part], -1, part, place)
    for copy in copies:
        copy.wait()


def scan_plan(count):
    bits = count.bit_length() - 1
    stages = []
    for stage in range(bits - 1):
        rising, falling = 1 + stage, bits - 1 - stage
        pairs = [(r, r ^ (1 << (falling if r & 1 else rising))) for r in range(count)]
        stages.append((rising, falling, pairs))
    return stages


def join_kernel(backward, done, final, *refs):
    count = lax.axis_size("seq")
    rank = lax.axis_index("seq")
    if backward:
        rank = count - 1 - rank
    odd = (rank & 1) == 1
    plan = scan_plan(count)
    keep, extra = (ref[...] for ref in refs[:2])
    came = refs[2:2 + done]
    total = keep + extra
    before = jnp.zeros_like(total)
    for (rising, falling, _), ref in zip(plan, came):
        high = (jnp.where(odd, rank >> falling, rank >> rising) & 1) == 1
        value = ref[...]
        before = before + jnp.where(odd | high, value, 0.0)
        total = total + jnp.where(odd, 0.0, value)
    if final:
        message_ref, state_ref = refs[-2:]
        message_ref[...] = before + jnp.where(odd, 0.0, keep)
        state_ref[...] = before + jnp.where(odd, extra, 0.0)
    else:
        rising, falling, _ = plan[done]
        high = (jnp.where(odd, rank >> falling, rank >> rising) & 1) == 1
        refs[-1][...] = jnp.where(odd, before + jnp.where(high, 0.0, total), total)


def join(backward, keep, extra, came, final, after):
    like = shape(keep.shape, F32)
    return run(
        functools.partial(join_kernel, backward, len(came), final), 4 * like.size,
        [VMEM] * (2 + len(came)) + [ANYWHERE] * len(after),
        [VMEM, VMEM] if final else VMEM,
        [like, like] if final else like,
        (keep, extra, *came, *after),
    )


def scan_states(keeps, extras, backward, beside, between):
    plan = scan_plan(lax.axis_size("seq"))
    came = [[] for _ in keeps]
    results, after = [], []
    for stage, (_, _, pairs) in enumerate(plan):
        messages = []
        for keep, extra, arrived in zip(keeps, extras, came):
            message = join(backward, keep, extra, arrived, False, after + messages)
            messages.append(message)
            arrived.append(move(message, pairs, backward))
        mine = beside[stage:] if stage == len(plan) - 1 else beside[stage:stage + 1]
        made = [work(messages) for work in mine]
        after = [item[-1] for item in made]
        results += made
    states, messages, early = [], [], ()
    for keep, extra, arrived in zip(keeps, extras, came):
        token = [*after, *messages, *early[-1:]]
        message, state = join(backward, keep, extra, arrived, True, token)
        states.append(state)
        messages.append(message)
        early = early or between(state, results)
    others = [nearby(message, backward) for message in messages[::-1]][::-1]
    return states, others, results, early


def move(value, pairs, backward):
    count = lax.axis_size("seq")
    if backward:
        pairs = [(count - 1 - a, count - 1 - b) for a, b in pairs]
    return lax.ppermute(value, "seq", pairs)


def nearby(value, backward):
    return move(value, [(r, r ^ 1) for r in range(lax.axis_size("seq"))], backward)


def shards(query, key_in, value, out_grad, gain):
    rows, width = query.shape
    half = width // 2
    heads = half // HEAD_DIM
    chunks = len(chunks_of(rows))
    peers = lax.axis_size("head")
    full = width * peers
    gain = gain.reshape(1, width)
    pin = lambda x: pltpu.with_memory_space_constraint(x, pltpu.HBM)
    query, key_in, value, out_grad = (pin(x) for x in (query, key_in, value, out_grad))
    unit = 2 * rows * half * HEAD_DIM
    partial = functools.partial

    count = heads // PIECE
    states = shape((PIECE, HEAD_DIM, HEAD_DIM), F32)
    inside = shape((chunks, heads, HEAD_DIM, HEAD_DIM), BF16)
    wide = shape((rows, half), F32)
    thin = shape((rows, half), BF16)
    lane_sums = shape((rows, HEAD_DIM), F32)
    whole = shape((rows, width), BF16)
    sems = pltpu.SemaphoreType.DMA((2 * chunks,))

    k1, v1, k2, v2, pre1, *sends = run(
        first_kernel, unit, [HBM, HBM], [VMEM] * (5 + count), [thin] * 4 + [inside] + [states] * count,
        (key_in, value), [sems, sems],
    )
    extras = [nearby(send, False) for send in sends]
    pre2, *keeps = run(
        sum_states, unit, [VMEM, VMEM], [VMEM] * (1 + count), [inside] + [states] * count, (k2, v2)
    )

    def inner_of(same, k, v, pre):
        return lambda messages: run(
            partial(inner_kernel, same), 6 * unit,
            [HBM, HBM, VMEM, VMEM, VMEM, VMEM] + [ANYWHERE] * len(messages), [VMEM] * 5,
            [
                thin, wide, wide,
                shape((half, rows), BF16), shape((heads, rows, rows // chunks), BF16),
            ],
            (query, out_grad, k, v, gain, pre, *messages),
            [pltpu.VMEM((rows, half), BF16), sems],
        )

    piece_wide = shape((rows, PIECE * HEAD_DIM), F32)

    def attn_of(number, inner, state, sums):
        last = number == 2 * count - 1
        return run(
            partial(attn_kernel, number % count, number == 0, last), unit // count,
            [VMEM] * (4 + len(sums)), [VMEM] * (2 if last else 3),
            [piece_wide] + ([shape((-(-chunks // 4) * 8, rows // chunks), F32)] if last else [lane_sums] * 2),
            (*inner, state, *sums),
        )

    state2, state1, made, early = scan_states(
        keeps, extras, False,
        [inner_of(True, k2, v2, pre2), inner_of(False, k1, v1, pre1)],
        lambda state, made: attn_of(0, made[0][:3], state, ()),
    )
    (q2, inner2, scaled2, qturned2, turned2), (q1, inner1, scaled1, qturned1, turned1) = made

    attn, *sums = early
    attns = [attn]
    for number, state in list(enumerate([*state2, *state1]))[1:]:
        inner = (q2, inner2, scaled2) if number < count else (q1, inner1, scaled1)
        attn, *sums = attn_of(number, inner, state, sums)
        attns.append(attn)
    sums = sums[0]
    parts = [sums] + [
        lax.ppermute(sums, "head", [(r, r ^ other) for r in range(peers)])
        for other in range(1, peers)
    ]

    posts = shape((chunks, PIECE, HEAD_DIM, HEAD_DIM), BF16)
    piece_out = [shape((rows, PIECE * HEAD_DIM), BF16), posts, states]

    def grads_of(pieces, first, attns, scaled, qturned):
        fresh = len(first) if first is parts else 0
        shapes = piece_out * len(pieces) + [lane_sums] * (2 if fresh else 0)
        made = run(
            partial(grad_kernel, pieces, full, fresh), unit * len(pieces) // count,
            [VMEM] * (len(first) + 2 + len(pieces)), [VMEM] * len(shapes), shapes,
            (*first, scaled, qturned, *attns),
        )
        return [made[i:i + 3] for i in range(0, 3 * len(pieces), 3)], made[3 * len(pieces):]

    made, factors = grads_of([0], parts, attns[:1], scaled2, qturned2)
    for piece in range(1, count):
        made += grads_of([piece], factors, attns[piece:piece + 1], scaled2, qturned2)[0]
    gs2, posts2, gsends = zip(*made)
    gextras = [nearby(gsend, True) for gsend in gsends]
    made = grads_of(list(range(count)), factors, attns[count:], scaled1, qturned1)[0]
    gs1, posts1, gkeeps = zip(*made)

    first_grads = []

    def local_of(second, *args):
        def work(messages):
            if second:
                specs, scratch = [HBM] + [VMEM] * 3, [pltpu.VMEM((rows, half), BF16), sems]
                shapes = [whole, shape((rows // chunks, half), BF16), wide, wide]
            else:
                specs, scratch, shapes = [VMEM] * 3, [], [thin, wide, wide]
            made = run(
                partial(local_kernel, count, second), 9 * unit,
                [VMEM] * (len(args) + len(first_grads)) + [ANYWHERE] * len(messages),
                specs, shapes, (*args, *first_grads, *messages), scratch,
            )
            first_grads.append(made[0])
            return made

        return work

    piece_thin = shape((rows, PIECE * HEAD_DIM), BF16)

    def final_of(jobs, ready=(), outs=(), fresh=0):
        plan = [item[1:] for item in ready]
        args = [leaf for job in jobs for leaf in job[2]] + [item[0] for item in ready]
        wholes = len(outs) + fresh
        kept = sum(job[1] is None for job in jobs)
        buffers = [pltpu.VMEM(piece_thin.shape, BF16)] * (2 * (len(jobs) - kept))
        return run(
            partial(final_kernel, [job[:2] for job in jobs], wholes, plan),
            2 * unit * len(jobs) // count, [VMEM] * len(args) + [HBM] * len(outs),
            [HBM] * wholes + [VMEM] * (2 * kept), [whole] * wholes + [piece_thin] * (2 * kept),
            (*args, *outs),
            buffers + [pltpu.SemaphoreType.DMA((len(plan) + 2 * chunks * (len(jobs) - kept) + 1,))],
            {len(args) + i: i for i in range(len(outs))},
        )

    gstate1, gstate2, made, early = scan_states(
        gkeeps, gextras, True,
        [
            local_of(0, q1, k1, v1, turned1, pre1, *state1, *gs1, *posts1),
            local_of(1, q2, k2, v2, turned2, pre2, *state2, *gs2, *posts2),
        ],
        lambda state, made: final_of([(0, None, (k1, v1, *made[0][1:], state))]),
    )
    near = (k1, v1, *made[0][1:])
    qgrad, tail, *far = made[1]
    far = (k2, v2, *far)
    every = slice(0, rows)
    jobs = [(i, (False, half, i), (*near, gstate1[i])) for i in range(1, count)]
    jobs += [(i, None, (*far, gstate2[i])) for i in range(count - 1)]
    ready = [(early[i], i, every, (False, half, 0)) for i in range(2)]
    kgrad, vgrad, *done = final_of(jobs, ready, (), 2)
    jobs = [(count - 1, (True, half, count - 1), (*far, gstate2[-1]))]
    ready = [(done[i], 1 + i % 2, every, (True, half, i // 2)) for i in range(len(done))]
    ready.append((tail, 0, chunks_of(rows)[-1], (True, half)))
    qgrad, kgrad, vgrad = final_of(jobs, ready, (qgrad, kgrad, vgrad))
    return qgrad, kgrad, vgrad


def solution(mesh):
    spec = P("seq", "head")
    return jax.shard_map(
        shards,
        mesh=mesh,
        in_specs=(spec, spec, spec, spec, P("head")),
        out_specs=(spec, spec, spec),
        check_vma=False,
    )
```

```python
import functools

import jax
import jax.numpy as jnp
from jax import lax
from jax.experimental import pallas as pl
from jax.experimental.pallas import tpu as pltpu
from jax.sharding import PartitionSpec as P

HEAD_DIM = 128
CHUNK = 256
PIECE = 2
VMEM_BYTES = 12 * 2**20
F32 = jnp.float32
BF16 = jnp.bfloat16
VMEM = pl.BlockSpec(memory_space=pltpu.VMEM)
HBM = pl.BlockSpec(memory_space=pltpu.HBM)
ANYWHERE = pl.BlockSpec(memory_space=pl.ANY)


def dot(a, b, contract_a=1, contract_b=0):
    dims = (((contract_a,), (contract_b,)), ((), ()))
    return lax.dot_general(a, b, dims, preferred_element_type=F32)


def chunks_of(rows):
    size = CHUNK if rows % CHUNK == 0 else rows
    return [slice(i, i + size) for i in range(0, rows, size)]


def shape(dims, dtype):
    return jax.ShapeDtypeStruct(dims, dtype)


def lanes_of(j):
    return slice(j * HEAD_DIM, (j + 1) * HEAD_DIM)


def heads_in(pieces):
    return [ref[j] for ref in pieces for j in range(ref.shape[0])]


def lower(size):
    row = lax.broadcasted_iota(jnp.int32, (size, size), 0)
    return row >= lax.broadcasted_iota(jnp.int32, (size, size), 1)


def upper(size):
    row = lax.broadcasted_iota(jnp.int32, (size, size), 0)
    return row <= lax.broadcasted_iota(jnp.int32, (size, size), 1)


def run(kernel, flops, in_specs, out_specs, out_shape, args, scratch=(), aliases=None):
    nbytes = sum(a.size * a.dtype.itemsize for a, spec in zip(args, in_specs) if spec is HBM)
    return pl.pallas_call(
        kernel,
        in_specs=in_specs,
        out_specs=out_specs,
        out_shape=out_shape,
        scratch_shapes=list(scratch),
        input_output_aliases=aliases or {},
        cost_estimate=pl.CostEstimate(flops=flops, bytes_accessed=nbytes, transcendentals=0),
        compiler_params=pltpu.CompilerParams(vmem_limit_bytes=VMEM_BYTES),
    )(*args)


def columns(same, width, piece=None):
    odd = lax.rem(lax.axis_index("seq"), 2)
    half = odd if same else 1 - odd
    if piece is None:
        return pl.ds(pl.multiple_of(half * width, width), width)
    size = PIECE * HEAD_DIM
    return pl.ds(pl.multiple_of(half * width + piece * size, size), size)


def fetches(sources, targets, sems, same):
    rows, width = targets[0].shape
    lanes = columns(same, width)
    copies = []
    for part in chunks_of(rows):
        for source, target in zip(sources, targets):
            sem = sems.at[len(copies)]
            copies.append(pltpu.make_async_copy(source.at[part, lanes], target.at[part], sem))
    return copies


def sum_states(k_ref, v_ref, pre_ref, *sum_refs, copies=()):
    heads = pre_ref.shape[1]
    totals = [None] * heads
    for i, part in enumerate(chunks_of(k_ref.shape[0])):
        for copy in copies[2 * i:2 * i + 2]:
            copy.wait()
        for j in range(heads):
            term = dot(k_ref[part, lanes_of(j)], v_ref[part, lanes_of(j)], 0, 0)
            if i:
                pre_ref[i, j] = totals[j].astype(BF16)
            else:
                pre_ref[i, j] = jnp.zeros_like(pre_ref[i, j])
            totals[j] = totals[j] + term if i else term
    for j in range(heads):
        sum_refs[j // PIECE][j % PIECE] = totals[j]


def first_kernel(k_hbm, v_hbm, k1, v1, k2, v2, pre_ref, *refs):
    *sum_refs, sems1, sems2 = refs
    now = fetches((k_hbm, v_hbm), (k1, v1), sems1, False)
    later = fetches((k_hbm, v_hbm), (k2, v2), sems2, True)
    for copy in now + later:
        copy.start()
    sum_states(k1, v1, pre_ref, *sum_refs, copies=now)
    for copy in later:
        copy.wait()


def inner_kernel(same, q_hbm, og_hbm, k_ref, v_ref, gain_ref, pre_ref, *refs):
    q_ref, inner_ref, scaled_ref, qturned_ref, turned_ref, og_ref, sems = refs[-7:]
    rows, width = q_ref.shape
    copies = fetches((q_hbm, og_hbm), (q_ref, og_ref), sems, same)
    for copy in copies:
        copy.start()
    gain = gain_ref[:, columns(same, width)]
    for i, part in enumerate(chunks_of(rows)):
        for copy in copies[2 * i:2 * i + 2]:
            copy.wait()
        for j in range(width // HEAD_DIM):
            lanes = lanes_of(j)
            q, k = q_ref[part, lanes], k_ref[part, lanes]
            size = q.shape[0]
            scores = jnp.where(lower(size), dot(q, k, 1, 1), 0.0).astype(BF16)
            turned_ref[j, part] = jnp.where(upper(size), dot(k, q, 1, 1), 0.0).astype(BF16)
            inner = dot(scores, v_ref[part, lanes])
            inner_ref[part, lanes] = inner + dot(q, pre_ref[i, j]) if i else inner
            scaled_ref[part, lanes] = gain[:, lanes] * og_ref[part, lanes].astype(F32)
            qturned_ref[lanes, part] = q.T


def attn_kernel(piece, first, last, q_ref, inner_ref, scaled_ref, state_ref, *refs):
    attn_ref = refs[0] if first else refs[2]
    parts = chunks_of(q_ref.shape[0])
    if last:
        refs[-1][...] = jnp.zeros_like(refs[-1])
    for i, part in enumerate(parts):
        square, cross = (None, None) if first else (refs[0][part], refs[1][part])
        for j in range(PIECE):
            lanes = lanes_of(piece * PIECE + j)
            state = state_ref[j].astype(BF16)
            attn = inner_ref[part, lanes] + dot(q_ref[part, lanes], state)
            attn_ref[part, lanes_of(j)] = attn
            more, crossed = attn * attn, scaled_ref[part, lanes] * attn
            square = more if square is None else square + more
            cross = crossed if cross is None else cross + crossed
        if last:
            other = refs[-1].shape[0] // 2 + i
            refs[-1][i:i + 1] = jnp.sum(square.T, axis=0, keepdims=True)
            refs[-1][other:other + 1] = jnp.sum(cross.T, axis=0, keepdims=True)
        else:
            refs[-2][part] = square
            refs[-1][part] = cross


def factors_kernel(full, parts, inv_ref, slope_ref, refs):
    total = refs[0][...]
    for ref in refs[1:parts]:
        total = total + ref[...]
    middle = total.shape[0] // 2
    inv = lax.rsqrt(total[:middle] / full + 1e-6)
    slope = (inv * inv * inv * (total[middle:] / full)).T
    inv = inv.T
    for i, part in enumerate(chunks_of(inv_ref.shape[0])):
        wide = (inv.shape[0], HEAD_DIM)
        inv_ref[part] = jnp.broadcast_to(inv[:, i:i + 1], wide)
        slope_ref[part] = jnp.broadcast_to(slope[:, i:i + 1], wide)


def grad_kernel(pieces, full, parts, *refs):
    if parts:
        inv_ref, slope_ref = refs[-2:]
        factors_kernel(full, parts, inv_ref, slope_ref, refs)
        refs = refs[parts:-2]
    else:
        inv_ref, slope_ref = refs[:2]
        refs = refs[2:]
    scaled_ref, qturned_ref = refs[:2]
    count = len(pieces)
    attns, outs = refs[2:2 + count], refs[2 + count:]
    for attn_ref, piece, at in zip(attns, pieces, range(0, 3 * count, 3)):
        g_ref, post_ref, sum_ref = outs[at:at + 3]
        totals = [None] * PIECE
        for i, part in reversed(list(enumerate(chunks_of(g_ref.shape[0])))):
            for j in range(PIECE):
                lanes = lanes_of(piece * PIECE + j)
                attn = attn_ref[part, lanes_of(j)]
                grad = inv_ref[part] * scaled_ref[part, lanes] - attn * slope_ref[part]
                grad = grad.astype(BF16)
                g_ref[part, lanes_of(j)] = grad
                term = dot(qturned_ref[lanes, part], grad)
                if totals[j] is None:
                    post_ref[i, j] = jnp.zeros_like(post_ref[i, j])
                    totals[j] = term
                else:
                    post_ref[i, j] = totals[j].astype(BF16)
                    totals[j] = totals[j] + term
        for j in range(PIECE):
            sum_ref[j] = totals[j]


def local_kernel(pieces, second, q_ref, k_ref, v_ref, turned_ref, pre_ref, *refs):
    if second:
        qgrad_hbm, tail_ref, kpart_ref, vpart_ref, qgrad_ref, sems = refs[-6:]
    else:
        qgrad_ref, kpart_ref, vpart_ref = refs[-3:]
    state = heads_in(refs[:pieces])
    g_refs, post_refs = refs[pieces:2 * pieces], refs[2 * pieces:3 * pieces]
    rows, width = q_ref.shape
    parts = chunks_of(rows)
    copies = []

    def send(source, same, part):
        target = qgrad_hbm.at[part, columns(same, width)]
        copies.append(pltpu.make_async_copy(source, target, sems.at[len(copies)]))
        copies[-1].start()

    if second:
        send(refs[3 * pieces], False, slice(0, rows))

    def scores(i, j):
        part, lanes = parts[i], lanes_of(j)
        v, g = v_ref[part, lanes], g_refs[j // PIECE][part, lanes_of(j % PIECE)]
        size = g.shape[0]
        gscores = jnp.where(lower(size), dot(g, v, 1, 1), 0.0).astype(BF16)
        gturned = jnp.where(upper(size), dot(v, g, 1, 1), 0.0).astype(BF16)
        return gscores, gturned

    def products(i, j, gscores, gturned):
        part, lanes = parts[i], lanes_of(j)
        q, k, v = (ref[part, lanes] for ref in (q_ref, k_ref, v_ref))
        g = g_refs[j // PIECE][part, lanes_of(j % PIECE)]
        before = state[j] + pre_ref[i, j].astype(F32) if i else state[j]
        qgrad = dot(g, before.astype(BF16), 1, 1) + dot(gscores, k)
        kgrad = dot(gturned, q)
        vgrad = dot(turned_ref[j, part], g)
        if i < len(parts) - 1:
            post = post_refs[j // PIECE][i, j % PIECE]
            kgrad = kgrad + dot(v, post, 1, 1)
            vgrad = vgrad + dot(k, post)
        if second and i == len(parts) - 1:
            tail_ref[:, lanes] = qgrad.astype(BF16)
        else:
            qgrad_ref[part, lanes] = qgrad.astype(BF16)
        kpart_ref[part, lanes] = kgrad
        vpart_ref[part, lanes] = vgrad

    places = [(i, j) for i in range(len(parts)) for j in range(width // HEAD_DIM)]
    ready = scores(*places[0])
    for place, following in zip(places, places[1:] + [None]):
        coming = scores(*following) if following else None
        products(*place, *ready)
        ready = coming
        if second and following and following[0] != place[0]:
            part = parts[place[0]]
            send(qgrad_ref.at[part], True, part)
    for copy in copies:
        copy.wait()


def final_part(piece, part, k_ref, v_ref, kpart_ref, vpart_ref, state_ref, kgrad_ref, vgrad_ref):
    for j in range(PIECE):
        lanes = lanes_of(piece * PIECE + j)
        state = state_ref[j].astype(BF16)
        kgrad = kpart_ref[part, lanes] + dot(v_ref[part, lanes], state, 1, 1)
        vgrad = vpart_ref[part, lanes] + dot(k_ref[part, lanes], state)
        kgrad_ref[part, lanes_of(j)] = kgrad.astype(BF16)
        vgrad_ref[part, lanes_of(j)] = vgrad.astype(BF16)


def final_kernel(jobs, wholes, plan, *refs):
    inputs = [refs[5 * i:5 * i + 5] for i in range(len(jobs))]
    refs = refs[5 * len(jobs):]
    sources, refs = refs[:len(plan)], refs[len(plan):]
    results, sems = refs[-1 - 2 * len(jobs):-1], refs[-1]
    outs = refs[:-1 - 2 * len(jobs)]
    outs = outs[len(outs) - wholes:]
    rows, copies = inputs[0][0].shape[0], []

    def send(source, out, part, place):
        target = outs[out].at[part, columns(*place)]
        copies.append(pltpu.make_async_copy(source, target, sems.at[len(copies)]))
        copies[-1].start()

    for source, (out, part, place) in zip(sources, plan):
        send(source, out, part, place)
    kept = [i for i, (_, place) in enumerate(jobs) if place is None]
    order = kept + [i for i in range(len(jobs)) if i not in kept]
    for i, (piece, place) in enumerate(jobs):
        at = 2 * order.index(i)
        kgrad_ref, vgrad_ref = results[at:at + 2]
        for part in chunks_of(rows):
            final_part(piece, part, *inputs[i], kgrad_ref, vgrad_ref)
            if place:
                send(kgrad_ref.at[part], -2, part, place)
                send(vgrad_ref.at[part], -1, part, place)
    for copy in copies:
        copy.wait()


def scan_plan(count):
    bits = count.bit_length() - 1
    stages = []
    for stage in range(bits - 1):
        rising, falling = 1 + stage, bits - 1 - stage
        pairs = [(r, r ^ (1 << (falling if r & 1 else rising))) for r in range(count)]
        stages.append((rising, falling, pairs))
    return stages


def join_kernel(backward, done, final, *refs):
    count = lax.axis_size("seq")
    rank = lax.axis_index("seq")
    if backward:
        rank = count - 1 - rank
    odd = (rank & 1) == 1
    plan = scan_plan(count)
    keep, extra = (ref[...] for ref in refs[:2])
    came = refs[2:2 + done]
    total = keep + extra
    before = jnp.zeros_like(total)
    for (rising, falling, _), ref in zip(plan, came):
        high = (jnp.where(odd, rank >> falling, rank >> rising) & 1) == 1
        value = ref[...]
        before = before + jnp.where(odd | high, value, 0.0)
        total = total + jnp.where(odd, 0.0, value)
    if final:
        message_ref, state_ref = refs[-2:]
        message_ref[...] = before + jnp.where(odd, 0.0, keep)
        state_ref[...] = before + jnp.where(odd, extra, 0.0)
    else:
        rising, falling, _ = plan[done]
        high = (jnp.where(odd, rank >> falling, rank >> rising) & 1) == 1
        refs[-1][...] = jnp.where(odd, before + jnp.where(high, 0.0, total), total)


def join(backward, keep, extra, came, final, after):
    like = shape(keep.shape, F32)
    return run(
        functools.partial(join_kernel, backward, len(came), final), 4 * like.size,
        [VMEM] * (2 + len(came)) + [ANYWHERE] * len(after),
        [VMEM, VMEM] if final else VMEM,
        [like, like] if final else like,
        (keep, extra, *came, *after),
    )


def scan_states(keeps, extras, backward, beside, between):
    plan = scan_plan(lax.axis_size("seq"))
    came = [[] for _ in keeps]
    results, after = [], []
    for stage, (_, _, pairs) in enumerate(plan):
        messages = []
        for keep, extra, arrived in zip(keeps, extras, came):
            message = join(backward, keep, extra, arrived, False, after + messages)
            messages.append(message)
            arrived.append(move(message, pairs, backward))
        mine = beside[stage:] if stage == len(plan) - 1 else beside[stage:stage + 1]
        made = [work(messages) for work in mine]
        after = [item[-1] for item in made]
        results += made
    states, messages, early = [], [], ()
    for keep, extra, arrived in zip(keeps, extras, came):
        token = [*after, *messages, *early[-1:]]
        message, state = join(backward, keep, extra, arrived, True, token)
        states.append(state)
        messages.append(message)
        early = early or between(state, results)
    others = [nearby(message, backward) for message in messages[::-1]][::-1]
    return states, others, results, early


def move(value, pairs, backward):
    count = lax.axis_size("seq")
    if backward:
        pairs = [(count - 1 - a, count - 1 - b) for a, b in pairs]
    return lax.ppermute(value, "seq", pairs)


def nearby(value, backward):
    return move(value, [(r, r ^ 1) for r in range(lax.axis_size("seq"))], backward)


def shards(query, key_in, value, out_grad, gain):
    rows, width = query.shape
    half = width // 2
    heads = half // HEAD_DIM
    chunks = len(chunks_of(rows))
    peers = lax.axis_size("head")
    full = width * peers
    gain = gain.reshape(1, width)
    pin = lambda x: pltpu.with_memory_space_constraint(x, pltpu.HBM)
    query, key_in, value, out_grad = (pin(x) for x in (query, key_in, value, out_grad))
    unit = 2 * rows * half * HEAD_DIM
    partial = functools.partial

    count = heads // PIECE
    states = shape((PIECE, HEAD_DIM, HEAD_DIM), F32)
    inside = shape((chunks, heads, HEAD_DIM, HEAD_DIM), BF16)
    wide = shape((rows, half), F32)
    thin = shape((rows, half), BF16)
    lane_sums = shape((rows, HEAD_DIM), F32)
    whole = shape((rows, width), BF16)
    sems = pltpu.SemaphoreType.DMA((2 * chunks,))

    k1, v1, k2, v2, pre1, *sends = run(
        first_kernel, unit, [HBM, HBM], [VMEM] * (5 + count), [thin] * 4 + [inside] + [states] * count,
        (key_in, value), [sems, sems],
    )
    extras = [nearby(send, False) for send in sends]
    pre2, *keeps = run(
        sum_states, unit, [VMEM, VMEM], [VMEM] * (1 + count), [inside] + [states] * count, (k2, v2)
    )

    def inner_of(same, k, v, pre):
        return lambda messages: run(
            partial(inner_kernel, same), 6 * unit,
            [HBM, HBM, VMEM, VMEM, VMEM, VMEM] + [ANYWHERE] * len(messages), [VMEM] * 5,
            [
                thin, wide, wide,
                shape((half, rows), BF16), shape((heads, rows, rows // chunks), BF16),
            ],
            (query, out_grad, k, v, gain, pre, *messages),
            [pltpu.VMEM((rows, half), BF16), sems],
        )

    piece_wide = shape((rows, PIECE * HEAD_DIM), F32)

    def attn_of(number, inner, state, sums):
        last = number == 2 * count - 1
        return run(
            partial(attn_kernel, number % count, number == 0, last), unit // count,
            [VMEM] * (4 + len(sums)), [VMEM] * (2 if last else 3),
            [piece_wide] + ([shape((-(-chunks // 8) * 16, rows // chunks), F32)] if last else [lane_sums] * 2),
            (*inner, state, *sums),
        )

    state2, state1, made, early = scan_states(
        keeps, extras, False,
        [inner_of(True, k2, v2, pre2), inner_of(False, k1, v1, pre1)],
        lambda state, made: attn_of(0, made[0][:3], state, ()),
    )
    (q2, inner2, scaled2, qturned2, turned2), (q1, inner1, scaled1, qturned1, turned1) = made

    attn, *sums = early
    attns = [attn]
    for number, state in list(enumerate([*state2, *state1]))[1:]:
        inner = (q2, inner2, scaled2) if number < count else (q1, inner1, scaled1)
        attn, *sums = attn_of(number, inner, state, sums)
        attns.append(attn)
    sums = sums[0]
    parts = [sums] + [
        lax.ppermute(sums, "head", [(r, r ^ other) for r in range(peers)])
        for other in range(1, peers)
    ]

    posts = shape((chunks, PIECE, HEAD_DIM, HEAD_DIM), BF16)
    piece_out = [shape((rows, PIECE * HEAD_DIM), BF16), posts, states]

    def grads_of(pieces, first, attns, scaled, qturned):
        fresh = len(first) if first is parts else 0
        shapes = piece_out * len(pieces) + [lane_sums] * (2 if fresh else 0)
        made = run(
            partial(grad_kernel, pieces, full, fresh), unit * len(pieces) // count,
            [VMEM] * (len(first) + 2 + len(pieces)), [VMEM] * len(shapes), shapes,
            (*first, scaled, qturned, *attns),
        )
        return [made[i:i + 3] for i in range(0, 3 * len(pieces), 3)], made[3 * len(pieces):]

    made, factors = grads_of([0], parts, attns[:1], scaled2, qturned2)
    for piece in range(1, count):
        made += grads_of([piece], factors, attns[piece:piece + 1], scaled2, qturned2)[0]
    gs2, posts2, gsends = zip(*made)
    gextras = [nearby(gsend, True) for gsend in gsends]
    made = grads_of(list(range(count)), factors, attns[count:], scaled1, qturned1)[0]
    gs1, posts1, gkeeps = zip(*made)

    first_grads = []

    def local_of(second, *args):
        def work(messages):
            if second:
                specs, scratch = [HBM] + [VMEM] * 3, [pltpu.VMEM((rows, half), BF16), sems]
                shapes = [whole, shape((rows // chunks, half), BF16), wide, wide]
            else:
                specs, scratch, shapes = [VMEM] * 3, [], [thin, wide, wide]
            made = run(
                partial(local_kernel, count, second), 9 * unit,
                [VMEM] * (len(args) + len(first_grads)) + [ANYWHERE] * len(messages),
                specs, shapes, (*args, *first_grads, *messages), scratch,
            )
            first_grads.append(made[0])
            return made

        return work

    piece_thin = shape((rows, PIECE * HEAD_DIM), BF16)

    def final_of(jobs, ready=(), outs=(), fresh=0):
        plan = [item[1:] for item in ready]
        args = [leaf for job in jobs for leaf in job[2]] + [item[0] for item in ready]
        wholes = len(outs) + fresh
        kept = sum(job[1] is None for job in jobs)
        buffers = [pltpu.VMEM(piece_thin.shape, BF16)] * (2 * (len(jobs) - kept))
        return run(
            partial(final_kernel, [job[:2] for job in jobs], wholes, plan),
            2 * unit * len(jobs) // count, [VMEM] * len(args) + [HBM] * len(outs),
            [HBM] * wholes + [VMEM] * (2 * kept), [whole] * wholes + [piece_thin] * (2 * kept),
            (*args, *outs),
            buffers + [pltpu.SemaphoreType.DMA((len(plan) + 2 * chunks * (len(jobs) - kept) + 1,))],
            {len(args) + i: i for i in range(len(outs))},
        )

    gstate1, gstate2, made, early = scan_states(
        gkeeps, gextras, True,
        [
            local_of(0, q1, k1, v1, turned1, pre1, *state1, *gs1, *posts1),
            local_of(1, q2, k2, v2, turned2, pre2, *state2, *gs2, *posts2),
        ],
        lambda state, made: final_of([(0, None, (k1, v1, *made[0][1:], state))]),
    )
    near = (k1, v1, *made[0][1:])
    qgrad, tail, *far = made[1]
    far = (k2, v2, *far)
    every = slice(0, rows)
    jobs = [(i, (False, half, i), (*near, gstate1[i])) for i in range(1, count)]
    jobs += [(i, None, (*far, gstate2[i])) for i in range(count - 1)]
    ready = [(early[i], i, every, (False, half, 0)) for i in range(2)]
    kgrad, vgrad, *done = final_of(jobs, ready, (), 2)
    jobs = [(count - 1, (True, half, count - 1), (*far, gstate2[-1]))]
    ready = [(done[i], 1 + i % 2, every, (True, half, i // 2)) for i in range(len(done))]
    ready.append((tail, 0, chunks_of(rows)[-1], (True, half)))
    qgrad, kgrad, vgrad = final_of(jobs, ready, (qgrad, kgrad, vgrad))
    return qgrad, kgrad, vgrad


def solution(mesh):
    spec = P("seq", "head")
    return jax.shard_map(
        shards,
        mesh=mesh,
        in_specs=(spec, spec, spec, spec, P("head")),
        out_specs=(spec, spec, spec),
        check_vma=False,
    )
```

```python
import functools

import jax
import jax.numpy as jnp
from jax import lax
from jax.experimental import pallas as pl
from jax.experimental.pallas import tpu as pltpu
from jax.sharding import PartitionSpec as P

HEAD_DIM = 128
CHUNK = 256
PIECE = 2
VMEM_BYTES = 12 * 2**20
F32 = jnp.float32
BF16 = jnp.bfloat16
VMEM = pl.BlockSpec(memory_space=pltpu.VMEM)
HBM = pl.BlockSpec(memory_space=pltpu.HBM)
ANYWHERE = pl.BlockSpec(memory_space=pl.ANY)


def dot(a, b, contract_a=1, contract_b=0):
    dims = (((contract_a,), (contract_b,)), ((), ()))
    return lax.dot_general(a, b, dims, preferred_element_type=F32)


def chunks_of(rows):
    size = CHUNK if rows % CHUNK == 0 else rows
    return [slice(i, i + size) for i in range(0, rows, size)]


def shape(dims, dtype):
    return jax.ShapeDtypeStruct(dims, dtype)


def lanes_of(j):
    return slice(j * HEAD_DIM, (j + 1) * HEAD_DIM)


def heads_in(pieces):
    return [ref[j] for ref in pieces for j in range(ref.shape[0])]


def lower(size):
    row = lax.broadcasted_iota(jnp.int32, (size, size), 0)
    return row >= lax.broadcasted_iota(jnp.int32, (size, size), 1)


def upper(size):
    row = lax.broadcasted_iota(jnp.int32, (size, size), 0)
    return row <= lax.broadcasted_iota(jnp.int32, (size, size), 1)


def run(kernel, flops, in_specs, out_specs, out_shape, args, scratch=(), aliases=None):
    nbytes = sum(a.size * a.dtype.itemsize for a, spec in zip(args, in_specs) if spec is HBM)
    return pl.pallas_call(
        kernel,
        in_specs=in_specs,
        out_specs=out_specs,
        out_shape=out_shape,
        scratch_shapes=list(scratch),
        input_output_aliases=aliases or {},
        cost_estimate=pl.CostEstimate(flops=flops, bytes_accessed=nbytes, transcendentals=0),
        compiler_params=pltpu.CompilerParams(vmem_limit_bytes=VMEM_BYTES),
    )(*args)


def columns(same, width, piece=None):
    odd = lax.rem(lax.axis_index("seq"), 2)
    half = odd if same else 1 - odd
    if piece is None:
        return pl.ds(pl.multiple_of(half * width, width), width)
    size = PIECE * HEAD_DIM
    return pl.ds(pl.multiple_of(half * width + piece * size, size), size)


def fetches(sources, targets, sems, same):
    rows, width = targets[0].shape
    lanes = columns(same, width)
    copies = []
    for part in chunks_of(rows):
        for source, target in zip(sources, targets):
            sem = sems.at[len(copies)]
            copies.append(pltpu.make_async_copy(source.at[part, lanes], target.at[part], sem))
    return copies


def sum_states(k_ref, v_ref, pre_ref, *sum_refs, copies=()):
    heads = pre_ref.shape[1]
    totals = [None] * heads
    for i, part in enumerate(chunks_of(k_ref.shape[0])):
        for copy in copies[2 * i:2 * i + 2]:
            copy.wait()
        for j in range(heads):
            term = dot(k_ref[part, lanes_of(j)], v_ref[part, lanes_of(j)], 0, 0)
            if i:
                pre_ref[i, j] = totals[j].astype(BF16)
            else:
                pre_ref[i, j] = jnp.zeros_like(pre_ref[i, j])
            totals[j] = totals[j] + term if i else term
    for j in range(heads):
        sum_refs[j // PIECE][j % PIECE] = totals[j]


def first_kernel(k_hbm, v_hbm, k1, v1, k2, v2, pre_ref, *refs):
    *sum_refs, sems1, sems2 = refs
    now = fetches((k_hbm, v_hbm), (k1, v1), sems1, False)
    later = fetches((k_hbm, v_hbm), (k2, v2), sems2, True)
    for copy in now + later:
        copy.start()
    sum_states(k1, v1, pre_ref, *sum_refs, copies=now)
    for copy in later:
        copy.wait()


def inner_kernel(same, query_ref, og_ref, k_ref, v_ref, gain_ref, pre_ref, *refs):
    q_ref, inner_ref, scaled_ref, qturned_ref, turned_ref = refs[-5:]
    rows, width = q_ref.shape
    odd = lax.rem(lax.axis_index("seq"), 2)
    first = (odd if same else 1 - odd) * width
    gain = gain_ref[:, columns(same, width)]
    for i, part in enumerate(chunks_of(rows)):
        for j in range(width // HEAD_DIM):
            lanes = lanes_of(j)
            source = pl.ds(pl.multiple_of(first + j * HEAD_DIM, HEAD_DIM), HEAD_DIM)
            q, k = query_ref[part, source], k_ref[part, lanes]
            q_ref[part, lanes] = q
            size = q.shape[0]
            scores = jnp.where(lower(size), dot(q, k, 1, 1), 0.0).astype(BF16)
            turned_ref[j, part] = jnp.where(upper(size), dot(k, q, 1, 1), 0.0).astype(BF16)
            inner = dot(scores, v_ref[part, lanes])
            inner_ref[part, lanes] = inner + dot(q, pre_ref[i, j]) if i else inner
            scaled_ref[part, lanes] = gain[:, lanes] * og_ref[part, source].astype(F32)
            qturned_ref[lanes, part] = q.T


def attn_kernel(piece, first, last, q_ref, inner_ref, scaled_ref, state_ref, *refs):
    attn_ref = refs[0] if first else refs[2]
    parts = chunks_of(q_ref.shape[0])
    if last:
        refs[-1][...] = jnp.zeros_like(refs[-1])
    for i, part in enumerate(parts):
        square, cross = (None, None) if first else (refs[0][part], refs[1][part])
        for j in range(PIECE):
            lanes = lanes_of(piece * PIECE + j)
            state = state_ref[j].astype(BF16)
            attn = inner_ref[part, lanes] + dot(q_ref[part, lanes], state)
            attn_ref[part, lanes_of(j)] = attn
            more, crossed = attn * attn, scaled_ref[part, lanes] * attn
            square = more if square is None else square + more
            cross = crossed if cross is None else cross + crossed
        if last:
            refs[-1][2 * i:2 * i + 1] = jnp.sum(square.T, axis=0, keepdims=True)
            refs[-1][2 * i + 1:2 * i + 2] = jnp.sum(cross.T, axis=0, keepdims=True)
        else:
            refs[-2][part] = square
            refs[-1][part] = cross


def factors_kernel(full, parts, inv_ref, slope_ref, refs):
    total = refs[0][...]
    for ref in refs[1:parts]:
        total = total + ref[...]
    rows = []
    for i, _ in enumerate(chunks_of(inv_ref.shape[0])):
        inv = lax.rsqrt(total[2 * i:2 * i + 1] / full + 1e-6)
        rows += [inv, inv * inv * inv * (total[2 * i + 1:2 * i + 2] / full)]
    both = jnp.concatenate(rows + [total[len(rows):]], axis=0).T
    for i, part in enumerate(chunks_of(inv_ref.shape[0])):
        wide = (both.shape[0], HEAD_DIM)
        inv_ref[part] = jnp.broadcast_to(both[:, 2 * i:2 * i + 1], wide)
        slope_ref[part] = jnp.broadcast_to(both[:, 2 * i + 1:2 * i + 2], wide)


def grad_kernel(pieces, full, parts, *refs):
    if parts:
        inv_ref, slope_ref = refs[-2:]
        factors_kernel(full, parts, inv_ref, slope_ref, refs)
        refs = refs[parts:-2]
    else:
        inv_ref, slope_ref = refs[:2]
        refs = refs[2:]
    scaled_ref, qturned_ref = refs[:2]
    count = len(pieces)
    attns, outs = refs[2:2 + count], refs[2 + count:]
    for attn_ref, piece, at in zip(attns, pieces, range(0, 3 * count, 3)):
        g_ref, post_ref, sum_ref = outs[at:at + 3]
        totals = [None] * PIECE
        for i, part in reversed(list(enumerate(chunks_of(g_ref.shape[0])))):
            for j in range(PIECE):
                lanes = lanes_of(piece * PIECE + j)
                attn = attn_ref[part, lanes_of(j)]
                grad = inv_ref[part] * scaled_ref[part, lanes] - attn * slope_ref[part]
                grad = grad.astype(BF16)
                g_ref[part, lanes_of(j)] = grad
                term = dot(qturned_ref[lanes, part], grad)
                if totals[j] is None:
                    post_ref[i, j] = jnp.zeros_like(post_ref[i, j])
                    totals[j] = term
                else:
                    post_ref[i, j] = totals[j].astype(BF16)
                    totals[j] = totals[j] + term
        for j in range(PIECE):
            sum_ref[j] = totals[j]


def local_kernel(pieces, second, q_ref, k_ref, v_ref, turned_ref, pre_ref, *refs):
    if second:
        qgrad_hbm, tail_ref, kpart_ref, vpart_ref, qgrad_ref, sems = refs[-6:]
    else:
        qgrad_ref, kpart_ref, vpart_ref = refs[-3:]
    state = heads_in(refs[:pieces])
    g_refs, post_refs = refs[pieces:2 * pieces], refs[2 * pieces:3 * pieces]
    rows, width = q_ref.shape
    parts = chunks_of(rows)
    copies = []

    def send(source, same, part):
        target = qgrad_hbm.at[part, columns(same, width)]
        copies.append(pltpu.make_async_copy(source, target, sems.at[len(copies)]))
        copies[-1].start()

    if second:
        send(refs[3 * pieces], False, slice(0, rows))

    def scores(i, j):
        part, lanes = parts[i], lanes_of(j)
        v, g = v_ref[part, lanes], g_refs[j // PIECE][part, lanes_of(j % PIECE)]
        size = g.shape[0]
        gscores = jnp.where(lower(size), dot(g, v, 1, 1), 0.0).astype(BF16)
        gturned = jnp.where(upper(size), dot(v, g, 1, 1), 0.0).astype(BF16)
        return gscores, gturned

    def products(i, j, gscores, gturned):
        part, lanes = parts[i], lanes_of(j)
        q, k, v = (ref[part, lanes] for ref in (q_ref, k_ref, v_ref))
        g = g_refs[j // PIECE][part, lanes_of(j % PIECE)]
        before = state[j] + pre_ref[i, j].astype(F32) if i else state[j]
        qgrad = dot(g, before.astype(BF16), 1, 1) + dot(gscores, k)
        kgrad = dot(gturned, q)
        vgrad = dot(turned_ref[j, part], g)
        if i < len(parts) - 1:
            post = post_refs[j // PIECE][i, j % PIECE]
            kgrad = kgrad + dot(v, post, 1, 1)
            vgrad = vgrad + dot(k, post)
        if second and i == len(parts) - 1:
            tail_ref[:, lanes] = qgrad.astype(BF16)
        else:
            qgrad_ref[part, lanes] = qgrad.astype(BF16)
        kpart_ref[part, lanes] = kgrad
        vpart_ref[part, lanes] = vgrad

    places = [(i, j) for i in range(len(parts)) for j in range(width // HEAD_DIM)]
    ready = scores(*places[0])
    for place, following in zip(places, places[1:] + [None]):
        coming = scores(*following) if following else None
        products(*place, *ready)
        ready = coming
        if second and following and following[0] != place[0]:
            part = parts[place[0]]
            send(qgrad_ref.at[part], True, part)
    for copy in copies:
        copy.wait()


def final_part(piece, part, k_ref, v_ref, kpart_ref, vpart_ref, state_ref, kgrad_ref, vgrad_ref):
    for j in range(PIECE):
        lanes = lanes_of(piece * PIECE + j)
        state = state_ref[j].astype(BF16)
        kgrad = kpart_ref[part, lanes] + dot(v_ref[part, lanes], state, 1, 1)
        vgrad = vpart_ref[part, lanes] + dot(k_ref[part, lanes], state)
        kgrad_ref[part, lanes_of(j)] = kgrad.astype(BF16)
        vgrad_ref[part, lanes_of(j)] = vgrad.astype(BF16)


def final_kernel(jobs, wholes, plan, *refs):
    inputs = [refs[5 * i:5 * i + 5] for i in range(len(jobs))]
    refs = refs[5 * len(jobs):]
    sources, refs = refs[:len(plan)], refs[len(plan):]
    results, sems = refs[-1 - 2 * len(jobs):-1], refs[-1]
    outs = refs[:-1 - 2 * len(jobs)]
    outs = outs[len(outs) - wholes:]
    rows, copies = inputs[0][0].shape[0], []

    def send(source, out, part, place):
        target = outs[out].at[part, columns(*place)]
        copies.append(pltpu.make_async_copy(source, target, sems.at[len(copies)]))
        copies[-1].start()

    for source, (out, part, place) in zip(sources, plan):
        send(source, out, part, place)
    kept = [i for i, (_, place) in enumerate(jobs) if place is None]
    order = kept + [i for i in range(len(jobs)) if i not in kept]
    for i, (piece, place) in enumerate(jobs):
        at = 2 * order.index(i)
        kgrad_ref, vgrad_ref = results[at:at + 2]
        for part in chunks_of(rows):
            final_part(piece, part, *inputs[i], kgrad_ref, vgrad_ref)
            if place:
                send(kgrad_ref.at[part], -2, part, place)
                send(vgrad_ref.at[part], -1, part, place)
    for copy in copies:
        copy.wait()


def scan_plan(count):
    bits = count.bit_length() - 1
    stages = []
    for stage in range(bits - 1):
        rising, falling = 1 + stage, bits - 1 - stage
        pairs = [(r, r ^ (1 << (falling if r & 1 else rising))) for r in range(count)]
        stages.append((rising, falling, pairs))
    return stages


def join_kernel(backward, done, final, *refs):
    count = lax.axis_size("seq")
    rank = lax.axis_index("seq")
    if backward:
        rank = count - 1 - rank
    odd = (rank & 1) == 1
    plan = scan_plan(count)
    keep, extra = (ref[...] for ref in refs[:2])
    came = refs[2:2 + done]
    total = keep + extra
    before = jnp.zeros_like(total)
    for (rising, falling, _), ref in zip(plan, came):
        high = (jnp.where(odd, rank >> falling, rank >> rising) & 1) == 1
        value = ref[...]
        before = before + jnp.where(odd | high, value, 0.0)
        total = total + jnp.where(odd, 0.0, value)
    if final:
        message_ref, state_ref = refs[-2:]
        message_ref[...] = before + jnp.where(odd, 0.0, keep)
        state_ref[...] = before + jnp.where(odd, extra, 0.0)
    else:
        rising, falling, _ = plan[done]
        high = (jnp.where(odd, rank >> falling, rank >> rising) & 1) == 1
        refs[-1][...] = jnp.where(odd, before + jnp.where(high, 0.0, total), total)


def join(backward, keep, extra, came, final, after):
    like = shape(keep.shape, F32)
    return run(
        functools.partial(join_kernel, backward, len(came), final), 4 * like.size,
        [VMEM] * (2 + len(came)) + [ANYWHERE] * len(after),
        [VMEM, VMEM] if final else VMEM,
        [like, like] if final else like,
        (keep, extra, *came, *after),
    )


def scan_states(keeps, extras, backward, beside, between):
    plan = scan_plan(lax.axis_size("seq"))
    came = [[] for _ in keeps]
    results, after = [], []
    for stage, (_, _, pairs) in enumerate(plan):
        messages = []
        for keep, extra, arrived in zip(keeps, extras, came):
            message = join(backward, keep, extra, arrived, False, after + messages)
            messages.append(message)
            arrived.append(move(message, pairs, backward))
        mine = beside[stage:] if stage == len(plan) - 1 else beside[stage:stage + 1]
        made = [work(messages) for work in mine]
        after = [item[-1] for item in made]
        results += made
    states, messages, early = [], [], ()
    for keep, extra, arrived in zip(keeps, extras, came):
        token = [*after, *messages, *early[-1:]]
        message, state = join(backward, keep, extra, arrived, True, token)
        states.append(state)
        messages.append(message)
        early = early or between(state, results)
    others = [nearby(message, backward) for message in messages[::-1]][::-1]
    return states, others, results, early


def move(value, pairs, backward):
    count = lax.axis_size("seq")
    if backward:
        pairs = [(count - 1 - a, count - 1 - b) for a, b in pairs]
    return lax.ppermute(value, "seq", pairs)


def nearby(value, backward):
    return move(value, [(r, r ^ 1) for r in range(lax.axis_size("seq"))], backward)


def shards(query, key_in, value, out_grad, gain):
    rows, width = query.shape
    half = width // 2
    heads = half // HEAD_DIM
    chunks = len(chunks_of(rows))
    peers = lax.axis_size("head")
    full = width * peers
    gain = gain.reshape(1, width)
    pin = lambda x: pltpu.with_memory_space_constraint(x, pltpu.HBM)
    key_in, value = pin(key_in), pin(value)
    unit = 2 * rows * half * HEAD_DIM
    partial = functools.partial

    count = heads // PIECE
    states = shape((PIECE, HEAD_DIM, HEAD_DIM), F32)
    inside = shape((chunks, heads, HEAD_DIM, HEAD_DIM), BF16)
    wide = shape((rows, half), F32)
    thin = shape((rows, half), BF16)
    lane_sums = shape((rows, HEAD_DIM), F32)
    whole = shape((rows, width), BF16)
    sems = pltpu.SemaphoreType.DMA((2 * chunks,))

    k1, v1, k2, v2, pre1, *sends = run(
        first_kernel, unit, [HBM, HBM], [VMEM] * (5 + count), [thin] * 4 + [inside] + [states] * count,
        (key_in, value), [sems, sems],
    )
    extras = [nearby(send, False) for send in sends]
    pre2, *keeps = run(
        sum_states, unit, [VMEM, VMEM], [VMEM] * (1 + count), [inside] + [states] * count, (k2, v2)
    )

    def inner_of(same, k, v, pre):
        return lambda messages: run(
            partial(inner_kernel, same), 6 * unit,
            [VMEM] * 6 + [ANYWHERE] * len(messages), [VMEM] * 5,
            [
                thin, wide, wide,
                shape((half, rows), BF16), shape((heads, rows, rows // chunks), BF16),
            ],
            (query, out_grad, k, v, gain, pre, *messages),
        )

    piece_wide = shape((rows, PIECE * HEAD_DIM), F32)

    def attn_of(number, inner, state, sums):
        last = number == 2 * count - 1
        return run(
            partial(attn_kernel, number % count, number == 0, last), unit // count,
            [VMEM] * (4 + len(sums)), [VMEM] * (2 if last else 3),
            [piece_wide] + ([shape((-(-chunks // 4) * 8, rows // chunks), F32)] if last else [lane_sums] * 2),
            (*inner, state, *sums),
        )

    state2, state1, made, early = scan_states(
        keeps, extras, False,
        [inner_of(True, k2, v2, pre2), inner_of(False, k1, v1, pre1)],
        lambda state, made: attn_of(0, made[0][:3], state, ()),
    )
    (q2, inner2, scaled2, qturned2, turned2), (q1, inner1, scaled1, qturned1, turned1) = made

    attn, *sums = early
    attns = [attn]
    for number, state in list(enumerate([*state2, *state1]))[1:]:
        inner = (q2, inner2, scaled2) if number < count else (q1, inner1, scaled1)
        attn, *sums = attn_of(number, inner, state, sums)
        attns.append(attn)
    sums = sums[0]
    parts = [sums] + [
        lax.ppermute(sums, "head", [(r, r ^ other) for r in range(peers)])
        for other in range(1, peers)
    ]

    posts = shape((chunks, PIECE, HEAD_DIM, HEAD_DIM), BF16)
    piece_out = [shape((rows, PIECE * HEAD_DIM), BF16), posts, states]

    def grads_of(pieces, first, attns, scaled, qturned):
        fresh = len(first) if first is parts else 0
        shapes = piece_out * len(pieces) + [lane_sums] * (2 if fresh else 0)
        made = run(
            partial(grad_kernel, pieces, full, fresh), unit * len(pieces) // count,
            [VMEM] * (len(first) + 2 + len(pieces)), [VMEM] * len(shapes), shapes,
            (*first, scaled, qturned, *attns),
        )
        return [made[i:i + 3] for i in range(0, 3 * len(pieces), 3)], made[3 * len(pieces):]

    made, factors = grads_of([0], parts, attns[:1], scaled2, qturned2)
    for piece in range(1, count):
        made += grads_of([piece], factors, attns[piece:piece + 1], scaled2, qturned2)[0]
    gs2, posts2, gsends = zip(*made)
    gextras = [nearby(gsend, True) for gsend in gsends]
    made = grads_of(list(range(count)), factors, attns[count:], scaled1, qturned1)[0]
    gs1, posts1, gkeeps = zip(*made)

    first_grads = []

    def local_of(second, *args):
        def work(messages):
            if second:
                specs, scratch = [HBM] + [VMEM] * 3, [pltpu.VMEM((rows, half), BF16), sems]
                shapes = [whole, shape((rows // chunks, half), BF16), wide, wide]
            else:
                specs, scratch, shapes = [VMEM] * 3, [], [thin, wide, wide]
            made = run(
                partial(local_kernel, count, second), 9 * unit,
                [VMEM] * (len(args) + len(first_grads)) + [ANYWHERE] * len(messages),
                specs, shapes, (*args, *first_grads, *messages), scratch,
            )
            first_grads.append(made[0])
            return made

        return work

    piece_thin = shape((rows, PIECE * HEAD_DIM), BF16)

    def final_of(jobs, ready=(), outs=(), fresh=0):
        plan = [item[1:] for item in ready]
        args = [leaf for job in jobs for leaf in job[2]] + [item[0] for item in ready]
        wholes = len(outs) + fresh
        kept = sum(job[1] is None for job in jobs)
        buffers = [pltpu.VMEM(piece_thin.shape, BF16)] * (2 * (len(jobs) - kept))
        return run(
            partial(final_kernel, [job[:2] for job in jobs], wholes, plan),
            2 * unit * len(jobs) // count, [VMEM] * len(args) + [HBM] * len(outs),
            [HBM] * wholes + [VMEM] * (2 * kept), [whole] * wholes + [piece_thin] * (2 * kept),
            (*args, *outs),
            buffers + [pltpu.SemaphoreType.DMA((len(plan) + 2 * chunks * (len(jobs) - kept) + 1,))],
            {len(args) + i: i for i in range(len(outs))},
        )

    gstate1, gstate2, made, early = scan_states(
        gkeeps, gextras, True,
        [
            local_of(0, q1, k1, v1, turned1, pre1, *state1, *gs1, *posts1),
            local_of(1, q2, k2, v2, turned2, pre2, *state2, *gs2, *posts2),
        ],
        lambda state, made: final_of([(0, None, (k1, v1, *made[0][1:], state))]),
    )
    near = (k1, v1, *made[0][1:])
    qgrad, tail, *far = made[1]
    far = (k2, v2, *far)
    every = slice(0, rows)
    jobs = [(i, (False, half, i), (*near, gstate1[i])) for i in range(1, count)]
    jobs += [(i, None, (*far, gstate2[i])) for i in range(count - 1)]
    ready = [(early[i], i, every, (False, half, 0)) for i in range(2)]
    kgrad, vgrad, *done = final_of(jobs, ready, (), 2)
    jobs = [(count - 1, (True, half, count - 1), (*far, gstate2[-1]))]
    ready = [(done[i], 1 + i % 2, every, (True, half, i // 2)) for i in range(len(done))]
    ready.append((tail, 0, chunks_of(rows)[-1], (True, half)))
    qgrad, kgrad, vgrad = final_of(jobs, ready, (qgrad, kgrad, vgrad))
    return qgrad, kgrad, vgrad


def solution(mesh):
    spec = P("seq", "head")
    return jax.shard_map(
        shards,
        mesh=mesh,
        in_specs=(spec, spec, spec, spec, P("head")),
        out_specs=(spec, spec, spec),
        check_vma=False,
    )
```

```python
import functools

import jax
import jax.numpy as jnp
from jax import lax
from jax.experimental import pallas as pl
from jax.experimental.pallas import tpu as pltpu
from jax.sharding import PartitionSpec as P

HEAD_DIM = 128
CHUNK = 256
PIECE = 2
VMEM_BYTES = 12 * 2**20
F32 = jnp.float32
BF16 = jnp.bfloat16
VMEM = pl.BlockSpec(memory_space=pltpu.VMEM)
HBM = pl.BlockSpec(memory_space=pltpu.HBM)
ANYWHERE = pl.BlockSpec(memory_space=pl.ANY)


def dot(a, b, contract_a=1, contract_b=0):
    dims = (((contract_a,), (contract_b,)), ((), ()))
    return lax.dot_general(a, b, dims, preferred_element_type=F32)


def chunks_of(rows):
    size = CHUNK if rows % CHUNK == 0 else rows
    return [slice(i, i + size) for i in range(0, rows, size)]


def shape(dims, dtype):
    return jax.ShapeDtypeStruct(dims, dtype)


def lanes_of(j):
    return slice(j * HEAD_DIM, (j + 1) * HEAD_DIM)


def heads_in(pieces):
    return [ref[j] for ref in pieces for j in range(ref.shape[0])]


def lower(size):
    row = lax.broadcasted_iota(jnp.int32, (size, size), 0)
    return row >= lax.broadcasted_iota(jnp.int32, (size, size), 1)


def upper(size):
    row = lax.broadcasted_iota(jnp.int32, (size, size), 0)
    return row <= lax.broadcasted_iota(jnp.int32, (size, size), 1)


def run(kernel, flops, in_specs, out_specs, out_shape, args, scratch=(), aliases=None):
    nbytes = sum(a.size * a.dtype.itemsize for a, spec in zip(args, in_specs) if spec is HBM)
    return pl.pallas_call(
        kernel,
        in_specs=in_specs,
        out_specs=out_specs,
        out_shape=out_shape,
        scratch_shapes=list(scratch),
        input_output_aliases=aliases or {},
        cost_estimate=pl.CostEstimate(flops=flops, bytes_accessed=nbytes, transcendentals=0),
        compiler_params=pltpu.CompilerParams(vmem_limit_bytes=VMEM_BYTES),
    )(*args)


def columns(same, width, piece=None):
    odd = lax.rem(lax.axis_index("seq"), 2)
    half = odd if same else 1 - odd
    if piece is None:
        return pl.ds(pl.multiple_of(half * width, width), width)
    size = PIECE * HEAD_DIM
    return pl.ds(pl.multiple_of(half * width + piece * size, size), size)


def fetches(sources, targets, sems, same):
    rows, width = targets[0].shape
    lanes = columns(same, width)
    copies = []
    for part in chunks_of(rows):
        for source, target in zip(sources, targets):
            sem = sems.at[len(copies)]
            copies.append(pltpu.make_async_copy(source.at[part, lanes], target.at[part], sem))
    return copies


def sum_states(k_ref, v_ref, pre_ref, *sum_refs, copies=()):
    heads = pre_ref.shape[1]
    totals = [None] * heads
    for i, part in enumerate(chunks_of(k_ref.shape[0])):
        for copy in copies[2 * i:2 * i + 2]:
            copy.wait()
        for j in range(heads):
            term = dot(k_ref[part, lanes_of(j)], v_ref[part, lanes_of(j)], 0, 0)
            if i:
                pre_ref[i, j] = totals[j].astype(BF16)
            else:
                pre_ref[i, j] = jnp.zeros_like(pre_ref[i, j])
            totals[j] = totals[j] + term if i else term
    for j in range(heads):
        sum_refs[j // PIECE][j % PIECE] = totals[j]


def first_kernel(k_hbm, v_hbm, k1, v1, pre_ref, *refs):
    *sum_refs, sems = refs
    copies = fetches((k_hbm, v_hbm), (k1, v1), sems, False)
    for copy in copies:
        copy.start()
    sum_states(k1, v1, pre_ref, *sum_refs, copies=copies)


def second_kernel(key_ref, value_ref, k2, v2, pre_ref, *sum_refs):
    rows, width = k2.shape
    first = lax.rem(lax.axis_index("seq"), 2) * width
    for part in chunks_of(rows):
        for j in range(width // HEAD_DIM):
            source = pl.ds(pl.multiple_of(first + j * HEAD_DIM, HEAD_DIM), HEAD_DIM)
            k2[part, lanes_of(j)] = key_ref[part, source]
            v2[part, lanes_of(j)] = value_ref[part, source]
    sum_states(k2, v2, pre_ref, *sum_refs)


def inner_kernel(same, query_ref, og_ref, k_ref, v_ref, gain_ref, pre_ref, *refs):
    q_ref, inner_ref, scaled_ref, qturned_ref, turned_ref = refs[-5:]
    rows, width = q_ref.shape
    odd = lax.rem(lax.axis_index("seq"), 2)
    first = (odd if same else 1 - odd) * width
    gain = gain_ref[:, columns(same, width)]
    for i, part in enumerate(chunks_of(rows)):
        for j in range(width // HEAD_DIM):
            lanes = lanes_of(j)
            source = pl.ds(pl.multiple_of(first + j * HEAD_DIM, HEAD_DIM), HEAD_DIM)
            q, k = query_ref[part, source], k_ref[part, lanes]
            q_ref[part, lanes] = q
            size = q.shape[0]
            scores = jnp.where(lower(size), dot(q, k, 1, 1), 0.0).astype(BF16)
            turned_ref[j, part] = jnp.where(upper(size), dot(k, q, 1, 1), 0.0).astype(BF16)
            inner = dot(scores, v_ref[part, lanes])
            inner_ref[part, lanes] = inner + dot(q, pre_ref[i, j]) if i else inner
            scaled_ref[part, lanes] = gain[:, lanes] * og_ref[part, source].astype(F32)
            qturned_ref[lanes, part] = q.T


def attn_kernel(piece, first, last, q_ref, inner_ref, scaled_ref, state_ref, *refs):
    attn_ref = refs[0] if first else refs[2]
    parts = chunks_of(q_ref.shape[0])
    if last:
        refs[-1][...] = jnp.zeros_like(refs[-1])
    for i, part in enumerate(parts):
        square, cross = (None, None) if first else (refs[0][part], refs[1][part])
        for j in range(PIECE):
            lanes = lanes_of(piece * PIECE + j)
            state = state_ref[j].astype(BF16)
            attn = inner_ref[part, lanes] + dot(q_ref[part, lanes], state)
            attn_ref[part, lanes_of(j)] = attn
            more, crossed = attn * attn, scaled_ref[part, lanes] * attn
            square = more if square is None else square + more
            cross = crossed if cross is None else cross + crossed
        if last:
            refs[-1][2 * i:2 * i + 1] = jnp.sum(square.T, axis=0, keepdims=True)
            refs[-1][2 * i + 1:2 * i + 2] = jnp.sum(cross.T, axis=0, keepdims=True)
        else:
            refs[-2][part] = square
            refs[-1][part] = cross


def factors_kernel(full, parts, inv_ref, slope_ref, refs):
    total = refs[0][...]
    for ref in refs[1:parts]:
        total = total + ref[...]
    rows = []
    for i, _ in enumerate(chunks_of(inv_ref.shape[0])):
        inv = lax.rsqrt(total[2 * i:2 * i + 1] / full + 1e-6)
        rows += [inv, inv * inv * inv * (total[2 * i + 1:2 * i + 2] / full)]
    both = jnp.concatenate(rows + [total[len(rows):]], axis=0).T
    for i, part in enumerate(chunks_of(inv_ref.shape[0])):
        wide = (both.shape[0], HEAD_DIM)
        inv_ref[part] = jnp.broadcast_to(both[:, 2 * i:2 * i + 1], wide)
        slope_ref[part] = jnp.broadcast_to(both[:, 2 * i + 1:2 * i + 2], wide)


def grad_kernel(pieces, full, parts, *refs):
    if parts:
        inv_ref, slope_ref = refs[-2:]
        factors_kernel(full, parts, inv_ref, slope_ref, refs)
        refs = refs[parts:-2]
    else:
        inv_ref, slope_ref = refs[:2]
        refs = refs[2:]
    scaled_ref, qturned_ref = refs[:2]
    count = len(pieces)
    attns, outs = refs[2:2 + count], refs[2 + count:]
    for attn_ref, piece, at in zip(attns, pieces, range(0, 3 * count, 3)):
        g_ref, post_ref, sum_ref = outs[at:at + 3]
        totals = [None] * PIECE
        for i, part in reversed(list(enumerate(chunks_of(g_ref.shape[0])))):
            for j in range(PIECE):
                lanes = lanes_of(piece * PIECE + j)
                attn = attn_ref[part, lanes_of(j)]
                grad = inv_ref[part] * scaled_ref[part, lanes] - attn * slope_ref[part]
                grad = grad.astype(BF16)
                g_ref[part, lanes_of(j)] = grad
                term = dot(qturned_ref[lanes, part], grad)
                if totals[j] is None:
                    post_ref[i, j] = jnp.zeros_like(post_ref[i, j])
                    totals[j] = term
                else:
                    post_ref[i, j] = totals[j].astype(BF16)
                    totals[j] = totals[j] + term
        for j in range(PIECE):
            sum_ref[j] = totals[j]


def local_kernel(pieces, second, q_ref, k_ref, v_ref, turned_ref, pre_ref, *refs):
    if second:
        qgrad_hbm, tail_ref, kpart_ref, vpart_ref, qgrad_ref, sems = refs[-6:]
    else:
        qgrad_ref, kpart_ref, vpart_ref = refs[-3:]
    state = heads_in(refs[:pieces])
    g_refs, post_refs = refs[pieces:2 * pieces], refs[2 * pieces:3 * pieces]
    rows, width = q_ref.shape
    parts = chunks_of(rows)
    copies = []

    def send(source, same, part):
        target = qgrad_hbm.at[part, columns(same, width)]
        copies.append(pltpu.make_async_copy(source, target, sems.at[len(copies)]))
        copies[-1].start()

    if second:
        send(refs[3 * pieces], False, slice(0, rows))

    def scores(i, j):
        part, lanes = parts[i], lanes_of(j)
        v, g = v_ref[part, lanes], g_refs[j // PIECE][part, lanes_of(j % PIECE)]
        size = g.shape[0]
        gscores = jnp.where(lower(size), dot(g, v, 1, 1), 0.0).astype(BF16)
        gturned = jnp.where(upper(size), dot(v, g, 1, 1), 0.0).astype(BF16)
        return gscores, gturned

    def products(i, j, gscores, gturned):
        part, lanes = parts[i], lanes_of(j)
        q, k, v = (ref[part, lanes] for ref in (q_ref, k_ref, v_ref))
        g = g_refs[j // PIECE][part, lanes_of(j % PIECE)]
        before = state[j] + pre_ref[i, j].astype(F32) if i else state[j]
        qgrad = dot(g, before.astype(BF16), 1, 1) + dot(gscores, k)
        kgrad = dot(gturned, q)
        vgrad = dot(turned_ref[j, part], g)
        if i < len(parts) - 1:
            post = post_refs[j // PIECE][i, j % PIECE]
            kgrad = kgrad + dot(v, post, 1, 1)
            vgrad = vgrad + dot(k, post)
        if second and i == len(parts) - 1:
            tail_ref[:, lanes] = qgrad.astype(BF16)
        else:
            qgrad_ref[part, lanes] = qgrad.astype(BF16)
        kpart_ref[part, lanes] = kgrad
        vpart_ref[part, lanes] = vgrad

    places = [(i, j) for i in range(len(parts)) for j in range(width // HEAD_DIM)]
    ready = scores(*places[0])
    for place, following in zip(places, places[1:] + [None]):
        coming = scores(*following) if following else None
        products(*place, *ready)
        ready = coming
        if second and following and following[0] != place[0]:
            part = parts[place[0]]
            send(qgrad_ref.at[part], True, part)
    for copy in copies:
        copy.wait()


def final_part(piece, part, k_ref, v_ref, kpart_ref, vpart_ref, state_ref, kgrad_ref, vgrad_ref):
    for j in range(PIECE):
        lanes = lanes_of(piece * PIECE + j)
        state = state_ref[j].astype(BF16)
        kgrad = kpart_ref[part, lanes] + dot(v_ref[part, lanes], state, 1, 1)
        vgrad = vpart_ref[part, lanes] + dot(k_ref[part, lanes], state)
        kgrad_ref[part, lanes_of(j)] = kgrad.astype(BF16)
        vgrad_ref[part, lanes_of(j)] = vgrad.astype(BF16)


def final_kernel(jobs, wholes, plan, *refs):
    inputs = [refs[5 * i:5 * i + 5] for i in range(len(jobs))]
    refs = refs[5 * len(jobs):]
    sources, refs = refs[:len(plan)], refs[len(plan):]
    results, sems = refs[-1 - 2 * len(jobs):-1], refs[-1]
    outs = refs[:-1 - 2 * len(jobs)]
    outs = outs[len(outs) - wholes:]
    rows, copies = inputs[0][0].shape[0], []

    def send(source, out, part, place):
        target = outs[out].at[part, columns(*place)]
        copies.append(pltpu.make_async_copy(source, target, sems.at[len(copies)]))
        copies[-1].start()

    for source, (out, part, place) in zip(sources, plan):
        send(source, out, part, place)
    kept = [i for i, (_, place) in enumerate(jobs) if place is None]
    order = kept + [i for i in range(len(jobs)) if i not in kept]
    for i, (piece, place) in enumerate(jobs):
        at = 2 * order.index(i)
        kgrad_ref, vgrad_ref = results[at:at + 2]
        for part in chunks_of(rows):
            final_part(piece, part, *inputs[i], kgrad_ref, vgrad_ref)
            if place:
                send(kgrad_ref.at[part], -2, part, place)
                send(vgrad_ref.at[part], -1, part, place)
    for copy in copies:
        copy.wait()


def scan_plan(count):
    bits = count.bit_length() - 1
    stages = []
    for stage in range(bits - 1):
        rising, falling = 1 + stage, bits - 1 - stage
        pairs = [(r, r ^ (1 << (falling if r & 1 else rising))) for r in range(count)]
        stages.append((rising, falling, pairs))
    return stages


def join_kernel(backward, done, final, *refs):
    count = lax.axis_size("seq")
    rank = lax.axis_index("seq")
    if backward:
        rank = count - 1 - rank
    odd = (rank & 1) == 1
    plan = scan_plan(count)
    keep, extra = (ref[...] for ref in refs[:2])
    came = refs[2:2 + done]
    total = keep + extra
    before = jnp.zeros_like(total)
    for (rising, falling, _), ref in zip(plan, came):
        high = (jnp.where(odd, rank >> falling, rank >> rising) & 1) == 1
        value = ref[...]
        before = before + jnp.where(odd | high, value, 0.0)
        total = total + jnp.where(odd, 0.0, value)
    if final:
        message_ref, state_ref = refs[-2:]
        message_ref[...] = before + jnp.where(odd, 0.0, keep)
        state_ref[...] = before + jnp.where(odd, extra, 0.0)
    else:
        rising, falling, _ = plan[done]
        high = (jnp.where(odd, rank >> falling, rank >> rising) & 1) == 1
        refs[-1][...] = jnp.where(odd, before + jnp.where(high, 0.0, total), total)


def join(backward, keep, extra, came, final, after):
    like = shape(keep.shape, F32)
    return run(
        functools.partial(join_kernel, backward, len(came), final), 4 * like.size,
        [VMEM] * (2 + len(came)) + [ANYWHERE] * len(after),
        [VMEM, VMEM] if final else VMEM,
        [like, like] if final else like,
        (keep, extra, *came, *after),
    )


def scan_states(keeps, extras, backward, beside, between):
    plan = scan_plan(lax.axis_size("seq"))
    came = [[] for _ in keeps]
    results, after = [], []
    for stage, (_, _, pairs) in enumerate(plan):
        messages = []
        for keep, extra, arrived in zip(keeps, extras, came):
            message = join(backward, keep, extra, arrived, False, after + messages)
            messages.append(message)
            arrived.append(move(message, pairs, backward))
        mine = beside[stage:] if stage == len(plan) - 1 else beside[stage:stage + 1]
        made = [work(messages) for work in mine]
        after = [item[-1] for item in made]
        results += made
    states, messages, early = [], [], ()
    for keep, extra, arrived in zip(keeps, extras, came):
        token = [*after, *messages, *early[-1:]]
        message, state = join(backward, keep, extra, arrived, True, token)
        states.append(state)
        messages.append(message)
        early = early or between(state, results)
    others = [nearby(message, backward) for message in messages[::-1]][::-1]
    return states, others, results, early


def move(value, pairs, backward):
    count = lax.axis_size("seq")
    if backward:
        pairs = [(count - 1 - a, count - 1 - b) for a, b in pairs]
    return lax.ppermute(value, "seq", pairs)


def nearby(value, backward):
    return move(value, [(r, r ^ 1) for r in range(lax.axis_size("seq"))], backward)


def shards(query, key_in, value, out_grad, gain):
    rows, width = query.shape
    half = width // 2
    heads = half // HEAD_DIM
    chunks = len(chunks_of(rows))
    peers = lax.axis_size("head")
    full = width * peers
    gain = gain.reshape(1, width)
    pin = lambda x: pltpu.with_memory_space_constraint(x, pltpu.HBM)
    unit = 2 * rows * half * HEAD_DIM
    partial = functools.partial

    count = heads // PIECE
    states = shape((PIECE, HEAD_DIM, HEAD_DIM), F32)
    inside = shape((chunks, heads, HEAD_DIM, HEAD_DIM), BF16)
    wide = shape((rows, half), F32)
    thin = shape((rows, half), BF16)
    lane_sums = shape((rows, HEAD_DIM), F32)
    whole = shape((rows, width), BF16)
    sems = pltpu.SemaphoreType.DMA((2 * chunks,))

    shapes = [thin, thin, inside] + [states] * count
    k1, v1, pre1, *sends = run(
        first_kernel, unit, [HBM, HBM], [VMEM] * len(shapes), shapes,
        (pin(key_in), pin(value)), [sems],
    )
    extras = [nearby(send, False) for send in sends]
    k2, v2, pre2, *keeps = run(
        second_kernel, unit, [VMEM, VMEM], [VMEM] * len(shapes), shapes, (key_in, value)
    )

    def inner_of(same, k, v, pre):
        return lambda messages: run(
            partial(inner_kernel, same), 6 * unit,
            [VMEM] * 6 + [ANYWHERE] * len(messages), [VMEM] * 5,
            [
                thin, wide, wide,
                shape((half, rows), BF16), shape((heads, rows, rows // chunks), BF16),
            ],
            (query, out_grad, k, v, gain, pre, *messages),
        )

    piece_wide = shape((rows, PIECE * HEAD_DIM), F32)

    def attn_of(number, inner, state, sums):
        last = number == 2 * count - 1
        return run(
            partial(attn_kernel, number % count, number == 0, last), unit // count,
            [VMEM] * (4 + len(sums)), [VMEM] * (2 if last else 3),
            [piece_wide] + ([shape((-(-chunks // 4) * 8, rows // chunks), F32)] if last else [lane_sums] * 2),
            (*inner, state, *sums),
        )

    state2, state1, made, early = scan_states(
        keeps, extras, False,
        [inner_of(True, k2, v2, pre2), inner_of(False, k1, v1, pre1)],
        lambda state, made: attn_of(0, made[0][:3], state, ()),
    )
    (q2, inner2, scaled2, qturned2, turned2), (q1, inner1, scaled1, qturned1, turned1) = made

    attn, *sums = early
    attns = [attn]
    for number, state in list(enumerate([*state2, *state1]))[1:]:
        inner = (q2, inner2, scaled2) if number < count else (q1, inner1, scaled1)
        attn, *sums = attn_of(number, inner, state, sums)
        attns.append(attn)
    sums = sums[0]
    parts = [sums] + [
        lax.ppermute(sums, "head", [(r, r ^ other) for r in range(peers)])
        for other in range(1, peers)
    ]

    posts = shape((chunks, PIECE, HEAD_DIM, HEAD_DIM), BF16)
    piece_out = [shape((rows, PIECE * HEAD_DIM), BF16), posts, states]

    def grads_of(pieces, first, attns, scaled, qturned):
        fresh = len(first) if first is parts else 0
        shapes = piece_out * len(pieces) + [lane_sums] * (2 if fresh else 0)
        made = run(
            partial(grad_kernel, pieces, full, fresh), unit * len(pieces) // count,
            [VMEM] * (len(first) + 2 + len(pieces)), [VMEM] * len(shapes), shapes,
            (*first, scaled, qturned, *attns),
        )
        return [made[i:i + 3] for i in range(0, 3 * len(pieces), 3)], made[3 * len(pieces):]

    made, factors = grads_of([0], parts, attns[:1], scaled2, qturned2)
    for piece in range(1, count):
        made += grads_of([piece], factors, attns[piece:piece + 1], scaled2, qturned2)[0]
    gs2, posts2, gsends = zip(*made)
    gextras = [nearby(gsend, True) for gsend in gsends]
    made = grads_of(list(range(count)), factors, attns[count:], scaled1, qturned1)[0]
    gs1, posts1, gkeeps = zip(*made)

    first_grads = []

    def local_of(second, *args):
        def work(messages):
            if second:
                specs, scratch = [HBM] + [VMEM] * 3, [pltpu.VMEM((rows, half), BF16), sems]
                shapes = [whole, shape((rows // chunks, half), BF16), wide, wide]
            else:
                specs, scratch, shapes = [VMEM] * 3, [], [thin, wide, wide]
            made = run(
                partial(local_kernel, count, second), 9 * unit,
                [VMEM] * (len(args) + len(first_grads)) + [ANYWHERE] * len(messages),
                specs, shapes, (*args, *first_grads, *messages), scratch,
            )
            first_grads.append(made[0])
            return made

        return work

    piece_thin = shape((rows, PIECE * HEAD_DIM), BF16)

    def final_of(jobs, ready=(), outs=(), fresh=0):
        plan = [item[1:] for item in ready]
        args = [leaf for job in jobs for leaf in job[2]] + [item[0] for item in ready]
        wholes = len(outs) + fresh
        kept = sum(job[1] is None for job in jobs)
        buffers = [pltpu.VMEM(piece_thin.shape, BF16)] * (2 * (len(jobs) - kept))
        return run(
            partial(final_kernel, [job[:2] for job in jobs], wholes, plan),
            2 * unit * len(jobs) // count, [VMEM] * len(args) + [HBM] * len(outs),
            [HBM] * wholes + [VMEM] * (2 * kept), [whole] * wholes + [piece_thin] * (2 * kept),
            (*args, *outs),
            buffers + [pltpu.SemaphoreType.DMA((len(plan) + 2 * chunks * (len(jobs) - kept) + 1,))],
            {len(args) + i: i for i in range(len(outs))},
        )

    gstate1, gstate2, made, early = scan_states(
        gkeeps, gextras, True,
        [
            local_of(0, q1, k1, v1, turned1, pre1, *state1, *gs1, *posts1),
            local_of(1, q2, k2, v2, turned2, pre2, *state2, *gs2, *posts2),
        ],
        lambda state, made: final_of([(0, None, (k1, v1, *made[0][1:], state))]),
    )
    near = (k1, v1, *made[0][1:])
    qgrad, tail, *far = made[1]
    far = (k2, v2, *far)
    every = slice(0, rows)
    jobs = [(i, (False, half, i), (*near, gstate1[i])) for i in range(1, count)]
    jobs += [(i, None, (*far, gstate2[i])) for i in range(count - 1)]
    ready = [(early[i], i, every, (False, half, 0)) for i in range(2)]
    kgrad, vgrad, *done = final_of(jobs, ready, (), 2)
    jobs = [(count - 1, (True, half, count - 1), (*far, gstate2[-1]))]
    ready = [(done[i], 1 + i % 2, every, (True, half, i // 2)) for i in range(len(done))]
    ready.append((tail, 0, chunks_of(rows)[-1], (True, half)))
    qgrad, kgrad, vgrad = final_of(jobs, ready, (qgrad, kgrad, vgrad))
    return qgrad, kgrad, vgrad


def solution(mesh):
    spec = P("seq", "head")
    return jax.shard_map(
        shards,
        mesh=mesh,
        in_specs=(spec, spec, spec, spec, P("head")),
        out_specs=(spec, spec, spec),
        check_vma=False,
    )
```
